32 devices in a mesh: dp: 4 (over y, x), head: 8 (over z, core).
Axes of the slice: x: 2, y: 2, z: 4, core: 2. Of those that a mesh axis runs over, the one named last changes fastest.
Arguments:
- tokens: bfloat16 [8192, 2048], P(('dp', 'head')), may hold values from -6 to 6
- keep_mask: int32 [8192], P('dp'), may hold values 0 or 1
- seq_lengths: int32 [4, 3], P('dp'), may hold values from 32 to 1984, as said below
- attn_gain: float32 [2048], replicated, may hold values from 0.5 to 1.5
- in_weight: bfloat16 [2048, 2560], P(None, 'head'), may hold values from -0.125 to 0.125
- out_weight: bfloat16 [2048, 2048], P('head'), may hold values from -2 to 2
- ffn_gain: float32 [2048], replicated, may hold values from 0.5 to 1.5
- gate_weight: bfloat16 [2048, 5632], P('dp', 'head'), may hold values from -0.125 to 0.125
- up_weight: bfloat16 [2048, 5632], P('dp', 'head'), may hold values from -0.125 to 0.125
- down_weight: bfloat16 [5632, 2048], P('head', 'dp'), may hold values from -0.078125 to 0.078125
- out_grad: bfloat16 [8192, 2048], P(('dp', 'head')), may hold values from -6 to 6
Outputs:
- output: bfloat16 [8192, 2048], P(('dp', 'head'))
- in_grad: float32 [8192, 2048], P(('dp', 'head'))
- attn_gain_grad: float32 [2048], replicated
- in_weight_grad: float32 [2048, 2560], P(None, 'head')
- out_weight_grad: float32 [2048, 2048], P('head')
- ffn_gain_grad: float32 [2048], replicated
- gate_grad: float32 [2048, 5632], P('dp', 'head')
- up_grad: float32 [2048, 5632], P('dp', 'head')
- down_grad: float32 [5632, 2048], P('head', 'dp')
The draws below stay inside these ranges and needn't reach their ends.
Inputs may be any that keep to these rules, and one draw needn't show every extreme that they name: `seq_lengths`: each row sums to 2048; one sequence of each group, at a slot drawn from the seed, holds all but at most 255 of the group's tokens.
All inputs are finite; a program needn't handle non-finite values. No bound on the sum of `keep_mask` on one device may be relied on, other than what follows from the above.
Results may differ from the reference program's by a relative error of at most 0.023.
Values may be sent and summed in bfloat16 or wider, within the bound.
No kernel may reach another device: no remote copies, remote signals or barrier semaphores. Data moves between devices by JAX's collectives and lax.ppermute only.
A program may use at most 256 MiB of HBM per device.

```python
import jax
import jax.numpy as jnp
from jax import lax

D = 2048
HEADS = 16
FD = 16
VD = 128
FF = 5632
TOK_DEV = 256
NSEQ = 3
GROUP_TOK = 2048
GROUPS = 4
TOKENS = 8192
N_HEAD = 8


def draw_seq_lengths(key, part):
    key = jax.random.fold_in(key, 11)
    short_key, slot_key = jax.random.split(key)
    shorter = jax.random.randint(short_key, (GROUPS, NSEQ), max(1, TOK_DEV // 8), (TOK_DEV - 1) // (NSEQ - 1) + 1)
    long_slot = jax.random.randint(slot_key, (GROUPS, 1), 0, NSEQ)
    is_long = jnp.arange(NSEQ, dtype=jnp.int32)[None, :] == long_slot
    shorter = jnp.where(is_long, 0, shorter)
    remainder = GROUP_TOK - jnp.sum(shorter, axis=1, keepdims=True)
    return jnp.where(is_long, remainder, shorter).astype(jnp.int32)


def plant(values, key, least, largest):
    dims = values.shape
    index_at = [jax.random.randint(jax.random.fold_in(key, axis), (), 0, dims[axis]) for axis in range(len(dims))]
    values = values.at[tuple(index_at)].set(least)
    longest = dims.index(max(dims))
    index_at[longest] = (index_at[longest] + 1) % dims[longest]
    return values.at[tuple(index_at)].set(largest)


def shard_levels(rng, extent, cuts, low, largest):
    gain, own = 1.0, jax.random.fold_in(rng, 6)
    for dim, shards_of in cuts:
        draws = jnp.exp(jax.random.uniform(jax.random.fold_in(own, dim), (shards_of,), jnp.float32, low / len(cuts), largest / len(cuts)))
        gain = gain * jnp.repeat(draws, extent[dim] // shards_of).reshape([-1 if axis == dim else 1 for axis in range(len(extent))])
    return gain


def noise(stream_key, shape, width, reach, shards=(), kind=jnp.bfloat16):
    gain = shard_levels(stream_key, shape, shards, -0.22, 0.18) if shards else 1.0
    entries = jax.random.normal(stream_key, shape, jnp.float32) * width * gain
    return jnp.minimum(jnp.maximum(entries, -reach), reach).astype(kind)


def setup_inputs(seed: int = 0) -> dict:
    splits = jax.random.split(jax.random.key(seed), 12)
    return {
        "tokens": noise(splits[0], (TOKENS, D), 1.0, 6.0, ((0, 32),)),
        "keep_mask": plant((jax.random.randint(splits[1], (TOKENS,), 0, 8) < 7).astype(jnp.int32), jax.random.fold_in(splits[1], 1), 0, 1),
        "seq_lengths": draw_seq_lengths(jax.random.fold_in(splits[11], 71), 0),
        "attn_gain": jnp.clip(1.0 + 0.1 * jax.random.normal(splits[3], (D,), jnp.float32), 0.5, 1.5),
        "in_weight": noise(splits[4], (D, HEADS * (2 * FD + VD)), D ** -0.5, 0.125, ((1, 8),)),
        "out_weight": noise(splits[5], (HEADS * VD, D), (max(1, D // 256)) ** -0.5, 2.0, ((0, 8),)),
        "ffn_gain": jnp.clip(1.0 + 0.1 * jax.random.normal(splits[6], (D,), jnp.float32), 0.5, 1.5),
        "gate_weight": noise(splits[7], (D, FF), D ** -0.5, 0.125, ((0, 4), (1, 8))),
        "up_weight": noise(splits[8], (D, FF), D ** -0.5, 0.125, ((0, 4), (1, 8))),
        "down_weight": noise(splits[9], (FF, D), FF ** -0.5, 0.078125, ((0, 8), (1, 4))),
        "out_grad": noise(splits[10], (TOKENS, D), 1.0, 6.0, ((0, 32),)),
    }


highest = lax.Precision.HIGHEST

@jax.custom_vjp
def low(v):
    return lax.optimization_barrier(v.astype(jnp.bfloat16)).astype(jnp.float32)

@jax.custom_vjp
def low_back(v):
    return v

def low_keep(v):
    return (low(v), None)

def low_pass(kept, grad):
    return (grad,)

def back_keep(v):
    return (v, None)

def back_low(kept, grad):
    return (low(grad),)
low.defvjp(low_keep, low_pass)
low_back.defvjp(back_keep, back_low)

def norm_rows(values, gain_vec):
    inv_scale = lax.rsqrt(lax.optimization_barrier(jnp.mean(values * values, axis=-1, keepdims=True)) + 1e-05)
    return values * inv_scale * gain_vec

def taylor_attention(queries, key_in, value_in, segment, keep_row):
    total_rows = queries.shape[0]
    block_rows = min(512, total_rows)
    positions = jnp.arange(total_rows, dtype=jnp.int32)

    def one_block(block_index):
        begin_row = block_index * block_rows
        query_block = lax.dynamic_slice_in_dim(queries, begin_row, block_rows, 0)
        seg_block = lax.dynamic_slice_in_dim(segment, begin_row, block_rows, 0)
        keep_block = lax.dynamic_slice_in_dim(keep_row, begin_row, block_rows, 0)
        pos_block = begin_row + jnp.arange(block_rows, dtype=jnp.int32)
        inner_prod = jnp.dot(query_block, key_in.T, precision=highest) * 0.25
        kernel = 1.0 + inner_prod + 0.5 * inner_prod * inner_prod
        allowed = (pos_block[:, None] >= positions[None, :]) & (seg_block[:, None] == segment[None, :])
        weights = jnp.where(allowed, kernel * keep_row[None, :], 0.0)
        numerator = jnp.dot(weights, value_in, precision=highest)
        denominator = lax.optimization_barrier(jnp.sum(weights, axis=1)) + 1.0 - keep_block
        return keep_block[:, None] * numerator / denominator[:, None]
    blocks_out = lax.map(jax.checkpoint(one_block), jnp.arange(total_rows // block_rows, dtype=jnp.int32))
    return blocks_out.reshape(total_rows, value_in.shape[1])

def group_forward(tokens_wide, params, segment, keep_row):
    attn_gain, in_weight, out_weight, ffn_gain, gate_weight, up_weight, down_weight = params
    total_rows = tokens_wide.shape[0]
    heads_local = HEADS // N_HEAD
    head_width = 2 * FD + VD
    normed = low(norm_rows(tokens_wide, attn_gain))
    mixed = jnp.zeros((total_rows, D), jnp.float32)
    for device_index in range(N_HEAD):
        col_low = device_index * heads_local * head_width
        local_in = low_back(normed)
        projected = jnp.dot(local_in, in_weight[:, col_low:col_low + heads_local * head_width], precision=highest)
        projected = low_back(low(projected))
        per_head = projected.reshape(total_rows, heads_local, head_width).transpose(1, 0, 2)

        def head_fn(head_cols):
            return taylor_attention(head_cols[:, :FD], head_cols[:, FD:2 * FD], head_cols[:, 2 * FD:], segment, keep_row)
        head_out = lax.map(head_fn, per_head)
        attended = low(head_out.transpose(1, 0, 2).reshape(total_rows, heads_local * VD))
        row_low = device_index * heads_local * VD
        mixed = mixed + low(jnp.dot(attended, out_weight[row_low:row_low + heads_local * VD], precision=highest))
    mixed = low_back(mixed)
    middle = tokens_wide + mixed
    normed_two = low(norm_rows(middle, ffn_gain))
    ffn_local = FF // N_HEAD
    branch_sum = jnp.zeros((total_rows, D), jnp.float32)
    for device_index in range(N_HEAD):
        unit_low = device_index * ffn_local
        local_in = low_back(normed_two)
        gate_pre = low_back(jnp.dot(local_in, gate_weight[:, unit_low:unit_low + ffn_local], precision=highest))
        up_pre = low_back(jnp.dot(local_in, up_weight[:, unit_low:unit_low + ffn_local], precision=highest))
        hidden = low(jax.nn.silu(gate_pre) * up_pre)
        branch_sum = branch_sum + low(jnp.dot(hidden, down_weight[unit_low:unit_low + ffn_local], precision=highest))
    return middle + branch_sum

def reference(tokens, keep_mask, seq_lengths, attn_gain, in_weight, out_weight, ffn_gain, gate_weight, up_weight, down_weight, out_grad):
    params = (attn_gain.astype(jnp.float32), in_weight.astype(jnp.float32), out_weight.astype(jnp.float32), ffn_gain.astype(jnp.float32), gate_weight.astype(jnp.float32), up_weight.astype(jnp.float32), down_weight.astype(jnp.float32))
    token_groups = tokens.astype(jnp.float32).reshape(GROUPS, GROUP_TOK, D)
    grad_groups = out_grad.astype(jnp.float32).reshape(GROUPS, GROUP_TOK, D)
    keep_groups = keep_mask.astype(jnp.float32).reshape(GROUPS, GROUP_TOK)
    positions = jnp.arange(GROUP_TOK, dtype=jnp.int32)

    def one_group(grad_carry, inputs):
        group_tokens, group_keep, group_lengths, group_grad = inputs
        ends = jnp.cumsum(group_lengths).astype(jnp.int32)
        segment = lax.optimization_barrier(jnp.sum((positions[:, None] >= ends[None, :]).astype(jnp.int32), axis=1))

        def forward_fn(tokens_wide, weights):
            return group_forward(tokens_wide, weights, segment, group_keep)
        result, pullback = jax.vjp(forward_fn, group_tokens, params)
        token_grad, weight_grads = pullback(group_grad)
        new_carry = jax.tree.map(lambda left, right: left + right, grad_carry, weight_grads)
        return (new_carry, (result.astype(jnp.bfloat16), token_grad))
    start_carry = jax.tree.map(jnp.zeros_like, params)
    grads, (outputs, token_grads) = lax.scan(one_group, start_carry, (token_groups, keep_groups, seq_lengths, grad_groups))
    return (outputs.reshape(TOKENS, D), token_grads.reshape(TOKENS, D), grads[0], grads[1], grads[2], grads[3], grads[4], grads[5], grads[6])
```

```python
import functools
import jax
import jax.numpy as jnp
from jax import lax
from jax.experimental import pallas as pl
from jax.experimental.pallas import tpu as pltpu
from jax.sharding import PartitionSpec as P

FD = 16
VD = 128
LANES = 128
epsilon = 1e-05
NT = (((1,), (1,)), ((), ()))
TN = (((0,), (0,)), ((), ()))


def head_lanes(block, rows, head, offset):
    lane = lax.broadcasted_iota(jnp.int32, (rows, LANES), 1)
    low = offset + head * FD
    return jnp.where((lane >= low) & (lane < low + FD), block, 0.0)


def segment_start(ends_ref, positions):
    start = jnp.zeros_like(positions)
    for slot in range(ends_ref.shape[0]):
        end = ends_ref[slot]
        start = jnp.where(positions >= end, jnp.maximum(start, end), start)
    return start


def attend_kernel(heads, rows, ends_ref, projected_ref, keep_ref, y_ref, inv_ref, att_ref, key_s, value_s):
    step = pl.program_id(0)
    own = pl.ds(step * rows, rows)
    keep = keep_ref[own, :]
    packed = projected_ref[own, heads * VD :].astype(jnp.float32)
    key_s[own, :] = pltpu.roll(packed, LANES - heads * FD, 1).astype(jnp.bfloat16)
    lane = lax.broadcasted_iota(jnp.int32, (rows, LANES), 1)
    ones = jnp.where(lane < 2, keep, 0.0).astype(jnp.bfloat16)
    for head in range(heads):
        value_s[head, own, :VD] = (
            projected_ref[own, head * VD : (head + 1) * VD].astype(jnp.float32) * keep
        ).astype(jnp.bfloat16)
        value_s[head, own, VD:] = ones
    queries = [(head_lanes(packed, rows, head, 0) * 0.25).astype(jnp.bfloat16) for head in range(heads)]
    row = step * rows + lax.broadcasted_iota(jnp.int32, (rows, 1), 0)
    start = segment_start(ends_ref, row)
    column = lax.broadcasted_iota(jnp.int32, (rows, rows), 1)

    def tile(block, totals, diagonal):
        at = pl.ds(pl.multiple_of(block * rows, rows), rows)
        allowed = column >= start - block * rows
        if diagonal:
            allowed &= column <= lax.broadcasted_iota(jnp.int32, (rows, rows), 0)
        keys = key_s[at, :]
        added = []
        for head in range(heads):
            inner = lax.dot_general(queries[head], keys, NT, preferred_element_type=jnp.float32)
            weights = jnp.where(allowed, (inner * 0.5 + 1.0) * inner + 1.0, 0.0).astype(jnp.bfloat16)
            added.append(
                totals[head]
                + jnp.dot(weights, value_s[head, at, :], preferred_element_type=jnp.float32)
            )
        return tuple(added)

    totals = tuple(jnp.zeros((rows, 2 * VD), jnp.float32) for _ in range(heads))
    totals = lax.fori_loop(0, step, lambda block, held: tile(block, held, False), totals)
    totals = tile(step, totals, True)
    inverses = jnp.zeros((rows, LANES), jnp.float32)
    for head in range(heads):
        inverse = 1.0 / (totals[head][:, VD : VD + 1] + 1.0 - keep)
        y = totals[head][:, :VD] * (keep * inverse)
        y_ref[:, head * VD : (head + 1) * VD] = y
        att_ref[:, head * VD : (head + 1) * VD] = y.astype(jnp.bfloat16)
        inverses = jnp.where(lane == head, inverse, inverses)
    inv_ref[...] = inverses


def attend(projected, keep, ends, heads):
    total = projected.shape[0]
    rows = min(512, total)
    width = projected.shape[1]
    pairs = total * (total + rows) // 2 * heads
    return pl.pallas_call(
        functools.partial(attend_kernel, heads, rows),
        grid_spec=pltpu.PrefetchScalarGridSpec(
            num_scalar_prefetch=1,
            grid=(total // rows,),
            in_specs=[
                pl.BlockSpec((total, width), lambda i, e: (0, 0)),
                pl.BlockSpec((total, 1), lambda i, e: (0, 0)),
            ],
            out_specs=[
                pl.BlockSpec((rows, heads * VD), lambda i, e: (i, 0)),
                pl.BlockSpec((rows, LANES), lambda i, e: (i, 0)),
                pl.BlockSpec((rows, heads * VD), lambda i, e: (i, 0)),
            ],
            scratch_shapes=[
                pltpu.VMEM((total, LANES), jnp.bfloat16),
                pltpu.VMEM((heads, total, 2 * VD), jnp.bfloat16),
            ],
        ),
        out_shape=[
            jax.ShapeDtypeStruct((total, heads * VD), jnp.float32),
            jax.ShapeDtypeStruct((total, LANES), jnp.float32),
            jax.ShapeDtypeStruct((total, heads * VD), jnp.bfloat16),
        ],
        compiler_params=pltpu.CompilerParams(
            dimension_semantics=("arbitrary",), vmem_limit_bytes=48 * 1024 * 1024
        ),
        cost_estimate=pl.CostEstimate(flops=pairs * 1024, bytes_accessed=8 << 20, transcendentals=0),
    )(ends, projected, keep)


def attend_back_kernel(
    heads, rows, ends_ref, projected_ref, keep_ref, y_ref, inv_ref, grad_ref, out_ref,
    key_s, query_s, value_s, error_s, dquery_s,
):
    step = pl.program_id(0)
    blocks = pl.num_programs(0)
    lane = lax.broadcasted_iota(jnp.int32, (rows, LANES), 1)

    @pl.when(step == 0)
    def _():
        dquery_s[...] = jnp.zeros_like(dquery_s)

        def fill(block, nothing):
            at = pl.ds(pl.multiple_of(block * rows, rows), rows)
            keep = keep_ref[at, :]
            packed = projected_ref[at, heads * VD :].astype(jnp.float32)
            rolled = pltpu.roll(packed, LANES - heads * FD, 1)
            ones = jnp.where(lane < 2, keep, 0.0).astype(jnp.bfloat16)
            inverses = inv_ref[at, :]
            for head in range(heads):
                columns = slice(head * VD, (head + 1) * VD)
                key_s[head, at, :] = head_lanes(rolled, rows, head, 0).astype(jnp.bfloat16)
                query_s[head, at, :] = (head_lanes(packed, rows, head, 0) * 0.25).astype(jnp.bfloat16)
                value_s[head, at, :VD] = (projected_ref[at, columns].astype(jnp.float32) * keep).astype(jnp.bfloat16)
                value_s[head, at, VD:] = ones
                inverse = inverses[:, head : head + 1]
                grad = grad_ref[at, columns].astype(jnp.float32)
                error_s[head, at, :VD] = (grad * (keep * inverse)).astype(jnp.bfloat16)
                offset = -jnp.sum(grad * y_ref[at, columns], axis=1, keepdims=True) * inverse
                high = offset.astype(jnp.bfloat16).astype(jnp.float32)
                error_s[head, at, VD:] = jnp.where(
                    lane == 0, high, jnp.where(lane == 1, offset - high, 0.0)
                ).astype(jnp.bfloat16)
            return nothing

        lax.fori_loop(0, blocks, fill, 0)

    own = pl.ds(pl.multiple_of(step * rows, rows), rows)
    row = lax.broadcasted_iota(jnp.int32, (rows, rows), 0)

    def tile(block, totals, diagonal):
        at = pl.ds(pl.multiple_of(block * rows, rows), rows)
        column = block * rows + lax.broadcasted_iota(jnp.int32, (1, rows), 1)
        allowed = row >= segment_start(ends_ref, column) - step * rows
        if diagonal:
            allowed &= row <= lax.broadcasted_iota(jnp.int32, (rows, rows), 1)
        dkey, dvalues = totals
        added = []
        for head in range(heads):
            query = query_s[head, at, :]
            error = error_s[head, at, :]
            keys = key_s[head, own, :]
            inner = lax.dot_general(keys, query, NT, preferred_element_type=jnp.float32)
            dweight = lax.dot_general(value_s[head, own, :], error, NT, preferred_element_type=jnp.float32)
            slope = inner + 1.0
            weights = jnp.where(allowed, (slope * slope + 1.0) * 0.5, 0.0).astype(jnp.bfloat16)
            dinner = jnp.where(allowed, slope * dweight, 0.0).astype(jnp.bfloat16)
            added.append(
                dvalues[head] + jnp.dot(weights, error[:, :VD], preferred_element_type=jnp.float32)
            )
            dkey = dkey + jnp.dot(dinner, query, preferred_element_type=jnp.float32)
            dquery_s[at, :] += lax.dot_general(dinner, keys, TN, preferred_element_type=jnp.float32)
        return dkey, tuple(added)

    totals = (
        jnp.zeros((rows, LANES), jnp.float32),
        tuple(jnp.zeros((rows, VD), jnp.float32) for _ in range(heads)),
    )
    totals = tile(step, totals, True)
    dkey, dvalues = lax.fori_loop(step + 1, blocks, lambda block, held: tile(block, held, False), totals)
    keep = keep_ref[own, :]
    for head in range(heads):
        out_ref[:, head * VD : (head + 1) * VD] = (dvalues[head] * keep).astype(jnp.bfloat16)
    out_ref[:, heads * VD :] = (
        dquery_s[own, :] * 0.25 + pltpu.roll(dkey, heads * FD, 1)
    ).astype(jnp.bfloat16)


def attend_back(projected, keep, ends, y, inverses, grad, heads):
    total = projected.shape[0]
    rows = min(512, total)
    width = projected.shape[1]
    pairs = total * (total + rows) // 2 * heads
    whole = lambda columns: pl.BlockSpec((total, columns), lambda i, e: (0, 0))
    return pl.pallas_call(
        functools.partial(attend_back_kernel, heads, rows),
        grid_spec=pltpu.PrefetchScalarGridSpec(
            num_scalar_prefetch=1,
            grid=(total // rows,),
            in_specs=[whole(width), whole(1), whole(heads * VD), whole(LANES), whole(heads * VD)],
            out_specs=pl.BlockSpec((rows, width), lambda i, e: (i, 0)),
            scratch_shapes=[
                pltpu.VMEM((heads, total, LANES), jnp.bfloat16),
                pltpu.VMEM((heads, total, LANES), jnp.bfloat16),
                pltpu.VMEM((heads, total, 2 * VD), jnp.bfloat16),
                pltpu.VMEM((heads, total, 2 * VD), jnp.bfloat16),
                pltpu.VMEM((total, LANES), jnp.float32),
            ],
        ),
        out_shape=jax.ShapeDtypeStruct((total, width), jnp.bfloat16),
        compiler_params=pltpu.CompilerParams(
            dimension_semantics=("arbitrary",), vmem_limit_bytes=56 * 1024 * 1024
        ),
        cost_estimate=pl.CostEstimate(flops=pairs * 2560, bytes_accessed=12 << 20, transcendentals=0),
    )(ends, projected, keep, y, inverses, grad)


def pack_columns(weight, heads):
    depth = weight.shape[0]
    per_head = weight.reshape(depth, heads, 2 * FD + VD)
    return jnp.concatenate(
        [
            per_head[:, :, 2 * FD :].reshape(depth, heads * VD),
            per_head[:, :, :FD].reshape(depth, heads * FD),
            per_head[:, :, FD : 2 * FD].reshape(depth, heads * FD),
            jnp.zeros((depth, LANES - 2 * heads * FD), weight.dtype),
        ],
        axis=1,
    )


def unpack_columns(packed, heads):
    depth = packed.shape[0]
    wide, narrow = heads * VD, heads * FD
    return jnp.concatenate(
        [
            packed[:, wide : wide + narrow].reshape(depth, heads, FD),
            packed[:, wide + narrow : wide + 2 * narrow].reshape(depth, heads, FD),
            packed[:, :wide].reshape(depth, heads, VD),
        ],
        axis=2,
    ).reshape(depth, heads * (2 * FD + VD))


def inv_root_mean(values):
    return lax.rsqrt(jnp.mean(values * values, axis=1, keepdims=True) + epsilon)


def per_device(
    tokens,
    keep_mask,
    seq_lengths,
    attn_gain,
    in_weight,
    out_weight,
    ffn_gain,
    gate_weight,
    up_weight,
    down_weight,
    out_grad,
):
    group = lax.all_gather(tokens, "head", axis=0, tiled=True)
    group_wide = group.astype(jnp.float32)
    normed = (group_wide * inv_root_mean(group_wide) * attn_gain).astype(jnp.bfloat16)
    heads_here = in_weight.shape[1] // (2 * FD + VD)
    in_packed = pack_columns(in_weight, heads_here)
    projected = jnp.dot(normed, in_packed, preferred_element_type=jnp.float32).astype(jnp.bfloat16)
    ends = jnp.cumsum(seq_lengths[0])
    keep_column = keep_mask.astype(jnp.float32)[:, None]
    attended_wide, inverses, attended = attend(projected, keep_column, ends, heads_here)
    tokens_wide = tokens.astype(jnp.float32)
    middle = tokens_wide + lax.psum_scatter(
        jnp.dot(attended, out_weight, preferred_element_type=jnp.float32).astype(jnp.bfloat16),
        "head",
        scatter_dimension=0,
        tiled=True,
    ).astype(jnp.float32)
    inv_two = inv_root_mean(middle)
    normed_two = lax.all_gather(
        (middle * inv_two * ffn_gain).astype(jnp.bfloat16), "head", axis=0, tiled=True
    )
    gate_all, up_all, down_all = (
        lax.all_gather(gate_weight, "dp", axis=0, tiled=True),
        lax.all_gather(up_weight, "dp", axis=0, tiled=True),
        lax.all_gather(down_weight, "dp", axis=1, tiled=True),
    )
    gate_pre = jnp.dot(normed_two, gate_all, preferred_element_type=jnp.float32)
    up_pre = jnp.dot(normed_two, up_all, preferred_element_type=jnp.float32)
    sigmoid_gate = jax.nn.sigmoid(gate_pre)
    silu_gate = gate_pre * sigmoid_gate
    hidden = (silu_gate * up_pre).astype(jnp.bfloat16)
    output = (
        middle
        + lax.psum_scatter(
            jnp.dot(hidden, down_all, preferred_element_type=jnp.float32).astype(jnp.bfloat16),
            "head",
            scatter_dimension=0,
            tiled=True,
        ).astype(jnp.float32)
    ).astype(jnp.bfloat16)
    grad_group = lax.all_gather(out_grad, "head", axis=0, tiled=True)
    d_hidden = jnp.dot(grad_group, down_all.T, preferred_element_type=jnp.float32)
    d_gate = (d_hidden * up_pre * sigmoid_gate * (1.0 + gate_pre * (1.0 - sigmoid_gate))).astype(
        jnp.bfloat16
    )
    d_up = (d_hidden * silu_gate).astype(jnp.bfloat16)
    down_grad = jnp.dot(hidden.T, grad_group, preferred_element_type=jnp.float32)
    gate_grad = jnp.dot(normed_two.T, d_gate, preferred_element_type=jnp.float32)
    up_grad = jnp.dot(normed_two.T, d_up, preferred_element_type=jnp.float32)
    d_normed_two = lax.psum_scatter(
        (
            jnp.dot(d_gate, gate_all.T, preferred_element_type=jnp.float32)
            + jnp.dot(d_up, up_all.T, preferred_element_type=jnp.float32)
        ).astype(jnp.bfloat16),
        "head",
        scatter_dimension=0,
        tiled=True,
    ).astype(jnp.float32)
    scaled_two = middle * inv_two
    error_two = d_normed_two * ffn_gain
    d_middle = out_grad.astype(jnp.float32) + inv_two * (
        error_two - scaled_two * jnp.mean(error_two * scaled_two, axis=1, keepdims=True)
    )
    ffn_gain_part = jnp.sum(d_normed_two * scaled_two, axis=0)
    d_mixed = lax.all_gather(d_middle.astype(jnp.bfloat16), "head", axis=0, tiled=True)
    d_attended = jnp.dot(d_mixed, out_weight.T, preferred_element_type=jnp.float32)
    out_weight_grad = jnp.dot(attended.T, d_mixed, preferred_element_type=jnp.float32)
    d_projected = attend_back(
        projected, keep_column, ends, attended_wide, inverses, d_attended, heads_here
    )
    in_weight_grad = jnp.dot(normed.T, d_projected, preferred_element_type=jnp.float32)
    d_normed = lax.psum_scatter(
        jnp.dot(d_projected, in_packed.T, preferred_element_type=jnp.float32).astype(jnp.bfloat16),
        "head",
        scatter_dimension=0,
        tiled=True,
    ).astype(jnp.float32)
    inv_one = inv_root_mean(tokens_wide)
    scaled_one = tokens_wide * inv_one
    error_one = d_normed * attn_gain
    in_grad = d_middle + inv_one * (
        error_one - scaled_one * jnp.mean(error_one * scaled_one, axis=1, keepdims=True)
    )
    attn_gain_part = jnp.sum(d_normed * scaled_one, axis=0)
    attn_gain_grad, ffn_gain_grad = lax.psum((attn_gain_part, ffn_gain_part), ("dp", "head"))
    in_weight_grad, out_weight_grad = (
        unpack_columns(
            lax.psum(in_weight_grad[:, : in_weight.shape[1]].astype(jnp.bfloat16), "dp"), heads_here
        ).astype(jnp.float32),
        lax.psum(out_weight_grad.astype(jnp.bfloat16), "dp").astype(jnp.float32),
    )
    gate_grad, up_grad, down_grad = (
        lax.psum_scatter(
            gate_grad.astype(jnp.bfloat16), "dp", scatter_dimension=0, tiled=True
        ).astype(jnp.float32),
        lax.psum_scatter(
            up_grad.astype(jnp.bfloat16), "dp", scatter_dimension=0, tiled=True
        ).astype(jnp.float32),
        lax.psum_scatter(
            down_grad.astype(jnp.bfloat16), "dp", scatter_dimension=1, tiled=True
        ).astype(jnp.float32),
    )
    return (
        output,
        in_grad,
        attn_gain_grad,
        in_weight_grad,
        out_weight_grad,
        ffn_gain_grad,
        gate_grad,
        up_grad,
        down_grad,
    )


def solution(mesh):
    return jax.shard_map(
        per_device,
        mesh=mesh,
        in_specs=(
            P(("dp", "head"), None),
            P("dp"),
            P("dp", None),
            P(),
            P(None, "head"),
            P("head", None),
            P(),
            P("dp", "head"),
            P("dp", "head"),
            P("head", "dp"),
            P(("dp", "head"), None),
        ),
        out_specs=(
            P(("dp", "head"), None),
            P(("dp", "head"), None),
            P(),
            P(None, "head"),
            P("head", None),
            P(),
            P("dp", "head"),
            P("dp", "head"),
            P("head", "dp"),
        ),
        check_vma=False,
    )
```

```python
import functools
import jax
import jax.numpy as jnp
from jax import lax
from jax.experimental import pallas as pl
from jax.experimental.pallas import tpu as pltpu
from jax.sharding import PartitionSpec as P

FD = 16
VD = 128
LANES = 128
epsilon = 1e-05
NT = (((1,), (1,)), ((), ()))
TN = (((0,), (0,)), ((), ()))


def head_lanes(block, rows, head, offset):
    lane = lax.broadcasted_iota(jnp.int32, (rows, LANES), 1)
    low = offset + head * FD
    return jnp.where((lane >= low) & (lane < low + FD), block, 0.0)


def segment_start(ends_ref, positions):
    start = jnp.zeros_like(positions)
    for slot in range(ends_ref.shape[0]):
        end = ends_ref[slot]
        start = jnp.where(positions >= end, jnp.maximum(start, end), start)
    return start


def attend_kernel(heads, rows, ends_ref, projected_ref, keep_ref, y_ref, inv_ref, att_ref, key_s, value_s):
    step = pl.program_id(0)
    own = pl.ds(step * rows, rows)
    keep = keep_ref[own, :]
    packed = projected_ref[own, heads * VD :].astype(jnp.float32)
    key_s[own, :] = pltpu.roll(packed, LANES - heads * FD, 1).astype(jnp.bfloat16)
    lane = lax.broadcasted_iota(jnp.int32, (rows, LANES), 1)
    ones = jnp.where(lane < 2, keep, 0.0).astype(jnp.bfloat16)
    for head in range(heads):
        value_s[head, own, :VD] = (
            projected_ref[own, head * VD : (head + 1) * VD].astype(jnp.float32) * keep
        ).astype(jnp.bfloat16)
        value_s[head, own, VD:] = ones
    queries = [(head_lanes(packed, rows, head, 0) * 0.25).astype(jnp.bfloat16) for head in range(heads)]
    row = step * rows + lax.broadcasted_iota(jnp.int32, (rows, 1), 0)
    start = segment_start(ends_ref, row)
    column = lax.broadcasted_iota(jnp.int32, (rows, rows), 1)

    def tile(block, totals, diagonal):
        at = pl.ds(pl.multiple_of(block * rows, rows), rows)
        allowed = column >= start - block * rows
        if diagonal:
            allowed &= column <= lax.broadcasted_iota(jnp.int32, (rows, rows), 0)
        keys = key_s[at, :]
        added = []
        for head in range(heads):
            inner = lax.dot_general(queries[head], keys, NT, preferred_element_type=jnp.float32)
            weights = jnp.where(allowed, (inner * 0.5 + 1.0) * inner + 1.0, 0.0).astype(jnp.bfloat16)
            added.append(
                totals[head]
                + jnp.dot(weights, value_s[head, at, :], preferred_element_type=jnp.float32)
            )
        return tuple(added)

    totals = tuple(jnp.zeros((rows, 2 * VD), jnp.float32) for _ in range(heads))
    totals = lax.fori_loop(0, step, lambda block, held: tile(block, held, False), totals)
    totals = tile(step, totals, True)
    inverses = jnp.zeros((rows, LANES), jnp.float32)
    for head in range(heads):
        inverse = 1.0 / (totals[head][:, VD : VD + 1] + 1.0 - keep)
        y = totals[head][:, :VD] * (keep * inverse)
        y_ref[:, head * VD : (head + 1) * VD] = y
        att_ref[:, head * VD : (head + 1) * VD] = y.astype(jnp.bfloat16)
        inverses = jnp.where(lane == head, inverse, inverses)
    inv_ref[...] = inverses


def attend(projected, keep, ends, heads):
    total = projected.shape[0]
    rows = min(512, total)
    width = projected.shape[1]
    pairs = total * (total + rows) // 2 * heads
    return pl.pallas_call(
        functools.partial(attend_kernel, heads, rows),
        grid_spec=pltpu.PrefetchScalarGridSpec(
            num_scalar_prefetch=1,
            grid=(total // rows,),
            in_specs=[
                pl.BlockSpec((total, width), lambda i, e: (0, 0)),
                pl.BlockSpec((total, 1), lambda i, e: (0, 0)),
            ],
            out_specs=[
                pl.BlockSpec((rows, heads * VD), lambda i, e: (i, 0)),
                pl.BlockSpec((rows, LANES), lambda i, e: (i, 0)),
                pl.BlockSpec((rows, heads * VD), lambda i, e: (i, 0)),
            ],
            scratch_shapes=[
                pltpu.VMEM((total, LANES), jnp.bfloat16),
                pltpu.VMEM((heads, total, 2 * VD), jnp.bfloat16),
            ],
        ),
        out_shape=[
            jax.ShapeDtypeStruct((total, heads * VD), jnp.float32),
            jax.ShapeDtypeStruct((total, LANES), jnp.float32),
            jax.ShapeDtypeStruct((total, heads * VD), jnp.bfloat16),
        ],
        compiler_params=pltpu.CompilerParams(
            dimension_semantics=("arbitrary",), vmem_limit_bytes=48 * 1024 * 1024
        ),
        cost_estimate=pl.CostEstimate(flops=pairs * 1024, bytes_accessed=8 << 20, transcendentals=0),
    )(ends, projected, keep)


def attend_back_kernel(
    heads, rows, ends_ref, projected_ref, keep_ref, y_ref, inv_ref, grad_ref, out_ref,
    key_s, query_s, value_s, error_s, dquery_s,
):
    step = pl.program_id(0)
    blocks = pl.num_programs(0)
    lane = lax.broadcasted_iota(jnp.int32, (rows, LANES), 1)

    @pl.when(step == 0)
    def _():
        dquery_s[...] = jnp.zeros_like(dquery_s)

        def fill(block, nothing):
            at = pl.ds(pl.multiple_of(block * rows, rows), rows)
            keep = keep_ref[at, :]
            packed = projected_ref[at, heads * VD :].astype(jnp.float32)
            rolled = pltpu.roll(packed, LANES - heads * FD, 1)
            ones = jnp.where(lane < 2, keep, 0.0).astype(jnp.bfloat16)
            inverses = inv_ref[at, :]
            for head in range(heads):
                columns = slice(head * VD, (head + 1) * VD)
                key_s[head, at, :] = head_lanes(rolled, rows, head, 0).astype(jnp.bfloat16)
                query_s[head, at, :] = (head_lanes(packed, rows, head, 0) * 0.25).astype(jnp.bfloat16)
                value_s[head, at, :VD] = (projected_ref[at, columns].astype(jnp.float32) * keep).astype(jnp.bfloat16)
                value_s[head, at, VD:] = ones
                inverse = inverses[:, head : head + 1]
                grad = grad_ref[at, columns].astype(jnp.float32)
                error_s[head, at, :VD] = (grad * (keep * inverse)).astype(jnp.bfloat16)
                offset = -jnp.sum(grad * y_ref[at, columns], axis=1, keepdims=True) * inverse
                high = offset.astype(jnp.bfloat16).astype(jnp.float32)
                error_s[head, at, VD:] = jnp.where(
                    lane == 0, high, jnp.where(lane == 1, offset - high, 0.0)
                ).astype(jnp.bfloat16)
            return nothing

        lax.fori_loop(0, blocks, fill, 0)

    own = pl.ds(pl.multiple_of(step * rows, rows), rows)
    row = lax.broadcasted_iota(jnp.int32, (rows, rows), 0)

    def tile(block, totals, diagonal):
        at = pl.ds(pl.multiple_of(block * rows, rows), rows)
        column = block * rows + lax.broadcasted_iota(jnp.int32, (1, rows), 1)
        allowed = row >= segment_start(ends_ref, column) - step * rows
        if diagonal:
            allowed &= row <= lax.broadcasted_iota(jnp.int32, (rows, rows), 1)
        dkey, dvalues = totals
        added = []
        for head in range(heads):
            query = query_s[head, at, :]
            error = error_s[head, at, :]
            keys = key_s[head, own, :]
            inner = lax.dot_general(keys, query, NT, preferred_element_type=jnp.float32)
            dweight = lax.dot_general(value_s[head, own, :], error, NT, preferred_element_type=jnp.float32)
            slope = inner + 1.0
            weights = jnp.where(allowed, (slope * slope + 1.0) * 0.5, 0.0).astype(jnp.bfloat16)
            dinner = jnp.where(allowed, slope * dweight, 0.0).astype(jnp.bfloat16)
            added.append(
                dvalues[head] + jnp.dot(weights, error[:, :VD], preferred_element_type=jnp.float32)
            )
            dkey = dkey + jnp.dot(dinner, query, preferred_element_type=jnp.float32)
            dquery_s[at, :] += lax.dot_general(dinner, keys, TN, preferred_element_type=jnp.float32)
        return dkey, tuple(added)

    totals = (
        jnp.zeros((rows, LANES), jnp.float32),
        tuple(jnp.zeros((rows, VD), jnp.float32) for _ in range(heads)),
    )
    totals = tile(step, totals, True)
    dkey, dvalues = lax.fori_loop(step + 1, blocks, lambda block, held: tile(block, held, False), totals)
    keep = keep_ref[own, :]
    for head in range(heads):
        out_ref[:, head * VD : (head + 1) * VD] = (dvalues[head] * keep).astype(jnp.bfloat16)
    out_ref[:, heads * VD :] = (
        dquery_s[own, :] * 0.25 + pltpu.roll(dkey, heads * FD, 1)
    ).astype(jnp.bfloat16)


def attend_back(projected, keep, ends, y, inverses, grad, heads):
    total = projected.shape[0]
    rows = min(512, total)
    width = projected.shape[1]
    pairs = total * (total + rows) // 2 * heads
    whole = lambda columns: pl.BlockSpec((total, columns), lambda i, e: (0, 0))
    return pl.pallas_call(
        functools.partial(attend_back_kernel, heads, rows),
        grid_spec=pltpu.PrefetchScalarGridSpec(
            num_scalar_prefetch=1,
            grid=(total // rows,),
            in_specs=[whole(width), whole(1), whole(heads * VD), whole(LANES), whole(heads * VD)],
            out_specs=pl.BlockSpec((rows, width), lambda i, e: (i, 0)),
            scratch_shapes=[
                pltpu.VMEM((heads, total, LANES), jnp.bfloat16),
                pltpu.VMEM((heads, total, LANES), jnp.bfloat16),
                pltpu.VMEM((heads, total, 2 * VD), jnp.bfloat16),
                pltpu.VMEM((heads, total, 2 * VD), jnp.bfloat16),
                pltpu.VMEM((total, LANES), jnp.float32),
            ],
        ),
        out_shape=jax.ShapeDtypeStruct((total, width), jnp.bfloat16),
        compiler_params=pltpu.CompilerParams(
            dimension_semantics=("arbitrary",), vmem_limit_bytes=56 * 1024 * 1024
        ),
        cost_estimate=pl.CostEstimate(flops=pairs * 2560, bytes_accessed=12 << 20, transcendentals=0),
    )(ends, projected, keep, y, inverses, grad)


def pack_columns(weight, heads):
    depth = weight.shape[0]
    per_head = weight.reshape(depth, heads, 2 * FD + VD)
    return jnp.concatenate(
        [
            per_head[:, :, 2 * FD :].reshape(depth, heads * VD),
            per_head[:, :, :FD].reshape(depth, heads * FD),
            per_head[:, :, FD : 2 * FD].reshape(depth, heads * FD),
        ],
        axis=1,
    )


def unpack_columns(packed, heads):
    depth = packed.shape[0]
    wide, narrow = heads * VD, heads * FD
    return jnp.concatenate(
        [
            packed[:, wide : wide + narrow].reshape(depth, heads, FD),
            packed[:, wide + narrow : wide + 2 * narrow].reshape(depth, heads, FD),
            packed[:, :wide].reshape(depth, heads, VD),
        ],
        axis=2,
    ).reshape(depth, heads * (2 * FD + VD))


def inv_root_mean(values):
    return lax.rsqrt(jnp.mean(values * values, axis=1, keepdims=True) + epsilon)


def wide(values):
    return values.astype(jnp.float32)


def low(values):
    return values.astype(jnp.bfloat16)


def pick(values, index, count, axis):
    size = values.shape[axis] // count
    if count == 2:
        first = lax.slice_in_dim(values, 0, size, axis=axis)
        second = lax.slice_in_dim(values, size, 2 * size, axis=axis)
        return jnp.where(index == 0, first, second)
    return lax.dynamic_slice_in_dim(values, index * size, size, axis)


def in_order(pieces, index, axis):
    count = len(pieces)
    if count == 1:
        return pieces[0]
    if count == 2:
        first = jnp.where(index == 0, pieces[0], pieces[1])
        second = jnp.where(index == 0, pieces[1], pieces[0])
        return jnp.concatenate([first, second], axis=axis)
    stacked = jnp.stack(pieces)
    placed = [
        lax.dynamic_index_in_dim(stacked, (index - place) % count, 0, keepdims=False)
        for place in range(count)
    ]
    return jnp.concatenate(placed, axis=axis)


class Wires:
    def __init__(self, mesh):
        self.dp, self.head = mesh.shape["dp"], mesh.shape["head"]
        self.ny, self.nz, self.nzh = self.dp // 2, self.head // 2, self.head // 4

    def place(self):
        p, h = lax.axis_index("dp"), lax.axis_index("head")
        self.p, self.h = p, h
        self.y, self.x, self.z, self.c = p // 2, p % 2, h // 2, h % 2
        self.zl, self.zh = self.z % 2, self.z // 2

    def over_x(self, values):
        return lax.ppermute(values, "dp", [(i, i ^ 1) for i in range(self.dp)])

    def over_y(self, values, shift):
        return lax.ppermute(
            values, "dp", [(i, ((i // 2 + shift) % self.ny) * 2 + i % 2) for i in range(self.dp)]
        )

    def over_core(self, values):
        return lax.ppermute(values, "head", [(i, i ^ 1) for i in range(self.head)])

    def over_zl(self, values):
        return lax.ppermute(values, "head", [(i, i ^ 2) for i in range(self.head)])

    def over_zh(self, values, shift):
        return lax.ppermute(
            values, "head", [(i, ((i // 4 + shift) % self.nzh) * 4 + i % 4) for i in range(self.head)]
        )

    def right(self, values, first, last):
        return lax.ppermute(
            values, "head", [(i, i + 2) for i in range(self.head) if first <= i // 2 <= last]
        )

    def left(self, values, first, last):
        return lax.ppermute(
            values, "head", [(i, i - 2) for i in range(self.head) if first <= i // 2 <= last]
        )

    def line_gather(self, block):
        n = self.nz
        rights, lefts = [block], [block]
        for step in range(1, n):
            rights.append(self.right(rights[-1], step - 1, n - 2))
            lefts.append(self.left(lefts[-1], 1, n - step))
        return [block] + [
            jnp.where(self.z >= s, rights[s], lefts[n - s]) for s in range(1, n)
        ]

    def line_reduce(self, parts):
        n = self.nz
        held = {s: wide(parts[s]) for s in range(n)}
        leftward, rightward = [None] * n, [None] * n
        to_left = jnp.zeros_like(held[0])
        to_right = jnp.zeros_like(held[0])
        for s in range(n - 1, 0, -1):
            to_left = wide(self.left(low(held[s] + to_left), s, n - 1))
            to_right = wide(self.right(low(held[n - s] + to_right), 0, n - 1 - s))
        return held[0] + to_left + to_right

    def square_gather(self, block):
        half = block.shape[0] // 2
        by_x, by_z = self.over_x(block), self.over_zl(block)
        corner = jnp.concatenate([self.over_zl(by_x[:half]), self.over_x(by_z[half:])], axis=0)
        mine = [block, by_x, by_z, corner]
        return [(own, self.over_core(own)) for own in mine]

    def square_reduce(self, pairs):
        sums = [low(wide(own) + wide(self.over_core(other))) for own, other in pairs]
        half = sums[0].shape[0] // 2
        to_z = self.over_x(sums[3][:half])
        to_x = self.over_zl(sums[3][half:])
        by_x = jnp.concatenate([sums[1][:half], low(wide(sums[1][half:]) + wide(to_x))], axis=0)
        by_z = jnp.concatenate([low(wide(sums[2][:half]) + wide(to_z)), sums[2][half:]], axis=0)
        return sums[0], self.over_x(by_x), self.over_zl(by_z)

    def whole_weight(self, shard):
        rows = shard.shape[0]
        part = lax.dynamic_slice_in_dim(
            shard, self.p * (shard.shape[1] // self.dp), shard.shape[1] // self.dp, 1
        )
        line = in_order([slot[None] for slot in self.line_gather(part)], self.z, 0)[None]
        line = jnp.where(
            self.x == 0,
            jnp.concatenate([line, self.over_x(line)], 0),
            jnp.concatenate([self.over_x(line), line], 0),
        )
        line = in_order([line] + [self.over_y(line, s) for s in range(1, self.ny)], self.y, 0)
        other = self.over_core(line)
        both = jnp.stack(
            [jnp.where(self.c == 0, line, other), jnp.where(self.c == 0, other, line)], axis=2
        )
        return both.reshape(self.dp, self.head * rows, shard.shape[1] // self.dp)

    def ffn_weights(self, stacked):
        own = pick(stacked, self.x, 2, 1)
        other = self.over_x(pick(stacked, 1 - self.x, 2, 1))
        pair = in_order([own, other], self.x, 2)
        pair = jnp.concatenate([pair] + [self.over_zh(pair, s) for s in range(1, self.nzh)], axis=1)
        return in_order([pair] + [self.over_y(pair, s) for s in range(1, self.ny)], self.y, 2)

    def ffn_grads(self, grad):
        total = wide(pick(grad, self.y, self.ny, 1))
        for s in range(1, self.ny):
            total = total + wide(self.over_y(low(pick(grad, (self.y + s) % self.ny, self.ny, 1)), s))
        rows = grad.shape[0] // self.nzh
        kept = total[:rows]
        for s in range(1, self.nzh):
            kept = kept + wide(self.over_zh(low(total[s * rows : (s + 1) * rows]), -s))
        own = pick(kept, self.x, 2, 1)
        other = wide(self.over_x(low(pick(kept, 1 - self.x, 2, 1))))
        return in_order([own, other], self.x, 0)

    def sum_y(self, values):
        total = wide(values)
        for s in range(1, self.ny):
            total = total + wide(self.over_y(values, s))
        return low(total)

    def sum_x(self, values):
        return low(wide(values) + wide(self.over_x(values)))

    def sum_dp(self, values):
        half = values.shape[0] // 2
        return jnp.concatenate(
            [self.sum_y(self.sum_x(values[:half])), self.sum_x(self.sum_y(values[half:]))], axis=0
        )

    def out_grads(self, grad):
        by_core = grad.reshape(self.nz, 2, *grad.shape[1:])
        other = self.over_core(pick(by_core, 1 - self.c, 2, 1)[:, 0])
        total = low(wide(pick(by_core, self.c, 2, 1)[:, 0]) + wide(other))
        mine = wide(pick(total, self.y, self.ny, 2))
        for s in range(1, self.ny):
            mine = mine + wide(self.over_y(pick(total, (self.y + s) % self.ny, self.ny, 2), s))
        mine = low(mine)
        sent = self.over_x(pick(mine, 1 - self.x, 2, 2))
        mine = low(wide(pick(mine, self.x, 2, 2)) + wide(sent))
        parts = [
            lax.dynamic_index_in_dim(mine, (self.z - s) % self.nz, 0, keepdims=False)
            for s in range(self.nz)
        ]
        part = low(self.line_reduce(parts))
        part = in_order([part, self.over_x(part)], self.x, 1)
        return in_order([part] + [self.over_y(part, s) for s in range(1, self.ny)], self.y, 1)

    def sum_all(self, values):
        values = values + self.over_core(values)
        values = values + self.over_zl(values)
        values = values + sum(self.over_zh(values, s) for s in range(1, self.nzh))
        values = values + self.over_x(values)
        return values + sum(self.over_y(values, s) for s in range(1, self.ny))


def mix_kernel(heads, attended_ref, weight_ref, tokens_ref, gain_ref, middle_ref, normed_ref):
    step = pl.program_id(0)
    width = weight_ref.shape[2]
    rows = attended_ref.shape[2]
    total = jnp.zeros((tokens_ref.shape[0], width), jnp.float32)
    for head in range(heads):
        total += jnp.dot(
            attended_ref[head],
            weight_ref[0, head * rows : (head + 1) * rows, :],
            preferred_element_type=jnp.float32,
        )
    at = pl.ds(pl.multiple_of(step * width, width), width)
    middle_ref[:, at] = total + tokens_ref[:, at].astype(jnp.float32)

    @pl.when(step == pl.num_programs(0) - 1)
    def _():
        middle = middle_ref[...]
        normed_ref[...] = (middle * inv_root_mean(middle) * gain_ref[...]).astype(jnp.bfloat16)


def mix(attended, weight, tokens, gain):
    heads, count, rows = attended.shape
    blocks, depth, width = weight.shape
    full = lambda *shape: pl.BlockSpec(shape, lambda i: (0,) * len(shape))
    return pl.pallas_call(
        functools.partial(mix_kernel, heads),
        grid=(blocks,),
        in_specs=[
            full(heads, count, rows),
            pl.BlockSpec((1, depth, width), lambda i: (i, 0, 0)),
            full(*tokens.shape),
            full(1, tokens.shape[1]),
        ],
        out_specs=[full(*tokens.shape), full(*tokens.shape)],
        out_shape=[
            jax.ShapeDtypeStruct(tokens.shape, jnp.float32),
            jax.ShapeDtypeStruct(tokens.shape, jnp.bfloat16),
        ],
        compiler_params=pltpu.CompilerParams(
            dimension_semantics=("arbitrary",), vmem_limit_bytes=40 * 1024 * 1024
        ),
        cost_estimate=pl.CostEstimate(
            flops=2 * count * heads * rows * tokens.shape[1], bytes_accessed=14 << 20, transcendentals=0
        ),
    )(attended, weight, tokens, gain)


def unmix_kernel(
    heads, a_ref, b_ref, c_ref, middle_ref, grad_ref, gain_ref, weight_ref,
    dmiddle_ref, dmixed_ref, part_ref, out_ref, total_s,
):
    step = pl.program_id(0)
    width = weight_ref.shape[2]
    rows = weight_ref.shape[1] // heads

    @pl.when(step == 0)
    def _():
        total_s[...] = jnp.zeros_like(total_s)
        middle = middle_ref[...]
        inv_two = inv_root_mean(middle)
        dnormed = wide(a_ref[...]) + wide(b_ref[...]) + wide(c_ref[...])
        scaled = middle * inv_two
        error = dnormed * gain_ref[...]
        dmiddle = wide(grad_ref[...]) + inv_two * (
            error - scaled * jnp.mean(error * scaled, axis=1, keepdims=True)
        )
        part_ref[...] = jnp.sum(dnormed * scaled, axis=0, keepdims=True)
        dmiddle_ref[...] = dmiddle
        dmixed_ref[...] = dmiddle.astype(jnp.bfloat16)

    at = pl.ds(pl.multiple_of(step * width, width), width)
    total_s[...] += lax.dot_general(
        dmixed_ref[:, at], weight_ref[0], NT, preferred_element_type=jnp.float32
    )

    @pl.when(step == pl.num_programs(0) - 1)
    def _():
        for head in range(heads):
            out_ref[head] = total_s[:, head * rows : (head + 1) * rows].astype(jnp.bfloat16)


def unmix(parts, middle, grad, gain, weight, heads):
    blocks, depth, width = weight.shape
    count, size = middle.shape
    rows = depth // heads
    full = lambda *shape: pl.BlockSpec(shape, lambda i: (0,) * len(shape))
    same = full(count, size)
    return pl.pallas_call(
        functools.partial(unmix_kernel, heads),
        grid=(blocks,),
        in_specs=[same] * 5 + [full(1, size), pl.BlockSpec((1, depth, width), lambda i: (i, 0, 0))],
        out_specs=[same, same, full(1, size), full(heads, count, rows)],
        out_shape=[
            jax.ShapeDtypeStruct((count, size), jnp.float32),
            jax.ShapeDtypeStruct((count, size), jnp.bfloat16),
            jax.ShapeDtypeStruct((1, size), jnp.float32),
            jax.ShapeDtypeStruct((heads, count, rows), jnp.bfloat16),
        ],
        scratch_shapes=[pltpu.VMEM((count, depth), jnp.float32)],
        compiler_params=pltpu.CompilerParams(
            dimension_semantics=("arbitrary",), vmem_limit_bytes=48 * 1024 * 1024
        ),
        cost_estimate=pl.CostEstimate(
            flops=2 * count * depth * size, bytes_accessed=18 << 20, transcendentals=0
        ),
    )(*parts, middle, grad, gain, weight)


def last_kernel(heads, proj_ref, weight_ref, tokens_ref, dmiddle_ref, gain_ref, grad_ref, part_ref):
    step = pl.program_id(0)
    width = weight_ref.shape[2]
    rows = proj_ref.shape[2]
    total = jnp.zeros((tokens_ref.shape[0], width), jnp.float32)
    for head in range(heads):
        total += jnp.dot(
            proj_ref[head],
            weight_ref[0, head * rows : (head + 1) * rows, :],
            preferred_element_type=jnp.float32,
        )
    grad_ref[:, pl.ds(pl.multiple_of(step * width, width), width)] = total

    @pl.when(step == pl.num_programs(0) - 1)
    def _():
        dnormed = grad_ref[...]
        tokens = wide(tokens_ref[...])
        inv_one = inv_root_mean(tokens)
        scaled = tokens * inv_one
        error = dnormed * gain_ref[...]
        part_ref[...] = jnp.sum(dnormed * scaled, axis=0, keepdims=True)
        grad_ref[...] = dmiddle_ref[...] + inv_one * (
            error - scaled * jnp.mean(error * scaled, axis=1, keepdims=True)
        )


def last(proj, weight, tokens, dmiddle, gain):
    heads, count, rows = proj.shape
    blocks, depth, width = weight.shape
    size = tokens.shape[1]
    full = lambda *shape: pl.BlockSpec(shape, lambda i: (0,) * len(shape))
    return pl.pallas_call(
        functools.partial(last_kernel, heads),
        grid=(blocks,),
        in_specs=[
            full(heads, count, rows),
            pl.BlockSpec((1, depth, width), lambda i: (i, 0, 0)),
            full(count, size),
            full(count, size),
            full(1, size),
        ],
        out_specs=[full(count, size), full(1, size)],
        out_shape=[
            jax.ShapeDtypeStruct((count, size), jnp.float32),
            jax.ShapeDtypeStruct((1, size), jnp.float32),
        ],
        compiler_params=pltpu.CompilerParams(
            dimension_semantics=("arbitrary",), vmem_limit_bytes=48 * 1024 * 1024
        ),
        cost_estimate=pl.CostEstimate(
            flops=2 * count * depth * size, bytes_accessed=18 << 20, transcendentals=0
        ),
    )(proj, weight, tokens, dmiddle, gain)


def ffn_kernel(count, *refs):
    normed, grads, weight_ref = refs[:count], refs[count : 2 * count], refs[2 * count]
    hidden_ref, dgate_ref, dup_ref = refs[2 * count + 1 : 2 * count + 4]
    branches, dnormed = refs[2 * count + 4 : 3 * count + 4], refs[3 * count + 4 :]
    rows = normed[0].shape[0]
    dot = functools.partial(jnp.dot, preferred_element_type=jnp.float32)
    across = functools.partial(
        lax.dot_general, dimension_numbers=NT, preferred_element_type=jnp.float32
    )
    for block in range(count):
        at = slice(block * rows, (block + 1) * rows)
        gate = across(normed[block][...], weight_ref[0])
        up = across(normed[block][...], weight_ref[1])
        dhidden = across(grads[block][...], weight_ref[2])
        sigmoid = jax.nn.sigmoid(gate)
        silu = gate * sigmoid
        hidden = (silu * up).astype(jnp.bfloat16)
        dgate = (dhidden * up * sigmoid * (1.0 + gate * (1.0 - sigmoid))).astype(jnp.bfloat16)
        dup = (dhidden * silu).astype(jnp.bfloat16)
        hidden_ref[at, :] = hidden
        dgate_ref[at, :] = dgate
        dup_ref[at, :] = dup
        dnormed[block][...] = (dot(dgate, weight_ref[0]) + dot(dup, weight_ref[1])).astype(jnp.bfloat16)
        branches[block][...] = dot(hidden, weight_ref[2]).astype(jnp.bfloat16)


def ffn(normed, grads, weights):
    count = len(normed)
    rows, depth = normed[0].shape
    units = weights.shape[1]
    wide_out = jax.ShapeDtypeStruct((rows, depth), jnp.bfloat16)
    unit_out = jax.ShapeDtypeStruct((count * rows, units), jnp.bfloat16)
    outs = pl.pallas_call(
        functools.partial(ffn_kernel, count),
        in_specs=[pl.BlockSpec(memory_space=pltpu.VMEM)] * (2 * count + 1),
        out_specs=[pl.BlockSpec(memory_space=pltpu.VMEM)] * (2 * count + 3),
        out_shape=[unit_out] * 3 + [wide_out] * (2 * count),
        compiler_params=pltpu.CompilerParams(vmem_limit_bytes=56 * 1024 * 1024),
        cost_estimate=pl.CostEstimate(
            flops=12 * count * rows * depth * units,
            bytes_accessed=20 << 20,
            transcendentals=count * rows * units,
        ),
    )(*normed, *grads, weights)
    return outs[:3], outs[3 : 3 + count], outs[3 + count :]


def per_device(
    wires,
    tokens,
    keep_mask,
    seq_lengths,
    attn_gain,
    in_weight,
    out_weight,
    ffn_gain,
    gate_weight,
    up_weight,
    down_weight,
    out_grad,
):
    wires.place()
    heads_here = in_weight.shape[1] // (2 * FD + VD)
    rows, depth = tokens.shape
    group_rows = rows * wires.head
    tokens_wide = wide(tokens)
    own_normed = low(tokens_wide * inv_root_mean(tokens_wide) * attn_gain)
    slots = wires.line_gather(own_normed)
    normed = jnp.zeros((group_rows, depth), jnp.bfloat16)
    for s, slot in enumerate(slots):
        chip = (wires.z - s) % wires.nz
        normed = lax.dynamic_update_slice(normed, slot, ((chip * 2 + wires.c) * rows, 0))
        normed = lax.dynamic_update_slice(
            normed, wires.over_core(slot), ((chip * 2 + 1 - wires.c) * rows, 0)
        )
    in_packed = pack_columns(in_weight, heads_here)
    packed_width = in_packed.shape[1]
    in_padded = jnp.pad(in_packed, ((0, 0), (0, heads_here * VD + LANES - packed_width)))
    projected = low(jnp.dot(normed, in_padded, preferred_element_type=jnp.float32))

    out_whole = wires.whole_weight(out_weight)
    ffn_whole = wires.ffn_weights(jnp.stack([gate_weight.T, up_weight.T, down_weight]))
    grads = wires.square_gather(out_grad)
    in_whole = wires.whole_weight(in_packed.T)

    ends = jnp.cumsum(seq_lengths[0])
    keep_column = keep_mask.astype(jnp.float32)[:, None]
    attended_wide, inverses, attended = attend(projected, keep_column, ends, heads_here)

    def swap(values):
        return lax.all_to_all(values, "head", split_axis=0, concat_axis=0, tiled=True)

    attended_here = swap(attended).reshape(wires.head, rows, heads_here * VD)
    middle, normed_two = mix(attended_here, out_whole, tokens, ffn_gain[None])
    pairs = wires.square_gather(normed_two)
    units, branch_pairs, dnormed_pairs = [], [], []
    for (own, other), (own_grad, other_grad) in zip(pairs, grads):
        unit, branch, dnormed = ffn([own, other], [own_grad, other_grad], ffn_whole)
        units.append(unit)
        branch_pairs.append(branch)
        dnormed_pairs.append(dnormed)
    dnormed_parts = wires.square_reduce(dnormed_pairs)
    d_middle, d_mixed, ffn_gain_part, d_attended = unmix(
        dnormed_parts, middle, out_grad, ffn_gain[None], out_whole, wires.head
    )
    d_attended = swap(d_attended).reshape(group_rows, heads_here * VD)
    d_projected = attend_back(
        projected, keep_column, ends, attended_wide, inverses, d_attended, heads_here
    )
    d_here = swap(d_projected[:, :packed_width]).reshape(wires.head, rows, packed_width)
    in_grad, attn_gain_part = last(d_here, in_whole, tokens, d_middle, attn_gain[None])

    a, b, c = wires.square_reduce(branch_pairs)
    output = low(middle + wide(a) + wide(b) + wide(c))

    normed_all = jnp.concatenate([block for pair in pairs for block in pair], axis=0)
    grad_all = jnp.concatenate([block for pair in grads for block in pair], axis=0)
    hidden, d_gate, d_up = (jnp.concatenate([unit[i] for unit in units], axis=0) for i in range(3))

    def weight_grad(left, right):
        return low(lax.dot_general(left, right, TN, preferred_element_type=jnp.float32))

    gate_grad = wires.ffn_grads(weight_grad(d_gate, normed_all)).T
    up_grad = wires.ffn_grads(weight_grad(d_up, normed_all)).T
    down_grad = wires.ffn_grads(weight_grad(hidden, grad_all))
    out_weight_grad = wide(
        wires.out_grads(
            low(jnp.einsum("htv,td->hvd", attended_here, d_mixed, preferred_element_type=jnp.float32))
        )
    )
    in_weight_grad = unpack_columns(
        wide(wires.sum_dp(weight_grad(normed, d_projected)[:, :packed_width])), heads_here
    )
    gains = wires.sum_all(jnp.concatenate([attn_gain_part, ffn_gain_part], axis=0))
    return (
        output,
        in_grad,
        gains[0],
        in_weight_grad,
        out_weight_grad,
        gains[1],
        gate_grad,
        up_grad,
        down_grad,
    )


def solution(mesh):
    return jax.shard_map(
        functools.partial(per_device, Wires(mesh)),
        mesh=mesh,
        in_specs=(
            P(("dp", "head"), None),
            P("dp"),
            P("dp", None),
            P(),
            P(None, "head"),
            P("head", None),
            P(),
            P("dp", "head"),
            P("dp", "head"),
            P("head", "dp"),
            P(("dp", "head"), None),
        ),
        out_specs=(
            P(("dp", "head"), None),
            P(("dp", "head"), None),
            P(),
            P(None, "head"),
            P("head", None),
            P(),
            P("dp", "head"),
            P("dp", "head"),
            P("head", "dp"),
        ),
        check_vma=False,
    )
```

```python
import functools
import jax
import jax.numpy as jnp
from jax import lax
from jax.experimental import pallas as pl
from jax.experimental.pallas import tpu as pltpu
from jax.sharding import PartitionSpec as P

FD = 16
VD = 128
LANES = 128
VMEM = 60 * 1024 * 1024
epsilon = 1e-05
NT = (((1,), (1,)), ((), ()))
TN = (((0,), (0,)), ((), ()))


def head_lanes(block, rows, head, offset):
    lane = lax.broadcasted_iota(jnp.int32, (rows, LANES), 1)
    low = offset + head * FD
    return jnp.where((lane >= low) & (lane < low + FD), block, 0.0)


def segment_start(ends_ref, positions):
    start = jnp.zeros_like(positions)
    for slot in range(ends_ref.shape[0]):
        end = ends_ref[slot]
        start = jnp.where(positions >= end, jnp.maximum(start, end), start)
    return start


def attend_kernel(heads, rows, pieces, ends_ref, at_ref, *refs):
    sources = refs[:pieces]
    weight_ref, keep_ref, projected_ref, normed_ref, y_ref, inv_ref, att_ref = refs[pieces : pieces + 7]
    normed_s, key_s, value_s, sems = refs[pieces + 7 :]
    step = pl.program_id(0)
    own = pl.ds(pl.multiple_of(step * rows, rows), rows)

    @pl.when(step == 0)
    def _():
        size = sources[0].shape[0]
        copies = [
            pltpu.make_async_copy(
                sources[i].at[:, pl.ds(0, normed_s.shape[1])], normed_s.at[pl.ds(pl.multiple_of(at_ref[i], size), size), :], sems.at[i]
            )
            for i in range(pieces)
        ]
        for copy in copies:
            copy.start()
        for copy in copies:
            copy.wait()

    keep = keep_ref[own, :]
    normed = normed_s[own, :]
    normed_ref[...] = normed
    projected = jnp.dot(normed, weight_ref[...], preferred_element_type=jnp.float32).astype(jnp.bfloat16)
    projected_ref[...] = projected
    packed = projected[:, heads * VD :].astype(jnp.float32)
    key_s[own, :] = pltpu.roll(packed, LANES - heads * FD, 1).astype(jnp.bfloat16)
    lane = lax.broadcasted_iota(jnp.int32, (rows, LANES), 1)
    ones = jnp.where(lane < 2, keep, 0.0).astype(jnp.bfloat16)
    for head in range(heads):
        value_s[head, own, :VD] = (
            projected[:, head * VD : (head + 1) * VD].astype(jnp.float32) * keep
        ).astype(jnp.bfloat16)
        value_s[head, own, VD:] = ones
    queries = [(head_lanes(packed, rows, head, 0) * 0.25).astype(jnp.bfloat16) for head in range(heads)]
    row = step * rows + lax.broadcasted_iota(jnp.int32, (rows, 1), 0)
    start = segment_start(ends_ref, row)
    column = lax.broadcasted_iota(jnp.int32, (rows, rows), 1)

    def tile(block, totals, diagonal):
        at = pl.ds(pl.multiple_of(block * rows, rows), rows)
        allowed = column >= start - block * rows
        if diagonal:
            allowed &= column <= lax.broadcasted_iota(jnp.int32, (rows, rows), 0)
        keys = key_s[at, :]
        added = []
        for head in range(heads):
            inner = lax.dot_general(queries[head], keys, NT, preferred_element_type=jnp.float32)
            weights = jnp.where(allowed, (inner * 0.5 + 1.0) * inner + 1.0, 0.0).astype(jnp.bfloat16)
            added.append(
                totals[head]
                + jnp.dot(weights, value_s[head, at, :], preferred_element_type=jnp.float32)
            )
        return tuple(added)

    totals = tuple(jnp.zeros((rows, 2 * VD), jnp.float32) for _ in range(heads))
    totals = lax.fori_loop(0, step, lambda block, held: tile(block, held, False), totals)
    totals = tile(step, totals, True)
    inverses = jnp.zeros((rows, LANES), jnp.float32)
    for head in range(heads):
        inverse = 1.0 / (totals[head][:, VD : VD + 1] + 1.0 - keep)
        y = totals[head][:, :VD] * (keep * inverse)
        y_ref[:, head * VD : (head + 1) * VD] = y
        att_ref[:, head * VD : (head + 1) * VD] = y.astype(jnp.bfloat16)
        inverses = jnp.where(lane == head, inverse, inverses)
    inv_ref[...] = inverses


def attend(pieces, places, weight, keep, ends, heads):
    size, depth = pieces[0].shape[0], weight.shape[0]
    total = size * len(pieces)
    rows = min(512, total)
    width = weight.shape[1]
    pairs = total * (total + rows) // 2 * heads
    blocked = lambda columns: pl.BlockSpec((rows, columns), lambda i, e, a: (i, 0))
    return pl.pallas_call(
        functools.partial(attend_kernel, heads, rows, len(pieces)),
        grid_spec=pltpu.PrefetchScalarGridSpec(
            num_scalar_prefetch=2,
            grid=(total // rows,),
            in_specs=[pl.BlockSpec(memory_space=pl.ANY)] * len(pieces)
            + [
                pl.BlockSpec((depth, width), lambda i, e, a: (0, 0)),
                pl.BlockSpec((total, 1), lambda i, e, a: (0, 0)),
            ],
            out_specs=[
                blocked(width), blocked(depth), blocked(heads * VD), blocked(LANES), blocked(heads * VD)
            ],
            scratch_shapes=[
                pltpu.VMEM((total, depth), jnp.bfloat16),
                pltpu.VMEM((total, LANES), jnp.bfloat16),
                pltpu.VMEM((heads, total, 2 * VD), jnp.bfloat16),
                pltpu.SemaphoreType.DMA((len(pieces),)),
            ],
        ),
        out_shape=[
            jax.ShapeDtypeStruct((total, width), jnp.bfloat16),
            jax.ShapeDtypeStruct((total, depth), jnp.bfloat16),
            jax.ShapeDtypeStruct((total, heads * VD), jnp.float32),
            jax.ShapeDtypeStruct((total, LANES), jnp.float32),
            jax.ShapeDtypeStruct((total, heads * VD), jnp.bfloat16),
        ],
        compiler_params=pltpu.CompilerParams(
            dimension_semantics=("arbitrary",), vmem_limit_bytes=VMEM
        ),
        cost_estimate=pl.CostEstimate(
            flops=pairs * 1024 + 2 * total * depth * width, bytes_accessed=28 << 20, transcendentals=0
        ),
    )(ends, places, *pieces, weight, keep)


def attend_back_kernel(
    heads, rows, ends_ref, projected_ref, keep_ref, y_ref, inv_ref, grad_ref, out_ref,
    key_s, query_s, value_s, error_s, dquery_s,
):
    step = pl.program_id(0)
    blocks = pl.num_programs(0)
    lane = lax.broadcasted_iota(jnp.int32, (rows, LANES), 1)

    @pl.when(step == 0)
    def _():
        dquery_s[...] = jnp.zeros_like(dquery_s)

        def fill(block, nothing):
            at = pl.ds(pl.multiple_of(block * rows, rows), rows)
            keep = keep_ref[at, :]
            packed = projected_ref[at, heads * VD :].astype(jnp.float32)
            rolled = pltpu.roll(packed, LANES - heads * FD, 1)
            ones = jnp.where(lane < 2, keep, 0.0).astype(jnp.bfloat16)
            inverses = inv_ref[at, :]
            for head in range(heads):
                columns = slice(head * VD, (head + 1) * VD)
                key_s[head, at, :] = head_lanes(rolled, rows, head, 0).astype(jnp.bfloat16)
                query_s[head, at, :] = (head_lanes(packed, rows, head, 0) * 0.25).astype(jnp.bfloat16)
                value_s[head, at, :VD] = (projected_ref[at, columns].astype(jnp.float32) * keep).astype(jnp.bfloat16)
                value_s[head, at, VD:] = ones
                inverse = inverses[:, head : head + 1]
                grad = grad_ref[at, columns].astype(jnp.float32)
                error_s[head, at, :VD] = (grad * (keep * inverse)).astype(jnp.bfloat16)
                offset = -jnp.sum(grad * y_ref[at, columns], axis=1, keepdims=True) * inverse
                high = offset.astype(jnp.bfloat16).astype(jnp.float32)
                error_s[head, at, VD:] = jnp.where(
                    lane == 0, high, jnp.where(lane == 1, offset - high, 0.0)
                ).astype(jnp.bfloat16)
            return nothing

        lax.fori_loop(0, blocks, fill, 0)

    own = pl.ds(pl.multiple_of(step * rows, rows), rows)
    row = lax.broadcasted_iota(jnp.int32, (rows, rows), 0)

    def tile(block, totals, diagonal):
        at = pl.ds(pl.multiple_of(block * rows, rows), rows)
        column = block * rows + lax.broadcasted_iota(jnp.int32, (1, rows), 1)
        allowed = row >= segment_start(ends_ref, column) - step * rows
        if diagonal:
            allowed &= row <= lax.broadcasted_iota(jnp.int32, (rows, rows), 1)
        dkey, dvalues = totals
        added = []
        for head in range(heads):
            query = query_s[head, at, :]
            error = error_s[head, at, :]
            keys = key_s[head, own, :]
            inner = lax.dot_general(keys, query, NT, preferred_element_type=jnp.float32)
            dweight = lax.dot_general(value_s[head, own, :], error, NT, preferred_element_type=jnp.float32)
            slope = inner + 1.0
            weights = jnp.where(allowed, (slope * slope + 1.0) * 0.5, 0.0).astype(jnp.bfloat16)
            dinner = jnp.where(allowed, slope * dweight, 0.0).astype(jnp.bfloat16)
            added.append(
                dvalues[head] + jnp.dot(weights, error[:, :VD], preferred_element_type=jnp.float32)
            )
            dkey = dkey + jnp.dot(dinner, query, preferred_element_type=jnp.float32)
            dquery_s[at, :] += lax.dot_general(dinner, keys, TN, preferred_element_type=jnp.float32)
        return dkey, tuple(added)

    totals = (
        jnp.zeros((rows, LANES), jnp.float32),
        tuple(jnp.zeros((rows, VD), jnp.float32) for _ in range(heads)),
    )
    totals = tile(step, totals, True)
    dkey, dvalues = lax.fori_loop(step + 1, blocks, lambda block, held: tile(block, held, False), totals)
    keep = keep_ref[own, :]
    for head in range(heads):
        out_ref[:, head * VD : (head + 1) * VD] = (dvalues[head] * keep).astype(jnp.bfloat16)
    packed = (dquery_s[own, :] * 0.25 + pltpu.roll(dkey, heads * FD, 1)).astype(jnp.bfloat16)
    out_ref[:, heads * VD :] = packed[:, : 2 * heads * FD]


def attend_back(projected, keep, ends, y, inverses, grad, heads):
    total = projected.shape[0]
    rows = min(512, total)
    width = projected.shape[1]
    pairs = total * (total + rows) // 2 * heads
    packed = heads * (2 * FD + VD)
    whole = lambda columns: pl.BlockSpec((total, columns), lambda i, e: (0, 0))
    return pl.pallas_call(
        functools.partial(attend_back_kernel, heads, rows),
        grid_spec=pltpu.PrefetchScalarGridSpec(
            num_scalar_prefetch=1,
            grid=(total // rows,),
            in_specs=[whole(width), whole(1), whole(heads * VD), whole(LANES), whole(heads * VD)],
            out_specs=pl.BlockSpec((rows, packed), lambda i, e: (i, 0)),
            scratch_shapes=[
                pltpu.VMEM((heads, total, LANES), jnp.bfloat16),
                pltpu.VMEM((heads, total, LANES), jnp.bfloat16),
                pltpu.VMEM((heads, total, 2 * VD), jnp.bfloat16),
                pltpu.VMEM((heads, total, 2 * VD), jnp.bfloat16),
                pltpu.VMEM((total, LANES), jnp.float32),
            ],
        ),
        out_shape=jax.ShapeDtypeStruct((total, packed), jnp.bfloat16),
        compiler_params=pltpu.CompilerParams(
            dimension_semantics=("arbitrary",), vmem_limit_bytes=VMEM
        ),
        cost_estimate=pl.CostEstimate(flops=pairs * 2560, bytes_accessed=12 << 20, transcendentals=0),
    )(ends, projected, keep, y, inverses, grad)


def pack_columns(weight, heads):
    depth = weight.shape[0]
    per_head = weight.reshape(depth, heads, 2 * FD + VD)
    return jnp.concatenate(
        [
            per_head[:, :, 2 * FD :].reshape(depth, heads * VD),
            per_head[:, :, :FD].reshape(depth, heads * FD),
            per_head[:, :, FD : 2 * FD].reshape(depth, heads * FD),
        ],
        axis=1,
    )


def unpack_columns(packed, heads):
    depth = packed.shape[0]
    wide, narrow = heads * VD, heads * FD
    return jnp.concatenate(
        [
            packed[:, wide : wide + narrow].reshape(depth, heads, FD),
            packed[:, wide + narrow : wide + 2 * narrow].reshape(depth, heads, FD),
            packed[:, :wide].reshape(depth, heads, VD),
        ],
        axis=2,
    ).reshape(depth, heads * (2 * FD + VD))


def inv_root_mean(values):
    return lax.rsqrt(jnp.mean(values * values, axis=1, keepdims=True) + epsilon)


def wide(values):
    return values.astype(jnp.float32)


def low(values):
    return values.astype(jnp.bfloat16)


def pick(values, index, count, axis):
    size = values.shape[axis] // count
    if count == 2:
        first = lax.slice_in_dim(values, 0, size, axis=axis)
        second = lax.slice_in_dim(values, size, 2 * size, axis=axis)
        return jnp.where(index == 0, first, second)
    return lax.dynamic_slice_in_dim(values, index * size, size, axis)


def in_order(pieces, index, axis):
    count = len(pieces)
    if count == 1:
        return pieces[0]
    if count == 2:
        first = jnp.where(index == 0, pieces[0], pieces[1])
        second = jnp.where(index == 0, pieces[1], pieces[0])
        return jnp.concatenate([first, second], axis=axis)
    stacked = jnp.stack(pieces)
    placed = [
        lax.dynamic_index_in_dim(stacked, (index - place) % count, 0, keepdims=False)
        for place in range(count)
    ]
    return jnp.concatenate(placed, axis=axis)


class Wires:
    def __init__(self, mesh):
        self.dp, self.head = mesh.shape["dp"], mesh.shape["head"]
        self.ny, self.nz, self.nzh = self.dp // 2, self.head // 2, self.head // 4

    def place(self):
        p, h = lax.axis_index("dp"), lax.axis_index("head")
        self.p, self.h = p, h
        self.y, self.x, self.z, self.c = p // 2, p % 2, h // 2, h % 2
        self.zh = self.z // 2

    def over_x(self, values):
        return lax.ppermute(values, "dp", [(i, i ^ 1) for i in range(self.dp)])

    def over_y(self, values, shift):
        return lax.ppermute(
            values, "dp", [(i, ((i // 2 + shift) % self.ny) * 2 + i % 2) for i in range(self.dp)]
        )

    def over_core(self, values):
        return lax.ppermute(values, "head", [(i, i ^ 1) for i in range(self.head)])

    def over_zl(self, values):
        return lax.ppermute(values, "head", [(i, i ^ 2) for i in range(self.head)])

    def over_zh(self, values, shift):
        return lax.ppermute(
            values, "head", [(i, ((i // 4 + shift) % self.nzh) * 4 + i % 4) for i in range(self.head)]
        )

    def over_z(self, values, shift):
        return lax.ppermute(
            values, "head", [(i, ((i // 2 + shift) % self.nz) * 2 + i % 2) for i in range(self.head)]
        )

    def right(self, values, first, last):
        return lax.ppermute(
            values, "head", [(i, i + 2) for i in range(self.head) if first <= i // 2 <= last]
        )

    def left(self, values, first, last):
        return lax.ppermute(
            values, "head", [(i, i - 2) for i in range(self.head) if first <= i // 2 <= last]
        )

    def spread(self, line):
        return self.over_x(line), [self.over_y(line, s) for s in range(1, self.ny)]

    def ends(self, values):
        pairs = [(i, i + 2 if i // 2 == self.nz - 2 else i - 2) for i in range(self.head)]
        return lax.ppermute(
            values, "head", [pair for pair in pairs if pair[0] // 2 in (1, self.nz - 2)]
        )

    def arrivals(self):
        orders = []
        for z in range(self.nz):
            order = []
            for step in range(1, self.nz):
                order += [(0, step)] if z >= step else []
                order += [(1, step)] if z + step < self.nz else []
            orders.append(order)
        return orders

    def by_place(self, values):
        chosen, taken = values[0], [values[0]]
        for value in values[1:]:
            if any(value is other for other in taken):
                continue
            taken.append(value)
            here = [z for z in range(self.nz) if values[z] is value]
            chosen = jnp.where(sum((self.z == z).astype(jnp.int32) for z in here) > 0, value, chosen)
        return chosen

    def sum_y(self, values):
        total = wide(values)
        for s in range(1, self.ny):
            total = total + wide(self.over_y(values, s))
        return low(total)

    def sum_x(self, values):
        return low(wide(values) + wide(self.over_x(values)))

    def sum_all(self, values):
        values = values + self.over_core(values)
        values = values + self.over_zl(values)
        values = values + sum(self.over_zh(values, s) for s in range(1, self.nzh))
        values = values + self.over_x(values)
        return values + sum(self.over_y(values, s) for s in range(1, self.ny))

    def quarter(self, shard):
        size = shard.shape[1] // self.dp
        return lax.dynamic_slice_in_dim(shard, self.p * size, size, 1)

    def line_of(self, part):
        return [part] + [self.over_z(part, s) for s in range(1, self.nz)]

    def whole_places(self, chips, rows, size):
        at_rows = [(chip * 2 + (self.c ^ r)) * rows for r in range(2) for chip in chips]
        at_columns = [
            (((self.y - s) % self.ny) * 2 + (self.x ^ t)) * size
            for s in range(self.ny)
            for t in range(2)
        ]
        return jnp.stack(at_rows + at_columns).astype(jnp.int32)

    def line(self, block, during):
        steps = self.nz
        right = left = block
        rights, lefts = {}, {}
        orders = self.arrivals()
        chunks, chips = [block], [self.z]
        for step in range(1, steps):
            if step < steps - 1:
                right = self.right(right, step - 1, steps - 2)
                left = self.left(left, 1, steps - step)
                right, left = during(step, (right, left))
            else:
                both = jnp.where(self.z == steps - 2, right, left)
                (right, both) = during(step, (self.ends(both), both))
                left = right
            rights[step], lefts[step] = right, left
            arrived = {(0, s): rights[s] for s in rights} | {(1, s): lefts[s] for s in lefts}
            while len(chunks) < steps and all(
                orders[z][len(chunks) - 1] in arrived for z in range(steps)
            ):
                order = [orders[z][len(chunks) - 1] for z in range(steps)]
                values = [arrived[key] for key in order]
                if step == steps - 1 and values[1] is lefts[steps - 2] and values[-2] is rights[steps - 2]:
                    values[1] = values[-2] = both
                chunks.append(self.by_place(values))
                chips.append(
                    self.by_place([z - key[1] * (1 - 2 * key[0]) for z, key in enumerate(order)])
                )
        return chunks, chips


class Whole:
    def __init__(self, wires, pieces, places, rows, size):
        self.layout = [(s, t, 0, wires.nz) for s in range(wires.ny) for t in range(2)]
        self.nz = wires.nz
        self.pieces, self.rows, self.size = pieces, rows, size
        self.places = places
        self.copies = 2 * sum(count for _, _, _, count in self.layout)
        self.shape = (wires.head * rows, wires.dp * size)

    def fill(self, places_ref, refs, scratch, sems):
        copies = []
        for core in range(2):
            for piece, (s, t, first, count) in enumerate(self.layout):
                column = pl.multiple_of(places_ref[2 * self.nz + 2 * s + t], self.size)
                for slot in range(count):
                    row = pl.multiple_of(places_ref[core * self.nz + first + slot], self.rows)
                    copies.append(
                        pltpu.make_async_copy(
                            refs[core * len(self.layout) + piece].at[slot],
                            scratch.at[pl.ds(row, self.rows), pl.ds(column, self.size)],
                            sems.at[len(copies)],
                        )
                    )
        for copy in copies:
            copy.start()
        return copies


def swapped(wires, pieces):
    return [*pieces, *[wires.over_core(piece) for piece in pieces]]


def side_by_side(blocks_ref):
    return jnp.concatenate([blocks_ref[i] for i in range(blocks_ref.shape[0])], axis=1)


def mix_kernel(whole, places_ref, *refs):
    count = len(whole.pieces)
    attended_ref, tokens_ref, gain_ref, middle_ref, normed_ref, weight_s, sems = refs[count:]
    for copy in whole.fill(places_ref, refs[:count], weight_s, sems):
        copy.wait()
    middle = jnp.dot(
        side_by_side(attended_ref), weight_s[...], preferred_element_type=jnp.float32
    ) + wide(tokens_ref[...])
    middle_ref[...] = middle
    normed_ref[...] = (middle * inv_root_mean(middle) * gain_ref[...]).astype(jnp.bfloat16)


def with_whole(kernel, whole, args, outs, flops):
    in_vmem = pl.BlockSpec(memory_space=pltpu.VMEM)
    return pl.pallas_call(
        functools.partial(kernel, whole),
        grid_spec=pltpu.PrefetchScalarGridSpec(
            num_scalar_prefetch=1,
            grid=(),
            in_specs=[pl.BlockSpec(memory_space=pl.ANY)] * len(whole.pieces) + [in_vmem] * len(args),
            out_specs=[in_vmem] * len(outs),
            scratch_shapes=[
                pltpu.VMEM(whole.shape, jnp.bfloat16),
                pltpu.SemaphoreType.DMA((whole.copies,)),
            ],
        ),
        out_shape=[jax.ShapeDtypeStruct(shape, kind) for shape, kind in outs],
        compiler_params=pltpu.CompilerParams(vmem_limit_bytes=VMEM),
        cost_estimate=pl.CostEstimate(flops=flops, bytes_accessed=16 << 20, transcendentals=0),
    )(whole.places, *whole.pieces, *args)


def mix(attended, whole, tokens, gain):
    return with_whole(
        mix_kernel,
        whole,
        (attended, tokens, gain),
        ((tokens.shape, jnp.float32), (tokens.shape, jnp.bfloat16)),
        2 * tokens.shape[0] * whole.shape[0] * whole.shape[1],
    )


def unmix_kernel(whole, places_ref, *refs):
    count = len(whole.pieces)
    a_ref, b_ref, c_ref, middle_ref, grad_ref, gain_ref = refs[count : count + 6]
    dmiddle_ref, dmixed_ref, part_ref, out_ref, weight_s, sems = refs[count + 6 :]
    copies = whole.fill(places_ref, refs[:count], weight_s, sems)
    middle = middle_ref[...]
    inv_two = inv_root_mean(middle)
    dnormed = wide(a_ref[...]) + wide(b_ref[...]) + wide(c_ref[...])
    scaled = middle * inv_two
    error = dnormed * gain_ref[...]
    dmiddle = wide(grad_ref[...]) + inv_two * (
        error - scaled * jnp.mean(error * scaled, axis=1, keepdims=True)
    )
    part_ref[...] = jnp.sum(dnormed * scaled, axis=0, keepdims=True)
    dmiddle_ref[...] = dmiddle
    dmixed = dmiddle.astype(jnp.bfloat16)
    dmixed_ref[...] = dmixed
    for copy in copies:
        copy.wait()
    width = out_ref.shape[2]
    for head in range(out_ref.shape[0]):
        out_ref[head] = lax.dot_general(
            dmixed, weight_s[head * width : (head + 1) * width, :], NT, preferred_element_type=jnp.float32
        ).astype(jnp.bfloat16)


def unmix(parts, middle, grad, gain, whole, heads):
    rows, depth = middle.shape
    return with_whole(
        unmix_kernel,
        whole,
        (*parts, middle, grad, gain),
        (
            (middle.shape, jnp.float32),
            (middle.shape, jnp.bfloat16),
            ((1, depth), jnp.float32),
            ((heads, rows, whole.shape[0] // heads), jnp.bfloat16),
        ),
        2 * rows * whole.shape[0] * whole.shape[1],
    )


def last_kernel(whole, places_ref, *refs):
    count = len(whole.pieces)
    proj_ref, tokens_ref, dmiddle_ref, gain_ref, grad_ref, weight_s, sems = refs[count:]
    for copy in whole.fill(places_ref, refs[:count], weight_s, sems):
        copy.wait()
    width = proj_ref.shape[2]
    dnormed = jnp.zeros(grad_ref.shape, jnp.float32)
    for head in range(proj_ref.shape[0]):
        dnormed += jnp.dot(
            proj_ref[head],
            weight_s[head * width : (head + 1) * width, :],
            preferred_element_type=jnp.float32,
        )
    tokens = wide(tokens_ref[...])
    inv_one = inv_root_mean(tokens)
    scaled = tokens * inv_one
    error = dnormed * gain_ref[...]
    grad_ref[...] = dmiddle_ref[...] + inv_one * (
        error - scaled * jnp.mean(error * scaled, axis=1, keepdims=True)
    )


def last(proj, whole, tokens, dmiddle, gain):
    return with_whole(
        last_kernel,
        whole,
        (proj, tokens, dmiddle, gain),
        ((tokens.shape, jnp.float32),),
        2 * tokens.shape[0] * whole.shape[0] * whole.shape[1],
    )[0]


class Units:
    def __init__(self, wires, pieces, matrices, rows, columns):
        self.matrices = matrices
        self.layout = [piece[1:] for piece in pieces]
        self.pieces = [piece[0] for piece in pieces]
        self.rows, self.columns = rows, columns
        self.places = jnp.stack([((wires.y - s) % wires.ny) * columns for s in range(wires.ny)]).astype(
            jnp.int32
        )
        self.shape = (matrices, wires.nzh * rows, wires.ny * columns)

    def fill(self, places_ref, refs, scratch, sems):
        copies = []
        for matrix in range(self.matrices):
            for ref, (first, count, zh, y) in zip(refs, self.layout):
                if not first <= matrix < first + count:
                    continue
                column = pl.multiple_of(places_ref[y], self.columns)
                copies.append(
                    pltpu.make_async_copy(
                        ref.at[matrix - first],
                        scratch.at[
                            matrix, pl.ds(zh * self.rows, self.rows), pl.ds(column, self.columns)
                        ],
                        sems.at[len(copies)],
                    )
                )
        for copy in copies:
            copy.start()
        return copies


def gate_kernel(units, places_ref, *refs):
    pieces, refs = refs[: len(units.pieces)], refs[len(units.pieces) :]
    blocks, (gate_ref, up_ref, normed_ref, weight_s, sems, in_sems) = refs[:2], refs[2:]
    rows = blocks[0].shape[0]
    copies = [
        pltpu.make_async_copy(blocks[i], normed_ref.at[pl.ds(i * rows, rows)], in_sems.at[i])
        for i in range(2)
    ]
    for copy in copies:
        copy.start()
    weights = units.fill(places_ref, pieces, weight_s, sems)
    each = len(weights) // units.matrices
    for copy in copies + weights[:each]:
        copy.wait()
    normed = normed_ref[...]
    gate_ref[...] = lax.dot_general(normed, weight_s[0], NT, preferred_element_type=jnp.float32)
    for copy in weights[each:]:
        copy.wait()
    up_ref[...] = lax.dot_general(normed, weight_s[1], NT, preferred_element_type=jnp.float32)


def with_units(kernel, units, blocks, values, outs, flops, transcendentals):
    in_vmem, anywhere = pl.BlockSpec(memory_space=pltpu.VMEM), pl.BlockSpec(memory_space=pl.ANY)
    copies = sum(count for _, count, _, _ in units.layout)
    return pl.pallas_call(
        functools.partial(kernel, units),
        grid_spec=pltpu.PrefetchScalarGridSpec(
            num_scalar_prefetch=1,
            grid=(),
            in_specs=[anywhere] * (len(units.pieces) + len(blocks)) + [in_vmem] * len(values),
            out_specs=[in_vmem] * len(outs),
            scratch_shapes=[
                pltpu.VMEM(units.shape, jnp.bfloat16),
                pltpu.SemaphoreType.DMA((copies,)),
                pltpu.SemaphoreType.DMA((len(blocks),)),
            ],
        ),
        out_shape=[jax.ShapeDtypeStruct(shape, kind) for shape, kind in outs],
        compiler_params=pltpu.CompilerParams(vmem_limit_bytes=VMEM),
        cost_estimate=pl.CostEstimate(
            flops=flops, bytes_accessed=20 << 20, transcendentals=transcendentals
        ),
    )(units.places, *units.pieces, *blocks, *values)


def gate_up(pair, units):
    rows, depth = pair[0].shape
    out = ((2 * rows, units.shape[1]), jnp.float32)
    return with_units(
        gate_kernel,
        units,
        pair,
        (),
        (out, out, ((2 * rows, depth), jnp.bfloat16)),
        8 * rows * depth * units.shape[1],
        0,
    )


def down_kernel(units, places_ref, *refs):
    pieces, refs = refs[: len(units.pieces)], refs[len(units.pieces) :]
    grads, (gate_ref, up_ref) = refs[:2], refs[2:4]
    hidden_ref, dgate_ref, dup_ref, grad_ref = refs[4:8]
    dnormed, branches = refs[8:10], refs[10:12]
    weight_s, sems, in_sems = refs[12:]
    rows = grads[0].shape[0]
    both = [slice(0, rows), slice(rows, 2 * rows)]
    copies = [
        pltpu.make_async_copy(grads[i], grad_ref.at[both[i]], in_sems.at[i]) for i in range(2)
    ]
    for copy in copies:
        copy.start()
    weights = units.fill(places_ref, pieces, weight_s, sems)
    each = len(weights) // units.matrices
    gate, up = gate_ref[...], up_ref[...]
    sigmoid = jax.nn.sigmoid(gate)
    silu = gate * sigmoid
    hidden = (silu * up).astype(jnp.bfloat16)
    hidden_ref[...] = hidden
    dot = functools.partial(jnp.dot, preferred_element_type=jnp.float32)
    for copy in copies + weights[:each]:
        copy.wait()
    dhidden = lax.dot_general(grad_ref[...], weight_s[0], NT, preferred_element_type=jnp.float32)
    branch = dot(hidden, weight_s[0]).astype(jnp.bfloat16)
    dgate = (dhidden * up * sigmoid * (1.0 + gate * (1.0 - sigmoid))).astype(jnp.bfloat16)
    dup = (dhidden * silu).astype(jnp.bfloat16)
    dgate_ref[...] = dgate
    dup_ref[...] = dup
    for copy in weights[each:]:
        copy.wait()
    back = (dot(dgate, weight_s[1]) + dot(dup, weight_s[2])).astype(jnp.bfloat16)
    for i in range(2):
        branches[i][...] = branch[both[i]]
        dnormed[i][...] = back[both[i]]


def down(grads, gate, up, units):
    rows, depth = grads[0].shape
    unit = (gate.shape, jnp.bfloat16)
    part = ((rows, depth), jnp.bfloat16)
    outs = with_units(
        down_kernel,
        units,
        grads,
        (gate, up),
        (unit, unit, unit, ((2 * rows, depth), jnp.bfloat16), part, part, part, part),
        16 * rows * depth * units.shape[1],
        2 * rows * units.shape[1],
    )
    return outs[:4], outs[4:6], outs[6:]


def unit_grad_kernel(count, ny, nzh, places_ref, *refs):
    lefts, rights = refs[:count], refs[count : 2 * count]
    mine_ref, sent_ref, total_s = refs[2 * count :]
    for i in range(count):
        added = lax.dot_general(lefts[i][...], rights[i][...], TN, preferred_element_type=jnp.float32)
        if i == 0:
            total_s[...] = added
        else:
            total_s[...] += added
    units, columns = mine_ref.shape[1:]
    for y in range(ny):
        for zh in range(nzh):
            block = total_s[
                pl.ds(pl.multiple_of(places_ref[ny + zh], units), units),
                pl.ds(pl.multiple_of(places_ref[y], columns), columns),
            ].astype(jnp.bfloat16)
            if y == 0:
                mine_ref[zh] = block
            else:
                sent_ref[y - 1, zh] = block


def unit_grad(wires, lefts, rights):
    ny, nzh = wires.ny, wires.nzh
    units, depth = lefts[0].shape[1], rights[0].shape[1]
    rows, columns = units // nzh, depth // ny
    places = jnp.stack(
        [((wires.y + s) % ny) * columns for s in range(ny)]
        + [s * rows for s in range(nzh)]
    ).astype(jnp.int32)
    in_vmem = pl.BlockSpec(memory_space=pltpu.VMEM)
    tokens = sum(left.shape[0] for left in lefts)
    return pl.pallas_call(
        functools.partial(unit_grad_kernel, len(lefts), ny, nzh),
        grid_spec=pltpu.PrefetchScalarGridSpec(
            num_scalar_prefetch=1,
            grid=(),
            in_specs=[in_vmem] * (2 * len(lefts)),
            out_specs=[in_vmem] * 2,
            scratch_shapes=[pltpu.VMEM((units, depth), jnp.float32)],
        ),
        out_shape=[
            jax.ShapeDtypeStruct((nzh, rows, columns), jnp.bfloat16),
            jax.ShapeDtypeStruct((ny - 1, nzh, rows, columns), jnp.bfloat16),
        ],
        compiler_params=pltpu.CompilerParams(vmem_limit_bytes=VMEM),
        cost_estimate=pl.CostEstimate(
            flops=2 * tokens * depth * units, bytes_accessed=14 << 20, transcendentals=0
        ),
    )(places, *lefts, *rights)


def out_grad_kernel(nz, ny, places_ref, left_ref, right_ref, mine_ref, sent_ref):
    step = pl.program_id(0)
    width = mine_ref.shape[4]
    for core, out_ref in ((0, mine_ref), (1, sent_ref)):
        left = left_ref[places_ref[core * nz + step]]
        total = lax.dot_general(left, right_ref[...], TN, preferred_element_type=jnp.float32)
        for x in range(2):
            for y in range(ny):
                out_ref[x, y, 0] = total[:, (x * ny + y) * width : (x * ny + y + 1) * width].astype(
                    jnp.bfloat16
                )


def out_grad_parts(wires, attended, d_mixed):
    heads, tokens, rows = attended.shape
    depth = d_mixed.shape[1]
    nz, ny, width = wires.nz, wires.ny, depth // wires.dp
    places = jnp.stack(
        [((wires.z - s) % nz) * 2 + (wires.c ^ r) for r in range(2) for s in range(nz)]
    ).astype(jnp.int32)
    columns = [((wires.y + s) % ny) * 2 + (wires.x ^ t) for t in range(2) for s in range(ny)]
    ordered = jnp.concatenate(
        [lax.dynamic_slice_in_dim(d_mixed, column * width, width, 1) for column in columns], axis=1
    )
    out = jax.ShapeDtypeStruct((2, ny, nz, rows, width), jnp.bfloat16)
    block = pl.BlockSpec((2, ny, 1, rows, width), lambda i, p: (0, 0, i, 0, 0))
    return pl.pallas_call(
        functools.partial(out_grad_kernel, nz, ny),
        grid_spec=pltpu.PrefetchScalarGridSpec(
            num_scalar_prefetch=1,
            grid=(nz,),
            in_specs=[
                pl.BlockSpec((heads, tokens, rows), lambda i, p: (0, 0, 0)),
                pl.BlockSpec((tokens, depth), lambda i, p: (0, 0)),
            ],
            out_specs=[block, block],
        ),
        out_shape=[out, out],
        compiler_params=pltpu.CompilerParams(
            dimension_semantics=("arbitrary",), vmem_limit_bytes=VMEM
        ),
        cost_estimate=pl.CostEstimate(
            flops=2 * tokens * depth * heads * rows, bytes_accessed=10 << 20, transcendentals=0
        ),
    )(places, attended, ordered)


def tie(*values):
    return lax.optimization_barrier(values)


def per_device(
    wires,
    tokens,
    keep_mask,
    seq_lengths,
    attn_gain,
    in_weight,
    out_weight,
    ffn_gain,
    gate_weight,
    up_weight,
    down_weight,
    out_grad,
):
    wires.place()
    heads_here = in_weight.shape[1] // (2 * FD + VD)
    rows, depth = tokens.shape
    group_rows = rows * wires.head
    half = rows // 2
    out_rows = heads_here * VD
    size = depth // wires.dp
    tokens_wide = wide(tokens)
    own = low(tokens_wide * inv_root_mean(tokens_wide) * attn_gain)
    across_y = range(1, wires.ny)

    def on_y(pieces):
        return [[wires.over_y(piece, s) for s in across_y] for piece in pieces]

    def swap(values):
        return lax.all_to_all(values, "head", split_axis=0, concat_axis=0, tiled=True)

    def add(*values):
        return low(sum(wide(value) for value in values))

    in_packed = pack_columns(in_weight, heads_here)
    packed_width = in_packed.shape[1]
    in_padded = jnp.pad(in_packed, ((0, 0), (0, heads_here * VD + LANES - packed_width)))
    in_part = wires.quarter(in_packed.T)
    keep_column = keep_mask.astype(jnp.float32)[:, None]
    ends = jnp.cumsum(seq_lengths[0])
    stacked = jnp.stack([gate_weight.T, up_weight.T, down_weight])
    unit_own = pick(stacked, wires.x, 2, 1)
    unit_other = pick(stacked, 1 - wires.x, 2, 1)
    share = out_rows * size // rows
    block = jnp.concatenate([own, wires.quarter(out_weight).reshape(rows, share)], axis=1)

    flying = {}

    def beside_line(step, values):
        if step == 1:
            by_x = wires.over_x(unit_other)
            values, flying["by_x"], flying["own"], flying["in_part"], flying["out_grad"], flying["swap"] = tie(
                values, by_x, unit_own, in_part, out_grad, wires.over_core(block)
            )
        elif step == 2:
            pair = in_order([flying["own"], flying["by_x"]], wires.x, 2)
            by_x = wires.over_x(flying["out_grad"])
            values, flying["grad_x"], flying["pair"], flying["out_grad"] = tie(
                values, by_x, pair, flying["out_grad"]
            )
        elif step == wires.nz - 1:
            by_y = [wires.over_y(flying["pair"][:2], s) for s in across_y]
            values, flying["by_y"], flying["pair"], flying["grad_x"] = tie(
                values, by_y, flying["pair"], flying["grad_x"]
            )
        else:
            (values,) = tie(values)
        return values

    chunks, chips = wires.line(block, beside_line)
    others = [flying["swap"]] + [wires.over_core(chunk) for chunk in chunks[1:]]
    pieces = [piece for pair in zip(chunks, others) for piece in pair]
    places = jnp.stack(
        [(chip * 2 + (wires.c ^ r)) * rows for chip in chips for r in range(2)]
    ).astype(jnp.int32)
    pieces, unit_pair, out_grad, grad_x = tie(
        pieces, flying["pair"], flying["out_grad"], flying["grad_x"]
    )

    def shares(blocks):
        return jnp.stack([piece[:, depth:].reshape(out_rows, size) for piece in blocks])

    by_zh_g = [wires.over_zh(unit_pair[:1], s) for s in range(1, wires.nzh)]
    out_line = shares(pieces[::2])
    out_x, out_y = wires.over_x(out_line), [wires.over_y(out_line, s) for s in across_y]
    projected, normed, attended_wide, inverses, attended = attend(
        pieces, places, in_padded, keep_column, ends, heads_here
    )
    attended, out_x, out_y, by_zh_g, unit_pair, out_grad = tie(
        attended, out_x, out_y, by_zh_g, unit_pair, out_grad
    )
    attended_here = swap(attended).reshape(wires.head, rows, out_rows)
    grad_z = wires.over_zl(out_grad)
    out_across = [wires.over_x(piece) for piece in out_y]
    by_zh_gy = on_y(by_zh_g)
    out_line_swap = shares(pieces[1::2])
    out_x_swap, out_y_swap = wires.over_core(out_x), [wires.over_core(piece) for piece in out_y]
    attended_here, out_across, grad_z, out_x_swap, out_y_swap, unit_pair, by_zh_gy = tie(
        attended_here, out_across, grad_z, out_x_swap, out_y_swap, unit_pair, by_zh_gy
    )
    out_across_swap = [wires.over_core(piece) for piece in out_across]

    def in_layout(line, by_x, by_y, across):
        pieces = [line, by_x]
        for piece in zip(by_y, across):
            pieces += piece
        return pieces

    out_pieces = in_layout(out_line, out_x, out_y, out_across)
    out_pieces += in_layout(out_line_swap, out_x_swap, out_y_swap, out_across_swap)
    out_whole = Whole(wires, out_pieces, wires.whole_places(chips, out_rows, size), out_rows, size)
    middle, normed_two = mix(attended_here, out_whole, tokens, ffn_gain[None])

    normed_two, unit_pair, grad_x, grad_z, out_grad = tie(normed_two, unit_pair, grad_x, grad_z, out_grad)
    two_x, two_z = wires.over_x(normed_two), wires.over_zl(normed_two)
    by_zh_u = [wires.over_zh(unit_pair[1:2], s) for s in range(1, wires.nzh)]
    by_y_d = [wires.over_y(unit_pair[2:], s) for s in across_y]
    two_swap = wires.over_core(normed_two)
    two_x, two_z, by_zh_u, two_swap, by_y_d, unit_pair = tie(
        two_x, two_z, by_zh_u, two_swap, by_y_d, unit_pair
    )
    two_corner = (wires.over_zl(two_x[:half]), wires.over_x(two_z[half:]))
    by_zh_uy = on_y(by_zh_u)
    two_swaps = [two_swap] + [wires.over_core(piece) for piece in (two_x, two_z)]
    two_corner, by_zh_uy, two_swaps, two_x, two_z, unit_pair = tie(
        two_corner, by_zh_uy, two_swaps, two_x, two_z, unit_pair
    )
    two_corner = jnp.concatenate(two_corner, axis=0)

    def spots(matrix, place, by_y, piece, on):
        units = [(unit_pair[matrix : matrix + 1], place, 1, 0, 0)]
        units += [(by_y[s - 1], place, 1, 0, s) for s in across_y]
        for zh in range(1, wires.nzh):
            units.append((piece[zh - 1], place, 1, zh, 0))
            units += [(on[zh - 1][s - 1], place, 1, zh, s) for s in across_y]
        return units

    spot = unit_pair.shape[1], unit_pair.shape[2]
    gu_pair = unit_pair[:2]
    gates = [(gu_pair, 0, 2, 0, 0)] + [(flying["by_y"][s - 1], 0, 2, 0, s) for s in across_y]
    for zh in range(1, wires.nzh):
        for place, piece, on in ((0, by_zh_g, by_zh_gy), (1, by_zh_u, by_zh_uy)):
            gates.append((piece[zh - 1], place, 1, zh, 0))
            gates += [(on[zh - 1][s - 1], place, 1, zh, s) for s in across_y]
    units = Units(wires, gates, 2, *spot)

    by_zh_d = [wires.over_zh(unit_pair[2:], s) for s in range(1, wires.nzh)]
    grad_corner = wires.over_x(grad_z)
    two_corner_swap = wires.over_core(two_corner)
    first = [gate_up(pair, units) for pair in zip([normed_two, two_x, two_z], two_swaps)]
    first, by_zh_d, grad_corner, two_corner, two_corner_swap, grad_z = tie(
        first, by_zh_d, grad_corner, two_corner, two_corner_swap, grad_z
    )
    by_zh_dy = on_y(by_zh_d)
    grad_all = [out_grad, grad_x, grad_z, grad_corner]
    grad_pairs = [(grad, wires.over_core(grad)) for grad in grad_all]
    first.append(gate_up((two_corner, two_corner_swap), units))
    first, by_zh_dy, grad_pairs = tie(first, by_zh_dy, grad_pairs)
    downs = [(unit_pair[2:], 0, 1, 0, 0)] + [(by_y_d[s - 1], 0, 1, 0, s) for s in across_y]
    for zh in range(1, wires.nzh):
        downs.append((by_zh_d[zh - 1], 0, 1, zh, 0))
        downs += [(by_zh_dy[zh - 1][s - 1], 0, 1, zh, s) for s in across_y]
    units = Units(
        wires, downs + [(array, at + 1, count, zh, s) for array, at, count, zh, s in gates], 3, *spot
    )

    def feed(place, *after):
        given, grads, *_ = tie(first[place], grad_pairs[place], *after)
        gate, up, normed = given
        outs, dnormed, branches = down(grads, gate, up, units)
        return (*outs[:3], normed, outs[3]), dnormed, branches

    in_part, grad_corner = tie(flying["in_part"], grad_corner)
    in_line = [in_part] + [wires.over_z(in_part, s) for s in range(1, wires.nz)]
    unit_c, dnormed_c, branch_c = feed(3)
    swap_c = wires.over_core(dnormed_c[1])
    unit_o, dnormed_o, branch_o = feed(0, unit_c)
    unit_o, swap_c, in_line = tie(unit_o, swap_c, in_line)
    sum_c = add(dnormed_c[0], swap_c)
    to_z, to_x = wires.over_x(sum_c[:half]), wires.over_zl(sum_c[half:])
    in_line = jnp.stack(in_line)
    in_y = [wires.over_y(in_line, s) for s in across_y]
    swap_o = wires.over_core(dnormed_o[1])
    unit_x, dnormed_x, branch_x = feed(1, unit_o, sum_c, in_line)
    unit_x, to_x, to_z, swap_o = tie(unit_x, to_x, to_z, swap_o)
    swap_x = wires.over_core(dnormed_x[1])
    in_x = wires.over_x(in_line)
    unit_z, dnormed_z, branch_z = feed(2, unit_x)
    swap_z = wires.over_core(dnormed_z[1])
    unit_z, swap_x, swap_z, in_x, in_y = tie(unit_z, swap_x, swap_z, in_x, in_y)
    sum_x = jnp.concatenate(
        [add(dnormed_x[0][:half], swap_x[:half]), add(dnormed_x[0][half:], swap_x[half:], to_x)], axis=0
    )
    final_x = wires.over_x(sum_x)
    sum_z = jnp.concatenate(
        [add(dnormed_z[0][:half], swap_z[:half], to_z), add(dnormed_z[0][half:], swap_z[half:])], axis=0
    )
    final_z = wires.over_zl(sum_z)
    sum_o = add(dnormed_o[0], swap_o)
    in_across = [wires.over_y(in_x, s) for s in across_y]

    every = [unit_o, unit_x, unit_z, unit_c]

    def grad_of(every, unit, token):
        return unit_grad(wires, [outs[unit] for outs in every], [outs[token] for outs in every])

    def grad_y(mine, sent):
        return mine, [wires.over_y(sent[s - 1], s) for s in across_y]

    def grad_zh(mine, sent):
        total = add(mine, *sent)
        return total[0], [wires.over_zh(total[s], -s) for s in range(1, wires.nzh)]

    def grad_x_swap(mine, sent):
        total = add(mine, *sent)
        return pick(total, wires.x, 2, 1), wires.over_x(pick(total, 1 - wires.x, 2, 1))

    def grad_last(mine, sent):
        return wide(in_order([mine, sent], wires.x, 0))

    every, sum_x, sum_z = tie(every, sum_x, sum_z)
    gate_mine, gate_sent = grad_of(every, 1, 3)
    in_swaps = [wires.over_core(piece) for piece in (in_line, in_x, *in_y)]
    final_x, final_z, gate_mine, gate_sent, in_swaps, in_across = tie(
        final_x, final_z, gate_mine, gate_sent, in_swaps, in_across
    )
    gate_back = grad_y(gate_mine, gate_sent)
    d_middle, d_mixed, ffn_gain_part, d_attended = unmix(
        (sum_o, final_x, final_z), middle, out_grad, ffn_gain[None], out_whole, wires.head
    )
    every, d_attended, d_mixed, branches = tie(
        every, d_attended, d_mixed, (branch_o, branch_x, branch_z, branch_c)
    )
    d_attended = swap(d_attended).reshape(group_rows, out_rows)
    out_mine, out_sent = out_grad_parts(wires, attended_here, d_mixed)
    up_parts = grad_of(every, 2, 3)
    down_parts = grad_of(every, 0, 4)
    out_sent = wires.over_core(out_sent)
    in_across_swap = [wires.over_core(piece) for piece in in_across]
    d_attended, out_mine, out_sent, up_parts, down_parts, gate_back, in_across_swap = tie(
        d_attended, out_mine, out_sent, up_parts, down_parts, gate_back, in_across_swap
    )
    up_back = grad_y(*up_parts)
    gate_back = grad_zh(*gate_back)
    out_total = add(out_mine, out_sent)
    out_sent = wires.over_x(out_total[1])
    d_attended, out_total = tie(d_attended, out_total)
    d_projected = attend_back(
        projected, keep_column, ends, attended_wide, inverses, d_attended, heads_here
    )
    swaps = [wires.over_core(branch[1]) for branch in branches]
    d_projected, gate_back, up_back, branches, swaps = tie(
        d_projected, gate_back, up_back, branches, swaps
    )
    d_here = swap(d_projected).reshape(wires.head, rows, packed_width)
    up_back = grad_zh(*up_back)
    down_back = grad_y(*down_parts)
    gate_back = grad_x_swap(*gate_back)
    sums = [add(branch[0], swap_) for branch, swap_ in zip(branches, swaps)]
    in_back = lax.dot_general(normed, d_projected, TN, preferred_element_type=jnp.float32)
    attn_gain_part = jnp.sum(in_back * wide(in_packed), axis=1) / attn_gain
    in_back = low(in_back)
    gains = jnp.stack([attn_gain_part, ffn_gain_part[0]])
    d_here, up_back, in_back, down_back, out_sent, sums, gate_back, gains = tie(
        d_here, up_back, in_back, down_back, out_sent, sums, gate_back, gains
    )
    in_pieces = in_layout(in_line, in_x, in_y, in_across)
    in_pieces += in_layout(in_swaps[0], in_swaps[1], in_swaps[2:], in_across_swap)
    in_chips = [(wires.z - s) % wires.nz for s in range(wires.nz)]
    in_whole = Whole(
        wires, in_pieces, wires.whole_places(in_chips, packed_width, size), packed_width, size
    )
    down_back = grad_zh(*down_back)
    up_back = grad_x_swap(*up_back)
    to_z, to_x = wires.over_x(sums[3][:half]), wires.over_zl(sums[3][half:])
    out_total = add(out_total[0], out_sent)
    out_y = [wires.over_y(out_total[s], s) for s in across_y]
    in_grad = last(d_here, in_whole, tokens, d_middle, attn_gain[None])
    gains = gains + wires.over_core(gains)
    in_grad, out_y, down_back, to_x, to_z, up_back, in_back, gains, sums = tie(
        in_grad, out_y, down_back, to_x, to_z, up_back, in_back, gains, sums
    )
    cut = depth // 2
    out_parts = add(out_total[0], *out_y)
    out_turns = [wires.over_z(out_parts[s], -s) for s in range(1, wires.nz)]
    in_halves = (wires.sum_x(in_back[:cut]), wires.sum_y(in_back[cut:]))
    out_parts, out_turns, in_halves, by_x, by_z = tie(
        out_parts, out_turns, in_halves, (sums[1], to_x), (sums[2], to_z)
    )
    out_part = add(out_parts[0], *out_turns)
    by_x = jnp.concatenate([by_x[0][:half], add(by_x[0][half:], by_x[1])], axis=0)
    by_z = jnp.concatenate([add(by_z[0][:half], by_z[1]), by_z[0][half:]], axis=0)
    final_x, final_z = wires.over_x(by_x), wires.over_zl(by_z)
    in_halves = (wires.sum_y(in_halves[0]), wires.sum_x(in_halves[1]))
    gains = gains + wires.over_zl(gains)
    final_x, final_z, in_halves, out_part, gains, down_back = tie(
        final_x, final_z, in_halves, out_part, gains, down_back
    )
    down_back = grad_x_swap(*down_back)
    out_x = wires.over_x(out_part)
    out_by_y = [wires.over_y(out_part, s) for s in across_y]
    gains = gains + sum(wires.over_zh(gains, s) for s in range(1, wires.nzh))
    out_x, out_by_y, gains, down_back = tie(out_x, out_by_y, gains, down_back)
    out_by_yx = [wires.over_y(out_x, s) for s in across_y]
    gains = gains + wires.over_x(gains)
    out_by_yx, gains = tie(out_by_yx, gains)
    gains = gains + sum(wires.over_y(gains, s) for s in across_y)
    out_weight_grad = wide(
        in_order(
            [
                in_order([a, b], wires.x, 1)
                for a, b in zip([out_part, *out_by_y], [out_x, *out_by_yx])
            ],
            wires.y,
            1,
        )
    )
    output = low(middle + wide(sums[0]) + wide(final_x) + wide(final_z))
    gate_grad = grad_last(*gate_back).T
    up_grad = grad_last(*up_back).T
    down_grad = grad_last(*down_back)
    in_weight_grad = unpack_columns(wide(jnp.concatenate(in_halves, axis=0)), heads_here)
    return (
        output,
        in_grad,
        gains[0],
        in_weight_grad,
        out_weight_grad,
        gains[1],
        gate_grad,
        up_grad,
        down_grad,
    )


def solution(mesh):
    return jax.shard_map(
        functools.partial(per_device, Wires(mesh)),
        mesh=mesh,
        in_specs=(
            P(("dp", "head"), None),
            P("dp"),
            P("dp", None),
            P(),
            P(None, "head"),
            P("head", None),
            P(),
            P("dp", "head"),
            P("dp", "head"),
            P("head", "dp"),
            P(("dp", "head"), None),
        ),
        out_specs=(
            P(("dp", "head"), None),
            P(("dp", "head"), None),
            P(),
            P(None, "head"),
            P("head", None),
            P(),
            P("dp", "head"),
            P("dp", "head"),
            P("head", "dp"),
        ),
        check_vma=False,
    )
```

```python
import functools
import jax
import jax.numpy as jnp
from jax import lax
from jax.experimental import pallas as pl
from jax.experimental.pallas import tpu as pltpu
from jax.sharding import PartitionSpec as P

FD = 16
VD = 128
LANES = 128
VMEM = 60 * 1024 * 1024
LITTLE = pl.CostEstimate(flops=1, bytes_accessed=1, transcendentals=0)
epsilon = 1e-05
NT = (((1,), (1,)), ((), ()))
TN = (((0,), (0,)), ((), ()))


def column_of(row):
    count = row.shape[1]
    same = lax.broadcasted_iota(jnp.int32, (count, count), 0) == lax.broadcasted_iota(
        jnp.int32, (count, count), 1
    )
    return jnp.sum(jnp.where(same, row, 0.0), axis=1, keepdims=True)


def padded(block):
    rows, columns = block.shape
    return jnp.concatenate([block, jnp.zeros((rows, -columns % LANES), block.dtype)], axis=1)


def lanes_from(block, low, count):
    width = block.shape[1]
    moved = (block if low == 0 else pltpu.roll(block, width - low, 1))[:, :LANES]
    if count == LANES:
        return moved
    lane = lax.broadcasted_iota(jnp.int32, moved.shape, 1)
    return jnp.where(lane < count, moved, 0.0)


def head_parts(block, head):
    low = head * (2 * FD + VD)
    query = lanes_from(block, low, FD) * 0.25
    return query, lanes_from(block, low + FD, FD), lanes_from(block, low + 2 * FD, VD)


def segment_start(ends_ref, positions):
    start = jnp.zeros_like(positions)
    for slot in range(ends_ref.shape[0]):
        end = ends_ref[slot]
        start = jnp.where(positions >= end, jnp.maximum(start, end), start)
    return start


def attend_kernel(heads, rows, pieces, ends_ref, at_ref, *refs):
    sources = refs[:pieces]
    weight_ref, keep_ref, projected_ref, normed_ref, y_ref, inv_ref, att_ref = refs[pieces : pieces + 7]
    normed_s, key_s, value_s, sems = refs[pieces + 7 :]
    step = pl.program_id(0)
    own = pl.ds(pl.multiple_of(step * rows, rows), rows)

    @pl.when(step == 0)
    def _():
        size = sources[0].shape[0]
        copies = [
            pltpu.make_async_copy(
                sources[i].at[:, pl.ds(0, normed_s.shape[1])], normed_s.at[pl.ds(pl.multiple_of(at_ref[i], size), size), :], sems.at[i]
            )
            for i in range(pieces)
        ]
        for copy in copies:
            copy.start()
        for copy in copies:
            copy.wait()

    keep = column_of(keep_ref[:, own])
    normed = normed_s[own, :]
    normed_ref[...] = normed
    projected = lax.dot_general(
        normed, weight_ref[...], NT, preferred_element_type=jnp.float32
    ).astype(jnp.bfloat16)
    projected_ref[...] = projected
    block = padded(projected.astype(jnp.float32))
    lane = lax.broadcasted_iota(jnp.int32, (rows, LANES), 1)
    ones = jnp.where(lane < 2, keep, 0.0).astype(jnp.bfloat16)
    queries = []
    for head in range(heads):
        query, key, value = head_parts(block, head)
        queries.append(query.astype(jnp.bfloat16))
        key_s[head, own, :] = key.astype(jnp.bfloat16)
        value_s[head, own, :VD] = (value * keep).astype(jnp.bfloat16)
        value_s[head, own, VD:] = ones
    row = step * rows + lax.broadcasted_iota(jnp.int32, (rows, 1), 0)
    start = segment_start(ends_ref, row)
    column = lax.broadcasted_iota(jnp.int32, (rows, rows), 1)

    def tile(block, totals, diagonal):
        at = pl.ds(pl.multiple_of(block * rows, rows), rows)
        allowed = column >= start - block * rows
        if diagonal:
            allowed &= column <= lax.broadcasted_iota(jnp.int32, (rows, rows), 0)
        added = []
        for head in range(heads):
            inner = lax.dot_general(
                queries[head], key_s[head, at, :], NT, preferred_element_type=jnp.float32
            )
            weights = jnp.where(allowed, (inner * 0.5 + 1.0) * inner + 1.0, 0.0).astype(jnp.bfloat16)
            added.append(
                totals[head]
                + jnp.dot(weights, value_s[head, at, :], preferred_element_type=jnp.float32)
            )
        return tuple(added)

    totals = tuple(jnp.zeros((rows, 2 * VD), jnp.float32) for _ in range(heads))
    totals = lax.fori_loop(0, step, lambda block, held: tile(block, held, False), totals)
    totals = tile(step, totals, True)
    inverses = jnp.zeros((rows, LANES), jnp.float32)
    for head in range(heads):
        inverse = 1.0 / (totals[head][:, VD : VD + 1] + 1.0 - keep)
        y = totals[head][:, :VD] * (keep * inverse)
        y_ref[:, head * VD : (head + 1) * VD] = y
        att_ref[:, head * VD : (head + 1) * VD] = y.astype(jnp.bfloat16)
        inverses = jnp.where(lane == head, inverse, inverses)
    inv_ref[...] = inverses


def attend(pieces, places, weight, keep, ends, heads):
    size, depth = pieces[0].shape[0], weight.shape[1]
    total = size * len(pieces)
    rows = min(512, total)
    width = weight.shape[0]
    pairs = total * (total + rows) // 2 * heads
    blocked = lambda columns: pl.BlockSpec((rows, columns), lambda i, e, a: (i, 0))
    return pl.pallas_call(
        functools.partial(attend_kernel, heads, rows, len(pieces)),
        grid_spec=pltpu.PrefetchScalarGridSpec(
            num_scalar_prefetch=2,
            grid=(total // rows,),
            in_specs=[pl.BlockSpec(memory_space=pl.ANY)] * len(pieces)
            + [
                pl.BlockSpec((width, depth), lambda i, e, a: (0, 0)),
                pl.BlockSpec((1, total), lambda i, e, a: (0, 0)),
            ],
            out_specs=[
                blocked(width), blocked(depth), blocked(heads * VD), blocked(LANES), blocked(heads * VD)
            ],
            scratch_shapes=[
                pltpu.VMEM((total, depth), jnp.bfloat16),
                pltpu.VMEM((heads, total, LANES), jnp.bfloat16),
                pltpu.VMEM((heads, total, 2 * VD), jnp.bfloat16),
                pltpu.SemaphoreType.DMA((len(pieces),)),
            ],
        ),
        out_shape=[
            jax.ShapeDtypeStruct((total, width), jnp.bfloat16),
            jax.ShapeDtypeStruct((total, depth), jnp.bfloat16),
            jax.ShapeDtypeStruct((total, heads * VD), jnp.float32),
            jax.ShapeDtypeStruct((total, LANES), jnp.float32),
            jax.ShapeDtypeStruct((total, heads * VD), jnp.bfloat16),
        ],
        compiler_params=pltpu.CompilerParams(
            dimension_semantics=("arbitrary",), vmem_limit_bytes=VMEM
        ),
        cost_estimate=LITTLE,
    )(ends, places, *pieces, weight, keep)


def attend_back_kernel(
    heads, rows, ends_ref, projected_ref, keep_ref, y_ref, inv_ref, grad_ref, out_ref,
    key_s, query_s, value_s, error_s, dquery_s,
):
    step = pl.program_id(0)
    blocks = pl.num_programs(0)
    lane = lax.broadcasted_iota(jnp.int32, (rows, LANES), 1)

    @pl.when(step == 0)
    def _():
        dquery_s[...] = jnp.zeros_like(dquery_s)

        def fill(block, nothing):
            at = pl.ds(pl.multiple_of(block * rows, rows), rows)
            keep = column_of(keep_ref[:, at])
            wide_block = padded(projected_ref[at, :].astype(jnp.float32))
            ones = jnp.where(lane < 2, keep, 0.0).astype(jnp.bfloat16)
            inverses = inv_ref[at, :]
            for head in range(heads):
                columns = slice(head * VD, (head + 1) * VD)
                query, key, value = head_parts(wide_block, head)
                key_s[head, at, :] = key.astype(jnp.bfloat16)
                query_s[head, at, :] = query.astype(jnp.bfloat16)
                value_s[head, at, :VD] = (value * keep).astype(jnp.bfloat16)
                value_s[head, at, VD:] = ones
                inverse = inverses[:, head : head + 1]
                grad = grad_ref[at, columns].astype(jnp.float32)
                error_s[head, at, :VD] = (grad * (keep * inverse)).astype(jnp.bfloat16)
                offset = -jnp.sum(grad * y_ref[at, columns], axis=1, keepdims=True) * inverse
                high = offset.astype(jnp.bfloat16).astype(jnp.float32)
                error_s[head, at, VD:] = jnp.where(
                    lane == 0, high, jnp.where(lane == 1, offset - high, 0.0)
                ).astype(jnp.bfloat16)
            return nothing

        lax.fori_loop(0, blocks, fill, 0)

    own = pl.ds(pl.multiple_of(step * rows, rows), rows)
    row = lax.broadcasted_iota(jnp.int32, (rows, rows), 0)

    def tile(block, totals, diagonal):
        at = pl.ds(pl.multiple_of(block * rows, rows), rows)
        column = block * rows + lax.broadcasted_iota(jnp.int32, (1, rows), 1)
        allowed = row >= segment_start(ends_ref, column) - step * rows
        if diagonal:
            allowed &= row <= lax.broadcasted_iota(jnp.int32, (rows, rows), 1)
        dkeys, dvalues = totals
        added, turned = [], []
        for head in range(heads):
            query = query_s[head, at, :]
            error = error_s[head, at, :]
            keys = key_s[head, own, :]
            inner = lax.dot_general(keys, query, NT, preferred_element_type=jnp.float32)
            dweight = lax.dot_general(value_s[head, own, :], error, NT, preferred_element_type=jnp.float32)
            slope = inner + 1.0
            weights = jnp.where(allowed, (slope * slope + 1.0) * 0.5, 0.0).astype(jnp.bfloat16)
            dinner = jnp.where(allowed, slope * dweight, 0.0).astype(jnp.bfloat16)
            added.append(
                dvalues[head] + jnp.dot(weights, error[:, :VD], preferred_element_type=jnp.float32)
            )
            turned.append(dkeys[head] + jnp.dot(dinner, query, preferred_element_type=jnp.float32))
            dquery_s[head, at, :] += lax.dot_general(dinner, keys, TN, preferred_element_type=jnp.float32)
        return tuple(turned), tuple(added)

    totals = (
        tuple(jnp.zeros((rows, LANES), jnp.float32) for _ in range(heads)),
        tuple(jnp.zeros((rows, VD), jnp.float32) for _ in range(heads)),
    )
    totals = tile(step, totals, True)
    dkeys, dvalues = lax.fori_loop(step + 1, blocks, lambda block, held: tile(block, held, False), totals)
    keep = column_of(keep_ref[:, own])
    width = out_ref.shape[2]
    total = jnp.zeros((rows, width + -width % LANES), jnp.float32)
    blank = jnp.zeros((rows, total.shape[1] - LANES), jnp.float32)

    def put(block, low):
        spread = jnp.concatenate([block, blank], axis=1)
        return spread if low == 0 else pltpu.roll(spread, low, 1)

    for head in range(heads):
        low = head * (2 * FD + VD)
        total += put(dquery_s[head, own, :] * 0.25, low)
        total += put(dkeys[head], low + FD)
        total += put(dvalues[head] * keep, low + 2 * FD)
    out_ref[...] = total[:, :width].astype(jnp.bfloat16).reshape(out_ref.shape)


def attend_back(projected, keep, ends, y, inverses, grad, heads, each):
    total = projected.shape[0]
    rows = min(512, total)
    width = projected.shape[1]
    whole = lambda columns: pl.BlockSpec((total, columns), lambda i, e: (0, 0))
    return pl.pallas_call(
        functools.partial(attend_back_kernel, heads, rows),
        grid_spec=pltpu.PrefetchScalarGridSpec(
            num_scalar_prefetch=1,
            grid=(total // rows,),
            in_specs=[whole(width), pl.BlockSpec((1, total), lambda i, e: (0, 0)), whole(heads * VD), whole(LANES), whole(heads * VD)],
            out_specs=pl.BlockSpec((rows // each, each, width), lambda i, e: (i, 0, 0)),
            scratch_shapes=[
                pltpu.VMEM((heads, total, LANES), jnp.bfloat16),
                pltpu.VMEM((heads, total, LANES), jnp.bfloat16),
                pltpu.VMEM((heads, total, 2 * VD), jnp.bfloat16),
                pltpu.VMEM((heads, total, 2 * VD), jnp.bfloat16),
                pltpu.VMEM((heads, total, LANES), jnp.float32),
            ],
        ),
        out_shape=jax.ShapeDtypeStruct((total // each, each, width), jnp.bfloat16),
        compiler_params=pltpu.CompilerParams(
            dimension_semantics=("arbitrary",), vmem_limit_bytes=VMEM
        ),
        cost_estimate=LITTLE,
    )(ends, projected, keep, y, inverses, grad)


def inv_root_mean(values):
    return lax.rsqrt(jnp.mean(values * values, axis=1, keepdims=True) + epsilon)


def wide(values):
    return values.astype(jnp.float32)


def low(values):
    return values.astype(jnp.bfloat16)


def pick(values, index, count, axis):
    size = values.shape[axis] // count
    if count == 2:
        first = lax.slice_in_dim(values, 0, size, axis=axis)
        second = lax.slice_in_dim(values, size, 2 * size, axis=axis)
        return jnp.where(index == 0, first, second)
    return lax.dynamic_slice_in_dim(values, index * size, size, axis)


def in_order(pieces, index, axis):
    count = len(pieces)
    if count == 1:
        return pieces[0]
    if count == 2:
        first = jnp.where(index == 0, pieces[0], pieces[1])
        second = jnp.where(index == 0, pieces[1], pieces[0])
        return jnp.concatenate([first, second], axis=axis)
    stacked = jnp.stack(pieces)
    placed = [
        lax.dynamic_index_in_dim(stacked, (index - place) % count, 0, keepdims=False)
        for place in range(count)
    ]
    return jnp.concatenate(placed, axis=axis)


class Wires:
    def __init__(self, mesh):
        self.dp, self.head = mesh.shape["dp"], mesh.shape["head"]
        self.ny, self.nz, self.nzh = self.dp // 2, self.head // 2, self.head // 4

    def place(self):
        p, h = lax.axis_index("dp"), lax.axis_index("head")
        self.p, self.h = p, h
        self.y, self.x, self.z, self.c = p // 2, p % 2, h // 2, h % 2
        self.zh = self.z // 2

    def over_x(self, values):
        return lax.ppermute(values, "dp", [(i, i ^ 1) for i in range(self.dp)])

    def over_y(self, values, shift):
        return lax.ppermute(
            values, "dp", [(i, ((i // 2 + shift) % self.ny) * 2 + i % 2) for i in range(self.dp)]
        )

    def over_dp(self, values, shift):
        return lax.ppermute(
            values, "dp", [(i, ((i // 2 + shift) % self.ny) * 2 + (i + 1) % 2) for i in range(self.dp)]
        )

    def over_core(self, values):
        return lax.ppermute(values, "head", [(i, i ^ 1) for i in range(self.head)])

    def over_zl(self, values):
        return lax.ppermute(values, "head", [(i, i ^ 2) for i in range(self.head)])

    def over_zh(self, values, shift):
        return lax.ppermute(
            values, "head", [(i, ((i // 4 + shift) % self.nzh) * 4 + i % 4) for i in range(self.head)]
        )

    def over_z(self, values, shift):
        return lax.ppermute(
            values, "head", [(i, ((i // 2 + shift) % self.nz) * 2 + i % 2) for i in range(self.head)]
        )

    def right(self, values, first, last):
        return lax.ppermute(
            values, "head", [(i, i + 2) for i in range(self.head) if first <= i // 2 <= last]
        )

    def left(self, values, first, last):
        return lax.ppermute(
            values, "head", [(i, i - 2) for i in range(self.head) if first <= i // 2 <= last]
        )

    def spread(self, line):
        return self.over_x(line), [self.over_y(line, s) for s in range(1, self.ny)]

    def ends(self, values):
        pairs = [(i, i + 2 if i // 2 == self.nz - 2 else i - 2) for i in range(self.head)]
        return lax.ppermute(
            values, "head", [pair for pair in pairs if pair[0] // 2 in (1, self.nz - 2)]
        )

    def arrivals(self):
        orders = []
        for z in range(self.nz):
            order = []
            for step in range(1, self.nz):
                order += [(0, step)] if z >= step else []
                order += [(1, step)] if z + step < self.nz else []
            orders.append(order)
        return orders

    def by_place(self, values):
        chosen, taken = values[0], [values[0]]
        for value in values[1:]:
            if any(value is other for other in taken):
                continue
            taken.append(value)
            here = [z for z in range(self.nz) if values[z] is value]
            chosen = jnp.where(sum((self.z == z).astype(jnp.int32) for z in here) > 0, value, chosen)
        return chosen

    def sum_y(self, values):
        total = wide(values)
        for s in range(1, self.ny):
            total = total + wide(self.over_y(values, s))
        return low(total)

    def sum_x(self, values):
        return low(wide(values) + wide(self.over_x(values)))

    def sum_all(self, values):
        values = values + self.over_core(values)
        values = values + self.over_zl(values)
        values = values + sum(self.over_zh(values, s) for s in range(1, self.nzh))
        values = values + self.over_x(values)
        return values + sum(self.over_y(values, s) for s in range(1, self.ny))

    def quarter(self, shard):
        size = shard.shape[1] // self.dp
        return lax.dynamic_slice_in_dim(shard, self.p * size, size, 1)

    def line_of(self, part):
        return [part] + [self.over_z(part, s) for s in range(1, self.nz)]

    def whole_places(self, chips, rows, size):
        at_rows = [(chip * 2 + (self.c ^ r)) * rows for r in range(2) for chip in chips]
        at_columns = [
            (((self.y - s) % self.ny) * 2 + (self.x ^ t)) * size
            for s in range(self.ny)
            for t in range(2)
        ]
        return jnp.stack(at_rows + at_columns).astype(jnp.int32)

    def line(self, block, during):
        steps = self.nz
        right = left = block
        rights, lefts = {}, {}
        orders = self.arrivals()
        chunks, chips = [block], [self.z]
        for step in range(1, steps):
            if step < steps - 1:
                right = self.right(right, step - 1, steps - 2)
                left = self.left(left, 1, steps - step)
                right, left = during(step, (right, left))
            else:
                both = jnp.where(self.z == steps - 2, right, left)
                (right, both) = during(step, (self.ends(both), both))
                left = right
            rights[step], lefts[step] = right, left
            arrived = {(0, s): rights[s] for s in rights} | {(1, s): lefts[s] for s in lefts}
            while len(chunks) < steps and all(
                orders[z][len(chunks) - 1] in arrived for z in range(steps)
            ):
                order = [orders[z][len(chunks) - 1] for z in range(steps)]
                values = [arrived[key] for key in order]
                if step == steps - 1 and values[1] is lefts[steps - 2] and values[-2] is rights[steps - 2]:
                    values[1] = values[-2] = both
                chunks.append(self.by_place(values))
                chips.append(
                    self.by_place([z - key[1] * (1 - 2 * key[0]) for z, key in enumerate(order)])
                )
        return chunks, chips


class Whole:
    def __init__(self, wires, pieces, places, rows, size):
        self.layout = [(s, t, 0, wires.nz) for s in range(wires.ny) for t in range(2)]
        self.nz = wires.nz
        self.pieces, self.rows, self.size = pieces, rows, size
        self.places = places
        self.copies = 2 * sum(count for _, _, _, count in self.layout)
        self.shape = (wires.head * rows, wires.dp * size)

    def fill(self, places_ref, refs, scratch, sems):
        copies = []
        for piece, (s, t, first, count) in enumerate(self.layout):
            column = pl.multiple_of(places_ref[2 * self.nz + 2 * s + t], self.size)
            for core in range(2):
                for slot in range(count):
                    row = pl.multiple_of(places_ref[core * self.nz + first + slot], self.rows)
                    copies.append(
                        pltpu.make_async_copy(
                            refs[core * len(self.layout) + piece].at[slot],
                            scratch.at[pl.ds(row, self.rows), pl.ds(column, self.size)],
                            sems.at[len(copies)],
                        )
                    )
        for copy in copies:
            copy.start()
        return copies


def swapped(wires, pieces):
    return [*pieces, *[wires.over_core(piece) for piece in pieces]]


def side_by_side(blocks_ref):
    return jnp.concatenate([blocks_ref[i] for i in range(blocks_ref.shape[0])], axis=1)


def by_columns(whole, places_ref, copies, weight_s, blocks, total_ref):
    each = len(copies) // len(whole.layout)
    for piece, (s, t, _, _) in enumerate(whole.layout):
        for copy in copies[piece * each : (piece + 1) * each]:
            copy.wait()
        at = pl.ds(pl.multiple_of(places_ref[2 * whole.nz + 2 * s + t], whole.size), whole.size)
        total, low = 0.0, 0
        for block in blocks:
            total += jnp.dot(
                block, weight_s[low : low + block.shape[1], at], preferred_element_type=jnp.float32
            )
            low += block.shape[1]
        total_ref[:, at] = total


def mix_kernel(whole, places_ref, *refs):
    count = len(whole.pieces)
    attended_ref, tokens_ref, gain_ref, middle_ref, normed_ref, weight_s, sems = refs[count:]
    copies = whole.fill(places_ref, refs[:count], weight_s, sems)
    by_columns(whole, places_ref, copies, weight_s, [side_by_side(attended_ref)], middle_ref)
    middle = middle_ref[...] + wide(tokens_ref[...])
    middle_ref[...] = middle
    normed_ref[...] = (middle * inv_root_mean(middle) * gain_ref[...]).astype(jnp.bfloat16)


def with_whole(kernel, whole, args, outs, flops):
    in_vmem = pl.BlockSpec(memory_space=pltpu.VMEM)
    return pl.pallas_call(
        functools.partial(kernel, whole),
        grid_spec=pltpu.PrefetchScalarGridSpec(
            num_scalar_prefetch=1,
            grid=(),
            in_specs=[pl.BlockSpec(memory_space=pl.ANY)] * len(whole.pieces) + [in_vmem] * len(args),
            out_specs=[in_vmem] * len(outs),
            scratch_shapes=[
                pltpu.VMEM(whole.shape, jnp.bfloat16),
                pltpu.SemaphoreType.DMA((whole.copies,)),
            ],
        ),
        out_shape=[jax.ShapeDtypeStruct(shape, kind) for shape, kind in outs],
        compiler_params=pltpu.CompilerParams(vmem_limit_bytes=VMEM),
        cost_estimate=LITTLE,
    )(whole.places, *whole.pieces, *args)


def mix(attended, whole, tokens, gain):
    return with_whole(
        mix_kernel,
        whole,
        (attended, tokens, gain),
        ((tokens.shape, jnp.float32), (tokens.shape, jnp.bfloat16)),
        2 * tokens.shape[0] * whole.shape[0] * whole.shape[1],
    )


def unmix_kernel(whole, places_ref, *refs):
    count = len(whole.pieces)
    a_ref, b_ref, c_ref, middle_ref, grad_ref, gain_ref = refs[count : count + 6]
    dmiddle_ref, dmixed_ref, part_ref, out_ref, weight_s, sems = refs[count + 6 :]
    copies = whole.fill(places_ref, refs[:count], weight_s, sems)
    middle = middle_ref[...]
    inv_two = inv_root_mean(middle)
    dnormed = wide(a_ref[...]) + wide(b_ref[...]) + wide(c_ref[...])
    scaled = middle * inv_two
    error = dnormed * gain_ref[...]
    dmiddle = wide(grad_ref[...]) + inv_two * (
        error - scaled * jnp.mean(error * scaled, axis=1, keepdims=True)
    )
    part_ref[...] = jnp.sum(dnormed * scaled, axis=0, keepdims=True)
    dmiddle_ref[...] = dmiddle
    dmixed = dmiddle.astype(jnp.bfloat16)
    dmixed_ref[...] = dmixed
    for copy in copies:
        copy.wait()
    width = out_ref.shape[2]
    for head in range(out_ref.shape[0]):
        out_ref[head] = lax.dot_general(
            dmixed, weight_s[head * width : (head + 1) * width, :], NT, preferred_element_type=jnp.float32
        ).astype(jnp.bfloat16)


def unmix(parts, middle, grad, gain, whole, heads):
    rows, depth = middle.shape
    return with_whole(
        unmix_kernel,
        whole,
        (*parts, middle, grad, gain),
        (
            (middle.shape, jnp.float32),
            (middle.shape, jnp.bfloat16),
            ((1, depth), jnp.float32),
            ((heads, rows, whole.shape[0] // heads), jnp.bfloat16),
        ),
        2 * rows * whole.shape[0] * whole.shape[1],
    )


def last_kernel(whole, places_ref, *refs):
    count = len(whole.pieces)
    proj_ref, tokens_ref, dmiddle_ref, gain_ref, grad_ref, weight_s, sems = refs[count:]
    copies = whole.fill(places_ref, refs[:count], weight_s, sems)
    blocks = [proj_ref[head] for head in range(proj_ref.shape[0])]
    by_columns(whole, places_ref, copies, weight_s, blocks, grad_ref)
    dnormed = grad_ref[...]
    tokens = wide(tokens_ref[...])
    inv_one = inv_root_mean(tokens)
    scaled = tokens * inv_one
    error = dnormed * gain_ref[...]
    grad_ref[...] = dmiddle_ref[...] + inv_one * (
        error - scaled * jnp.mean(error * scaled, axis=1, keepdims=True)
    )


def last(proj, whole, tokens, dmiddle, gain):
    return with_whole(
        last_kernel,
        whole,
        (proj, tokens, dmiddle, gain),
        ((tokens.shape, jnp.float32),),
        2 * tokens.shape[0] * whole.shape[0] * whole.shape[1],
    )[0]


class Units:
    def __init__(self, wires, pieces, matrices, rows, columns):
        self.matrices = matrices
        self.layout = [piece[1:] for piece in pieces]
        self.pieces = [piece[0] for piece in pieces]
        self.rows, self.columns = rows, columns
        self.places = jnp.stack([((wires.y - s) % wires.ny) * columns for s in range(wires.ny)]).astype(
            jnp.int32
        )
        self.shape = (matrices, wires.nzh * rows, wires.ny * columns)

    def fill(self, places_ref, refs, scratch, sems):
        copies = []
        for matrix in range(self.matrices):
            for ref, (first, count, zh, y) in zip(refs, self.layout):
                if not first <= matrix < first + count:
                    continue
                column = pl.multiple_of(places_ref[y], self.columns)
                copies.append(
                    pltpu.make_async_copy(
                        ref.at[matrix - first],
                        scratch.at[
                            matrix, pl.ds(zh * self.rows, self.rows), pl.ds(column, self.columns)
                        ],
                        sems.at[len(copies)],
                    )
                )
        for copy in copies:
            copy.start()
        return copies


def with_units(kernel, units, blocks, outs, scratch, flops, transcendentals):
    anywhere = pl.BlockSpec(memory_space=pl.ANY)
    copies = sum(count for _, count, _, _ in units.layout)
    return pl.pallas_call(
        functools.partial(kernel, units),
        grid_spec=pltpu.PrefetchScalarGridSpec(
            num_scalar_prefetch=1,
            grid=(),
            in_specs=[anywhere] * (len(units.pieces) + len(blocks)),
            out_specs=[anywhere] * len(outs),
            scratch_shapes=[
                pltpu.VMEM(units.shape, jnp.bfloat16),
                pltpu.SemaphoreType.DMA((copies,)),
            ]
            + scratch,
        ),
        out_shape=[jax.ShapeDtypeStruct(shape, kind) for shape, kind in outs],
        compiler_params=pltpu.CompilerParams(vmem_limit_bytes=VMEM),
        cost_estimate=LITTLE,
    )(units.places, *units.pieces, *blocks)


def started(copies):
    for copy in copies:
        copy.start()
    return copies


def awaited(copies):
    for copy in copies:
        copy.wait()


def gate_kernel(count, units, places_ref, *refs):
    pieces, refs = refs[: len(units.pieces)], refs[len(units.pieces) :]
    blocks, (gate_ref, up_ref, normed_ref) = refs[: 2 * count], refs[2 * count : 2 * count + 3]
    weight_s, sems, normed_s, gate_s, up_s, in_sems, out_sems = refs[2 * count + 3 :]
    rows = blocks[0].shape[0]
    arrivals = [
        pltpu.make_async_copy(
            blocks[i], normed_s.at[i // 2, pl.ds(i % 2 * rows, rows)], in_sems.at[i]
        )
        for i in range(2 * count)
    ]
    started(arrivals[:2])
    weights = units.fill(places_ref, pieces, weight_s, sems)
    started(arrivals[2:])
    each = len(weights) // units.matrices
    sent = []
    for chunk in range(count):
        awaited(arrivals[2 * chunk : 2 * chunk + 2])
        sent += started(
            [pltpu.make_async_copy(normed_s.at[chunk], normed_ref.at[chunk], out_sems.at[3 * chunk])]
        )
        normed = normed_s[chunk]
        awaited(weights[:each] if chunk == 0 else [])
        gate_s[chunk] = lax.dot_general(normed, weight_s[0], NT, preferred_element_type=jnp.float32)
        sent += started(
            [pltpu.make_async_copy(gate_s.at[chunk], gate_ref.at[chunk], out_sems.at[3 * chunk + 1])]
        )
        awaited(weights[each:] if chunk == 0 else [])
        up_s[chunk] = lax.dot_general(normed, weight_s[1], NT, preferred_element_type=jnp.float32)
        sent += started(
            [pltpu.make_async_copy(up_s.at[chunk], up_ref.at[chunk], out_sems.at[3 * chunk + 2])]
        )
    awaited(sent)


def gate_up(pairs, units):
    count = len(pairs)
    rows, depth = pairs[0][0].shape
    unit, full = (count, 2 * rows, units.shape[1]), (count, 2 * rows, depth)
    return with_units(
        functools.partial(gate_kernel, count),
        units,
        [block for pair in pairs for block in pair],
        ((unit, jnp.float32), (unit, jnp.float32), (full, jnp.bfloat16)),
        [
            pltpu.VMEM(full, jnp.bfloat16),
            pltpu.VMEM(unit, jnp.float32),
            pltpu.VMEM(unit, jnp.float32),
            pltpu.SemaphoreType.DMA((2 * count,)),
            pltpu.SemaphoreType.DMA((3 * count,)),
        ],
        8 * count * rows * depth * units.shape[1],
        0,
    )


def down_kernel(places, units, places_ref, *refs):
    count = len(places)
    pieces, refs = refs[: len(units.pieces)], refs[len(units.pieces) :]
    blocks, refs = refs[: 4 * count], refs[4 * count :]
    unit_refs, grad_ref, refs = refs[:3], refs[3], refs[4:]
    dnormed, branches = refs[: 2 * count], refs[2 * count : 4 * count]
    weight_s, sems, pre_s, grad_s, unit_s, back_s, branch_s, in_sems, out_sems = refs[4 * count :]
    rows = blocks[0].shape[0]
    both = [pl.ds(0, rows), pl.ds(rows, rows)]
    arrivals = []
    for chunk, place in enumerate(places):
        one, two, gate, up = blocks[4 * chunk : 4 * chunk + 4]
        for i, (source, target) in enumerate(
            (
                (gate.at[place], pre_s.at[chunk, 0]),
                (up.at[place], pre_s.at[chunk, 1]),
                (one, grad_s.at[chunk, both[0]]),
                (two, grad_s.at[chunk, both[1]]),
            )
        ):
            arrivals.append(pltpu.make_async_copy(source, target, in_sems.at[4 * chunk + i]))
    started(arrivals[:4])
    weights = units.fill(places_ref, pieces, weight_s, sems)
    started(arrivals[4:])
    each = len(weights) // units.matrices
    dot = functools.partial(jnp.dot, preferred_element_type=jnp.float32)
    sent = []

    def send(source, target):
        sent.append(pltpu.make_async_copy(source, target, out_sems.at[len(sent)]))
        sent[-1].start()

    for chunk in range(count):
        awaited(arrivals[4 * chunk : 4 * chunk + 2])
        gate, up = pre_s[chunk, 0], pre_s[chunk, 1]
        sigmoid = jax.nn.sigmoid(gate)
        silu = gate * sigmoid
        hidden = (silu * up).astype(jnp.bfloat16)
        unit_s[chunk, 0] = hidden
        send(unit_s.at[chunk, 0], unit_refs[0].at[chunk])
        awaited(arrivals[4 * chunk + 2 : 4 * chunk + 4])
        send(grad_s.at[chunk], grad_ref.at[chunk])
        awaited(weights[:each] if chunk == 0 else [])
        dhidden = lax.dot_general(grad_s[chunk], weight_s[0], NT, preferred_element_type=jnp.float32)
        dgate = (dhidden * up * sigmoid * (1.0 + gate * (1.0 - sigmoid))).astype(jnp.bfloat16)
        dup = (dhidden * silu).astype(jnp.bfloat16)
        unit_s[chunk, 1] = dgate
        unit_s[chunk, 2] = dup
        send(unit_s.at[chunk, 1], unit_refs[1].at[chunk])
        send(unit_s.at[chunk, 2], unit_refs[2].at[chunk])
        awaited(weights[each:] if chunk == 0 else [])
        back_s[chunk] = (dot(dgate, weight_s[1]) + dot(dup, weight_s[2])).astype(jnp.bfloat16)
        for i in range(2):
            send(back_s.at[chunk, both[i]], dnormed[2 * chunk + i])
        branch_s[chunk] = dot(hidden, weight_s[0]).astype(jnp.bfloat16)
        for i in range(2):
            send(branch_s.at[chunk, both[i]], branches[2 * chunk + i])
    awaited(sent)


def down(given, units):
    count = len(given)
    rows, depth = given[0][0].shape
    unit, full = (count, 2 * rows, units.shape[1]), (count, 2 * rows, depth)
    part = ((rows, depth), jnp.bfloat16)
    outs = with_units(
        functools.partial(down_kernel, [chunk[4] for chunk in given]),
        units,
        [block for chunk in given for block in chunk[:4]],
        ((unit, jnp.bfloat16),) * 3 + ((full, jnp.bfloat16),) + (part,) * (4 * count),
        [
            pltpu.VMEM((count, 2, 2 * rows, units.shape[1]), jnp.float32),
            pltpu.VMEM(full, jnp.bfloat16),
            pltpu.VMEM((count, 3, 2 * rows, units.shape[1]), jnp.bfloat16),
            pltpu.VMEM(full, jnp.bfloat16),
            pltpu.VMEM(full, jnp.bfloat16),
            pltpu.SemaphoreType.DMA((4 * count,)),
            pltpu.SemaphoreType.DMA((8 * count,)),
        ],
        16 * count * rows * depth * units.shape[1],
        2 * count * rows * units.shape[1],
    )
    halves = lambda parts: [parts[2 * i : 2 * i + 2] for i in range(count)]
    return outs[:4], halves(outs[4 : 4 + 2 * count]), halves(outs[4 + 2 * count :])


def unit_grad_kernel(order, ny, nzh, places_ref, *refs):
    arrays, (mine_ref, sent_ref, total_s) = refs[:-3], refs[-3:]
    for i, (left, at, right, to) in enumerate(order):
        added = lax.dot_general(
            arrays[left][at], arrays[right][to], TN, preferred_element_type=jnp.float32
        )
        if i == 0:
            total_s[...] = added
        else:
            total_s[...] += added
    units, columns = mine_ref.shape[1:]
    for y in range(ny):
        for zh in range(nzh):
            block = total_s[
                pl.ds(pl.multiple_of(places_ref[ny + zh], units), units),
                pl.ds(pl.multiple_of(places_ref[y], columns), columns),
            ].astype(jnp.bfloat16)
            if y == 0:
                mine_ref[zh] = block
            else:
                sent_ref[y - 1, zh] = block


def unit_grad(wires, lefts, rights):
    ny, nzh = wires.ny, wires.nzh
    arrays = []

    def index(array):
        for i, other in enumerate(arrays):
            if other is array:
                return i
        arrays.append(array)
        return len(arrays) - 1

    order = [(index(left), at, index(right), to) for (left, at), (right, to) in zip(lefts, rights)]
    units, depth = lefts[0][0].shape[2], rights[0][0].shape[2]
    tokens = len(lefts) * lefts[0][0].shape[1]
    rows, columns = units // nzh, depth // ny
    places = jnp.stack(
        [((wires.y + s) % ny) * columns for s in range(ny)] + [s * rows for s in range(nzh)]
    ).astype(jnp.int32)
    in_vmem = pl.BlockSpec(memory_space=pltpu.VMEM)
    return pl.pallas_call(
        functools.partial(unit_grad_kernel, order, ny, nzh),
        grid_spec=pltpu.PrefetchScalarGridSpec(
            num_scalar_prefetch=1,
            grid=(),
            in_specs=[in_vmem] * len(arrays),
            out_specs=[in_vmem] * 2,
            scratch_shapes=[pltpu.VMEM((units, depth), jnp.float32)],
        ),
        out_shape=[
            jax.ShapeDtypeStruct((nzh, rows, columns), jnp.bfloat16),
            jax.ShapeDtypeStruct((ny - 1, nzh, rows, columns), jnp.bfloat16),
        ],
        compiler_params=pltpu.CompilerParams(vmem_limit_bytes=VMEM),
        cost_estimate=LITTLE,
    )(places, *arrays)


def out_grad_kernel(nz, ny, places_ref, mine_ref, other_ref, grad_ref, other_grad_ref, *refs):
    outs, (left_s, right_s) = refs[: 2 * ny], refs[2 * ny :]
    step = pl.program_id(0)
    tokens, width = grad_ref.shape[0], outs[0].shape[2]

    @pl.when(step == 0)
    def _():
        right_s[:tokens] = grad_ref[...]
        right_s[tokens:] = other_grad_ref[...]

    left_s[:tokens] = mine_ref[places_ref[step]]
    left_s[tokens:] = other_ref[places_ref[step] // 2]
    left = left_s[...]
    for i, out_ref in enumerate(outs):
        column = pl.multiple_of(places_ref[nz + i], width)
        out_ref[0] = lax.dot_general(
            left, right_s[:, pl.ds(column, width)], TN, preferred_element_type=jnp.float32
        ).astype(jnp.bfloat16)


def out_grad_parts(wires, mine, other, d_mixed, other_d_mixed):
    heads, tokens, rows = mine.shape
    depth = d_mixed.shape[1]
    nz, ny, width = wires.nz, wires.ny, depth // wires.dp
    places = jnp.stack(
        [z * 2 + wires.c for z in range(nz)]
        + [(((wires.y + s) % ny) * 2 + (wires.x ^ t)) * width for t in range(2) for s in range(ny)]
    ).astype(jnp.int32)
    full = lambda *shape: pl.BlockSpec(shape, lambda i, p: (0,) * len(shape))
    outs = pl.pallas_call(
        functools.partial(out_grad_kernel, nz, ny),
        grid_spec=pltpu.PrefetchScalarGridSpec(
            num_scalar_prefetch=1,
            grid=(nz,),
            in_specs=[
                full(heads, tokens, rows),
                full(nz, tokens, rows),
                full(tokens, depth),
                full(tokens, depth),
            ],
            out_specs=[pl.BlockSpec((1, rows, width), lambda i, p: (i, 0, 0))] * (2 * ny),
            scratch_shapes=[
                pltpu.VMEM((2 * tokens, rows), jnp.bfloat16),
                pltpu.VMEM((2 * tokens, depth), jnp.bfloat16),
            ],
        ),
        out_shape=[jax.ShapeDtypeStruct((nz, rows, width), jnp.bfloat16)] * (2 * ny),
        compiler_params=pltpu.CompilerParams(
            dimension_semantics=("arbitrary",), vmem_limit_bytes=VMEM
        ),
        cost_estimate=LITTLE,
    )(places, mine, other, d_mixed, other_d_mixed)
    return outs[:ny], outs[ny:]


def in_grad_kernel(normed_ref, grad_ref, weight_ref, gain_ref, out_ref, part_ref):
    blocks, rows, width = grad_ref.shape
    grad = grad_ref[...].reshape(blocks * rows, width)
    total = lax.dot_general(grad, normed_ref[...], TN, preferred_element_type=jnp.float32)
    out_ref[...] = total.astype(jnp.bfloat16)
    part_ref[...] = jnp.sum(total * wide(weight_ref[...]), axis=0, keepdims=True) / gain_ref[...]


def in_grad_parts(normed, grad, weight, gain):
    tokens, depth = normed.shape
    width = grad.shape[2]
    size = min(512, depth)
    block = lambda rows: pl.BlockSpec((rows, size), lambda i: (0, i))
    return pl.pallas_call(
        in_grad_kernel,
        grid=(depth // size,),
        in_specs=[
            block(tokens),
            pl.BlockSpec(grad.shape, lambda i: (0, 0, 0)),
            block(width),
            block(1),
        ],
        out_specs=[block(width), block(1)],
        out_shape=[
            jax.ShapeDtypeStruct((width, depth), jnp.bfloat16),
            jax.ShapeDtypeStruct((1, depth), jnp.float32),
        ],
        compiler_params=pltpu.CompilerParams(
            dimension_semantics=("arbitrary",), vmem_limit_bytes=VMEM
        ),
        cost_estimate=LITTLE,
    )(normed, grad, weight, gain)


def tie(*values):
    return lax.optimization_barrier(values)


def per_device(
    wires,
    tokens,
    keep_mask,
    seq_lengths,
    attn_gain,
    in_weight,
    out_weight,
    ffn_gain,
    gate_weight,
    up_weight,
    down_weight,
    out_grad,
):
    wires.place()
    heads_here = in_weight.shape[1] // (2 * FD + VD)
    rows, depth = tokens.shape
    group_rows = rows * wires.head
    out_rows = heads_here * VD
    size = depth // wires.dp
    tokens_wide = wide(tokens)
    own = low(tokens_wide * inv_root_mean(tokens_wide) * attn_gain)
    across_y = range(1, wires.ny)

    def on_y(pieces):
        return [[wires.over_y(piece, s) for s in across_y] for piece in pieces]

    def swap(values):
        return lax.all_to_all(values, "head", split_axis=0, concat_axis=0, tiled=True)

    def add(*values):
        return low(sum(wide(value) for value in values))

    packed_width = in_weight.shape[1]
    in_turned = in_weight.T
    in_part = wires.quarter(in_turned)
    keep_row = keep_mask.astype(jnp.float32)[None]
    ends = jnp.cumsum(seq_lengths[0])
    stacked = jnp.stack([gate_weight.T, up_weight.T, down_weight])
    unit_own = pick(stacked, wires.x, 2, 1)
    unit_other = pick(stacked, 1 - wires.x, 2, 1)
    share = out_rows * size // rows
    block = jnp.concatenate([own, wires.quarter(out_weight).reshape(rows, share)], axis=1)

    flying = {}

    def beside_line(step, values):
        if step == 1:
            by_x = wires.over_x(unit_other)
            values, flying["by_x"], flying["own"], flying["in_part"], flying["out_grad"], flying["swap"] = tie(
                values, by_x, unit_own, in_part, out_grad, wires.over_core(block)
            )
        elif step == 2:
            pair = in_order([flying["own"], flying["by_x"]], wires.x, 2)
            by_x = wires.over_x(flying["out_grad"])
            values, flying["grad_x"], flying["pair"], flying["out_grad"] = tie(
                values, by_x, pair, flying["out_grad"]
            )
        elif step == wires.nz - 1:
            by_y = [wires.over_y(flying["pair"][:2], s) for s in across_y]
            values, flying["by_y"], flying["pair"], flying["grad_x"] = tie(
                values, by_y, flying["pair"], flying["grad_x"]
            )
        else:
            (values,) = tie(values)
        return values

    chunks, chips = wires.line(block, beside_line)
    others = [flying["swap"]] + [wires.over_core(chunk) for chunk in chunks[1:]]
    pieces = [piece for pair in zip(chunks, others) for piece in pair]
    places = jnp.stack(
        [(chip * 2 + (wires.c ^ r)) * rows for chip in chips for r in range(2)]
    ).astype(jnp.int32)
    pieces, unit_pair, out_grad, grad_x = tie(
        pieces, flying["pair"], flying["out_grad"], flying["grad_x"]
    )

    def shares(blocks):
        return jnp.stack([piece[:, depth:].reshape(out_rows, size) for piece in blocks])

    by_zh_g = [wires.over_zh(unit_pair[:1], s) for s in range(1, wires.nzh)]
    out_line = shares(pieces[::2])
    out_x, out_y = wires.over_x(out_line), [wires.over_y(out_line, s) for s in across_y]
    projected, normed, attended_wide, inverses, attended = attend(
        pieces, places, in_turned, keep_row, ends, heads_here
    )
    attended, out_x, out_y, by_zh_g, unit_pair, out_grad = tie(
        attended, out_x, out_y, by_zh_g, unit_pair, out_grad
    )
    attended_here = swap(attended).reshape(wires.head, rows, out_rows)
    grad_z = wires.over_zl(out_grad)
    out_across = [wires.over_x(piece) for piece in out_y]
    by_zh_gy = on_y(by_zh_g)
    out_line_swap = shares(pieces[1::2])
    out_x_swap, out_y_swap = wires.over_core(out_x), [wires.over_core(piece) for piece in out_y]
    attended_here, out_across, grad_z, out_x_swap, out_y_swap, unit_pair, by_zh_gy, out_line_swap = tie(
        attended_here, out_across, grad_z, out_x_swap, out_y_swap, unit_pair, by_zh_gy, out_line_swap
    )
    out_across_swap = [wires.over_core(piece) for piece in out_across]

    def in_layout(line, by_x, by_y, across):
        pieces = [line, by_x]
        for piece in zip(by_y, across):
            pieces += piece
        return pieces

    out_pieces = in_layout(out_line, out_x, out_y, out_across)
    out_pieces += in_layout(out_line_swap, out_x_swap, out_y_swap, out_across_swap)
    out_whole = Whole(wires, out_pieces, wires.whole_places(chips, out_rows, size), out_rows, size)
    middle, normed_two = mix(attended_here, out_whole, tokens, ffn_gain[None])

    normed_two, unit_pair, grad_x, grad_z, out_grad = tie(
        normed_two, unit_pair, grad_x, grad_z, out_grad
    )
    two_x, two_z = wires.over_x(normed_two), wires.over_zl(normed_two)
    by_zh_u = [wires.over_zh(unit_pair[1:2], s) for s in range(1, wires.nzh)]
    by_y_d = [wires.over_y(unit_pair[2:], s) for s in across_y]
    two_swap = wires.over_core(normed_two)
    two_x, two_z, by_zh_u, two_swap, by_y_d, unit_pair = tie(
        two_x, two_z, by_zh_u, two_swap, by_y_d, unit_pair
    )
    two_corner = wires.over_x(two_z)
    by_zh_uy = on_y(by_zh_u)
    by_zh_d = [wires.over_zh(unit_pair[2:], s) for s in range(1, wires.nzh)]
    two_swaps = [two_swap] + [wires.over_core(piece) for piece in (two_x, two_z)]
    two_corner, by_zh_uy, two_swaps, two_x, two_z, grad_z, attended_here, by_zh_d = tie(
        two_corner, by_zh_uy, two_swaps, two_x, two_z, grad_z, attended_here, by_zh_d
    )

    spot = unit_pair.shape[1], unit_pair.shape[2]
    gu_pair = unit_pair[:2]
    gates = [(gu_pair, 0, 2, 0, 0)] + [(flying["by_y"][s - 1], 0, 2, 0, s) for s in across_y]
    for zh in range(1, wires.nzh):
        for place, piece, on in ((0, by_zh_g, by_zh_gy), (1, by_zh_u, by_zh_uy)):
            gates.append((piece[zh - 1], place, 1, zh, 0))
            gates += [(on[zh - 1][s - 1], place, 1, zh, s) for s in across_y]
    units = Units(wires, gates, 2, *spot)

    grad_corner = wires.over_x(grad_z)
    two_corner_swap = wires.over_core(two_corner)
    for_other = pick(attended_here.reshape(wires.nz, 2, rows, out_rows), 1 - wires.c, 2, 1)[:, 0]
    attended_other = wires.over_core(for_other)
    by_zh_dy = on_y(by_zh_d)
    first = gate_up(list(zip([normed_two, two_x, two_z], two_swaps)), units)
    first, grad_corner, two_corner, two_corner_swap, grad_z, attended_other, by_zh_dy = tie(
        first, grad_corner, two_corner, two_corner_swap, grad_z, attended_other, by_zh_dy
    )
    grad_swaps = [wires.over_core(grad) for grad in (out_grad, grad_x, grad_z, grad_corner)]
    second = gate_up([(two_corner, two_corner_swap)], units)
    second, grad_swaps = tie(second, grad_swaps)
    grad_pairs = list(zip([out_grad, grad_x, grad_z, grad_corner], grad_swaps))
    downs = [(unit_pair[2:], 0, 1, 0, 0)] + [(by_y_d[s - 1], 0, 1, 0, s) for s in across_y]
    for zh in range(1, wires.nzh):
        downs.append((by_zh_d[zh - 1], 0, 1, zh, 0))
        downs += [(by_zh_dy[zh - 1][s - 1], 0, 1, zh, s) for s in across_y]
    units = Units(
        wires, downs + [(array, at + 1, count, zh, s) for array, at, count, zh, s in gates], 3, *spot
    )

    in_part, grad_corner = tie(flying["in_part"], grad_corner)
    in_line = [in_part] + [wires.over_z(in_part, s) for s in range(1, wires.nz)]
    outs_co, (dnormed_c, dnormed_o), (branch_c, branch_o) = down(
        [(*grad_pairs[3], second[0], second[1], 0), (*grad_pairs[0], first[0], first[1], 0)], units
    )
    outs_co, in_line, dnormed_c, dnormed_o = tie(outs_co, in_line, dnormed_c, dnormed_o)
    swap_c, swap_o = wires.over_core(dnormed_c[1]), wires.over_core(dnormed_o[1])
    swap_c, swap_o, outs_co, in_line = tie(swap_c, swap_o, outs_co, in_line)
    sum_c = add(dnormed_c[0], swap_c)
    to_z = wires.over_x(sum_c)
    in_line = jnp.stack(in_line)
    in_y = [wires.over_y(in_line, s) for s in across_y]
    grad_x_pair, grad_z_pair, *_ = tie(grad_pairs[1], grad_pairs[2], sum_c, outs_co)
    outs_xz, (dnormed_x, dnormed_z), (branch_x, branch_z) = down(
        [(*grad_x_pair, first[0], first[1], 1), (*grad_z_pair, first[0], first[1], 2)], units
    )
    dnormed_x, dnormed_z, to_z, in_y = tie(dnormed_x, dnormed_z, to_z, in_y)
    swap_x, swap_z = wires.over_core(dnormed_x[1]), wires.over_core(dnormed_z[1])
    swap_x, swap_z, to_z = tie(swap_x, swap_z, to_z)
    sum_x = add(dnormed_x[0], swap_x)
    final_x = wires.over_x(sum_x)
    sum_z = add(dnormed_z[0], swap_z, to_z)
    final_z = wires.over_zl(sum_z)
    sum_o = add(dnormed_o[0], swap_o)

    every = (outs_co, outs_xz, first[2], second[2])

    def grad_of(every, unit, token):
        co, xz, normed_oxz, normed_c = every
        lefts = [(co[unit], 0), (co[unit], 1), (xz[unit], 0), (xz[unit], 1)]
        if token:
            rights = [(co[3], 0), (co[3], 1), (xz[3], 0), (xz[3], 1)]
        else:
            rights = [(normed_c, 0), (normed_oxz, 0), (normed_oxz, 1), (normed_oxz, 2)]
        return unit_grad(wires, lefts, rights)

    def grad_y(mine, sent):
        return mine, [wires.over_y(sent[s - 1], s) for s in across_y]

    def grad_last(mine, sent):
        return wide(in_order([mine, sent], wires.x, 0))

    every, sum_x, sum_z = tie(every, sum_x, sum_z)
    gate_mine, gate_sent = grad_of(every, 1, False)
    in_swaps = [wires.over_core(piece) for piece in (in_line, *in_y)]
    final_x, final_z, gate_mine, gate_sent, in_swaps, sum_o, in_line = tie(
        final_x, final_z, gate_mine, gate_sent, in_swaps, sum_o, in_line
    )
    gate_back = grad_y(gate_mine, gate_sent)
    d_middle, d_mixed, ffn_gain_part, d_attended = unmix(
        (sum_o, final_x, final_z), middle, out_grad, ffn_gain[None], out_whole, wires.head
    )
    every, d_attended, d_mixed, branches, in_line, in_y = tie(
        every, d_attended, d_mixed, (branch_o, branch_x, branch_z, branch_c), in_line, in_y
    )
    d_attended = swap(d_attended).reshape(group_rows, out_rows)
    other_d_mixed = wires.over_core(d_mixed)
    in_x = wires.over_x(in_line)
    swap_c, swap_x, swap_z = (wires.over_core(branches[i][1]) for i in (3, 1, 2))
    up_parts = grad_of(every, 2, False)
    out_own, out_sent = out_grad_parts(wires, attended_here, attended_other, d_mixed, other_d_mixed)
    down_parts = grad_of(every, 0, True)
    d_attended, out_own, out_sent, up_parts, down_parts, gate_back, in_x, swap_c, swap_x, swap_z = tie(
        d_attended, out_own, out_sent, up_parts, down_parts, gate_back, in_x, swap_c, swap_x, swap_z
    )

    def total_of(mine, sent):
        return [add(mine[s], *[piece[s] for piece in sent]) for s in range(wires.nzh)]

    def on_zh(totals):
        return totals[0], [wires.over_zh(totals[s], -s) for s in range(1, wires.nzh)]

    sum_c = add(branches[3][0], swap_c)
    gate_totals = total_of(*gate_back)
    gate_totals, d_attended, sum_c, out_sent, up_parts = tie(
        gate_totals, d_attended, sum_c, out_sent, up_parts
    )
    up_back = grad_y(*up_parts)
    gate_back = on_zh(gate_totals)
    out_first = [wires.over_x(out_sent[s]) for s in across_y]
    to_x = wires.over_zl(sum_c)
    d_projected = attend_back(
        projected, keep_row, ends, attended_wide, inverses, d_attended, heads_here, rows
    )
    d_projected, gate_back, up_back, to_x, out_first = tie(d_projected, gate_back, up_back, to_x, out_first)
    d_projected, down_parts, in_y, out_own, out_first, in_x = tie(
        d_projected, down_parts, in_y, out_own, out_first, in_x
    )
    d_here = swap(d_projected)
    down_back = grad_y(*down_parts)
    in_across = [wires.over_x(piece) for piece in in_y]
    up_totals = total_of(*up_back)
    in_back, attn_gain_part = in_grad_parts(normed, d_projected, in_turned, attn_gain[None])
    d_here, in_back, attn_gain_part, down_back, up_totals, in_across = tie(
        d_here, in_back, attn_gain_part, down_back, up_totals, in_across
    )
    in_across_swap = [wires.over_core(piece) for piece in in_across]
    in_x_swap = wires.over_core(in_x)
    down_totals = total_of(*down_back)
    out_total = [add(out_own[s], out_first[s - 1]) for s in across_y]
    down_totals, up_totals, out_total, out_own, branches, in_across, in_across_swap, in_x_swap, gains, d_here = tie(
        down_totals,
        up_totals,
        out_total,
        out_own,
        branches,
        in_across,
        in_across_swap,
        in_x_swap,
        jnp.concatenate([attn_gain_part, ffn_gain_part], axis=0),
        d_here,
    )
    cut = packed_width // 2
    in_pieces = in_layout(in_line, in_x, in_y, in_across)
    in_pieces += in_layout(in_swaps[0], in_x_swap, in_swaps[1:], in_across_swap)
    in_chips = [(wires.z - s) % wires.nz for s in range(wires.nz)]
    in_whole = Whole(
        wires, in_pieces, wires.whole_places(in_chips, packed_width, size), packed_width, size
    )
    up_back = on_zh(up_totals)
    out_last = wires.over_x(out_sent[0])
    out_y = [wires.over_y(total, s) for total, s in zip(out_total, across_y)]
    final_z = wires.over_zl(add(branches[2][0], swap_z))
    in_grad = last(d_here, in_whole, tokens, d_middle, attn_gain[None])
    in_grad, up_back, down_totals, out_last, out_y, final_z, in_back, gains, branches, swap_x, to_x = tie(
        in_grad, up_back, down_totals, out_last, out_y, final_z, in_back, gains, branches, swap_x, to_x
    )
    down_back = on_zh(down_totals)
    final_x = wires.over_x(add(branches[1][0], swap_x, to_x))
    in_x, in_y = wires.over_x(in_back[:cut]), [wires.over_y(in_back[cut:], s) for s in across_y]
    swap_o = wires.over_core(branches[0][1])
    out_total = add(out_own[0], out_last, *out_y)
    firsts = [add(mine, *sent) for mine, sent in (gate_back, up_back)]
    gains = gains + wires.over_core(gains)
    down_back, final_x, in_x, in_y, swap_o, out_total, firsts, gains = tie(
        down_back, final_x, in_x, in_y, swap_o, out_total, firsts, gains
    )
    in_halves = (add(in_back[:cut], in_x), add(in_back[cut:], *in_y))
    out_turns = lax.all_to_all(
        out_total,
        "head",
        split_axis=0,
        concat_axis=0,
        tiled=True,
        axis_index_groups=[[z * 2 + c for z in range(wires.nz)] for c in range(2)],
    )
    others = wires.over_x(jnp.stack([pick(total, 1 - wires.x, 2, 1) for total in firsts]))
    in_halves = (wires.sum_y(in_halves[0]), wires.sum_x(in_halves[1]))
    output = low(middle + wide(branches[0][0]) + wide(swap_o) + wide(final_x) + wide(final_z))
    gains = gains + wires.over_zl(gains)
    down_total = add(down_back[0], *down_back[1])
    out_turns, others, in_halves, gains, output, down_total = tie(
        out_turns, others, in_halves, gains, output, down_total
    )
    out_part = add(*[out_turns[z] for z in range(wires.nz)])
    out_x = wires.over_x(out_part)
    out_by_y = [wires.over_y(out_part, s) for s in across_y]
    others = [others[0], others[1], wires.over_x(pick(down_total, 1 - wires.x, 2, 1))]
    totals = [*firsts, down_total]
    gains = gains + sum(wires.over_zh(gains, s) for s in range(1, wires.nzh))
    out_x, out_by_y, gains, others = tie(out_x, out_by_y, gains, others)
    out_by_yx = [wires.over_y(out_x, s) for s in across_y]
    gains_x = wires.over_x(gains)
    gains = gains + gains_x + sum(
        wires.over_y(gains, s) + wires.over_dp(gains, s) for s in across_y
    )
    out_weight_grad = wide(
        in_order(
            [
                in_order([a, b], wires.x, 1)
                for a, b in zip([out_part, *out_by_y], [out_x, *out_by_yx])
            ],
            wires.y,
            1,
        )
    )
    gate_grad, up_grad, down_grad = (
        grad_last(pick(total, wires.x, 2, 1), others[i]) for i, total in enumerate(totals)
    )
    gate_grad, up_grad = gate_grad.T, up_grad.T
    in_weight_grad = wide(jnp.concatenate(in_halves, axis=0)).T
    return (
        output,
        in_grad,
        gains[0],
        in_weight_grad,
        out_weight_grad,
        gains[1],
        gate_grad,
        up_grad,
        down_grad,
    )


def solution(mesh):
    return jax.shard_map(
        functools.partial(per_device, Wires(mesh)),
        mesh=mesh,
        in_specs=(
            P(("dp", "head"), None),
            P("dp"),
            P("dp", None),
            P(),
            P(None, "head"),
            P("head", None),
            P(),
            P("dp", "head"),
            P("dp", "head"),
            P("head", "dp"),
            P(("dp", "head"), None),
        ),
        out_specs=(
            P(("dp", "head"), None),
            P(("dp", "head"), None),
            P(),
            P(None, "head"),
            P("head", None),
            P(),
            P("dp", "head"),
            P("dp", "head"),
            P("head", "dp"),
        ),
        check_vma=False,
    )
```

```python
import functools
import jax
import jax.numpy as jnp
from jax import lax
from jax.experimental import pallas as pl
from jax.experimental.pallas import tpu as pltpu
from jax.sharding import PartitionSpec as P

FD = 16
VD = 128
LANES = 128
VMEM = 60 * 1024 * 1024
LITTLE = pl.CostEstimate(flops=1, bytes_accessed=1, transcendentals=0)
epsilon = 1e-05
NT = (((1,), (1,)), ((), ()))
TN = (((0,), (0,)), ((), ()))


def column_of(row):
    count = row.shape[1]
    same = lax.broadcasted_iota(jnp.int32, (count, count), 0) == lax.broadcasted_iota(
        jnp.int32, (count, count), 1
    )
    return jnp.sum(jnp.where(same, row, 0.0), axis=1, keepdims=True)


def padded(block):
    rows, columns = block.shape
    return jnp.concatenate([block, jnp.zeros((rows, -columns % LANES), block.dtype)], axis=1)


def lanes_from(block, low, count):
    width = block.shape[1]
    moved = (block if low == 0 else pltpu.roll(block, width - low, 1))[:, :LANES]
    if count == LANES:
        return moved
    lane = lax.broadcasted_iota(jnp.int32, moved.shape, 1)
    return jnp.where(lane < count, moved, 0.0)


def head_parts(block, head):
    low = head * (2 * FD + VD)
    query = lanes_from(block, low, FD) * 0.25
    return query, lanes_from(block, low + FD, FD), lanes_from(block, low + 2 * FD, VD)


def segment_start(ends_ref, positions):
    start = jnp.zeros_like(positions)
    for slot in range(ends_ref.shape[0]):
        end = ends_ref[slot]
        start = jnp.where(positions >= end, jnp.maximum(start, end), start)
    return start


def attend_kernel(heads, rows, pieces, ends_ref, at_ref, *refs):
    sources = refs[:pieces]
    weight_ref, keep_ref, projected_ref, normed_ref, y_ref, inv_ref, att_ref = refs[pieces : pieces + 7]
    normed_s, key_s, value_s, sems = refs[pieces + 7 :]
    step = pl.program_id(0)
    own = pl.ds(pl.multiple_of(step * rows, rows), rows)

    @pl.when(step == 0)
    def _():
        size = sources[0].shape[0]
        copies = [
            pltpu.make_async_copy(
                sources[i].at[:, pl.ds(0, normed_s.shape[1])], normed_s.at[pl.ds(pl.multiple_of(at_ref[i], size), size), :], sems.at[i]
            )
            for i in range(pieces)
        ]
        for copy in copies:
            copy.start()
        for copy in copies:
            copy.wait()

    keep = column_of(keep_ref[:, own])
    normed = normed_s[own, :]
    normed_ref[...] = normed
    projected = lax.dot_general(
        normed, weight_ref[...], NT, preferred_element_type=jnp.float32
    ).astype(jnp.bfloat16)
    projected_ref[...] = projected
    block = padded(projected.astype(jnp.float32))
    lane = lax.broadcasted_iota(jnp.int32, (rows, LANES), 1)
    ones = jnp.where(lane < 2, keep, 0.0).astype(jnp.bfloat16)
    queries = []
    for head in range(heads):
        query, key, value = head_parts(block, head)
        queries.append(query.astype(jnp.bfloat16))
        key_s[head, own, :] = key.astype(jnp.bfloat16)
        value_s[head, own, :VD] = (value * keep).astype(jnp.bfloat16)
        value_s[head, own, VD:] = ones
    row = step * rows + lax.broadcasted_iota(jnp.int32, (rows, 1), 0)
    start = segment_start(ends_ref, row)
    column = lax.broadcasted_iota(jnp.int32, (rows, rows), 1)

    def tile(block, totals, diagonal):
        at = pl.ds(pl.multiple_of(block * rows, rows), rows)
        allowed = column >= start - block * rows
        if diagonal:
            allowed &= column <= lax.broadcasted_iota(jnp.int32, (rows, rows), 0)
        added = []
        for head in range(heads):
            inner = lax.dot_general(
                queries[head], key_s[head, at, :], NT, preferred_element_type=jnp.float32
            )
            weights = jnp.where(allowed, (inner * 0.5 + 1.0) * inner + 1.0, 0.0).astype(jnp.bfloat16)
            added.append(
                totals[head]
                + jnp.dot(weights, value_s[head, at, :], preferred_element_type=jnp.float32)
            )
        return tuple(added)

    totals = tuple(jnp.zeros((rows, 2 * VD), jnp.float32) for _ in range(heads))
    totals = lax.fori_loop(0, step, lambda block, held: tile(block, held, False), totals)
    totals = tile(step, totals, True)
    inverses = jnp.zeros((rows, LANES), jnp.float32)
    for head in range(heads):
        inverse = 1.0 / (totals[head][:, VD : VD + 1] + 1.0 - keep)
        y = totals[head][:, :VD] * (keep * inverse)
        y_ref[:, head * VD : (head + 1) * VD] = y
        att_ref[:, head * VD : (head + 1) * VD] = y.astype(jnp.bfloat16)
        inverses = jnp.where(lane == head, inverse, inverses)
    inv_ref[...] = inverses


def attend(pieces, places, weight, keep, ends, heads):
    size, depth = pieces[0].shape[0], weight.shape[1]
    total = size * len(pieces)
    rows = min(512, total)
    width = weight.shape[0]
    pairs = total * (total + rows) // 2 * heads
    blocked = lambda columns: pl.BlockSpec((rows, columns), lambda i, e, a: (i, 0))
    return pl.pallas_call(
        functools.partial(attend_kernel, heads, rows, len(pieces)),
        grid_spec=pltpu.PrefetchScalarGridSpec(
            num_scalar_prefetch=2,
            grid=(total // rows,),
            in_specs=[pl.BlockSpec(memory_space=pl.ANY)] * len(pieces)
            + [
                pl.BlockSpec((width, depth), lambda i, e, a: (0, 0)),
                pl.BlockSpec((1, total), lambda i, e, a: (0, 0)),
            ],
            out_specs=[
                blocked(width), blocked(depth), blocked(heads * VD), blocked(LANES), blocked(heads * VD)
            ],
            scratch_shapes=[
                pltpu.VMEM((total, depth), jnp.bfloat16),
                pltpu.VMEM((heads, total, LANES), jnp.bfloat16),
                pltpu.VMEM((heads, total, 2 * VD), jnp.bfloat16),
                pltpu.SemaphoreType.DMA((len(pieces),)),
            ],
        ),
        out_shape=[
            jax.ShapeDtypeStruct((total, width), jnp.bfloat16),
            jax.ShapeDtypeStruct((total, depth), jnp.bfloat16),
            jax.ShapeDtypeStruct((total, heads * VD), jnp.float32),
            jax.ShapeDtypeStruct((total, LANES), jnp.float32),
            jax.ShapeDtypeStruct((total, heads * VD), jnp.bfloat16),
        ],
        compiler_params=pltpu.CompilerParams(
            dimension_semantics=("arbitrary",), vmem_limit_bytes=VMEM
        ),
        cost_estimate=LITTLE,
    )(ends, places, *pieces, weight, keep)


def attend_back_kernel(
    heads, rows, ends_ref, projected_ref, keep_ref, y_ref, inv_ref, grad_ref, out_ref,
    key_s, query_s, value_s, error_s, dquery_s,
):
    step = pl.program_id(0)
    blocks = pl.num_programs(0)
    lane = lax.broadcasted_iota(jnp.int32, (rows, LANES), 1)

    @pl.when(step == 0)
    def _():
        dquery_s[...] = jnp.zeros_like(dquery_s)

        def fill(block, nothing):
            at = pl.ds(pl.multiple_of(block * rows, rows), rows)
            keep = column_of(keep_ref[:, at])
            wide_block = padded(projected_ref[at, :].astype(jnp.float32))
            ones = jnp.where(lane < 2, keep, 0.0).astype(jnp.bfloat16)
            inverses = inv_ref[at, :]
            for head in range(heads):
                columns = slice(head * VD, (head + 1) * VD)
                query, key, value = head_parts(wide_block, head)
                key_s[head, at, :] = key.astype(jnp.bfloat16)
                query_s[head, at, :] = query.astype(jnp.bfloat16)
                value_s[head, at, :VD] = (value * keep).astype(jnp.bfloat16)
                value_s[head, at, VD:] = ones
                inverse = inverses[:, head : head + 1]
                grad = grad_ref[at, columns].astype(jnp.float32)
                error_s[head, at, :VD] = (grad * (keep * inverse)).astype(jnp.bfloat16)
                offset = -jnp.sum(grad * y_ref[at, columns], axis=1, keepdims=True) * inverse
                high = offset.astype(jnp.bfloat16).astype(jnp.float32)
                error_s[head, at, VD:] = jnp.where(
                    lane == 0, high, jnp.where(lane == 1, offset - high, 0.0)
                ).astype(jnp.bfloat16)
            return nothing

        lax.fori_loop(0, blocks, fill, 0)

    own = pl.ds(pl.multiple_of(step * rows, rows), rows)
    row = lax.broadcasted_iota(jnp.int32, (rows, rows), 0)

    def tile(block, totals, diagonal):
        at = pl.ds(pl.multiple_of(block * rows, rows), rows)
        column = block * rows + lax.broadcasted_iota(jnp.int32, (1, rows), 1)
        allowed = row >= segment_start(ends_ref, column) - step * rows
        if diagonal:
            allowed &= row <= lax.broadcasted_iota(jnp.int32, (rows, rows), 1)
        dkeys, dvalues = totals
        added, turned = [], []
        for head in range(heads):
            query = query_s[head, at, :]
            error = error_s[head, at, :]
            keys = key_s[head, own, :]
            inner = lax.dot_general(keys, query, NT, preferred_element_type=jnp.float32)
            dweight = lax.dot_general(value_s[head, own, :], error, NT, preferred_element_type=jnp.float32)
            slope = inner + 1.0
            weights = jnp.where(allowed, (slope * slope + 1.0) * 0.5, 0.0).astype(jnp.bfloat16)
            dinner = jnp.where(allowed, slope * dweight, 0.0).astype(jnp.bfloat16)
            added.append(
                dvalues[head] + jnp.dot(weights, error[:, :VD], preferred_element_type=jnp.float32)
            )
            turned.append(dkeys[head] + jnp.dot(dinner, query, preferred_element_type=jnp.float32))
            dquery_s[head, at, :] += lax.dot_general(dinner, keys, TN, preferred_element_type=jnp.float32)
        return tuple(turned), tuple(added)

    totals = (
        tuple(jnp.zeros((rows, LANES), jnp.float32) for _ in range(heads)),
        tuple(jnp.zeros((rows, VD), jnp.float32) for _ in range(heads)),
    )
    totals = tile(step, totals, True)
    dkeys, dvalues = lax.fori_loop(step + 1, blocks, lambda block, held: tile(block, held, False), totals)
    keep = column_of(keep_ref[:, own])
    width = out_ref.shape[2]
    total = jnp.zeros((rows, width + -width % LANES), jnp.float32)
    blank = jnp.zeros((rows, total.shape[1] - LANES), jnp.float32)

    def put(block, low):
        spread = jnp.concatenate([block, blank], axis=1)
        return spread if low == 0 else pltpu.roll(spread, low, 1)

    for head in range(heads):
        low = head * (2 * FD + VD)
        total += put(dquery_s[head, own, :] * 0.25, low)
        total += put(dkeys[head], low + FD)
        total += put(dvalues[head] * keep, low + 2 * FD)
    out_ref[...] = total[:, :width].astype(jnp.bfloat16).reshape(out_ref.shape)


def attend_back(projected, keep, ends, y, inverses, grad, heads, each):
    total = projected.shape[0]
    rows = min(512, total)
    width = projected.shape[1]
    whole = lambda columns: pl.BlockSpec((total, columns), lambda i, e: (0, 0))
    return pl.pallas_call(
        functools.partial(attend_back_kernel, heads, rows),
        grid_spec=pltpu.PrefetchScalarGridSpec(
            num_scalar_prefetch=1,
            grid=(total // rows,),
            in_specs=[whole(width), pl.BlockSpec((1, total), lambda i, e: (0, 0)), whole(heads * VD), whole(LANES), whole(heads * VD)],
            out_specs=pl.BlockSpec((rows // each, each, width), lambda i, e: (i, 0, 0)),
            scratch_shapes=[
                pltpu.VMEM((heads, total, LANES), jnp.bfloat16),
                pltpu.VMEM((heads, total, LANES), jnp.bfloat16),
                pltpu.VMEM((heads, total, 2 * VD), jnp.bfloat16),
                pltpu.VMEM((heads, total, 2 * VD), jnp.bfloat16),
                pltpu.VMEM((heads, total, LANES), jnp.float32),
            ],
        ),
        out_shape=jax.ShapeDtypeStruct((total // each, each, width), jnp.bfloat16),
        compiler_params=pltpu.CompilerParams(
            dimension_semantics=("arbitrary",), vmem_limit_bytes=VMEM
        ),
        cost_estimate=LITTLE,
    )(ends, projected, keep, y, inverses, grad)


def inv_root_mean(values):
    return lax.rsqrt(jnp.mean(values * values, axis=1, keepdims=True) + epsilon)


def wide(values):
    return values.astype(jnp.float32)


def low(values):
    return values.astype(jnp.bfloat16)


def pick(values, index, count, axis):
    size = values.shape[axis] // count
    if count == 2:
        first = lax.slice_in_dim(values, 0, size, axis=axis)
        second = lax.slice_in_dim(values, size, 2 * size, axis=axis)
        return jnp.where(index == 0, first, second)
    return lax.dynamic_slice_in_dim(values, index * size, size, axis)


def in_order(pieces, index, axis):
    count = len(pieces)
    if count == 1:
        return pieces[0]
    if count == 2:
        first = jnp.where(index == 0, pieces[0], pieces[1])
        second = jnp.where(index == 0, pieces[1], pieces[0])
        return jnp.concatenate([first, second], axis=axis)
    stacked = jnp.stack(pieces)
    placed = [
        lax.dynamic_index_in_dim(stacked, (index - place) % count, 0, keepdims=False)
        for place in range(count)
    ]
    return jnp.concatenate(placed, axis=axis)


class Wires:
    def __init__(self, mesh):
        self.dp, self.head = mesh.shape["dp"], mesh.shape["head"]
        self.ny, self.nz, self.nzh = self.dp // 2, self.head // 2, self.head // 4

    def place(self):
        p, h = lax.axis_index("dp"), lax.axis_index("head")
        self.p, self.h = p, h
        self.y, self.x, self.z, self.c = p // 2, p % 2, h // 2, h % 2
        self.zh = self.z // 2

    def over_x(self, values):
        return lax.ppermute(values, "dp", [(i, i ^ 1) for i in range(self.dp)])

    def over_y(self, values, shift):
        return lax.ppermute(
            values, "dp", [(i, ((i // 2 + shift) % self.ny) * 2 + i % 2) for i in range(self.dp)]
        )

    def over_dp(self, values, shift):
        return lax.ppermute(
            values, "dp", [(i, ((i // 2 + shift) % self.ny) * 2 + (i + 1) % 2) for i in range(self.dp)]
        )

    def over_core(self, values):
        return lax.ppermute(values, "head", [(i, i ^ 1) for i in range(self.head)])

    def over_zl(self, values):
        return lax.ppermute(values, "head", [(i, i ^ 2) for i in range(self.head)])

    def over_zh(self, values, shift):
        return lax.ppermute(
            values, "head", [(i, ((i // 4 + shift) % self.nzh) * 4 + i % 4) for i in range(self.head)]
        )

    def over_zh_half(self, values, shift, parity):
        pairs = [
            (i, ((i // 4 + shift) % self.nzh) * 4 + i % 4)
            for i in range(self.head)
            if (i // 4 + i // 2 % 2) % 2 == parity
        ]
        return lax.ppermute(values, "head", pairs)

    def from_halves(self, first, second, shift):
        even = (self.zh - shift + self.z) % 2 == 0
        return jnp.where(even, first, second)

    def over_z(self, values, shift):
        return lax.ppermute(
            values, "head", [(i, ((i // 2 + shift) % self.nz) * 2 + i % 2) for i in range(self.head)]
        )

    def right(self, values, first, last):
        return lax.ppermute(
            values, "head", [(i, i + 2) for i in range(self.head) if first <= i // 2 <= last]
        )

    def left(self, values, first, last):
        return lax.ppermute(
            values, "head", [(i, i - 2) for i in range(self.head) if first <= i // 2 <= last]
        )

    def spread(self, line):
        return self.over_x(line), [self.over_y(line, s) for s in range(1, self.ny)]

    def ends(self, values):
        pairs = [(i, i + 2 if i // 2 == self.nz - 2 else i - 2) for i in range(self.head)]
        return lax.ppermute(
            values, "head", [pair for pair in pairs if pair[0] // 2 in (1, self.nz - 2)]
        )

    def arrivals(self):
        orders = []
        for z in range(self.nz):
            order = []
            for step in range(1, self.nz):
                order += [(0, step)] if z >= step else []
                order += [(1, step)] if z + step < self.nz else []
            orders.append(order)
        return orders

    def by_place(self, values):
        chosen, taken = values[0], [values[0]]
        for value in values[1:]:
            if any(value is other for other in taken):
                continue
            taken.append(value)
            here = [z for z in range(self.nz) if values[z] is value]
            chosen = jnp.where(sum((self.z == z).astype(jnp.int32) for z in here) > 0, value, chosen)
        return chosen

    def sum_y(self, values):
        total = wide(values)
        for s in range(1, self.ny):
            total = total + wide(self.over_y(values, s))
        return low(total)

    def sum_x(self, values):
        return low(wide(values) + wide(self.over_x(values)))

    def sum_all(self, values):
        values = values + self.over_core(values)
        values = values + self.over_zl(values)
        values = values + sum(self.over_zh(values, s) for s in range(1, self.nzh))
        values = values + self.over_x(values)
        return values + sum(self.over_y(values, s) for s in range(1, self.ny))

    def quarter(self, shard):
        size = shard.shape[1] // self.dp
        return lax.dynamic_slice_in_dim(shard, self.p * size, size, 1)

    def line_of(self, part):
        return [part] + [self.over_z(part, s) for s in range(1, self.nz)]

    def whole_places(self, chips, rows, size):
        at_rows = [(chip * 2 + (self.c ^ r)) * rows for r in range(2) for chip in chips]
        at_columns = [
            (((self.y - s) % self.ny) * 2 + (self.x ^ t)) * size
            for s in range(self.ny)
            for t in range(2)
        ]
        return jnp.stack(at_rows + at_columns).astype(jnp.int32)

    def line(self, block, during):
        steps = self.nz
        right = left = block
        rights, lefts = {}, {}
        orders = self.arrivals()
        chunks, chips = [block], [self.z]
        for step in range(1, steps):
            if step < steps - 1:
                right = self.right(right, step - 1, steps - 2)
                left = self.left(left, 1, steps - step)
                right, left = during(step, (right, left))
            else:
                both = jnp.where(self.z == steps - 2, right, left)
                (right, both) = during(step, (self.ends(both), both))
                left = right
            rights[step], lefts[step] = right, left
            arrived = {(0, s): rights[s] for s in rights} | {(1, s): lefts[s] for s in lefts}
            while len(chunks) < steps and all(
                orders[z][len(chunks) - 1] in arrived for z in range(steps)
            ):
                order = [orders[z][len(chunks) - 1] for z in range(steps)]
                values = [arrived[key] for key in order]
                if step == steps - 1 and values[1] is lefts[steps - 2] and values[-2] is rights[steps - 2]:
                    values[1] = values[-2] = both
                chunks.append(self.by_place(values))
                chips.append(
                    self.by_place([z - key[1] * (1 - 2 * key[0]) for z, key in enumerate(order)])
                )
        return chunks, chips


class Whole:
    def __init__(self, wires, pieces, places, rows, size):
        self.layout = [(s, t, 0, wires.nz) for s in range(wires.ny) for t in range(2)]
        self.nz = wires.nz
        self.pieces, self.rows, self.size = pieces, rows, size
        self.places = places
        self.copies = 2 * sum(count for _, _, _, count in self.layout)
        self.shape = (wires.head * rows, wires.dp * size)

    def fill(self, places_ref, refs, scratch, sems):
        copies = []
        for piece, (s, t, first, count) in enumerate(self.layout):
            column = pl.multiple_of(places_ref[2 * self.nz + 2 * s + t], self.size)
            for core in range(2):
                for slot in range(count):
                    row = pl.multiple_of(places_ref[core * self.nz + first + slot], self.rows)
                    copies.append(
                        pltpu.make_async_copy(
                            refs[core * len(self.layout) + piece].at[slot],
                            scratch.at[pl.ds(row, self.rows), pl.ds(column, self.size)],
                            sems.at[len(copies)],
                        )
                    )
        for copy in copies:
            copy.start()
        return copies


def swapped(wires, pieces):
    return [*pieces, *[wires.over_core(piece) for piece in pieces]]


def side_by_side(blocks_ref):
    return jnp.concatenate([blocks_ref[i] for i in range(blocks_ref.shape[0])], axis=1)


def by_columns(whole, places_ref, copies, weight_s, blocks, total_ref):
    each = len(copies) // len(whole.layout)
    for piece, (s, t, _, _) in enumerate(whole.layout):
        for copy in copies[piece * each : (piece + 1) * each]:
            copy.wait()
        at = pl.ds(pl.multiple_of(places_ref[2 * whole.nz + 2 * s + t], whole.size), whole.size)
        total, low = 0.0, 0
        for block in blocks:
            total += jnp.dot(
                block, weight_s[low : low + block.shape[1], at], preferred_element_type=jnp.float32
            )
            low += block.shape[1]
        total_ref[:, at] = total


def mix_kernel(whole, places_ref, *refs):
    count = len(whole.pieces)
    attended_ref, tokens_ref, gain_ref, middle_ref, normed_ref, weight_s, sems = refs[count:]
    copies = whole.fill(places_ref, refs[:count], weight_s, sems)
    by_columns(whole, places_ref, copies, weight_s, [side_by_side(attended_ref)], middle_ref)
    middle = middle_ref[...] + wide(tokens_ref[...])
    middle_ref[...] = middle
    normed_ref[...] = (middle * inv_root_mean(middle) * gain_ref[...]).astype(jnp.bfloat16)


def with_whole(kernel, whole, args, outs, flops):
    in_vmem = pl.BlockSpec(memory_space=pltpu.VMEM)
    return pl.pallas_call(
        functools.partial(kernel, whole),
        grid_spec=pltpu.PrefetchScalarGridSpec(
            num_scalar_prefetch=1,
            grid=(),
            in_specs=[pl.BlockSpec(memory_space=pl.ANY)] * len(whole.pieces) + [in_vmem] * len(args),
            out_specs=[in_vmem] * len(outs),
            scratch_shapes=[
                pltpu.VMEM(whole.shape, jnp.bfloat16),
                pltpu.SemaphoreType.DMA((whole.copies,)),
            ],
        ),
        out_shape=[jax.ShapeDtypeStruct(shape, kind) for shape, kind in outs],
        compiler_params=pltpu.CompilerParams(vmem_limit_bytes=VMEM),
        cost_estimate=LITTLE,
    )(whole.places, *whole.pieces, *args)


def mix(attended, whole, tokens, gain):
    return with_whole(
        mix_kernel,
        whole,
        (attended, tokens, gain),
        ((tokens.shape, jnp.float32), (tokens.shape, jnp.bfloat16)),
        2 * tokens.shape[0] * whole.shape[0] * whole.shape[1],
    )


def unmix_kernel(whole, places_ref, *refs):
    count = len(whole.pieces)
    a_ref, b_ref, c_ref, middle_ref, grad_ref, gain_ref = refs[count : count + 6]
    dmiddle_ref, dmixed_ref, part_ref, out_ref, weight_s, sems = refs[count + 6 :]
    copies = whole.fill(places_ref, refs[:count], weight_s, sems)
    middle = middle_ref[...]
    inv_two = inv_root_mean(middle)
    dnormed = wide(a_ref[...]) + wide(b_ref[...]) + wide(c_ref[...])
    scaled = middle * inv_two
    error = dnormed * gain_ref[...]
    dmiddle = wide(grad_ref[...]) + inv_two * (
        error - scaled * jnp.mean(error * scaled, axis=1, keepdims=True)
    )
    part_ref[...] = jnp.sum(dnormed * scaled, axis=0, keepdims=True)
    dmiddle_ref[...] = dmiddle
    dmixed = dmiddle.astype(jnp.bfloat16)
    dmixed_ref[...] = dmixed
    for copy in copies:
        copy.wait()
    width = out_ref.shape[2]
    for head in range(out_ref.shape[0]):
        out_ref[head] = lax.dot_general(
            dmixed, weight_s[head * width : (head + 1) * width, :], NT, preferred_element_type=jnp.float32
        ).astype(jnp.bfloat16)


def unmix(parts, middle, grad, gain, whole, heads):
    rows, depth = middle.shape
    return with_whole(
        unmix_kernel,
        whole,
        (*parts, middle, grad, gain),
        (
            (middle.shape, jnp.float32),
            (middle.shape, jnp.bfloat16),
            ((1, depth), jnp.float32),
            ((heads, rows, whole.shape[0] // heads), jnp.bfloat16),
        ),
        2 * rows * whole.shape[0] * whole.shape[1],
    )


def last_kernel(whole, places_ref, *refs):
    count = len(whole.pieces)
    proj_ref, tokens_ref, dmiddle_ref, gain_ref, grad_ref, weight_s, sems = refs[count:]
    copies = whole.fill(places_ref, refs[:count], weight_s, sems)
    blocks = [proj_ref[head] for head in range(proj_ref.shape[0])]
    by_columns(whole, places_ref, copies, weight_s, blocks, grad_ref)
    dnormed = grad_ref[...]
    tokens = wide(tokens_ref[...])
    inv_one = inv_root_mean(tokens)
    scaled = tokens * inv_one
    error = dnormed * gain_ref[...]
    grad_ref[...] = dmiddle_ref[...] + inv_one * (
        error - scaled * jnp.mean(error * scaled, axis=1, keepdims=True)
    )


def last(proj, whole, tokens, dmiddle, gain):
    return with_whole(
        last_kernel,
        whole,
        (proj, tokens, dmiddle, gain),
        ((tokens.shape, jnp.float32),),
        2 * tokens.shape[0] * whole.shape[0] * whole.shape[1],
    )[0]


class Units:
    def __init__(self, wires, pieces, matrices, rows, columns):
        self.matrices = matrices
        self.layout = [piece[1:] for piece in pieces]
        self.pieces = [piece[0] for piece in pieces]
        self.rows, self.columns = rows, columns
        self.places = jnp.stack([((wires.y - s) % wires.ny) * columns for s in range(wires.ny)]).astype(
            jnp.int32
        )
        self.shape = (matrices, wires.nzh * rows, wires.ny * columns)

    def fill(self, places_ref, refs, scratch, sems):
        copies = []
        for matrix in range(self.matrices):
            for ref, (first, count, zh, y) in zip(refs, self.layout):
                if not first <= matrix < first + count:
                    continue
                column = pl.multiple_of(places_ref[y], self.columns)
                copies.append(
                    pltpu.make_async_copy(
                        ref.at[matrix - first],
                        scratch.at[
                            matrix, pl.ds(zh * self.rows, self.rows), pl.ds(column, self.columns)
                        ],
                        sems.at[len(copies)],
                    )
                )
        for copy in copies:
            copy.start()
        return copies


def with_units(kernel, units, blocks, outs, scratch, flops, transcendentals):
    anywhere = pl.BlockSpec(memory_space=pl.ANY)
    copies = sum(count for _, count, _, _ in units.layout)
    return pl.pallas_call(
        functools.partial(kernel, units),
        grid_spec=pltpu.PrefetchScalarGridSpec(
            num_scalar_prefetch=1,
            grid=(),
            in_specs=[anywhere] * (len(units.pieces) + len(blocks)),
            out_specs=[anywhere] * len(outs),
            scratch_shapes=[
                pltpu.VMEM(units.shape, jnp.bfloat16),
                pltpu.SemaphoreType.DMA((copies,)),
            ]
            + scratch,
        ),
        out_shape=[jax.ShapeDtypeStruct(shape, kind) for shape, kind in outs],
        compiler_params=pltpu.CompilerParams(vmem_limit_bytes=VMEM),
        cost_estimate=LITTLE,
    )(units.places, *units.pieces, *blocks)


def started(copies):
    for copy in copies:
        copy.start()
    return copies


def awaited(copies):
    for copy in copies:
        copy.wait()


def gate_kernel(count, units, places_ref, *refs):
    pieces, refs = refs[: len(units.pieces)], refs[len(units.pieces) :]
    blocks, (unit_ref, normed_ref) = refs[: 2 * count], refs[2 * count : 2 * count + 2]
    weight_s, sems, normed_s, unit_s, in_sems, out_sems = refs[2 * count + 2 :]
    rows = blocks[0].shape[0]

    def arrive(chunk):
        started(
            [
                pltpu.make_async_copy(
                    blocks[2 * chunk + i], normed_s.at[chunk, pl.ds(i * rows, rows)], in_sems.at[chunk]
                )
                for i in range(2)
            ]
        )

    arrive(0)
    weights = units.fill(places_ref, pieces, weight_s, sems)
    for chunk in range(1, count):
        arrive(chunk)
    each = len(weights) // units.matrices

    def sent(chunk, which):
        source, target = ((normed_s, normed_ref), (unit_s, unit_ref))[which]
        return pltpu.make_async_copy(source.at[chunk], target.at[chunk], out_sems.at[which, chunk])

    def work(chunk, nothing):
        pltpu.make_async_copy(normed_ref.at[chunk], normed_s.at[chunk], in_sems.at[chunk]).wait()
        sent(chunk, 0).start()
        pl.when(chunk == 0)(lambda: awaited(weights[:each]))
        normed = normed_s[chunk]
        gate = lax.dot_general(normed, weight_s[0], NT, preferred_element_type=jnp.float32)
        pl.when(chunk == 0)(lambda: awaited(weights[each:]))
        up = lax.dot_general(normed, weight_s[1], NT, preferred_element_type=jnp.float32)
        sigmoid = jax.nn.sigmoid(gate)
        silu = gate * sigmoid
        unit_s[chunk, 0] = (silu * up).astype(jnp.bfloat16)
        unit_s[chunk, 1] = (up * sigmoid * (1.0 + gate * (1.0 - sigmoid))).astype(jnp.bfloat16)
        unit_s[chunk, 2] = silu.astype(jnp.bfloat16)
        sent(chunk, 1).start()
        return nothing

    lax.fori_loop(0, count, work, 0)
    for chunk in range(count):
        awaited([sent(chunk, 0), sent(chunk, 1)])


def gate_up(pairs, units):
    count = len(pairs)
    rows, depth = pairs[0][0].shape
    unit, full = (count, 3, 2 * rows, units.shape[1]), (count, 2 * rows, depth)
    return with_units(
        functools.partial(gate_kernel, count),
        units,
        [block for pair in pairs for block in pair],
        ((unit, jnp.bfloat16), (full, jnp.bfloat16)),
        [
            pltpu.VMEM(full, jnp.bfloat16),
            pltpu.VMEM(unit, jnp.bfloat16),
            pltpu.SemaphoreType.DMA((count,)),
            pltpu.SemaphoreType.DMA((2, count)),
        ],
        8 * count * rows * depth * units.shape[1],
        0,
    )


def down_kernel(places, units, places_ref, *refs):
    count = len(places)
    pieces, refs = refs[: len(units.pieces)], refs[len(units.pieces) :]
    blocks, refs = refs[: 3 * count], refs[3 * count :]
    unit_ref, grad_ref, refs = refs[0], refs[1], refs[2:]
    dnormed, branches = refs[: 2 * count], refs[2 * count : 4 * count]
    weight_s, sems, given_s, grad_s, unit_s, back_s, branch_s, in_sems, out_sems = refs[4 * count :]
    rows = blocks[0].shape[0]
    both = [pl.ds(0, rows), pl.ds(rows, rows)]

    def arrive(chunk):
        one, two, given = blocks[3 * chunk : 3 * chunk + 3]
        started(
            [
                pltpu.make_async_copy(one, grad_s.at[chunk, both[0]], in_sems.at[0, chunk]),
                pltpu.make_async_copy(two, grad_s.at[chunk, both[1]], in_sems.at[0, chunk]),
                pltpu.make_async_copy(given.at[places[chunk]], given_s.at[chunk], in_sems.at[1, chunk]),
            ]
        )

    arrive(0)
    weights = units.fill(places_ref, pieces, weight_s, sems)
    for chunk in range(1, count):
        arrive(chunk)
    each = len(weights) // units.matrices
    dot = functools.partial(jnp.dot, preferred_element_type=jnp.float32)

    def sent(chunk, which):
        source, target = ((grad_s, grad_ref), (unit_s, unit_ref))[which]
        return pltpu.make_async_copy(source.at[chunk], target.at[chunk], out_sems.at[which, chunk])

    def halves_sent(chunk, source, targets, place):
        return [
            pltpu.make_async_copy(
                source.at[chunk, both[i]], targets[2 * chunk + i], out_sems.at[place + i, chunk]
            )
            for i in range(2)
        ]

    def work(chunk, nothing):
        pltpu.make_async_copy(grad_ref.at[chunk], grad_s.at[chunk], in_sems.at[0, chunk]).wait()
        sent(chunk, 0).start()
        pl.when(chunk == 0)(lambda: awaited(weights[:each]))
        dhidden = lax.dot_general(grad_s[chunk], weight_s[0], NT, preferred_element_type=jnp.float32)
        pltpu.make_async_copy(given_s.at[chunk], given_s.at[chunk], in_sems.at[1, chunk]).wait()
        dgate = (dhidden * wide(given_s[chunk, 1])).astype(jnp.bfloat16)
        dup = (dhidden * wide(given_s[chunk, 2])).astype(jnp.bfloat16)
        unit_s[chunk, 0] = dgate
        unit_s[chunk, 1] = dup
        sent(chunk, 1).start()
        branch_s[chunk] = dot(given_s[chunk, 0], weight_s[0]).astype(jnp.bfloat16)
        for k in range(count):
            pl.when(chunk == k)(lambda k=k: started(halves_sent(k, branch_s, branches, 2)) and None)
        pl.when(chunk == 0)(lambda: awaited(weights[each:]))
        back_s[chunk] = (dot(dgate, weight_s[1]) + dot(dup, weight_s[2])).astype(jnp.bfloat16)
        for k in range(count):
            pl.when(chunk == k)(lambda k=k: started(halves_sent(k, back_s, dnormed, 4)) and None)
        return nothing

    lax.fori_loop(0, count, work, 0)
    for chunk in range(count):
        awaited([sent(chunk, 0), sent(chunk, 1)])
        awaited(halves_sent(chunk, branch_s, branches, 2))
        awaited(halves_sent(chunk, back_s, dnormed, 4))


def down(given, units):
    count = len(given)
    rows, depth = given[0][0].shape
    size = units.shape[1]
    full = (count, 2 * rows, depth)
    part = ((rows, depth), jnp.bfloat16)
    outs = with_units(
        functools.partial(down_kernel, [chunk[3] for chunk in given]),
        units,
        [block for chunk in given for block in chunk[:3]],
        (((count, 2, 2 * rows, size), jnp.bfloat16), (full, jnp.bfloat16)) + (part,) * (4 * count),
        [
            pltpu.VMEM((count, 3, 2 * rows, size), jnp.bfloat16),
            pltpu.VMEM(full, jnp.bfloat16),
            pltpu.VMEM((count, 2, 2 * rows, size), jnp.bfloat16),
            pltpu.VMEM(full, jnp.bfloat16),
            pltpu.VMEM(full, jnp.bfloat16),
            pltpu.SemaphoreType.DMA((2, count)),
            pltpu.SemaphoreType.DMA((6, count)),
        ],
        16 * count * rows * depth * size,
        0,
    )
    halves = lambda parts: [parts[2 * i : 2 * i + 2] for i in range(count)]
    return outs[:2], halves(outs[2 : 2 + 2 * count]), halves(outs[2 + 2 * count :])


def unit_grad_kernel(order, ny, nzh, places_ref, *refs):
    count = len(order)
    scratch = refs[-4:]
    arrays, outs = refs[: -4 - ny * nzh], refs[-4 - ny * nzh : -4]
    left_s, right_s, total_s, sems = scratch
    for i, (left, at, right, to) in enumerate(order):
        started(
            [
                pltpu.make_async_copy(arrays[left].at[at], left_s.at[i], sems.at[0, i]),
                pltpu.make_async_copy(arrays[right].at[to], right_s.at[i], sems.at[1, i]),
            ]
        )
    total_s[...] = jnp.zeros_like(total_s)

    def work(i, nothing):
        pltpu.make_async_copy(left_s.at[i], left_s.at[i], sems.at[0, i]).wait()
        pltpu.make_async_copy(right_s.at[i], right_s.at[i], sems.at[1, i]).wait()
        total_s[...] += lax.dot_general(left_s[i], right_s[i], TN, preferred_element_type=jnp.float32)
        return nothing

    lax.fori_loop(0, count, work, 0)
    units, columns = outs[0].shape
    for y in range(ny):
        for zh in range(nzh):
            outs[y * nzh + zh][...] = total_s[
                pl.ds(zh * units, units), pl.ds(pl.multiple_of(places_ref[y], columns), columns)
            ].astype(jnp.bfloat16)


def unit_grad(wires, lefts, rights):
    ny, nzh = wires.ny, wires.nzh
    arrays = []

    def index(array):
        for i, other in enumerate(arrays):
            if other is array:
                return i
        arrays.append(array)
        return len(arrays) - 1

    order = [(index(left), at, index(right), to) for (left, at), (right, to) in zip(lefts, rights)]
    tokens, units = lefts[0][0].shape[-2:]
    depth = rights[0][0].shape[-1]
    rows, columns = units // nzh, depth // ny
    places = jnp.stack([((wires.y + s) % ny) * columns for s in range(ny)]).astype(jnp.int32)
    in_vmem = pl.BlockSpec(memory_space=pltpu.VMEM)
    outs = pl.pallas_call(
        functools.partial(unit_grad_kernel, order, ny, nzh),
        grid_spec=pltpu.PrefetchScalarGridSpec(
            num_scalar_prefetch=1,
            grid=(),
            in_specs=[pl.BlockSpec(memory_space=pl.ANY)] * len(arrays),
            out_specs=[in_vmem] * (ny * nzh),
            scratch_shapes=[
                pltpu.VMEM((len(order), tokens, units), jnp.bfloat16),
                pltpu.VMEM((len(order), tokens, depth), jnp.bfloat16),
                pltpu.VMEM((units, depth), jnp.float32),
                pltpu.SemaphoreType.DMA((2, len(order))),
            ],
        ),
        out_shape=[jax.ShapeDtypeStruct((rows, columns), jnp.bfloat16)] * (ny * nzh),
        compiler_params=pltpu.CompilerParams(vmem_limit_bytes=VMEM),
        cost_estimate=LITTLE,
    )(places, *arrays)
    return [outs[zh::nzh] for zh in range(nzh)]


def out_grad_kernel(nz, ny, places_ref, mine_ref, other_ref, grad_ref, other_grad_ref, *refs):
    outs, (left_s, right_s) = refs[: 2 * ny], refs[2 * ny :]
    step = pl.program_id(0)
    tokens, width = grad_ref.shape[0], outs[0].shape[2]

    @pl.when(step == 0)
    def _():
        right_s[:tokens] = grad_ref[...]
        right_s[tokens:] = other_grad_ref[...]

    left_s[:tokens] = mine_ref[places_ref[step]]
    left_s[tokens:] = other_ref[places_ref[step] // 2]
    left = left_s[...]
    for i, out_ref in enumerate(outs):
        column = pl.multiple_of(places_ref[nz + i], width)
        out_ref[0] = lax.dot_general(
            left, right_s[:, pl.ds(column, width)], TN, preferred_element_type=jnp.float32
        ).astype(jnp.bfloat16)


def out_grad_parts(wires, mine, other, d_mixed, other_d_mixed):
    heads, tokens, rows = mine.shape
    depth = d_mixed.shape[1]
    nz, ny, width = wires.nz, wires.ny, depth // wires.dp
    places = jnp.stack(
        [z * 2 + wires.c for z in range(nz)]
        + [(((wires.y + s) % ny) * 2 + (wires.x ^ t)) * width for t in range(2) for s in range(ny)]
    ).astype(jnp.int32)
    full = lambda *shape: pl.BlockSpec(shape, lambda i, p: (0,) * len(shape))
    outs = pl.pallas_call(
        functools.partial(out_grad_kernel, nz, ny),
        grid_spec=pltpu.PrefetchScalarGridSpec(
            num_scalar_prefetch=1,
            grid=(nz,),
            in_specs=[
                full(heads, tokens, rows),
                full(nz, tokens, rows),
                full(tokens, depth),
                full(tokens, depth),
            ],
            out_specs=[pl.BlockSpec((1, rows, width), lambda i, p: (i, 0, 0))] * (2 * ny),
            scratch_shapes=[
                pltpu.VMEM((2 * tokens, rows), jnp.bfloat16),
                pltpu.VMEM((2 * tokens, depth), jnp.bfloat16),
            ],
        ),
        out_shape=[jax.ShapeDtypeStruct((nz, rows, width), jnp.bfloat16)] * (2 * ny),
        compiler_params=pltpu.CompilerParams(
            dimension_semantics=("arbitrary",), vmem_limit_bytes=VMEM
        ),
        cost_estimate=LITTLE,
    )(places, mine, other, d_mixed, other_d_mixed)
    return outs[:ny], outs[ny:]


def in_grad_kernel(normed_ref, grad_ref, weight_ref, gain_ref, out_ref, part_ref):
    blocks, rows, width = grad_ref.shape
    grad = grad_ref[...].reshape(blocks * rows, width)
    total = lax.dot_general(grad, normed_ref[...], TN, preferred_element_type=jnp.float32)
    out_ref[...] = total.astype(jnp.bfloat16)
    part_ref[...] = jnp.sum(total * wide(weight_ref[...]), axis=0, keepdims=True) / gain_ref[...]


def in_grad_parts(normed, grad, weight, gain):
    tokens, depth = normed.shape
    width = grad.shape[2]
    size = min(512, depth)
    block = lambda rows: pl.BlockSpec((rows, size), lambda i: (0, i))
    return pl.pallas_call(
        in_grad_kernel,
        grid=(depth // size,),
        in_specs=[
            block(tokens),
            pl.BlockSpec(grad.shape, lambda i: (0, 0, 0)),
            block(width),
            block(1),
        ],
        out_specs=[block(width), block(1)],
        out_shape=[
            jax.ShapeDtypeStruct((width, depth), jnp.bfloat16),
            jax.ShapeDtypeStruct((1, depth), jnp.float32),
        ],
        compiler_params=pltpu.CompilerParams(
            dimension_semantics=("arbitrary",), vmem_limit_bytes=VMEM
        ),
        cost_estimate=LITTLE,
    )(normed, grad, weight, gain)


def tie(*values):
    return lax.optimization_barrier(values)


def per_device(
    wires,
    tokens,
    keep_mask,
    seq_lengths,
    attn_gain,
    in_weight,
    out_weight,
    ffn_gain,
    gate_weight,
    up_weight,
    down_weight,
    out_grad,
):
    wires.place()
    heads_here = in_weight.shape[1] // (2 * FD + VD)
    rows, depth = tokens.shape
    group_rows = rows * wires.head
    out_rows = heads_here * VD
    size = depth // wires.dp
    tokens_wide = wide(tokens)
    own = low(tokens_wide * inv_root_mean(tokens_wide) * attn_gain)
    across_y = range(1, wires.ny)

    def on_y(pieces):
        return [[wires.over_y(piece, s) for s in across_y] for piece in pieces]

    def swap(values):
        return lax.all_to_all(values, "head", split_axis=0, concat_axis=0, tiled=True)

    turned = dict(split_axis=0, concat_axis=0, tiled=True)
    same_core = [[z * 2 + c for z in range(wires.nz)] for c in range(2)]

    def add(*values):
        return low(sum(wide(value) for value in values))

    packed_width = in_weight.shape[1]
    in_turned = in_weight.T
    in_part = wires.quarter(in_turned)
    keep_row = keep_mask.astype(jnp.float32)[None]
    ends = jnp.cumsum(seq_lengths[0])
    stacked = jnp.stack([gate_weight.T, up_weight.T, down_weight])
    unit_own = pick(stacked, wires.x, 2, 1)
    unit_other = pick(stacked, 1 - wires.x, 2, 1)
    share = out_rows * size // rows
    block = jnp.concatenate([own, wires.quarter(out_weight).reshape(rows, share)], axis=1)

    flying = {}

    def beside_line(step, values):
        if step == 1:
            by_x = wires.over_x(unit_other)
            values, flying["by_x"], flying["own"], flying["in_part"], flying["out_grad"], flying["swap"] = tie(
                values, by_x, unit_own, in_part, out_grad, wires.over_core(block)
            )
        elif step == 2:
            pair = in_order([flying["own"], flying["by_x"]], wires.x, 2)
            by_x = wires.over_x(flying["out_grad"])
            values, flying["grad_x"], flying["pair"], flying["out_grad"] = tie(
                values, by_x, pair, flying["out_grad"]
            )
        elif step == wires.nz - 1:
            by_y = [wires.over_y(flying["pair"][:2], s) for s in across_y]
            halves = [wires.over_zh_half(flying["pair"][:2], s, 0) for s in range(1, wires.nzh)]
            values, flying["by_y"], flying["pair"], flying["grad_x"], flying["halves"] = tie(
                values, by_y, flying["pair"], flying["grad_x"], halves
            )
        else:
            (values,) = tie(values)
        return values

    chunks, chips = wires.line(block, beside_line)
    others = [flying["swap"]] + [wires.over_core(chunk) for chunk in chunks[1:]]
    pieces = [piece for pair in zip(chunks, others) for piece in pair]
    places = jnp.stack(
        [(chip * 2 + (wires.c ^ r)) * rows for chip in chips for r in range(2)]
    ).astype(jnp.int32)
    pieces, unit_pair, out_grad, grad_x = tie(
        pieces, flying["pair"], flying["out_grad"], flying["grad_x"]
    )

    def shares(blocks):
        return jnp.stack([piece[:, depth:].reshape(out_rows, size) for piece in blocks])

    halves = [wires.over_zh_half(unit_pair[:2], s, 1) for s in range(1, wires.nzh)]
    out_line = shares(pieces[::2])
    out_x, out_y = wires.over_x(out_line), [wires.over_y(out_line, s) for s in across_y]
    projected, normed, attended_wide, inverses, attended = attend(
        pieces, places, in_turned, keep_row, ends, heads_here
    )
    attended, out_x, out_y, halves, unit_pair = tie(attended, out_x, out_y, halves, unit_pair)
    attended_here = swap(attended).reshape(wires.head, rows, out_rows)
    out_across = [wires.over_x(piece) for piece in out_y]
    by_zh_gu = [
        wires.from_halves(flying["halves"][s - 1], halves[s - 1], s) for s in range(1, wires.nzh)
    ]
    by_zh_guy = on_y(by_zh_gu)
    out_line_swap = shares(pieces[1::2])
    out_x_swap, out_y_swap = wires.over_core(out_x), [wires.over_core(piece) for piece in out_y]
    attended_here, out_across, out_x_swap, out_y_swap, unit_pair, by_zh_gu, by_zh_guy, out_line_swap = tie(
        attended_here, out_across, out_x_swap, out_y_swap, unit_pair, by_zh_gu, by_zh_guy, out_line_swap
    )
    out_across_swap = [wires.over_core(piece) for piece in out_across]

    def in_layout(line, by_x, by_y, across):
        pieces = [line, by_x]
        for piece in zip(by_y, across):
            pieces += piece
        return pieces

    out_pieces = in_layout(out_line, out_x, out_y, out_across)
    out_pieces += in_layout(out_line_swap, out_x_swap, out_y_swap, out_across_swap)
    out_whole = Whole(wires, out_pieces, wires.whole_places(chips, out_rows, size), out_rows, size)
    middle, normed_two = mix(attended_here, out_whole, tokens, ffn_gain[None])

    normed_two, unit_pair, grad_x, out_grad = tie(normed_two, unit_pair, grad_x, out_grad)
    two_x, two_z = wires.over_x(normed_two), wires.over_zl(normed_two)
    by_zh_d = [wires.over_zh(unit_pair[2:], s) for s in range(1, wires.nzh)]
    by_y_d = [wires.over_y(unit_pair[2:], s) for s in across_y]
    two_swap = wires.over_core(normed_two)
    two_x, two_z, by_zh_d, two_swap, by_y_d, unit_pair, out_grad = tie(
        two_x, two_z, by_zh_d, two_swap, by_y_d, unit_pair, out_grad
    )
    two_corner = wires.over_x(two_z)
    by_zh_dy = on_y(by_zh_d)
    grad_z = wires.over_zl(out_grad)
    two_swaps = [two_swap] + [wires.over_core(piece) for piece in (two_x, two_z)]
    two_corner, by_zh_dy, two_swaps, two_x, two_z, grad_z, attended_here = tie(
        two_corner, by_zh_dy, two_swaps, two_x, two_z, grad_z, attended_here
    )

    spot = unit_pair.shape[1], unit_pair.shape[2]
    gates = [(unit_pair[:2], 0, 2, 0, 0)] + [(flying["by_y"][s - 1], 0, 2, 0, s) for s in across_y]
    for zh in range(1, wires.nzh):
        gates.append((by_zh_gu[zh - 1], 0, 2, zh, 0))
        gates += [(by_zh_guy[zh - 1][s - 1], 0, 2, zh, s) for s in across_y]
    units = Units(wires, gates, 2, *spot)

    in_line = lax.all_to_all(
        jnp.concatenate([flying["in_part"]] * wires.nz, axis=0), "head", axis_index_groups=same_core, **turned
    ).reshape(wires.nz, packed_width, size)
    grad_corner = wires.over_x(grad_z)
    two_corner_swap = wires.over_core(two_corner)
    for_other = pick(attended_here.reshape(wires.nz, 2, rows, out_rows), 1 - wires.c, 2, 1)[:, 0]
    attended_other = wires.over_core(for_other)
    grad_swaps = [wires.over_core(grad) for grad in (out_grad, grad_x)]
    first = gate_up(list(zip([normed_two, two_x, two_z], two_swaps)), units)
    first, grad_corner, two_corner, two_corner_swap, grad_z, attended_other, grad_swaps = tie(
        first, grad_corner, two_corner, two_corner_swap, grad_z, attended_other, grad_swaps
    )
    grad_swaps += [wires.over_core(grad) for grad in (grad_z, grad_corner)]
    second = gate_up([(two_corner, two_corner_swap)], units)
    second, grad_swaps, in_line = tie(second, grad_swaps, in_line)
    grad_pairs = list(zip([out_grad, grad_x, grad_z, grad_corner], grad_swaps))
    downs = [(unit_pair[2:], 0, 1, 0, 0)] + [(by_y_d[s - 1], 0, 1, 0, s) for s in across_y]
    for zh in range(1, wires.nzh):
        downs.append((by_zh_d[zh - 1], 0, 1, zh, 0))
        downs += [(by_zh_dy[zh - 1][s - 1], 0, 1, zh, s) for s in across_y]
    units = Units(
        wires, downs + [(array, at + 1, count, zh, s) for array, at, count, zh, s in gates], 3, *spot
    )

    in_x, in_y = wires.over_x(in_line), [wires.over_y(in_line, s) for s in across_y]
    in_line_swap = wires.over_core(in_line)
    outs_co, (dnormed_c, dnormed_o), (branch_c, branch_o) = down(
        [(*grad_pairs[3], second[0], 0), (*grad_pairs[0], first[0], 0)], units
    )
    outs_co, in_x, in_y, dnormed_c, dnormed_o, branch_c, in_line_swap = tie(
        outs_co, in_x, in_y, dnormed_c, dnormed_o, branch_c, in_line_swap
    )
    swap_c, swap_o = wires.over_core(dnormed_c[1]), wires.over_core(dnormed_o[1])
    swap_b = wires.over_core(branch_c[1])
    swap_c, swap_o, swap_b, outs_co, in_x = tie(swap_c, swap_o, swap_b, outs_co, in_x)
    sum_c, sum_b = add(dnormed_c[0], swap_c), add(branch_c[0], swap_b)
    to_z, to_x = wires.over_x(sum_c), wires.over_zl(sum_b)
    in_across = [wires.over_y(in_x, s) for s in across_y]
    in_swaps = [wires.over_core(piece) for piece in (in_x, *in_y)]
    grad_x_pair, grad_z_pair, *_ = tie(grad_pairs[1], grad_pairs[2], sum_c, sum_b, outs_co)
    outs_xz, (dnormed_x, dnormed_z), (branch_x, branch_z) = down(
        [(*grad_x_pair, first[0], 1), (*grad_z_pair, first[0], 2)], units
    )
    outs_xz, dnormed_x, dnormed_z, branch_x, branch_z, to_z, to_x, in_across, in_swaps = tie(
        outs_xz, dnormed_x, dnormed_z, branch_x, branch_z, to_z, to_x, in_across, in_swaps
    )
    swap_x, swap_z = wires.over_core(dnormed_x[1]), wires.over_core(dnormed_z[1])
    swap_x, swap_z, to_z = tie(swap_x, swap_z, to_z)
    sum_x = add(dnormed_x[0], swap_x)
    final_x = wires.over_x(sum_x)
    sum_z = add(dnormed_z[0], swap_z, to_z)
    final_z = wires.over_zl(sum_z)
    sum_o = add(dnormed_o[0], swap_o)

    every = (outs_co, outs_xz, first, second)

    def grad_of(every, unit):
        (units_co, grad_co), (units_xz, grad_xz), (made, normed_oxz), (made_c, normed_c) = every
        if unit == 0:
            lefts = [(made_c, (0, 0)), (made, (0, 0)), (made, (1, 0)), (made, (2, 0))]
            rights = [(grad_co, 0), (grad_co, 1), (grad_xz, 0), (grad_xz, 1)]
        else:
            lefts = [(array, (i, unit - 1)) for array in (units_co, units_xz) for i in range(2)]
            rights = [(normed_c, 0), (normed_oxz, 0), (normed_oxz, 1), (normed_oxz, 2)]
        return unit_grad(wires, lefts, rights)

    def on_y_steps(blocks):
        return [wires.over_y(blocks[s], s) for s in across_y]

    def on_zh(totals):
        return [wires.over_zh(total, -s) for s, total in enumerate(totals, 1)]

    def totals_of(parts, sent):
        return [add(part[0], *more) for part, more in zip(parts, sent)]

    def grad_last(mine, sent):
        return wide(in_order([mine, sent], wires.x, 0))

    every, sum_x, sum_z, branch_x, branch_z = tie(every, sum_x, sum_z, branch_x, branch_z)
    swap_x, swap_z = wires.over_core(branch_x[1]), wires.over_core(branch_z[1])
    in_across_swap = [wires.over_core(piece) for piece in in_across]
    gate_parts = grad_of(every, 1)
    sum_x, sum_z = add(branch_x[0], swap_x, to_x), add(branch_z[0], swap_z)
    final_x, final_z, gate_parts, sum_o, sum_x, sum_z, in_across_swap = tie(
        final_x, final_z, gate_parts, sum_o, sum_x, sum_z, in_across_swap
    )
    gate_sent = [on_y_steps(part) for part in gate_parts[1:]]
    d_middle, d_mixed, ffn_gain_part, d_attended = unmix(
        (sum_o, final_x, final_z), middle, out_grad, ffn_gain[None], out_whole, wires.head
    )
    every, d_attended, d_mixed, gate_parts, gate_sent, sum_x, sum_z = tie(
        every, d_attended, d_mixed, gate_parts, gate_sent, sum_x, sum_z
    )
    d_attended = swap(d_attended).reshape(group_rows, out_rows)
    final_x, final_z = wires.over_x(sum_x), wires.over_zl(sum_z)
    gate_back = on_zh(totals_of(gate_parts[1:], gate_sent))
    gate_sent = on_y_steps(gate_parts[0])
    other_d_mixed = wires.over_core(d_mixed)
    up_parts = grad_of(every, 2)
    up_sent = [on_y_steps(part) for part in up_parts[1:]]
    out_own, out_sent = out_grad_parts(wires, attended_here, attended_other, d_mixed, other_d_mixed)
    down_parts = grad_of(every, 0)
    d_attended, final_x, final_z, gate_back, gate_sent, up_parts, up_sent, out_own, out_sent, down_parts = tie(
        d_attended, final_x, final_z, gate_back, gate_sent, up_parts, up_sent, out_own, out_sent, down_parts
    )
    up_totals = totals_of(up_parts[1:], up_sent)
    up_totals, d_attended, out_sent, up_parts, down_parts = tie(
        up_totals, d_attended, out_sent, up_parts, down_parts
    )
    up_back = on_zh(up_totals)
    up_sent = on_y_steps(up_parts[0])
    down_sent = [on_y_steps(part) for part in down_parts[1:]]
    out_first = [wires.over_x(out_sent[s]) for s in across_y]
    d_projected = attend_back(
        projected, keep_row, ends, attended_wide, inverses, d_attended, heads_here, rows
    )
    d_projected, up_back, up_sent, down_sent, out_first = tie(
        d_projected, up_back, up_sent, down_sent, out_first
    )
    down_totals = totals_of(down_parts[1:], down_sent)
    out_total = [add(out_own[s], out_first[s - 1]) for s in across_y]
    down_totals, out_total, d_projected, down_parts, in_line, in_x, in_y, in_across = tie(
        down_totals, out_total, d_projected, down_parts, in_line, in_x, in_y, in_across
    )
    d_here = swap(d_projected)
    down_sent = on_y_steps(down_parts[0])
    out_last = wires.over_x(out_sent[0])
    swap_o = wires.over_core(branch_o[1])
    out_y = [wires.over_y(total, s) for total, s in zip(out_total, across_y)]
    in_back, attn_gain_part = in_grad_parts(normed, d_projected, in_turned, attn_gain[None])
    firsts = [
        add(parts[0][0], *sent, *back)
        for parts, sent, back in ((gate_parts, gate_sent, gate_back), (up_parts, up_sent, up_back))
    ]
    d_here, in_back, attn_gain_part, down_sent, out_last, out_y, firsts, down_totals, swap_o = tie(
        d_here, in_back, attn_gain_part, down_sent, out_last, out_y, firsts, down_totals, swap_o
    )
    cut = packed_width // 2
    gains = jnp.concatenate([attn_gain_part, ffn_gain_part], axis=0)
    in_pieces = in_layout(in_line, in_x, in_y, in_across)
    in_pieces += in_layout(in_line_swap, in_swaps[0], in_swaps[1:], in_across_swap)
    in_whole = Whole(
        wires, in_pieces, wires.whole_places(range(wires.nz), packed_width, size), packed_width, size
    )
    down_back = on_zh(down_totals)
    out_total = add(out_own[0], out_last, *out_y)
    in_x, in_y = wires.over_x(in_back[:cut]), [wires.over_y(in_back[cut:], s) for s in across_y]
    others = wires.over_x(jnp.stack([pick(total, 1 - wires.x, 2, 1) for total in firsts]))
    in_grad = last(d_here, in_whole, tokens, d_middle, attn_gain[None])
    in_grad, out_total, in_x, in_y, others, down_sent, down_back = tie(
        in_grad, out_total, in_x, in_y, others, down_sent, down_back
    )
    out_turns = lax.all_to_all(out_total, "head", axis_index_groups=same_core, **turned)
    in_halves = (wires.sum_y(add(in_back[:cut], in_x)), wires.sum_x(add(in_back[cut:], *in_y)))
    totals = [*firsts, add(down_parts[0][0], *down_sent, *down_back)]
    others = [others[0], others[1], wires.over_x(pick(totals[2], 1 - wires.x, 2, 1))]
    gains = gains + wires.over_core(gains)
    out_turns, gains, others, in_halves, totals = tie(out_turns, gains, others, in_halves, totals)
    out_part = add(*[out_turns[z] for z in range(wires.nz)])
    out_x = wires.over_x(out_part)
    out_by_y = [wires.over_y(out_part, s) for s in across_y]
    output = low(middle + wide(branch_o[0]) + wide(swap_o) + wide(final_x) + wide(final_z))
    gains = gains + wires.over_zl(gains)
    gains = gains + sum(wires.over_zh(gains, s) for s in range(1, wires.nzh))
    gate_grad, up_grad, down_grad = (
        grad_last(pick(total, wires.x, 2, 1), other) for total, other in zip(totals, others)
    )
    gate_grad, up_grad = gate_grad.T, up_grad.T
    out_x, out_by_y, gains, output, gate_grad, up_grad, down_grad = tie(
        out_x, out_by_y, gains, output, gate_grad, up_grad, down_grad
    )
    out_by_yx = [wires.over_y(out_x, s) for s in across_y]
    gains_x = wires.over_x(gains)
    gains = gains + gains_x + sum(
        wires.over_y(gains, s) + wires.over_dp(gains, s) for s in across_y
    )
    out_weight_grad = wide(
        in_order(
            [
                in_order([a, b], wires.x, 1)
                for a, b in zip([out_part, *out_by_y], [out_x, *out_by_yx])
            ],
            wires.y,
            1,
        )
    )
    in_weight_grad = wide(jnp.concatenate(in_halves, axis=0)).T
    return (
        output,
        in_grad,
        gains[0],
        in_weight_grad,
        out_weight_grad,
        gains[1],
        gate_grad,
        up_grad,
        down_grad,
    )


def solution(mesh):
    return jax.shard_map(
        functools.partial(per_device, Wires(mesh)),
        mesh=mesh,
        in_specs=(
            P(("dp", "head"), None),
            P("dp"),
            P("dp", None),
            P(),
            P(None, "head"),
            P("head", None),
            P(),
            P("dp", "head"),
            P("dp", "head"),
            P("head", "dp"),
            P(("dp", "head"), None),
        ),
        out_specs=(
            P(("dp", "head"), None),
            P(("dp", "head"), None),
            P(),
            P(None, "head"),
            P("head", None),
            P(),
            P("dp", "head"),
            P("dp", "head"),
            P("head", "dp"),
        ),
        check_vma=False,
    )
```

```python
import functools
import jax
import jax.numpy as jnp
from jax import lax
from jax.experimental import pallas as pl
from jax.experimental.pallas import tpu as pltpu
from jax.sharding import PartitionSpec as P

FD = 16
VD = 128
LANES = 128
VMEM = 60 * 1024 * 1024
LITTLE = pl.CostEstimate(flops=1, bytes_accessed=1, transcendentals=0)
epsilon = 1e-05
NT = (((1,), (1,)), ((), ()))
TN = (((0,), (0,)), ((), ()))


def column_of(row):
    count = row.shape[1]
    same = lax.broadcasted_iota(jnp.int32, (count, count), 0) == lax.broadcasted_iota(
        jnp.int32, (count, count), 1
    )
    return jnp.sum(jnp.where(same, row, 0.0), axis=1, keepdims=True)


def padded(block):
    rows, columns = block.shape
    return jnp.concatenate([block, jnp.zeros((rows, -columns % LANES), block.dtype)], axis=1)


def lanes_from(block, low, count):
    width = block.shape[1]
    moved = (block if low == 0 else pltpu.roll(block, width - low, 1))[:, :LANES]
    if count == LANES:
        return moved
    lane = lax.broadcasted_iota(jnp.int32, moved.shape, 1)
    return jnp.where(lane < count, moved, 0.0)


def head_parts(block, head):
    low = head * (2 * FD + VD)
    query = lanes_from(block, low, FD) * 0.25
    return query, lanes_from(block, low + FD, FD), lanes_from(block, low + 2 * FD, VD)


def segment_start(ends_ref, positions):
    start = jnp.zeros_like(positions)
    for slot in range(ends_ref.shape[0]):
        end = ends_ref[slot]
        start = jnp.where(positions >= end, jnp.maximum(start, end), start)
    return start


def attend_kernel(heads, rows, pieces, ends_ref, at_ref, *refs):
    sources = refs[:pieces]
    weight_ref, keep_ref, projected_ref, normed_ref, y_ref, inv_ref, att_ref = refs[pieces : pieces + 7]
    normed_s, key_s, value_s, sems = refs[pieces + 7 :]
    step = pl.program_id(0)
    own = pl.ds(pl.multiple_of(step * rows, rows), rows)

    @pl.when(step == 0)
    def _():
        size = sources[0].shape[0]
        copies = [
            pltpu.make_async_copy(
                sources[i].at[:, pl.ds(0, normed_s.shape[1])], normed_s.at[pl.ds(pl.multiple_of(at_ref[i], size), size), :], sems.at[i]
            )
            for i in range(pieces)
        ]
        for copy in copies:
            copy.start()
        for copy in copies:
            copy.wait()

    keep = column_of(keep_ref[:, own])
    normed = normed_s[own, :]
    normed_ref[...] = normed
    projected = lax.dot_general(
        normed, weight_ref[...], NT, preferred_element_type=jnp.float32
    ).astype(jnp.bfloat16)
    projected_ref[...] = projected
    block = padded(projected.astype(jnp.float32))
    lane = lax.broadcasted_iota(jnp.int32, (rows, LANES), 1)
    ones = jnp.where(lane < 2, keep, 0.0).astype(jnp.bfloat16)
    queries = []
    for head in range(heads):
        query, key, value = head_parts(block, head)
        queries.append(query.astype(jnp.bfloat16))
        key_s[head, own, :] = key.astype(jnp.bfloat16)
        value_s[head, own, :VD] = (value * keep).astype(jnp.bfloat16)
        value_s[head, own, VD:] = ones
    row = step * rows + lax.broadcasted_iota(jnp.int32, (rows, 1), 0)
    start = segment_start(ends_ref, row)
    column = lax.broadcasted_iota(jnp.int32, (rows, rows), 1)

    def tile(block, totals, diagonal):
        at = pl.ds(pl.multiple_of(block * rows, rows), rows)
        allowed = column >= start - block * rows
        if diagonal:
            allowed &= column <= lax.broadcasted_iota(jnp.int32, (rows, rows), 0)
        added = []
        for head in range(heads):
            inner = lax.dot_general(
                queries[head], key_s[head, at, :], NT, preferred_element_type=jnp.float32
            )
            weights = jnp.where(allowed, (inner * 0.5 + 1.0) * inner + 1.0, 0.0).astype(jnp.bfloat16)
            added.append(
                totals[head]
                + jnp.dot(weights, value_s[head, at, :], preferred_element_type=jnp.float32)
            )
        return tuple(added)

    totals = tuple(jnp.zeros((rows, 2 * VD), jnp.float32) for _ in range(heads))
    totals = lax.fori_loop(0, step, lambda block, held: tile(block, held, False), totals)
    totals = tile(step, totals, True)
    inverses = jnp.zeros((rows, LANES), jnp.float32)
    for head in range(heads):
        inverse = 1.0 / (totals[head][:, VD : VD + 1] + 1.0 - keep)
        y = totals[head][:, :VD] * (keep * inverse)
        y_ref[:, head * VD : (head + 1) * VD] = y
        att_ref[:, head * VD : (head + 1) * VD] = y.astype(jnp.bfloat16)
        inverses = jnp.where(lane == head, inverse, inverses)
    inv_ref[...] = inverses


def attend(pieces, places, weight, keep, ends, heads):
    size, depth = pieces[0].shape[0], weight.shape[1]
    total = size * len(pieces)
    rows = min(512, total)
    width = weight.shape[0]
    pairs = total * (total + rows) // 2 * heads
    blocked = lambda columns: pl.BlockSpec((rows, columns), lambda i, e, a: (i, 0))
    return pl.pallas_call(
        functools.partial(attend_kernel, heads, rows, len(pieces)),
        grid_spec=pltpu.PrefetchScalarGridSpec(
            num_scalar_prefetch=2,
            grid=(total // rows,),
            in_specs=[pl.BlockSpec(memory_space=pl.ANY)] * len(pieces)
            + [
                pl.BlockSpec((width, depth), lambda i, e, a: (0, 0)),
                pl.BlockSpec((1, total), lambda i, e, a: (0, 0)),
            ],
            out_specs=[
                blocked(width), blocked(depth), blocked(heads * VD), blocked(LANES), blocked(heads * VD)
            ],
            scratch_shapes=[
                pltpu.VMEM((total, depth), jnp.bfloat16),
                pltpu.VMEM((heads, total, LANES), jnp.bfloat16),
                pltpu.VMEM((heads, total, 2 * VD), jnp.bfloat16),
                pltpu.SemaphoreType.DMA((len(pieces),)),
            ],
        ),
        out_shape=[
            jax.ShapeDtypeStruct((total, width), jnp.bfloat16),
            jax.ShapeDtypeStruct((total, depth), jnp.bfloat16),
            jax.ShapeDtypeStruct((total, heads * VD), jnp.float32),
            jax.ShapeDtypeStruct((total, LANES), jnp.float32),
            jax.ShapeDtypeStruct((total, heads * VD), jnp.bfloat16),
        ],
        compiler_params=pltpu.CompilerParams(
            dimension_semantics=("arbitrary",), vmem_limit_bytes=VMEM
        ),
        cost_estimate=LITTLE,
    )(ends, places, *pieces, weight, keep)


def attend_back_kernel(
    heads, rows, ends_ref, projected_ref, keep_ref, y_ref, inv_ref, grad_ref, out_ref,
    key_s, query_s, value_s, error_s, dquery_s,
):
    step = pl.program_id(0)
    blocks = pl.num_programs(0)
    lane = lax.broadcasted_iota(jnp.int32, (rows, LANES), 1)

    @pl.when(step == 0)
    def _():
        dquery_s[...] = jnp.zeros_like(dquery_s)

        def fill(block, nothing):
            at = pl.ds(pl.multiple_of(block * rows, rows), rows)
            keep = column_of(keep_ref[:, at])
            wide_block = padded(projected_ref[at, :].astype(jnp.float32))
            ones = jnp.where(lane < 2, keep, 0.0).astype(jnp.bfloat16)
            inverses = inv_ref[at, :]
            for head in range(heads):
                columns = slice(head * VD, (head + 1) * VD)
                query, key, value = head_parts(wide_block, head)
                key_s[head, at, :] = key.astype(jnp.bfloat16)
                query_s[head, at, :] = query.astype(jnp.bfloat16)
                value_s[head, at, :VD] = (value * keep).astype(jnp.bfloat16)
                value_s[head, at, VD:] = ones
                inverse = inverses[:, head : head + 1]
                grad = grad_ref[at, columns].astype(jnp.float32)
                error_s[head, at, :VD] = (grad * (keep * inverse)).astype(jnp.bfloat16)
                offset = -jnp.sum(grad * y_ref[at, columns], axis=1, keepdims=True) * inverse
                high = offset.astype(jnp.bfloat16).astype(jnp.float32)
                error_s[head, at, VD:] = jnp.where(
                    lane == 0, high, jnp.where(lane == 1, offset - high, 0.0)
                ).astype(jnp.bfloat16)
            return nothing

        lax.fori_loop(0, blocks, fill, 0)

    own = pl.ds(pl.multiple_of(step * rows, rows), rows)
    row = lax.broadcasted_iota(jnp.int32, (rows, rows), 0)

    def tile(block, totals, diagonal):
        at = pl.ds(pl.multiple_of(block * rows, rows), rows)
        column = block * rows + lax.broadcasted_iota(jnp.int32, (1, rows), 1)
        allowed = row >= segment_start(ends_ref, column) - step * rows
        if diagonal:
            allowed &= row <= lax.broadcasted_iota(jnp.int32, (rows, rows), 1)
        dkeys, dvalues = totals
        added, turned = [], []
        for head in range(heads):
            query = query_s[head, at, :]
            error = error_s[head, at, :]
            keys = key_s[head, own, :]
            inner = lax.dot_general(keys, query, NT, preferred_element_type=jnp.float32)
            dweight = lax.dot_general(value_s[head, own, :], error, NT, preferred_element_type=jnp.float32)
            slope = inner + 1.0
            weights = jnp.where(allowed, (slope * slope + 1.0) * 0.5, 0.0).astype(jnp.bfloat16)
            dinner = jnp.where(allowed, slope * dweight, 0.0).astype(jnp.bfloat16)
            added.append(
                dvalues[head] + jnp.dot(weights, error[:, :VD], preferred_element_type=jnp.float32)
            )
            turned.append(dkeys[head] + jnp.dot(dinner, query, preferred_element_type=jnp.float32))
            dquery_s[head, at, :] += lax.dot_general(dinner, keys, TN, preferred_element_type=jnp.float32)
        return tuple(turned), tuple(added)

    totals = (
        tuple(jnp.zeros((rows, LANES), jnp.float32) for _ in range(heads)),
        tuple(jnp.zeros((rows, VD), jnp.float32) for _ in range(heads)),
    )
    totals = tile(step, totals, True)
    dkeys, dvalues = lax.fori_loop(step + 1, blocks, lambda block, held: tile(block, held, False), totals)
    keep = column_of(keep_ref[:, own])
    width = out_ref.shape[2]
    total = jnp.zeros((rows, width + -width % LANES), jnp.float32)
    blank = jnp.zeros((rows, total.shape[1] - LANES), jnp.float32)

    def put(block, low):
        spread = jnp.concatenate([block, blank], axis=1)
        return spread if low == 0 else pltpu.roll(spread, low, 1)

    for head in range(heads):
        low = head * (2 * FD + VD)
        total += put(dquery_s[head, own, :] * 0.25, low)
        total += put(dkeys[head], low + FD)
        total += put(dvalues[head] * keep, low + 2 * FD)
    out_ref[...] = total[:, :width].astype(jnp.bfloat16).reshape(out_ref.shape)


def attend_back(projected, keep, ends, y, inverses, grad, heads, each):
    total = projected.shape[0]
    rows = min(512, total)
    width = projected.shape[1]
    whole = lambda columns: pl.BlockSpec((total, columns), lambda i, e: (0, 0))
    return pl.pallas_call(
        functools.partial(attend_back_kernel, heads, rows),
        grid_spec=pltpu.PrefetchScalarGridSpec(
            num_scalar_prefetch=1,
            grid=(total // rows,),
            in_specs=[whole(width), pl.BlockSpec((1, total), lambda i, e: (0, 0)), whole(heads * VD), whole(LANES), whole(heads * VD)],
            out_specs=pl.BlockSpec((rows // each, each, width), lambda i, e: (i, 0, 0)),
            scratch_shapes=[
                pltpu.VMEM((heads, total, LANES), jnp.bfloat16),
                pltpu.VMEM((heads, total, LANES), jnp.bfloat16),
                pltpu.VMEM((heads, total, 2 * VD), jnp.bfloat16),
                pltpu.VMEM((heads, total, 2 * VD), jnp.bfloat16),
                pltpu.VMEM((heads, total, LANES), jnp.float32),
            ],
        ),
        out_shape=jax.ShapeDtypeStruct((total // each, each, width), jnp.bfloat16),
        compiler_params=pltpu.CompilerParams(
            dimension_semantics=("arbitrary",), vmem_limit_bytes=VMEM
        ),
        cost_estimate=LITTLE,
    )(ends, projected, keep, y, inverses, grad)


def inv_root_mean(values):
    return lax.rsqrt(jnp.mean(values * values, axis=1, keepdims=True) + epsilon)


def wide(values):
    return values.astype(jnp.float32)


def low(values):
    return values.astype(jnp.bfloat16)


def pick(values, index, count, axis):
    size = values.shape[axis] // count
    if count == 2:
        first = lax.slice_in_dim(values, 0, size, axis=axis)
        second = lax.slice_in_dim(values, size, 2 * size, axis=axis)
        return jnp.where(index == 0, first, second)
    return lax.dynamic_slice_in_dim(values, index * size, size, axis)


def in_order(pieces, index, axis):
    count = len(pieces)
    if count == 1:
        return pieces[0]
    if count == 2:
        first = jnp.where(index == 0, pieces[0], pieces[1])
        second = jnp.where(index == 0, pieces[1], pieces[0])
        return jnp.concatenate([first, second], axis=axis)
    stacked = jnp.stack(pieces)
    placed = [
        lax.dynamic_index_in_dim(stacked, (index - place) % count, 0, keepdims=False)
        for place in range(count)
    ]
    return jnp.concatenate(placed, axis=axis)


class Wires:
    def __init__(self, mesh):
        self.dp, self.head = mesh.shape["dp"], mesh.shape["head"]
        self.ny, self.nz, self.nzh = self.dp // 2, self.head // 2, self.head // 4

    def place(self):
        p, h = lax.axis_index("dp"), lax.axis_index("head")
        self.p, self.h = p, h
        self.y, self.x, self.z, self.c = p // 2, p % 2, h // 2, h % 2
        self.zh = self.z // 2

    def over_x(self, values):
        return lax.ppermute(values, "dp", [(i, i ^ 1) for i in range(self.dp)])

    def over_y(self, values, shift):
        return lax.ppermute(
            values, "dp", [(i, ((i // 2 + shift) % self.ny) * 2 + i % 2) for i in range(self.dp)]
        )

    def over_dp(self, values, shift):
        return lax.ppermute(
            values, "dp", [(i, ((i // 2 + shift) % self.ny) * 2 + (i + 1) % 2) for i in range(self.dp)]
        )

    def over_core(self, values):
        return lax.ppermute(values, "head", [(i, i ^ 1) for i in range(self.head)])

    def over_zl(self, values):
        return lax.ppermute(values, "head", [(i, i ^ 2) for i in range(self.head)])

    def over_zh(self, values, shift):
        return lax.ppermute(
            values, "head", [(i, ((i // 4 + shift) % self.nzh) * 4 + i % 4) for i in range(self.head)]
        )

    def over_zh_half(self, values, shift, parity):
        pairs = [
            (i, ((i // 4 + shift) % self.nzh) * 4 + i % 4)
            for i in range(self.head)
            if (i // 4 + i // 2 % 2) % 2 == parity
        ]
        return lax.ppermute(values, "head", pairs)

    def from_halves(self, first, second, shift):
        even = (self.zh - shift + self.z) % 2 == 0
        return jnp.where(even, first, second)

    def over_z(self, values, shift):
        return lax.ppermute(
            values, "head", [(i, ((i // 2 + shift) % self.nz) * 2 + i % 2) for i in range(self.head)]
        )

    def right(self, values, first, last):
        return lax.ppermute(
            values, "head", [(i, i + 2) for i in range(self.head) if first <= i // 2 <= last]
        )

    def left(self, values, first, last):
        return lax.ppermute(
            values, "head", [(i, i - 2) for i in range(self.head) if first <= i // 2 <= last]
        )

    def spread(self, line):
        return self.over_x(line), [self.over_y(line, s) for s in range(1, self.ny)]

    def ends(self, values):
        pairs = [(i, i + 2 if i // 2 == self.nz - 2 else i - 2) for i in range(self.head)]
        return lax.ppermute(
            values, "head", [pair for pair in pairs if pair[0] // 2 in (1, self.nz - 2)]
        )

    def arrivals(self):
        orders = []
        for z in range(self.nz):
            order = []
            for step in range(1, self.nz):
                order += [(0, step)] if z >= step else []
                order += [(1, step)] if z + step < self.nz else []
            orders.append(order)
        return orders

    def by_place(self, values):
        chosen, taken = values[0], [values[0]]
        for value in values[1:]:
            if any(value is other for other in taken):
                continue
            taken.append(value)
            here = [z for z in range(self.nz) if values[z] is value]
            chosen = jnp.where(sum((self.z == z).astype(jnp.int32) for z in here) > 0, value, chosen)
        return chosen

    def sum_y(self, values):
        total = wide(values)
        for s in range(1, self.ny):
            total = total + wide(self.over_y(values, s))
        return low(total)

    def sum_x(self, values):
        return low(wide(values) + wide(self.over_x(values)))

    def sum_all(self, values):
        values = values + self.over_core(values)
        values = values + self.over_zl(values)
        values = values + sum(self.over_zh(values, s) for s in range(1, self.nzh))
        values = values + self.over_x(values)
        return values + sum(self.over_y(values, s) for s in range(1, self.ny))

    def quarter(self, shard):
        size = shard.shape[1] // self.dp
        return lax.dynamic_slice_in_dim(shard, self.p * size, size, 1)

    def line_of(self, part):
        return [part] + [self.over_z(part, s) for s in range(1, self.nz)]

    def whole_places(self, chips, rows, size):
        at_rows = [(chip * 2 + (self.c ^ r)) * rows for r in range(2) for chip in chips]
        at_columns = [
            (((self.y - s) % self.ny) * 2 + (self.x ^ t)) * size
            for s in range(self.ny)
            for t in range(2)
        ]
        return jnp.stack(at_rows + at_columns).astype(jnp.int32)

    def line(self, block, during):
        steps = self.nz
        right = left = block
        rights, lefts = {}, {}
        orders = self.arrivals()
        chunks, chips = [block], [self.z]
        for step in range(1, steps):
            if step < steps - 1:
                right = self.right(right, step - 1, steps - 2)
                left = self.left(left, 1, steps - step)
                right, left = during(step, (right, left))
            else:
                both = jnp.where(self.z == steps - 2, right, left)
                (right, both) = during(step, (self.ends(both), both))
                left = right
            rights[step], lefts[step] = right, left
            arrived = {(0, s): rights[s] for s in rights} | {(1, s): lefts[s] for s in lefts}
            while len(chunks) < steps and all(
                orders[z][len(chunks) - 1] in arrived for z in range(steps)
            ):
                order = [orders[z][len(chunks) - 1] for z in range(steps)]
                values = [arrived[key] for key in order]
                if step == steps - 1 and values[1] is lefts[steps - 2] and values[-2] is rights[steps - 2]:
                    values[1] = values[-2] = both
                chunks.append(self.by_place(values))
                chips.append(
                    self.by_place([z - key[1] * (1 - 2 * key[0]) for z, key in enumerate(order)])
                )
        return chunks, chips


class Whole:
    def __init__(self, wires, pieces, places, rows, size):
        self.layout = [(s, t, 0, wires.nz) for s in range(wires.ny) for t in range(2)]
        self.nz = wires.nz
        self.pieces, self.rows, self.size = pieces, rows, size
        self.places = places
        self.copies = 2 * sum(count for _, _, _, count in self.layout)
        self.shape = (wires.head * rows, wires.dp * size)

    def fill(self, places_ref, refs, scratch, sems):
        copies = []
        for piece, (s, t, first, count) in enumerate(self.layout):
            column = pl.multiple_of(places_ref[2 * self.nz + 2 * s + t], self.size)
            for core in range(2):
                for slot in range(count):
                    row = pl.multiple_of(places_ref[core * self.nz + first + slot], self.rows)
                    copies.append(
                        pltpu.make_async_copy(
                            refs[core * len(self.layout) + piece].at[slot],
                            scratch.at[pl.ds(row, self.rows), pl.ds(column, self.size)],
                            sems.at[len(copies)],
                        )
                    )
        for copy in copies:
            copy.start()
        return copies


def swapped(wires, pieces):
    return [*pieces, *[wires.over_core(piece) for piece in pieces]]


def side_by_side(blocks_ref):
    return jnp.concatenate([blocks_ref[i] for i in range(blocks_ref.shape[0])], axis=1)


def by_columns(whole, places_ref, copies, weight_s, blocks, total_ref):
    each = len(copies) // len(whole.layout)
    for piece, (s, t, _, _) in enumerate(whole.layout):
        for copy in copies[piece * each : (piece + 1) * each]:
            copy.wait()
        at = pl.ds(pl.multiple_of(places_ref[2 * whole.nz + 2 * s + t], whole.size), whole.size)
        total, low = 0.0, 0
        for block in blocks:
            total += jnp.dot(
                block, weight_s[low : low + block.shape[1], at], preferred_element_type=jnp.float32
            )
            low += block.shape[1]
        total_ref[:, at] = total


def mix_kernel(whole, places_ref, *refs):
    count = len(whole.pieces)
    attended_ref, tokens_ref, gain_ref, middle_ref, normed_ref, weight_s, sems = refs[count:]
    copies = whole.fill(places_ref, refs[:count], weight_s, sems)
    by_columns(whole, places_ref, copies, weight_s, [side_by_side(attended_ref)], middle_ref)
    middle = middle_ref[...] + wide(tokens_ref[...])
    middle_ref[...] = middle
    normed_ref[...] = (middle * inv_root_mean(middle) * gain_ref[...]).astype(jnp.bfloat16)


def with_whole(kernel, whole, args, outs, flops):
    in_vmem = pl.BlockSpec(memory_space=pltpu.VMEM)
    return pl.pallas_call(
        functools.partial(kernel, whole),
        grid_spec=pltpu.PrefetchScalarGridSpec(
            num_scalar_prefetch=1,
            grid=(),
            in_specs=[pl.BlockSpec(memory_space=pl.ANY)] * len(whole.pieces) + [in_vmem] * len(args),
            out_specs=[in_vmem] * len(outs),
            scratch_shapes=[
                pltpu.VMEM(whole.shape, jnp.bfloat16),
                pltpu.SemaphoreType.DMA((whole.copies,)),
            ],
        ),
        out_shape=[jax.ShapeDtypeStruct(shape, kind) for shape, kind in outs],
        compiler_params=pltpu.CompilerParams(vmem_limit_bytes=VMEM),
        cost_estimate=LITTLE,
    )(whole.places, *whole.pieces, *args)


def mix(attended, whole, tokens, gain):
    return with_whole(
        mix_kernel,
        whole,
        (attended, tokens, gain),
        ((tokens.shape, jnp.float32), (tokens.shape, jnp.bfloat16)),
        2 * tokens.shape[0] * whole.shape[0] * whole.shape[1],
    )


def unmix_kernel(whole, places_ref, *refs):
    count = len(whole.pieces)
    parts, (middle_ref, grad_ref, gain_ref) = refs[count : count + 4], refs[count + 4 : count + 7]
    dmiddle_ref, dmixed_ref, part_ref, out_ref, weight_s, sems = refs[count + 7 :]
    copies = whole.fill(places_ref, refs[:count], weight_s, sems)
    middle = middle_ref[...]
    inv_two = inv_root_mean(middle)
    dnormed = sum(wide(part[...]) for part in parts)
    scaled = middle * inv_two
    error = dnormed * gain_ref[...]
    dmiddle = wide(grad_ref[...]) + inv_two * (
        error - scaled * jnp.mean(error * scaled, axis=1, keepdims=True)
    )
    part_ref[...] = jnp.sum(dnormed * scaled, axis=0, keepdims=True)
    dmiddle_ref[...] = dmiddle
    dmixed = dmiddle.astype(jnp.bfloat16)
    dmixed_ref[...] = dmixed
    for copy in copies:
        copy.wait()
    width = out_ref.shape[2]
    for head in range(out_ref.shape[0]):
        out_ref[head] = lax.dot_general(
            dmixed, weight_s[head * width : (head + 1) * width, :], NT, preferred_element_type=jnp.float32
        ).astype(jnp.bfloat16)


def unmix(parts, middle, grad, gain, whole, heads):
    rows, depth = middle.shape
    return with_whole(
        unmix_kernel,
        whole,
        (*parts, middle, grad, gain),
        (
            (middle.shape, jnp.float32),
            (middle.shape, jnp.bfloat16),
            ((1, depth), jnp.float32),
            ((heads, rows, whole.shape[0] // heads), jnp.bfloat16),
        ),
        2 * rows * whole.shape[0] * whole.shape[1],
    )


def last_kernel(whole, places_ref, *refs):
    count = len(whole.pieces)
    proj_ref, tokens_ref, dmiddle_ref, gain_ref, grad_ref, weight_s, sems = refs[count:]
    copies = whole.fill(places_ref, refs[:count], weight_s, sems)
    blocks = [proj_ref[head] for head in range(proj_ref.shape[0])]
    by_columns(whole, places_ref, copies, weight_s, blocks, grad_ref)
    dnormed = grad_ref[...]
    tokens = wide(tokens_ref[...])
    inv_one = inv_root_mean(tokens)
    scaled = tokens * inv_one
    error = dnormed * gain_ref[...]
    grad_ref[...] = dmiddle_ref[...] + inv_one * (
        error - scaled * jnp.mean(error * scaled, axis=1, keepdims=True)
    )


def last(proj, whole, tokens, dmiddle, gain):
    return with_whole(
        last_kernel,
        whole,
        (proj, tokens, dmiddle, gain),
        ((tokens.shape, jnp.float32),),
        2 * tokens.shape[0] * whole.shape[0] * whole.shape[1],
    )[0]


class Units:
    def __init__(self, wires, pieces, matrices, rows, columns):
        self.matrices = matrices
        self.layout = [piece[1:] for piece in pieces]
        self.pieces = [piece[0] for piece in pieces]
        self.rows, self.columns = rows, columns
        self.places = jnp.stack([((wires.y - s) % wires.ny) * columns for s in range(wires.ny)]).astype(
            jnp.int32
        )
        self.shape = (matrices, wires.nzh * rows, wires.ny * columns)

    def fill(self, places_ref, refs, scratch, sems):
        copies = []
        for matrix in range(self.matrices):
            for ref, (first, count, zh, y) in zip(refs, self.layout):
                if not first <= matrix < first + count:
                    continue
                column = pl.multiple_of(places_ref[y], self.columns)
                copies.append(
                    pltpu.make_async_copy(
                        ref.at[matrix - first],
                        scratch.at[
                            matrix, pl.ds(zh * self.rows, self.rows), pl.ds(column, self.columns)
                        ],
                        sems.at[len(copies)],
                    )
                )
        for copy in copies:
            copy.start()
        return copies


def with_units(kernel, units, blocks, outs, scratch, flops, transcendentals):
    anywhere = pl.BlockSpec(memory_space=pl.ANY)
    copies = sum(count for _, count, _, _ in units.layout)
    return pl.pallas_call(
        functools.partial(kernel, units),
        grid_spec=pltpu.PrefetchScalarGridSpec(
            num_scalar_prefetch=1,
            grid=(),
            in_specs=[anywhere] * (len(units.pieces) + len(blocks)),
            out_specs=[anywhere] * len(outs),
            scratch_shapes=[
                pltpu.VMEM(units.shape, jnp.bfloat16),
                pltpu.SemaphoreType.DMA((copies,)),
            ]
            + scratch,
        ),
        out_shape=[jax.ShapeDtypeStruct(shape, kind) for shape, kind in outs],
        compiler_params=pltpu.CompilerParams(vmem_limit_bytes=VMEM),
        cost_estimate=LITTLE,
    )(units.places, *units.pieces, *blocks)


def started(copies):
    for copy in copies:
        copy.start()
    return copies


def awaited(copies):
    for copy in copies:
        copy.wait()


def gate_kernel(count, units, places_ref, *refs):
    pieces, refs = refs[: len(units.pieces)], refs[len(units.pieces) :]
    blocks, (unit_ref, normed_ref) = refs[: 2 * count], refs[2 * count : 2 * count + 2]
    weight_s, sems, normed_s, unit_s, in_sems, out_sems = refs[2 * count + 2 :]
    rows = blocks[0].shape[0]

    def arrive(chunk):
        started(
            [
                pltpu.make_async_copy(
                    blocks[2 * chunk + i], normed_s.at[chunk, pl.ds(i * rows, rows)], in_sems.at[chunk]
                )
                for i in range(2)
            ]
        )

    arrive(0)
    weights = units.fill(places_ref, pieces, weight_s, sems)
    for chunk in range(1, count):
        arrive(chunk)
    each = len(weights) // units.matrices

    def sent(chunk, which):
        source, target = ((normed_s, normed_ref), (unit_s, unit_ref))[which]
        return pltpu.make_async_copy(source.at[chunk], target.at[chunk], out_sems.at[which, chunk])

    def work(chunk, nothing):
        pltpu.make_async_copy(normed_ref.at[chunk], normed_s.at[chunk], in_sems.at[chunk]).wait()
        sent(chunk, 0).start()
        pl.when(chunk == 0)(lambda: awaited(weights[:each]))
        normed = normed_s[chunk]
        gate = lax.dot_general(normed, weight_s[0], NT, preferred_element_type=jnp.float32)
        pl.when(chunk == 0)(lambda: awaited(weights[each:]))
        up = lax.dot_general(normed, weight_s[1], NT, preferred_element_type=jnp.float32)
        sigmoid = jax.nn.sigmoid(gate)
        silu = gate * sigmoid
        unit_s[chunk, 0] = (silu * up).astype(jnp.bfloat16)
        unit_s[chunk, 1] = (up * sigmoid * (1.0 + gate * (1.0 - sigmoid))).astype(jnp.bfloat16)
        unit_s[chunk, 2] = silu.astype(jnp.bfloat16)
        sent(chunk, 1).start()
        return nothing

    lax.fori_loop(0, count, work, 0)
    for chunk in range(count):
        awaited([sent(chunk, 0), sent(chunk, 1)])


def gate_up(pairs, units):
    count = len(pairs)
    rows, depth = pairs[0][0].shape
    unit, full = (count, 3, 2 * rows, units.shape[1]), (count, 2 * rows, depth)
    return with_units(
        functools.partial(gate_kernel, count),
        units,
        [block for pair in pairs for block in pair],
        ((unit, jnp.bfloat16), (full, jnp.bfloat16)),
        [
            pltpu.VMEM(full, jnp.bfloat16),
            pltpu.VMEM(unit, jnp.bfloat16),
            pltpu.SemaphoreType.DMA((count,)),
            pltpu.SemaphoreType.DMA((2, count)),
        ],
        8 * count * rows * depth * units.shape[1],
        0,
    )


def down_kernel(places, units, places_ref, *refs):
    count = len(places)
    pieces, refs = refs[: len(units.pieces)], refs[len(units.pieces) :]
    blocks, refs = refs[: 3 * count], refs[3 * count :]
    unit_ref, grad_ref, refs = refs[0], refs[1], refs[2:]
    dnormed, branches = refs[: 2 * count], refs[2 * count : 4 * count]
    weight_s, sems, given_s, grad_s, unit_s, back_s, branch_s, in_sems, out_sems = refs[4 * count :]
    rows = blocks[0].shape[0]
    both = [pl.ds(0, rows), pl.ds(rows, rows)]

    def arrive(chunk):
        one, two, given = blocks[3 * chunk : 3 * chunk + 3]
        started(
            [
                pltpu.make_async_copy(one, grad_s.at[chunk, both[0]], in_sems.at[0, chunk]),
                pltpu.make_async_copy(two, grad_s.at[chunk, both[1]], in_sems.at[0, chunk]),
                pltpu.make_async_copy(given.at[places[chunk]], given_s.at[chunk], in_sems.at[1, chunk]),
            ]
        )

    arrive(0)
    weights = units.fill(places_ref, pieces, weight_s, sems)
    for chunk in range(1, count):
        arrive(chunk)
    each = len(weights) // units.matrices
    dot = functools.partial(jnp.dot, preferred_element_type=jnp.float32)

    def sent(chunk, which):
        source, target = ((grad_s, grad_ref), (unit_s, unit_ref))[which]
        return pltpu.make_async_copy(source.at[chunk], target.at[chunk], out_sems.at[which, chunk])

    def halves_sent(chunk, source, targets, place):
        return [
            pltpu.make_async_copy(
                source.at[chunk, both[i]], targets[2 * chunk + i], out_sems.at[place + i, chunk]
            )
            for i in range(2)
        ]

    def work(chunk, nothing):
        pltpu.make_async_copy(grad_ref.at[chunk], grad_s.at[chunk], in_sems.at[0, chunk]).wait()
        sent(chunk, 0).start()
        pl.when(chunk == 0)(lambda: awaited(weights[:each]))
        dhidden = lax.dot_general(grad_s[chunk], weight_s[0], NT, preferred_element_type=jnp.float32)
        pltpu.make_async_copy(given_s.at[chunk], given_s.at[chunk], in_sems.at[1, chunk]).wait()
        dgate = (dhidden * wide(given_s[chunk, 1])).astype(jnp.bfloat16)
        dup = (dhidden * wide(given_s[chunk, 2])).astype(jnp.bfloat16)
        unit_s[chunk, 0] = dgate
        unit_s[chunk, 1] = dup
        sent(chunk, 1).start()
        branch_s[chunk] = dot(given_s[chunk, 0], weight_s[0]).astype(jnp.bfloat16)
        for k in range(count):
            pl.when(chunk == k)(lambda k=k: started(halves_sent(k, branch_s, branches, 2)) and None)
        pl.when(chunk == 0)(lambda: awaited(weights[each:]))
        back_s[chunk] = (dot(dgate, weight_s[1]) + dot(dup, weight_s[2])).astype(jnp.bfloat16)
        for k in range(count):
            pl.when(chunk == k)(lambda k=k: started(halves_sent(k, back_s, dnormed, 4)) and None)
        return nothing

    lax.fori_loop(0, count, work, 0)
    for chunk in range(count):
        awaited([sent(chunk, 0), sent(chunk, 1)])
        awaited(halves_sent(chunk, branch_s, branches, 2))
        awaited(halves_sent(chunk, back_s, dnormed, 4))


def down(given, units):
    count = len(given)
    rows, depth = given[0][0].shape
    size = units.shape[1]
    full = (count, 2 * rows, depth)
    part = ((rows, depth), jnp.bfloat16)
    outs = with_units(
        functools.partial(down_kernel, [chunk[3] for chunk in given]),
        units,
        [block for chunk in given for block in chunk[:3]],
        (((count, 2, 2 * rows, size), jnp.bfloat16), (full, jnp.bfloat16)) + (part,) * (4 * count),
        [
            pltpu.VMEM((count, 3, 2 * rows, size), jnp.bfloat16),
            pltpu.VMEM(full, jnp.bfloat16),
            pltpu.VMEM((count, 2, 2 * rows, size), jnp.bfloat16),
            pltpu.VMEM(full, jnp.bfloat16),
            pltpu.VMEM(full, jnp.bfloat16),
            pltpu.SemaphoreType.DMA((2, count)),
            pltpu.SemaphoreType.DMA((6, count)),
        ],
        16 * count * rows * depth * size,
        0,
    )
    halves = lambda parts: [parts[2 * i : 2 * i + 2] for i in range(count)]
    return outs[:2], halves(outs[2 : 2 + 2 * count]), halves(outs[2 + 2 * count :])


def unit_grad_kernel(order, ny, nzh, places_ref, *refs):
    count = len(order)
    scratch = refs[-4:]
    arrays, outs = refs[: -4 - ny * nzh], refs[-4 - ny * nzh : -4]
    left_s, right_s, total_s, sems = scratch
    for i, (left, at, right, to) in enumerate(order):
        started(
            [
                pltpu.make_async_copy(arrays[left].at[at], left_s.at[i], sems.at[0, i]),
                pltpu.make_async_copy(arrays[right].at[to], right_s.at[i], sems.at[1, i]),
            ]
        )
    total_s[...] = jnp.zeros_like(total_s)

    def work(i, nothing):
        pltpu.make_async_copy(left_s.at[i], left_s.at[i], sems.at[0, i]).wait()
        pltpu.make_async_copy(right_s.at[i], right_s.at[i], sems.at[1, i]).wait()
        total_s[...] += lax.dot_general(left_s[i], right_s[i], TN, preferred_element_type=jnp.float32)
        return nothing

    lax.fori_loop(0, count, work, 0)
    units, columns = outs[0].shape
    for y in range(ny):
        for zh in range(nzh):
            outs[y * nzh + zh][...] = total_s[
                pl.ds(zh * units, units), pl.ds(pl.multiple_of(places_ref[y], columns), columns)
            ].astype(jnp.bfloat16)


def unit_grad(wires, lefts, rights):
    ny, nzh = wires.ny, wires.nzh
    arrays = []

    def index(array):
        for i, other in enumerate(arrays):
            if other is array:
                return i
        arrays.append(array)
        return len(arrays) - 1

    order = [(index(left), at, index(right), to) for (left, at), (right, to) in zip(lefts, rights)]
    tokens, units = lefts[0][0].shape[-2:]
    depth = rights[0][0].shape[-1]
    rows, columns = units // nzh, depth // ny
    places = jnp.stack([((wires.y + s) % ny) * columns for s in range(ny)]).astype(jnp.int32)
    in_vmem = pl.BlockSpec(memory_space=pltpu.VMEM)
    outs = pl.pallas_call(
        functools.partial(unit_grad_kernel, order, ny, nzh),
        grid_spec=pltpu.PrefetchScalarGridSpec(
            num_scalar_prefetch=1,
            grid=(),
            in_specs=[pl.BlockSpec(memory_space=pl.ANY)] * len(arrays),
            out_specs=[in_vmem] * (ny * nzh),
            scratch_shapes=[
                pltpu.VMEM((len(order), tokens, units), jnp.bfloat16),
                pltpu.VMEM((len(order), tokens, depth), jnp.bfloat16),
                pltpu.VMEM((units, depth), jnp.float32),
                pltpu.SemaphoreType.DMA((2, len(order))),
            ],
        ),
        out_shape=[jax.ShapeDtypeStruct((rows, columns), jnp.bfloat16)] * (ny * nzh),
        compiler_params=pltpu.CompilerParams(vmem_limit_bytes=VMEM),
        cost_estimate=LITTLE,
    )(places, *arrays)
    return [outs[zh::nzh] for zh in range(nzh)]


def out_grad_kernel(nz, ny, places_ref, mine_ref, other_ref, grad_ref, other_grad_ref, *refs):
    outs, (left_s, right_s) = refs[: 2 * ny], refs[2 * ny :]
    step = pl.program_id(0)
    tokens, width = grad_ref.shape[0], outs[0].shape[2]

    @pl.when(step == 0)
    def _():
        right_s[:tokens] = grad_ref[...]
        right_s[tokens:] = other_grad_ref[...]

    left_s[:tokens] = mine_ref[places_ref[step]]
    left_s[tokens:] = other_ref[places_ref[step] // 2]
    left = left_s[...]
    for i, out_ref in enumerate(outs):
        column = pl.multiple_of(places_ref[nz + i], width)
        out_ref[0] = lax.dot_general(
            left, right_s[:, pl.ds(column, width)], TN, preferred_element_type=jnp.float32
        ).astype(jnp.bfloat16)


def out_grad_parts(wires, mine, other, d_mixed, other_d_mixed):
    heads, tokens, rows = mine.shape
    depth = d_mixed.shape[1]
    nz, ny, width = wires.nz, wires.ny, depth // wires.dp
    places = jnp.stack(
        [z * 2 + wires.c for z in range(nz)]
        + [(((wires.y + s) % ny) * 2 + (wires.x ^ t)) * width for t in range(2) for s in range(ny)]
    ).astype(jnp.int32)
    full = lambda *shape: pl.BlockSpec(shape, lambda i, p: (0,) * len(shape))
    outs = pl.pallas_call(
        functools.partial(out_grad_kernel, nz, ny),
        grid_spec=pltpu.PrefetchScalarGridSpec(
            num_scalar_prefetch=1,
            grid=(nz,),
            in_specs=[
                full(heads, tokens, rows),
                full(nz, tokens, rows),
                full(tokens, depth),
                full(tokens, depth),
            ],
            out_specs=[pl.BlockSpec((1, rows, width), lambda i, p: (i, 0, 0))] * (2 * ny),
            scratch_shapes=[
                pltpu.VMEM((2 * tokens, rows), jnp.bfloat16),
                pltpu.VMEM((2 * tokens, depth), jnp.bfloat16),
            ],
        ),
        out_shape=[jax.ShapeDtypeStruct((nz, rows, width), jnp.bfloat16)] * (2 * ny),
        compiler_params=pltpu.CompilerParams(
            dimension_semantics=("arbitrary",), vmem_limit_bytes=VMEM
        ),
        cost_estimate=LITTLE,
    )(places, mine, other, d_mixed, other_d_mixed)
    return outs[:ny], outs[ny:]


def in_grad_kernel(normed_ref, grad_ref, weight_ref, gain_ref, out_ref, part_ref):
    blocks, rows, width = grad_ref.shape
    grad = grad_ref[...].reshape(blocks * rows, width)
    total = lax.dot_general(grad, normed_ref[...], TN, preferred_element_type=jnp.float32)
    out_ref[...] = total.astype(jnp.bfloat16)
    part_ref[...] = jnp.sum(total * wide(weight_ref[...]), axis=0, keepdims=True) / gain_ref[...]


def in_grad_parts(normed, grad, weight, gain):
    tokens, depth = normed.shape
    width = grad.shape[2]
    size = min(512, depth)
    block = lambda rows: pl.BlockSpec((rows, size), lambda i: (0, i))
    return pl.pallas_call(
        in_grad_kernel,
        grid=(depth // size,),
        in_specs=[
            block(tokens),
            pl.BlockSpec(grad.shape, lambda i: (0, 0, 0)),
            block(width),
            block(1),
        ],
        out_specs=[block(width), block(1)],
        out_shape=[
            jax.ShapeDtypeStruct((width, depth), jnp.bfloat16),
            jax.ShapeDtypeStruct((1, depth), jnp.float32),
        ],
        compiler_params=pltpu.CompilerParams(
            dimension_semantics=("arbitrary",), vmem_limit_bytes=VMEM
        ),
        cost_estimate=LITTLE,
    )(normed, grad, weight, gain)


def tie(*values):
    return lax.optimization_barrier(values)


def per_device(
    wires,
    tokens,
    keep_mask,
    seq_lengths,
    attn_gain,
    in_weight,
    out_weight,
    ffn_gain,
    gate_weight,
    up_weight,
    down_weight,
    out_grad,
):
    wires.place()
    heads_here = in_weight.shape[1] // (2 * FD + VD)
    rows, depth = tokens.shape
    group_rows = rows * wires.head
    out_rows = heads_here * VD
    size = depth // wires.dp
    tokens_wide = wide(tokens)
    own = low(tokens_wide * inv_root_mean(tokens_wide) * attn_gain)
    across_y = range(1, wires.ny)

    def on_y(pieces):
        return [[wires.over_y(piece, s) for s in across_y] for piece in pieces]

    def swap(values):
        return lax.all_to_all(values, "head", split_axis=0, concat_axis=0, tiled=True)

    turned = dict(split_axis=0, concat_axis=0, tiled=True)
    same_core = [[z * 2 + c for z in range(wires.nz)] for c in range(2)]

    def add(*values):
        return low(sum(wide(value) for value in values))

    packed_width = in_weight.shape[1]
    in_turned = in_weight.T
    in_part = wires.quarter(in_turned)
    keep_row = keep_mask.astype(jnp.float32)[None]
    ends = jnp.cumsum(seq_lengths[0])
    stacked = jnp.stack([gate_weight.T, up_weight.T, down_weight])
    unit_own = pick(stacked, wires.x, 2, 1)
    unit_other = pick(stacked, 1 - wires.x, 2, 1)
    share = out_rows * size // rows
    block = jnp.concatenate([own, wires.quarter(out_weight).reshape(rows, share)], axis=1)

    flying = {}

    def beside_line(step, values):
        if step == 1:
            by_x = wires.over_x(unit_other)
            values, flying["by_x"], flying["own"], flying["in_part"], flying["out_grad"], flying["swap"] = tie(
                values, by_x, unit_own, in_part, out_grad, wires.over_core(block)
            )
        elif step == 2:
            pair = in_order([flying["own"], flying["by_x"]], wires.x, 2)
            by_x = wires.over_x(flying["out_grad"])
            values, flying["grad_x"], flying["pair"], flying["out_grad"] = tie(
                values, by_x, pair, flying["out_grad"]
            )
        elif step == wires.nz - 1:
            by_y = [wires.over_y(flying["pair"][:2], s) for s in across_y]
            halves = [wires.over_zh_half(flying["pair"][:2], s, 0) for s in range(1, wires.nzh)]
            values, flying["by_y"], flying["pair"], flying["grad_x"], flying["halves"] = tie(
                values, by_y, flying["pair"], flying["grad_x"], halves
            )
        else:
            (values,) = tie(values)
        return values

    chunks, chips = wires.line(block, beside_line)
    others = [flying["swap"]] + [wires.over_core(chunk) for chunk in chunks[1:]]
    pieces = [piece for pair in zip(chunks, others) for piece in pair]
    places = jnp.stack(
        [(chip * 2 + (wires.c ^ r)) * rows for chip in chips for r in range(2)]
    ).astype(jnp.int32)
    pieces, unit_pair, out_grad, grad_x = tie(
        pieces, flying["pair"], flying["out_grad"], flying["grad_x"]
    )

    def shares(blocks):
        return jnp.stack([piece[:, depth:].reshape(out_rows, size) for piece in blocks])

    halves = [wires.over_zh_half(unit_pair[:2], s, 1) for s in range(1, wires.nzh)]
    out_line = shares(pieces[::2])
    out_x, out_y = wires.over_x(out_line), [wires.over_y(out_line, s) for s in across_y]
    projected, normed, attended_wide, inverses, attended = attend(
        pieces, places, in_turned, keep_row, ends, heads_here
    )
    attended, out_x, out_y, unit_pair = tie(attended, out_x, out_y, unit_pair)
    attended_here = swap(attended).reshape(wires.head, rows, out_rows)
    out_across = [wires.over_x(piece) for piece in out_y]
    by_zh_gu = [
        wires.from_halves(flying["halves"][s - 1], halves[s - 1], s) for s in range(1, wires.nzh)
    ]
    by_zh_guy = on_y(by_zh_gu)
    out_line_swap = shares(pieces[1::2])
    out_x_swap, out_y_swap = wires.over_core(out_x), [wires.over_core(piece) for piece in out_y]
    attended_here, out_across, out_x_swap, out_y_swap, unit_pair, by_zh_gu, out_line_swap = tie(
        attended_here, out_across, out_x_swap, out_y_swap, unit_pair, by_zh_gu, out_line_swap
    )
    out_across_swap = [wires.over_core(piece) for piece in out_across]

    def in_layout(line, by_x, by_y, across):
        pieces = [line, by_x]
        for piece in zip(by_y, across):
            pieces += piece
        return pieces

    out_pieces = in_layout(out_line, out_x, out_y, out_across)
    out_pieces += in_layout(out_line_swap, out_x_swap, out_y_swap, out_across_swap)
    out_whole = Whole(wires, out_pieces, wires.whole_places(chips, out_rows, size), out_rows, size)
    middle, normed_two = mix(attended_here, out_whole, tokens, ffn_gain[None])

    normed_two, unit_pair, grad_x, out_grad = tie(normed_two, unit_pair, grad_x, out_grad)
    two_x, two_z = wires.over_x(normed_two), wires.over_zl(normed_two)
    by_zh_d = [wires.over_zh(unit_pair[2:], s) for s in range(1, wires.nzh)]
    by_y_d = [wires.over_y(unit_pair[2:], s) for s in across_y]
    two_swap = wires.over_core(normed_two)
    two_x, two_z, by_zh_d, two_swap, by_y_d, unit_pair, out_grad, by_zh_guy = tie(
        two_x, two_z, by_zh_d, two_swap, by_y_d, unit_pair, out_grad, by_zh_guy
    )
    two_corner = wires.over_x(two_z)
    by_zh_dy = on_y(by_zh_d)
    grad_z = wires.over_zl(out_grad)
    two_swaps = [two_swap] + [wires.over_core(piece) for piece in (two_x, two_z)]
    two_corner, by_zh_dy, two_swaps, two_x, two_z, grad_z, attended_here = tie(
        two_corner, by_zh_dy, two_swaps, two_x, two_z, grad_z, attended_here
    )

    spot = unit_pair.shape[1], unit_pair.shape[2]
    gates = [(unit_pair[:2], 0, 2, 0, 0)] + [(flying["by_y"][s - 1], 0, 2, 0, s) for s in across_y]
    for zh in range(1, wires.nzh):
        gates.append((by_zh_gu[zh - 1], 0, 2, zh, 0))
        gates += [(by_zh_guy[zh - 1][s - 1], 0, 2, zh, s) for s in across_y]
    units = Units(wires, gates, 2, *spot)

    in_line = lax.all_to_all(
        jnp.concatenate([flying["in_part"]] * wires.nz, axis=0), "head", axis_index_groups=same_core, **turned
    ).reshape(wires.nz, packed_width, size)
    grad_corner = wires.over_x(grad_z)
    two_corner_swap = wires.over_core(two_corner)
    for_other = pick(attended_here.reshape(wires.nz, 2, rows, out_rows), 1 - wires.c, 2, 1)[:, 0]
    attended_other = wires.over_core(for_other)
    grad_swaps = [wires.over_core(grad) for grad in (out_grad, grad_x)]
    first = gate_up(list(zip([normed_two, two_x, two_z], two_swaps)), units)
    first, grad_corner, two_corner, two_corner_swap, grad_z, attended_other, grad_swaps = tie(
        first, grad_corner, two_corner, two_corner_swap, grad_z, attended_other, grad_swaps
    )
    grad_swaps += [wires.over_core(grad) for grad in (grad_z, grad_corner)]
    second = gate_up([(two_corner, two_corner_swap)], units)
    second, grad_swaps, in_line = tie(second, grad_swaps, in_line)
    grad_pairs = list(zip([out_grad, grad_x, grad_z, grad_corner], grad_swaps))
    downs = [(unit_pair[2:], 0, 1, 0, 0)] + [(by_y_d[s - 1], 0, 1, 0, s) for s in across_y]
    for zh in range(1, wires.nzh):
        downs.append((by_zh_d[zh - 1], 0, 1, zh, 0))
        downs += [(by_zh_dy[zh - 1][s - 1], 0, 1, zh, s) for s in across_y]
    units = Units(
        wires, downs + [(array, at + 1, count, zh, s) for array, at, count, zh, s in gates], 3, *spot
    )

    in_x, in_y = wires.over_x(in_line), [wires.over_y(in_line, s) for s in across_y]
    in_line_swap = wires.over_core(in_line)
    outs_co, (dnormed_c, dnormed_o), (branch_c, branch_o) = down(
        [(*grad_pairs[3], second[0], 0), (*grad_pairs[0], first[0], 0)], units
    )
    outs_co, in_x, in_y, dnormed_c, dnormed_o, branch_c, in_line_swap = tie(
        outs_co, in_x, in_y, dnormed_c, dnormed_o, branch_c, in_line_swap
    )
    swap_c, swap_o = wires.over_core(dnormed_c[1]), wires.over_core(dnormed_o[1])
    swap_b = wires.over_core(branch_c[1])
    swap_c, swap_o, swap_b, outs_co, in_x = tie(swap_c, swap_o, swap_b, outs_co, in_x)
    sum_c, sum_b = add(dnormed_c[0], swap_c), add(branch_c[0], swap_b)
    to_z, to_x = wires.over_x(sum_c), wires.over_zl(sum_b)
    in_across = [wires.over_y(in_x, s) for s in across_y]
    in_swaps = [wires.over_core(piece) for piece in (in_x, *in_y)]
    grad_x_pair, grad_z_pair, *_ = tie(grad_pairs[1], grad_pairs[2], sum_c, sum_b, outs_co)
    outs_xz, (dnormed_x, dnormed_z), (branch_x, branch_z) = down(
        [(*grad_x_pair, first[0], 1), (*grad_z_pair, first[0], 2)], units
    )
    outs_xz, dnormed_x, dnormed_z, branch_x, branch_z, to_z, to_x, in_across, in_swaps = tie(
        outs_xz, dnormed_x, dnormed_z, branch_x, branch_z, to_z, to_x, in_across, in_swaps
    )
    swap_x, swap_z = wires.over_core(dnormed_x[1]), wires.over_core(dnormed_z[1])
    sum_x = add(dnormed_x[0], swap_x)
    final_x = wires.over_x(sum_x)
    sum_z = add(dnormed_z[0], swap_z, to_z)
    final_z = wires.over_zl(sum_z)

    every = (outs_co, outs_xz, first, second)

    def grad_of(every, unit):
        (units_co, grad_co), (units_xz, grad_xz), (made, normed_oxz), (made_c, normed_c) = every
        if unit == 0:
            lefts = [(made_c, (0, 0)), (made, (0, 0)), (made, (1, 0)), (made, (2, 0))]
            rights = [(grad_co, 0), (grad_co, 1), (grad_xz, 0), (grad_xz, 1)]
        else:
            lefts = [(array, (i, unit - 1)) for array in (units_co, units_xz) for i in range(2)]
            rights = [(normed_c, 0), (normed_oxz, 0), (normed_oxz, 1), (normed_oxz, 2)]
        return unit_grad(wires, lefts, rights)

    def on_y_steps(blocks):
        return [wires.over_y(blocks[s], s) for s in across_y]

    def on_zh(totals):
        return [wires.over_zh(total, -s) for s, total in enumerate(totals, 1)]

    def totals_of(parts, sent):
        return [add(part[0], *more) for part, more in zip(parts, sent)]

    def grad_last(mine, sent):
        return wide(in_order([mine, sent], wires.x, 0))

    every, sum_x, sum_z, branch_x, branch_z = tie(every, sum_x, sum_z, branch_x, branch_z)
    swap_x, swap_z = wires.over_core(branch_x[1]), wires.over_core(branch_z[1])
    in_across_swap = [wires.over_core(piece) for piece in in_across]
    gate_parts = grad_of(every, 1)
    sum_x, sum_z = add(branch_x[0], swap_x, to_x), add(branch_z[0], swap_z)
    final_x, final_z, gate_parts, sum_x, sum_z, in_across_swap = tie(
        final_x, final_z, gate_parts, sum_x, sum_z, in_across_swap
    )
    gate_sent = [on_y_steps(part) for part in gate_parts[1:]]
    d_middle, d_mixed, ffn_gain_part, d_attended = unmix(
        (dnormed_o[0], swap_o, final_x, final_z), middle, out_grad, ffn_gain[None], out_whole, wires.head
    )
    every, d_attended, d_mixed, gate_parts, sum_x, sum_z = tie(
        every, d_attended, d_mixed, gate_parts, sum_x, sum_z
    )
    d_attended = swap(d_attended).reshape(group_rows, out_rows)
    final_x, final_z = wires.over_x(sum_x), wires.over_zl(sum_z)
    gate_back = on_zh(totals_of(gate_parts[1:], gate_sent))
    gate_sent = on_y_steps(gate_parts[0])
    other_d_mixed = wires.over_core(d_mixed)
    up_parts = grad_of(every, 2)
    up_sent = [on_y_steps(part) for part in up_parts[1:]]
    out_own, out_sent = out_grad_parts(wires, attended_here, attended_other, d_mixed, other_d_mixed)
    down_parts = grad_of(every, 0)
    d_attended, final_x, final_z, gate_back, gate_sent, up_parts, up_sent, out_own, out_sent, down_parts = tie(
        d_attended, final_x, final_z, gate_back, gate_sent, up_parts, up_sent, out_own, out_sent, down_parts
    )
    up_totals = totals_of(up_parts[1:], up_sent)
    up_back = on_zh(up_totals)
    up_sent = on_y_steps(up_parts[0])
    down_sent = [on_y_steps(part) for part in down_parts[1:]]
    out_first = [wires.over_x(out_sent[s]) for s in across_y]
    d_projected = attend_back(
        projected, keep_row, ends, attended_wide, inverses, d_attended, heads_here, rows
    )
    d_projected, up_back, up_sent, down_sent, out_first = tie(
        d_projected, up_back, up_sent, down_sent, out_first
    )
    d_here = swap(d_projected)
    down_totals = totals_of(down_parts[1:], down_sent)
    out_total = [add(out_own[s], out_first[s - 1]) for s in across_y]
    down_sent = on_y_steps(down_parts[0])
    out_last = wires.over_x(out_sent[0])
    swap_o = wires.over_core(branch_o[1])
    in_back, attn_gain_part = in_grad_parts(normed, d_projected, in_turned, attn_gain[None])
    firsts = [
        add(parts[0][0], *sent, *back)
        for parts, sent, back in ((gate_parts, gate_sent, gate_back), (up_parts, up_sent, up_back))
    ]
    d_here, in_back, attn_gain_part, down_sent, out_last, out_total, firsts, down_totals, swap_o = tie(
        d_here, in_back, attn_gain_part, down_sent, out_last, out_total, firsts, down_totals, swap_o
    )
    cut = packed_width // 2
    gains = jnp.concatenate([attn_gain_part, ffn_gain_part], axis=0)
    in_pieces = in_layout(in_line, in_x, in_y, in_across)
    in_pieces += in_layout(in_line_swap, in_swaps[0], in_swaps[1:], in_across_swap)
    in_whole = Whole(
        wires, in_pieces, wires.whole_places(range(wires.nz), packed_width, size), packed_width, size
    )
    down_back = on_zh(down_totals)
    out_y = [wires.over_y(total, s) for total, s in zip(out_total, across_y)]
    in_x, in_y = wires.over_x(in_back[:cut]), [wires.over_y(in_back[cut:], s) for s in across_y]
    others = wires.over_x(jnp.stack([pick(total, 1 - wires.x, 2, 1) for total in firsts]))
    in_grad = last(d_here, in_whole, tokens, d_middle, attn_gain[None])
    in_grad, out_y, in_x, in_y, others, down_sent, down_back, gains = tie(
        in_grad, out_y, in_x, in_y, others, down_sent, down_back, gains
    )
    out_total = add(out_own[0], out_last, *out_y)
    out_turns = lax.all_to_all(out_total, "head", axis_index_groups=same_core, **turned)
    in_halves = (wires.sum_y(add(in_back[:cut], in_x)), wires.sum_x(add(in_back[cut:], *in_y)))
    totals = [*firsts, add(down_parts[0][0], *down_sent, *down_back)]
    others = [others[0], others[1], wires.over_x(pick(totals[2], 1 - wires.x, 2, 1))]
    gains = gains + wires.over_core(gains)
    out_turns, gains, others, in_halves, totals = tie(out_turns, gains, others, in_halves, totals)
    out_part = add(*[out_turns[z] for z in range(wires.nz)])
    out_x = wires.over_x(out_part)
    out_by_y = [wires.over_y(out_part, s) for s in across_y]
    output = low(middle + wide(branch_o[0]) + wide(swap_o) + wide(final_x) + wide(final_z))
    gains = gains + wires.over_zl(gains)
    gains = gains + sum(wires.over_zh(gains, s) for s in range(1, wires.nzh))
    gate_grad, up_grad, down_grad = (
        grad_last(pick(total, wires.x, 2, 1), other) for total, other in zip(totals, others)
    )
    gate_grad, up_grad = gate_grad.T, up_grad.T
    out_x, out_by_y, gains, output, gate_grad, up_grad, down_grad = tie(
        out_x, out_by_y, gains, output, gate_grad, up_grad, down_grad
    )
    out_by_yx = [wires.over_y(out_x, s) for s in across_y]
    gains_x = wires.over_x(gains)
    gains = gains + gains_x + sum(
        wires.over_y(gains, s) + wires.over_dp(gains, s) for s in across_y
    )
    out_weight_grad = wide(
        in_order(
            [
                in_order([a, b], wires.x, 1)
                for a, b in zip([out_part, *out_by_y], [out_x, *out_by_yx])
            ],
            wires.y,
            1,
        )
    )
    in_weight_grad = wide(jnp.concatenate(in_halves, axis=0)).T
    return (
        output,
        in_grad,
        gains[0],
        in_weight_grad,
        out_weight_grad,
        gains[1],
        gate_grad,
        up_grad,
        down_grad,
    )


def solution(mesh):
    return jax.shard_map(
        functools.partial(per_device, Wires(mesh)),
        mesh=mesh,
        in_specs=(
            P(("dp", "head"), None),
            P("dp"),
            P("dp", None),
            P(),
            P(None, "head"),
            P("head", None),
            P(),
            P("dp", "head"),
            P("dp", "head"),
            P("head", "dp"),
            P(("dp", "head"), None),
        ),
        out_specs=(
            P(("dp", "head"), None),
            P(("dp", "head"), None),
            P(),
            P(None, "head"),
            P("head", None),
            P(),
            P("dp", "head"),
            P("dp", "head"),
            P("head", "dp"),
        ),
        check_vma=False,
    )
```

```python
import functools
import jax
import jax.numpy as jnp
from jax import lax
from jax.experimental import pallas as pl
from jax.experimental.pallas import tpu as pltpu
from jax.sharding import PartitionSpec as P

FD = 16
VD = 128
LANES = 128
VMEM = 60 * 1024 * 1024
LITTLE = pl.CostEstimate(flops=1, bytes_accessed=1, transcendentals=0)
epsilon = 1e-05
NT = (((1,), (1,)), ((), ()))
TN = (((0,), (0,)), ((), ()))


def column_of(row):
    count = row.shape[1]
    same = lax.broadcasted_iota(jnp.int32, (count, count), 0) == lax.broadcasted_iota(
        jnp.int32, (count, count), 1
    )
    return jnp.sum(jnp.where(same, row, 0.0), axis=1, keepdims=True)


def padded(block):
    rows, columns = block.shape
    return jnp.concatenate([block, jnp.zeros((rows, -columns % LANES), block.dtype)], axis=1)


def lanes_from(block, low, count):
    width = block.shape[1]
    moved = (block if low == 0 else pltpu.roll(block, width - low, 1))[:, :LANES]
    if count == LANES:
        return moved
    lane = lax.broadcasted_iota(jnp.int32, moved.shape, 1)
    return jnp.where(lane < count, moved, 0.0)


def head_parts(block, head):
    low = head * (2 * FD + VD)
    query = lanes_from(block, low, FD) * 0.25
    return query, lanes_from(block, low + FD, FD), lanes_from(block, low + 2 * FD, VD)


def segment_start(ends_ref, positions):
    start = jnp.zeros_like(positions)
    for slot in range(ends_ref.shape[0]):
        end = ends_ref[slot]
        start = jnp.where(positions >= end, jnp.maximum(start, end), start)
    return start


def attend_kernel(heads, rows, pieces, ends_ref, at_ref, *refs):
    sources = refs[:pieces]
    weight_ref, keep_ref, projected_ref, normed_ref, y_ref, inv_ref, att_ref = refs[pieces : pieces + 7]
    normed_s, key_s, value_s, sems = refs[pieces + 7 :]
    step = pl.program_id(0)
    own = pl.ds(pl.multiple_of(step * rows, rows), rows)

    @pl.when(step == 0)
    def _():
        size = sources[0].shape[0]
        copies = [
            pltpu.make_async_copy(
                sources[i].at[:, pl.ds(0, normed_s.shape[1])], normed_s.at[pl.ds(pl.multiple_of(at_ref[i], size), size), :], sems.at[i]
            )
            for i in range(pieces)
        ]
        for copy in copies:
            copy.start()
        for copy in copies:
            copy.wait()

    keep = column_of(keep_ref[:, own])
    normed = normed_s[own, :]
    normed_ref[...] = normed
    projected = lax.dot_general(
        normed, weight_ref[...], NT, preferred_element_type=jnp.float32
    ).astype(jnp.bfloat16)
    projected_ref[...] = projected
    block = padded(projected.astype(jnp.float32))
    lane = lax.broadcasted_iota(jnp.int32, (rows, LANES), 1)
    ones = jnp.where(lane < 2, keep, 0.0).astype(jnp.bfloat16)
    queries = []
    for head in range(heads):
        query, key, value = head_parts(block, head)
        queries.append(query.astype(jnp.bfloat16))
        key_s[head, own, :] = key.astype(jnp.bfloat16)
        value_s[head, own, :VD] = (value * keep).astype(jnp.bfloat16)
        value_s[head, own, VD:] = ones
    row = step * rows + lax.broadcasted_iota(jnp.int32, (rows, 1), 0)
    start = segment_start(ends_ref, row)
    column = lax.broadcasted_iota(jnp.int32, (rows, rows), 1)

    def tile(block, totals, diagonal):
        at = pl.ds(pl.multiple_of(block * rows, rows), rows)
        allowed = column >= start - block * rows
        if diagonal:
            allowed &= column <= lax.broadcasted_iota(jnp.int32, (rows, rows), 0)
        added = []
        for head in range(heads):
            inner = lax.dot_general(
                queries[head], key_s[head, at, :], NT, preferred_element_type=jnp.float32
            )
            weights = jnp.where(allowed, (inner * 0.5 + 1.0) * inner + 1.0, 0.0).astype(jnp.bfloat16)
            added.append(
                totals[head]
                + jnp.dot(weights, value_s[head, at, :], preferred_element_type=jnp.float32)
            )
        return tuple(added)

    totals = tuple(jnp.zeros((rows, 2 * VD), jnp.float32) for _ in range(heads))
    totals = lax.fori_loop(0, step, lambda block, held: tile(block, held, False), totals)
    totals = tile(step, totals, True)
    inverses = jnp.zeros((rows, LANES), jnp.float32)
    for head in range(heads):
        inverse = 1.0 / (totals[head][:, VD : VD + 1] + 1.0 - keep)
        y = totals[head][:, :VD] * (keep * inverse)
        y_ref[:, head * VD : (head + 1) * VD] = y
        att_ref[:, head * VD : (head + 1) * VD] = y.astype(jnp.bfloat16)
        inverses = jnp.where(lane == head, inverse, inverses)
    inv_ref[...] = inverses


def attend(pieces, places, weight, keep, ends, heads):
    size, depth = pieces[0].shape[0], weight.shape[1]
    total = size * len(pieces)
    rows = min(512, total)
    width = weight.shape[0]
    pairs = total * (total + rows) // 2 * heads
    blocked = lambda columns: pl.BlockSpec((rows, columns), lambda i, e, a: (i, 0))
    return pl.pallas_call(
        functools.partial(attend_kernel, heads, rows, len(pieces)),
        grid_spec=pltpu.PrefetchScalarGridSpec(
            num_scalar_prefetch=2,
            grid=(total // rows,),
            in_specs=[pl.BlockSpec(memory_space=pl.ANY)] * len(pieces)
            + [
                pl.BlockSpec((width, depth), lambda i, e, a: (0, 0)),
                pl.BlockSpec((1, total), lambda i, e, a: (0, 0)),
            ],
            out_specs=[
                blocked(width), blocked(depth), blocked(heads * VD), blocked(LANES), blocked(heads * VD)
            ],
            scratch_shapes=[
                pltpu.VMEM((total, depth), jnp.bfloat16),
                pltpu.VMEM((heads, total, LANES), jnp.bfloat16),
                pltpu.VMEM((heads, total, 2 * VD), jnp.bfloat16),
                pltpu.SemaphoreType.DMA((len(pieces),)),
            ],
        ),
        out_shape=[
            jax.ShapeDtypeStruct((total, width), jnp.bfloat16),
            jax.ShapeDtypeStruct((total, depth), jnp.bfloat16),
            jax.ShapeDtypeStruct((total, heads * VD), jnp.float32),
            jax.ShapeDtypeStruct((total, LANES), jnp.float32),
            jax.ShapeDtypeStruct((total, heads * VD), jnp.bfloat16),
        ],
        compiler_params=pltpu.CompilerParams(
            dimension_semantics=("arbitrary",), vmem_limit_bytes=VMEM
        ),
        cost_estimate=LITTLE,
    )(ends, places, *pieces, weight, keep)


def attend_back_kernel(
    heads, rows, ends_ref, projected_ref, keep_ref, y_ref, inv_ref, grad_ref, out_ref,
    key_s, query_s, value_s, error_s, dquery_s,
):
    step = pl.program_id(0)
    blocks = pl.num_programs(0)
    lane = lax.broadcasted_iota(jnp.int32, (rows, LANES), 1)

    @pl.when(step == 0)
    def _():
        dquery_s[...] = jnp.zeros_like(dquery_s)

        def fill(block, nothing):
            at = pl.ds(pl.multiple_of(block * rows, rows), rows)
            keep = column_of(keep_ref[:, at])
            wide_block = padded(projected_ref[at, :].astype(jnp.float32))
            ones = jnp.where(lane < 2, keep, 0.0).astype(jnp.bfloat16)
            inverses = inv_ref[at, :]
            for head in range(heads):
                columns = slice(head * VD, (head + 1) * VD)
                query, key, value = head_parts(wide_block, head)
                key_s[head, at, :] = key.astype(jnp.bfloat16)
                query_s[head, at, :] = query.astype(jnp.bfloat16)
                value_s[head, at, :VD] = (value * keep).astype(jnp.bfloat16)
                value_s[head, at, VD:] = ones
                inverse = inverses[:, head : head + 1]
                grad = grad_ref[at, columns].astype(jnp.float32)
                error_s[head, at, :VD] = (grad * (keep * inverse)).astype(jnp.bfloat16)
                offset = -jnp.sum(grad * y_ref[at, columns], axis=1, keepdims=True) * inverse
                high = offset.astype(jnp.bfloat16).astype(jnp.float32)
                error_s[head, at, VD:] = jnp.where(
                    lane == 0, high, jnp.where(lane == 1, offset - high, 0.0)
                ).astype(jnp.bfloat16)
            return nothing

        lax.fori_loop(0, blocks, fill, 0)

    own = pl.ds(pl.multiple_of(step * rows, rows), rows)
    row = lax.broadcasted_iota(jnp.int32, (rows, rows), 0)

    def tile(block, totals, diagonal):
        at = pl.ds(pl.multiple_of(block * rows, rows), rows)
        column = block * rows + lax.broadcasted_iota(jnp.int32, (1, rows), 1)
        allowed = row >= segment_start(ends_ref, column) - step * rows
        if diagonal:
            allowed &= row <= lax.broadcasted_iota(jnp.int32, (rows, rows), 1)
        dkeys, dvalues = totals
        added, turned = [], []
        for head in range(heads):
            query = query_s[head, at, :]
            error = error_s[head, at, :]
            keys = key_s[head, own, :]
            inner = lax.dot_general(keys, query, NT, preferred_element_type=jnp.float32)
            dweight = lax.dot_general(value_s[head, own, :], error, NT, preferred_element_type=jnp.float32)
            slope = inner + 1.0
            weights = jnp.where(allowed, (slope * slope + 1.0) * 0.5, 0.0).astype(jnp.bfloat16)
            dinner = jnp.where(allowed, slope * dweight, 0.0).astype(jnp.bfloat16)
            added.append(
                dvalues[head] + jnp.dot(weights, error[:, :VD], preferred_element_type=jnp.float32)
            )
            turned.append(dkeys[head] + jnp.dot(dinner, query, preferred_element_type=jnp.float32))
            dquery_s[head, at, :] += lax.dot_general(dinner, keys, TN, preferred_element_type=jnp.float32)
        return tuple(turned), tuple(added)

    totals = (
        tuple(jnp.zeros((rows, LANES), jnp.float32) for _ in range(heads)),
        tuple(jnp.zeros((rows, VD), jnp.float32) for _ in range(heads)),
    )
    totals = tile(step, totals, True)
    dkeys, dvalues = lax.fori_loop(step + 1, blocks, lambda block, held: tile(block, held, False), totals)
    keep = column_of(keep_ref[:, own])
    width = out_ref.shape[2]
    total = jnp.zeros((rows, width + -width % LANES), jnp.float32)
    blank = jnp.zeros((rows, total.shape[1] - LANES), jnp.float32)

    def put(block, low):
        spread = jnp.concatenate([block, blank], axis=1)
        return spread if low == 0 else pltpu.roll(spread, low, 1)

    for head in range(heads):
        low = head * (2 * FD + VD)
        total += put(dquery_s[head, own, :] * 0.25, low)
        total += put(dkeys[head], low + FD)
        total += put(dvalues[head] * keep, low + 2 * FD)
    out_ref[...] = total[:, :width].astype(jnp.bfloat16).reshape(out_ref.shape)


def attend_back(projected, keep, ends, y, inverses, grad, heads, each):
    total = projected.shape[0]
    rows = min(512, total)
    width = projected.shape[1]
    whole = lambda columns: pl.BlockSpec((total, columns), lambda i, e: (0, 0))
    return pl.pallas_call(
        functools.partial(attend_back_kernel, heads, rows),
        grid_spec=pltpu.PrefetchScalarGridSpec(
            num_scalar_prefetch=1,
            grid=(total // rows,),
            in_specs=[whole(width), pl.BlockSpec((1, total), lambda i, e: (0, 0)), whole(heads * VD), whole(LANES), whole(heads * VD)],
            out_specs=pl.BlockSpec((rows // each, each, width), lambda i, e: (i, 0, 0)),
            scratch_shapes=[
                pltpu.VMEM((heads, total, LANES), jnp.bfloat16),
                pltpu.VMEM((heads, total, LANES), jnp.bfloat16),
                pltpu.VMEM((heads, total, 2 * VD), jnp.bfloat16),
                pltpu.VMEM((heads, total, 2 * VD), jnp.bfloat16),
                pltpu.VMEM((heads, total, LANES), jnp.float32),
            ],
        ),
        out_shape=jax.ShapeDtypeStruct((total // each, each, width), jnp.bfloat16),
        compiler_params=pltpu.CompilerParams(
            dimension_semantics=("arbitrary",), vmem_limit_bytes=VMEM
        ),
        cost_estimate=LITTLE,
    )(ends, projected, keep, y, inverses, grad)


def inv_root_mean(values):
    return lax.rsqrt(jnp.mean(values * values, axis=1, keepdims=True) + epsilon)


def wide(values):
    return values.astype(jnp.float32)


def low(values):
    return values.astype(jnp.bfloat16)


def pick(values, index, count, axis):
    size = values.shape[axis] // count
    if count == 2:
        first = lax.slice_in_dim(values, 0, size, axis=axis)
        second = lax.slice_in_dim(values, size, 2 * size, axis=axis)
        return jnp.where(index == 0, first, second)
    return lax.dynamic_slice_in_dim(values, index * size, size, axis)


def in_order(pieces, index, axis):
    count = len(pieces)
    if count == 1:
        return pieces[0]
    if count == 2:
        first = jnp.where(index == 0, pieces[0], pieces[1])
        second = jnp.where(index == 0, pieces[1], pieces[0])
        return jnp.concatenate([first, second], axis=axis)
    stacked = jnp.stack(pieces)
    placed = [
        lax.dynamic_index_in_dim(stacked, (index - place) % count, 0, keepdims=False)
        for place in range(count)
    ]
    return jnp.concatenate(placed, axis=axis)


class Wires:
    def __init__(self, mesh):
        self.dp, self.head = mesh.shape["dp"], mesh.shape["head"]
        self.ny, self.nz, self.nzh = self.dp // 2, self.head // 2, self.head // 4

    def place(self):
        p, h = lax.axis_index("dp"), lax.axis_index("head")
        self.p, self.h = p, h
        self.y, self.x, self.z, self.c = p // 2, p % 2, h // 2, h % 2
        self.zh = self.z // 2

    def over_x(self, values):
        return lax.ppermute(values, "dp", [(i, i ^ 1) for i in range(self.dp)])

    def over_y(self, values, shift):
        return lax.ppermute(
            values, "dp", [(i, ((i // 2 + shift) % self.ny) * 2 + i % 2) for i in range(self.dp)]
        )

    def over_dp(self, values, shift):
        return lax.ppermute(
            values, "dp", [(i, ((i // 2 + shift) % self.ny) * 2 + (i + 1) % 2) for i in range(self.dp)]
        )

    def over_core(self, values):
        return lax.ppermute(values, "head", [(i, i ^ 1) for i in range(self.head)])

    def over_zl(self, values):
        return lax.ppermute(values, "head", [(i, i ^ 2) for i in range(self.head)])

    def over_zh(self, values, shift):
        return lax.ppermute(
            values, "head", [(i, ((i // 4 + shift) % self.nzh) * 4 + i % 4) for i in range(self.head)]
        )

    def over_zh_half(self, values, shift, parity):
        pairs = [
            (i, ((i // 4 + shift) % self.nzh) * 4 + i % 4)
            for i in range(self.head)
            if (i // 4 + i // 2 % 2) % 2 == parity
        ]
        return lax.ppermute(values, "head", pairs)

    def from_halves(self, first, second, shift):
        even = (self.zh - shift + self.z) % 2 == 0
        return jnp.where(even, first, second)

    def over_z(self, values, shift):
        return lax.ppermute(
            values, "head", [(i, ((i // 2 + shift) % self.nz) * 2 + i % 2) for i in range(self.head)]
        )

    def right(self, values, first, last):
        return lax.ppermute(
            values, "head", [(i, i + 2) for i in range(self.head) if first <= i // 2 <= last]
        )

    def left(self, values, first, last):
        return lax.ppermute(
            values, "head", [(i, i - 2) for i in range(self.head) if first <= i // 2 <= last]
        )

    def spread(self, line):
        return self.over_x(line), [self.over_y(line, s) for s in range(1, self.ny)]

    def ends(self, values):
        pairs = [(i, i + 2 if i // 2 == self.nz - 2 else i - 2) for i in range(self.head)]
        return lax.ppermute(
            values, "head", [pair for pair in pairs if pair[0] // 2 in (1, self.nz - 2)]
        )

    def arrivals(self):
        orders = []
        for z in range(self.nz):
            order = []
            for step in range(1, self.nz):
                order += [(0, step)] if z >= step else []
                order += [(1, step)] if z + step < self.nz else []
            orders.append(order)
        return orders

    def by_place(self, values):
        chosen, taken = values[0], [values[0]]
        for value in values[1:]:
            if any(value is other for other in taken):
                continue
            taken.append(value)
            here = [z for z in range(self.nz) if values[z] is value]
            chosen = jnp.where(sum((self.z == z).astype(jnp.int32) for z in here) > 0, value, chosen)
        return chosen

    def sum_y(self, values):
        total = wide(values)
        for s in range(1, self.ny):
            total = total + wide(self.over_y(values, s))
        return low(total)

    def sum_x(self, values):
        return low(wide(values) + wide(self.over_x(values)))

    def sum_all(self, values):
        values = values + self.over_core(values)
        values = values + self.over_zl(values)
        values = values + sum(self.over_zh(values, s) for s in range(1, self.nzh))
        values = values + self.over_x(values)
        return values + sum(self.over_y(values, s) for s in range(1, self.ny))

    def quarter(self, shard):
        size = shard.shape[1] // self.dp
        return lax.dynamic_slice_in_dim(shard, self.p * size, size, 1)

    def line_of(self, part):
        return [part] + [self.over_z(part, s) for s in range(1, self.nz)]

    def whole_places(self, chips, rows, size):
        at_rows = [(chip * 2 + (self.c ^ r)) * rows for r in range(2) for chip in chips]
        at_columns = [
            (((self.y - s) % self.ny) * 2 + (self.x ^ t)) * size
            for s in range(self.ny)
            for t in range(2)
        ]
        return jnp.stack(at_rows + at_columns).astype(jnp.int32)

    def line(self, block, during):
        steps = self.nz
        right = left = block
        rights, lefts = {}, {}
        orders = self.arrivals()
        chunks, chips = [block], [self.z]
        for step in range(1, steps):
            if step < steps - 1:
                right = self.right(right, step - 1, steps - 2)
                left = self.left(left, 1, steps - step)
                right, left = during(step, (right, left))
            else:
                both = jnp.where(self.z == steps - 2, right, left)
                (right, both) = during(step, (self.ends(both), both))
                left = right
            rights[step], lefts[step] = right, left
            arrived = {(0, s): rights[s] for s in rights} | {(1, s): lefts[s] for s in lefts}
            while len(chunks) < steps and all(
                orders[z][len(chunks) - 1] in arrived for z in range(steps)
            ):
                order = [orders[z][len(chunks) - 1] for z in range(steps)]
                values = [arrived[key] for key in order]
                if step == steps - 1 and values[1] is lefts[steps - 2] and values[-2] is rights[steps - 2]:
                    values[1] = values[-2] = both
                chunks.append(self.by_place(values))
                chips.append(
                    self.by_place([z - key[1] * (1 - 2 * key[0]) for z, key in enumerate(order)])
                )
        return chunks, chips


class Whole:
    def __init__(self, wires, pieces, places, rows, size):
        self.layout = [(s, t, 0, wires.nz) for s in range(wires.ny) for t in range(2)]
        self.nz = wires.nz
        self.pieces, self.rows, self.size = pieces, rows, size
        self.places = places
        self.copies = 2 * sum(count for _, _, _, count in self.layout)
        self.shape = (wires.head * rows, wires.dp * size)

    def fill(self, places_ref, refs, scratch, sems):
        copies = []
        for piece, (s, t, first, count) in enumerate(self.layout):
            column = pl.multiple_of(places_ref[2 * self.nz + 2 * s + t], self.size)
            for core in range(2):
                for slot in range(count):
                    row = pl.multiple_of(places_ref[core * self.nz + first + slot], self.rows)
                    copies.append(
                        pltpu.make_async_copy(
                            refs[core * len(self.layout) + piece].at[slot],
                            scratch.at[pl.ds(row, self.rows), pl.ds(column, self.size)],
                            sems.at[len(copies)],
                        )
                    )
        for copy in copies:
            copy.start()
        return copies


def swapped(wires, pieces):
    return [*pieces, *[wires.over_core(piece) for piece in pieces]]


def side_by_side(blocks_ref):
    return jnp.concatenate([blocks_ref[i] for i in range(blocks_ref.shape[0])], axis=1)


def by_columns(whole, places_ref, copies, weight_s, blocks, total_ref):
    each = len(copies) // len(whole.layout)
    for piece, (s, t, _, _) in enumerate(whole.layout):
        for copy in copies[piece * each : (piece + 1) * each]:
            copy.wait()
        at = pl.ds(pl.multiple_of(places_ref[2 * whole.nz + 2 * s + t], whole.size), whole.size)
        total, low = 0.0, 0
        for block in blocks:
            total += jnp.dot(
                block, weight_s[low : low + block.shape[1], at], preferred_element_type=jnp.float32
            )
            low += block.shape[1]
        total_ref[:, at] = total


def mix_kernel(whole, places_ref, *refs):
    count = len(whole.pieces)
    attended_ref, tokens_ref, gain_ref, middle_ref, normed_ref, weight_s, sems = refs[count:]
    copies = whole.fill(places_ref, refs[:count], weight_s, sems)
    by_columns(whole, places_ref, copies, weight_s, [side_by_side(attended_ref)], middle_ref)
    middle = middle_ref[...] + wide(tokens_ref[...])
    middle_ref[...] = middle
    normed_ref[...] = (middle * inv_root_mean(middle) * gain_ref[...]).astype(jnp.bfloat16)


def with_whole(kernel, whole, args, outs, flops):
    in_vmem = pl.BlockSpec(memory_space=pltpu.VMEM)
    return pl.pallas_call(
        functools.partial(kernel, whole),
        grid_spec=pltpu.PrefetchScalarGridSpec(
            num_scalar_prefetch=1,
            grid=(),
            in_specs=[pl.BlockSpec(memory_space=pl.ANY)] * len(whole.pieces) + [in_vmem] * len(args),
            out_specs=[in_vmem] * len(outs),
            scratch_shapes=[
                pltpu.VMEM(whole.shape, jnp.bfloat16),
                pltpu.SemaphoreType.DMA((whole.copies,)),
            ],
        ),
        out_shape=[jax.ShapeDtypeStruct(shape, kind) for shape, kind in outs],
        compiler_params=pltpu.CompilerParams(vmem_limit_bytes=VMEM),
        cost_estimate=LITTLE,
    )(whole.places, *whole.pieces, *args)


def mix(attended, whole, tokens, gain):
    return with_whole(
        mix_kernel,
        whole,
        (attended, tokens, gain),
        ((tokens.shape, jnp.float32), (tokens.shape, jnp.bfloat16)),
        2 * tokens.shape[0] * whole.shape[0] * whole.shape[1],
    )


def unmix_kernel(whole, places_ref, *refs):
    count = len(whole.pieces)
    parts, (middle_ref, grad_ref, gain_ref) = refs[count : count + 4], refs[count + 4 : count + 7]
    dmiddle_ref, dmixed_ref, part_ref, out_ref, weight_s, sems = refs[count + 7 :]
    copies = whole.fill(places_ref, refs[:count], weight_s, sems)
    middle = middle_ref[...]
    inv_two = inv_root_mean(middle)
    dnormed = sum(wide(part[...]) for part in parts)
    scaled = middle * inv_two
    error = dnormed * gain_ref[...]
    dmiddle = wide(grad_ref[...]) + inv_two * (
        error - scaled * jnp.mean(error * scaled, axis=1, keepdims=True)
    )
    part_ref[...] = jnp.sum(dnormed * scaled, axis=0, keepdims=True)
    dmiddle_ref[...] = dmiddle
    dmixed = dmiddle.astype(jnp.bfloat16)
    dmixed_ref[...] = dmixed
    for copy in copies:
        copy.wait()
    width = out_ref.shape[2]
    for head in range(out_ref.shape[0]):
        out_ref[head] = lax.dot_general(
            dmixed, weight_s[head * width : (head + 1) * width, :], NT, preferred_element_type=jnp.float32
        ).astype(jnp.bfloat16)


def unmix(parts, middle, grad, gain, whole, heads):
    rows, depth = middle.shape
    return with_whole(
        unmix_kernel,
        whole,
        (*parts, middle, grad, gain),
        (
            (middle.shape, jnp.float32),
            (middle.shape, jnp.bfloat16),
            ((1, depth), jnp.float32),
            ((heads, rows, whole.shape[0] // heads), jnp.bfloat16),
        ),
        2 * rows * whole.shape[0] * whole.shape[1],
    )


def last_kernel(whole, places_ref, *refs):
    count = len(whole.pieces)
    proj_ref, tokens_ref, dmiddle_ref, gain_ref, grad_ref, weight_s, sems = refs[count:]
    copies = whole.fill(places_ref, refs[:count], weight_s, sems)
    blocks = [proj_ref[head] for head in range(proj_ref.shape[0])]
    by_columns(whole, places_ref, copies, weight_s, blocks, grad_ref)
    dnormed = grad_ref[...]
    tokens = wide(tokens_ref[...])
    inv_one = inv_root_mean(tokens)
    scaled = tokens * inv_one
    error = dnormed * gain_ref[...]
    grad_ref[...] = dmiddle_ref[...] + inv_one * (
        error - scaled * jnp.mean(error * scaled, axis=1, keepdims=True)
    )


def last(proj, whole, tokens, dmiddle, gain):
    return with_whole(
        last_kernel,
        whole,
        (proj, tokens, dmiddle, gain),
        ((tokens.shape, jnp.float32),),
        2 * tokens.shape[0] * whole.shape[0] * whole.shape[1],
    )[0]


class Units:
    def __init__(self, wires, pieces, matrices, rows, columns):
        self.matrices = matrices
        self.layout = [piece[1:] for piece in pieces]
        self.pieces = [piece[0] for piece in pieces]
        self.rows, self.columns = rows, columns
        self.places = jnp.stack([((wires.y - s) % wires.ny) * columns for s in range(wires.ny)]).astype(
            jnp.int32
        )
        self.shape = (matrices, wires.nzh * rows, wires.ny * columns)

    def fill(self, places_ref, refs, scratch, sems):
        copies = []
        for matrix in range(self.matrices):
            for ref, (first, count, zh, y) in zip(refs, self.layout):
                if not first <= matrix < first + count:
                    continue
                column = pl.multiple_of(places_ref[y], self.columns)
                copies.append(
                    pltpu.make_async_copy(
                        ref.at[matrix - first],
                        scratch.at[
                            matrix, pl.ds(zh * self.rows, self.rows), pl.ds(column, self.columns)
                        ],
                        sems.at[len(copies)],
                    )
                )
        for copy in copies:
            copy.start()
        return copies


def with_units(kernel, units, blocks, outs, scratch, flops, transcendentals):
    anywhere = pl.BlockSpec(memory_space=pl.ANY)
    copies = sum(count for _, count, _, _ in units.layout)
    return pl.pallas_call(
        functools.partial(kernel, units),
        grid_spec=pltpu.PrefetchScalarGridSpec(
            num_scalar_prefetch=1,
            grid=(),
            in_specs=[anywhere] * (len(units.pieces) + len(blocks)),
            out_specs=[anywhere] * len(outs),
            scratch_shapes=[
                pltpu.VMEM(units.shape, jnp.bfloat16),
                pltpu.SemaphoreType.DMA((copies,)),
            ]
            + scratch,
        ),
        out_shape=[jax.ShapeDtypeStruct(shape, kind) for shape, kind in outs],
        compiler_params=pltpu.CompilerParams(vmem_limit_bytes=VMEM),
        cost_estimate=LITTLE,
    )(units.places, *units.pieces, *blocks)


def started(copies):
    for copy in copies:
        copy.start()
    return copies


def awaited(copies):
    for copy in copies:
        copy.wait()


def gate_kernel(count, units, places_ref, *refs):
    pieces, refs = refs[: len(units.pieces)], refs[len(units.pieces) :]
    blocks, (unit_ref, normed_ref) = refs[: 2 * count], refs[2 * count : 2 * count + 2]
    weight_s, sems, normed_s, unit_s, in_sems, out_sems = refs[2 * count + 2 :]
    rows = blocks[0].shape[0]

    def arrive(chunk):
        started(
            [
                pltpu.make_async_copy(
                    blocks[2 * chunk + i], normed_s.at[chunk, pl.ds(i * rows, rows)], in_sems.at[chunk]
                )
                for i in range(2)
            ]
        )

    arrive(0)
    weights = units.fill(places_ref, pieces, weight_s, sems)
    for chunk in range(1, count):
        arrive(chunk)
    each = len(weights) // units.matrices

    def sent(chunk, which):
        source, target = ((normed_s, normed_ref), (unit_s, unit_ref))[which]
        return pltpu.make_async_copy(source.at[chunk], target.at[chunk], out_sems.at[which, chunk])

    def work(chunk, nothing):
        pltpu.make_async_copy(normed_ref.at[chunk], normed_s.at[chunk], in_sems.at[chunk]).wait()
        sent(chunk, 0).start()
        pl.when(chunk == 0)(lambda: awaited(weights[:each]))
        normed = normed_s[chunk]
        gate = lax.dot_general(normed, weight_s[0], NT, preferred_element_type=jnp.float32)
        pl.when(chunk == 0)(lambda: awaited(weights[each:]))
        up = lax.dot_general(normed, weight_s[1], NT, preferred_element_type=jnp.float32)
        sigmoid = jax.nn.sigmoid(gate)
        silu = gate * sigmoid
        unit_s[chunk, 0] = (silu * up).astype(jnp.bfloat16)
        unit_s[chunk, 1] = (up * sigmoid * (1.0 + gate * (1.0 - sigmoid))).astype(jnp.bfloat16)
        unit_s[chunk, 2] = silu.astype(jnp.bfloat16)
        sent(chunk, 1).start()
        return nothing

    lax.fori_loop(0, count, work, 0)
    for chunk in range(count):
        awaited([sent(chunk, 0), sent(chunk, 1)])


def gate_up(pairs, units):
    count = len(pairs)
    rows, depth = pairs[0][0].shape
    unit, full = (count, 3, 2 * rows, units.shape[1]), (count, 2 * rows, depth)
    return with_units(
        functools.partial(gate_kernel, count),
        units,
        [block for pair in pairs for block in pair],
        ((unit, jnp.bfloat16), (full, jnp.bfloat16)),
        [
            pltpu.VMEM(full, jnp.bfloat16),
            pltpu.VMEM(unit, jnp.bfloat16),
            pltpu.SemaphoreType.DMA((count,)),
            pltpu.SemaphoreType.DMA((2, count)),
        ],
        8 * count * rows * depth * units.shape[1],
        0,
    )


def down_kernel(places, units, places_ref, *refs):
    count = len(places)
    pieces, refs = refs[: len(units.pieces)], refs[len(units.pieces) :]
    blocks, refs = refs[: 3 * count], refs[3 * count :]
    unit_ref, grad_ref, refs = refs[0], refs[1], refs[2:]
    dnormed, branches = refs[: 2 * count], refs[2 * count : 4 * count]
    weight_s, sems, given_s, grad_s, unit_s, back_s, branch_s, in_sems, out_sems = refs[4 * count :]
    rows = blocks[0].shape[0]
    both = [pl.ds(0, rows), pl.ds(rows, rows)]

    def arrive(chunk):
        one, two, given = blocks[3 * chunk : 3 * chunk + 3]
        started(
            [
                pltpu.make_async_copy(one, grad_s.at[chunk, both[0]], in_sems.at[0, chunk]),
                pltpu.make_async_copy(two, grad_s.at[chunk, both[1]], in_sems.at[0, chunk]),
                pltpu.make_async_copy(given.at[places[chunk]], given_s.at[chunk], in_sems.at[1, chunk]),
            ]
        )

    arrive(0)
    weights = units.fill(places_ref, pieces, weight_s, sems)
    for chunk in range(1, count):
        arrive(chunk)
    each = len(weights) // units.matrices
    dot = functools.partial(jnp.dot, preferred_element_type=jnp.float32)

    def sent(chunk, which):
        source, target = ((grad_s, grad_ref), (unit_s, unit_ref))[which]
        return pltpu.make_async_copy(source.at[chunk], target.at[chunk], out_sems.at[which, chunk])

    def halves_sent(chunk, source, targets, place):
        return [
            pltpu.make_async_copy(
                source.at[chunk, both[i]], targets[2 * chunk + i], out_sems.at[place + i, chunk]
            )
            for i in range(2)
        ]

    def work(chunk, nothing):
        pltpu.make_async_copy(grad_ref.at[chunk], grad_s.at[chunk], in_sems.at[0, chunk]).wait()
        sent(chunk, 0).start()
        pl.when(chunk == 0)(lambda: awaited(weights[:each]))
        dhidden = lax.dot_general(grad_s[chunk], weight_s[0], NT, preferred_element_type=jnp.float32)
        pltpu.make_async_copy(given_s.at[chunk], given_s.at[chunk], in_sems.at[1, chunk]).wait()
        dgate = (dhidden * wide(given_s[chunk, 1])).astype(jnp.bfloat16)
        dup = (dhidden * wide(given_s[chunk, 2])).astype(jnp.bfloat16)
        unit_s[chunk, 0] = dgate
        unit_s[chunk, 1] = dup
        sent(chunk, 1).start()
        branch_s[chunk] = dot(given_s[chunk, 0], weight_s[0]).astype(jnp.bfloat16)
        for k in range(count):
            pl.when(chunk == k)(lambda k=k: started(halves_sent(k, branch_s, branches, 2)) and None)
        pl.when(chunk == 0)(lambda: awaited(weights[each:]))
        back_s[chunk] = (dot(dgate, weight_s[1]) + dot(dup, weight_s[2])).astype(jnp.bfloat16)
        for k in range(count):
            pl.when(chunk == k)(lambda k=k: started(halves_sent(k, back_s, dnormed, 4)) and None)
        return nothing

    lax.fori_loop(0, count, work, 0)
    for chunk in range(count):
        awaited([sent(chunk, 0), sent(chunk, 1)])
        awaited(halves_sent(chunk, branch_s, branches, 2))
        awaited(halves_sent(chunk, back_s, dnormed, 4))


def down(given, units):
    count = len(given)
    rows, depth = given[0][0].shape
    size = units.shape[1]
    full = (count, 2 * rows, depth)
    part = ((rows, depth), jnp.bfloat16)
    outs = with_units(
        functools.partial(down_kernel, [chunk[3] for chunk in given]),
        units,
        [block for chunk in given for block in chunk[:3]],
        (((count, 2, 2 * rows, size), jnp.bfloat16), (full, jnp.bfloat16)) + (part,) * (4 * count),
        [
            pltpu.VMEM((count, 3, 2 * rows, size), jnp.bfloat16),
            pltpu.VMEM(full, jnp.bfloat16),
            pltpu.VMEM((count, 2, 2 * rows, size), jnp.bfloat16),
            pltpu.VMEM(full, jnp.bfloat16),
            pltpu.VMEM(full, jnp.bfloat16),
            pltpu.SemaphoreType.DMA((2, count)),
            pltpu.SemaphoreType.DMA((6, count)),
        ],
        16 * count * rows * depth * size,
        0,
    )
    halves = lambda parts: [parts[2 * i : 2 * i + 2] for i in range(count)]
    return outs[:2], halves(outs[2 : 2 + 2 * count]), halves(outs[2 + 2 * count :])


def unit_grad_kernel(order, ny, nzh, places_ref, *refs):
    count = len(order)
    scratch = refs[-4:]
    arrays, outs = refs[: -4 - ny * nzh], refs[-4 - ny * nzh : -4]
    left_s, right_s, total_s, sems = scratch
    for i, (left, at, right, to) in enumerate(order):
        started(
            [
                pltpu.make_async_copy(arrays[left].at[at], left_s.at[i], sems.at[0, i]),
                pltpu.make_async_copy(arrays[right].at[to], right_s.at[i], sems.at[1, i]),
            ]
        )
    total_s[...] = jnp.zeros_like(total_s)

    def work(i, nothing):
        pltpu.make_async_copy(left_s.at[i], left_s.at[i], sems.at[0, i]).wait()
        pltpu.make_async_copy(right_s.at[i], right_s.at[i], sems.at[1, i]).wait()
        total_s[...] += lax.dot_general(left_s[i], right_s[i], TN, preferred_element_type=jnp.float32)
        return nothing

    lax.fori_loop(0, count, work, 0)
    units, columns = outs[0].shape
    for y in range(ny):
        for zh in range(nzh):
            outs[y * nzh + zh][...] = total_s[
                pl.ds(zh * units, units), pl.ds(pl.multiple_of(places_ref[y], columns), columns)
            ].astype(jnp.bfloat16)


def unit_grad(wires, lefts, rights):
    ny, nzh = wires.ny, wires.nzh
    arrays = []

    def index(array):
        for i, other in enumerate(arrays):
            if other is array:
                return i
        arrays.append(array)
        return len(arrays) - 1

    order = [(index(left), at, index(right), to) for (left, at), (right, to) in zip(lefts, rights)]
    tokens, units = lefts[0][0].shape[-2:]
    depth = rights[0][0].shape[-1]
    rows, columns = units // nzh, depth // ny
    places = jnp.stack([((wires.y + s) % ny) * columns for s in range(ny)]).astype(jnp.int32)
    in_vmem = pl.BlockSpec(memory_space=pltpu.VMEM)
    outs = pl.pallas_call(
        functools.partial(unit_grad_kernel, order, ny, nzh),
        grid_spec=pltpu.PrefetchScalarGridSpec(
            num_scalar_prefetch=1,
            grid=(),
            in_specs=[pl.BlockSpec(memory_space=pl.ANY)] * len(arrays),
            out_specs=[in_vmem] * (ny * nzh),
            scratch_shapes=[
                pltpu.VMEM((len(order), tokens, units), jnp.bfloat16),
                pltpu.VMEM((len(order), tokens, depth), jnp.bfloat16),
                pltpu.VMEM((units, depth), jnp.float32),
                pltpu.SemaphoreType.DMA((2, len(order))),
            ],
        ),
        out_shape=[jax.ShapeDtypeStruct((rows, columns), jnp.bfloat16)] * (ny * nzh),
        compiler_params=pltpu.CompilerParams(vmem_limit_bytes=VMEM),
        cost_estimate=LITTLE,
    )(places, *arrays)
    return [outs[zh::nzh] for zh in range(nzh)]


def out_grad_kernel(nz, ny, places_ref, mine_ref, other_ref, grad_ref, other_grad_ref, *refs):
    outs, (left_s, right_s) = refs[: 2 * ny], refs[2 * ny :]
    step = pl.program_id(0)
    tokens, width = grad_ref.shape[0], outs[0].shape[2]

    @pl.when(step == 0)
    def _():
        right_s[:tokens] = grad_ref[...]
        right_s[tokens:] = other_grad_ref[...]

    left_s[:tokens] = mine_ref[places_ref[step]]
    left_s[tokens:] = other_ref[places_ref[step] // 2]
    left = left_s[...]
    for i, out_ref in enumerate(outs):
        column = pl.multiple_of(places_ref[nz + i], width)
        out_ref[0] = lax.dot_general(
            left, right_s[:, pl.ds(column, width)], TN, preferred_element_type=jnp.float32
        ).astype(jnp.bfloat16)


def out_grad_parts(wires, mine, other, d_mixed, other_d_mixed):
    heads, tokens, rows = mine.shape
    depth = d_mixed.shape[1]
    nz, ny, width = wires.nz, wires.ny, depth // wires.dp
    places = jnp.stack(
        [z * 2 + wires.c for z in range(nz)]
        + [(((wires.y + s) % ny) * 2 + (wires.x ^ t)) * width for t in range(2) for s in range(ny)]
    ).astype(jnp.int32)
    full = lambda *shape: pl.BlockSpec(shape, lambda i, p: (0,) * len(shape))
    outs = pl.pallas_call(
        functools.partial(out_grad_kernel, nz, ny),
        grid_spec=pltpu.PrefetchScalarGridSpec(
            num_scalar_prefetch=1,
            grid=(nz,),
            in_specs=[
                full(heads, tokens, rows),
                full(nz, tokens, rows),
                full(tokens, depth),
                full(tokens, depth),
            ],
            out_specs=[pl.BlockSpec((1, rows, width), lambda i, p: (i, 0, 0))] * (2 * ny),
            scratch_shapes=[
                pltpu.VMEM((2 * tokens, rows), jnp.bfloat16),
                pltpu.VMEM((2 * tokens, depth), jnp.bfloat16),
            ],
        ),
        out_shape=[jax.ShapeDtypeStruct((nz, rows, width), jnp.bfloat16)] * (2 * ny),
        compiler_params=pltpu.CompilerParams(
            dimension_semantics=("arbitrary",), vmem_limit_bytes=VMEM
        ),
        cost_estimate=LITTLE,
    )(places, mine, other, d_mixed, other_d_mixed)
    return outs[:ny], outs[ny:]


def in_grad_kernel(normed_ref, grad_ref, weight_ref, gain_ref, out_ref, part_ref):
    blocks, rows, width = grad_ref.shape
    grad = grad_ref[...].reshape(blocks * rows, width)
    total = lax.dot_general(grad, normed_ref[...], TN, preferred_element_type=jnp.float32)
    out_ref[...] = total.astype(jnp.bfloat16)
    part_ref[...] = jnp.sum(total * wide(weight_ref[...]), axis=0, keepdims=True) / gain_ref[...]


def in_grad_parts(normed, grad, weight, gain):
    tokens, depth = normed.shape
    width = grad.shape[2]
    size = min(512, depth)
    block = lambda rows: pl.BlockSpec((rows, size), lambda i: (0, i))
    return pl.pallas_call(
        in_grad_kernel,
        grid=(depth // size,),
        in_specs=[
            block(tokens),
            pl.BlockSpec(grad.shape, lambda i: (0, 0, 0)),
            block(width),
            block(1),
        ],
        out_specs=[block(width), block(1)],
        out_shape=[
            jax.ShapeDtypeStruct((width, depth), jnp.bfloat16),
            jax.ShapeDtypeStruct((1, depth), jnp.float32),
        ],
        compiler_params=pltpu.CompilerParams(
            dimension_semantics=("arbitrary",), vmem_limit_bytes=VMEM
        ),
        cost_estimate=LITTLE,
    )(normed, grad, weight, gain)


def tie(*values):
    return lax.optimization_barrier(values)


def per_device(
    wires,
    tokens,
    keep_mask,
    seq_lengths,
    attn_gain,
    in_weight,
    out_weight,
    ffn_gain,
    gate_weight,
    up_weight,
    down_weight,
    out_grad,
):
    wires.place()
    heads_here = in_weight.shape[1] // (2 * FD + VD)
    rows, depth = tokens.shape
    group_rows = rows * wires.head
    out_rows = heads_here * VD
    size = depth // wires.dp
    tokens_wide = wide(tokens)
    own = low(tokens_wide * inv_root_mean(tokens_wide) * attn_gain)
    across_y = range(1, wires.ny)

    def on_y(pieces):
        return [[wires.over_y(piece, s) for s in across_y] for piece in pieces]

    def swap(values):
        return lax.all_to_all(values, "head", split_axis=0, concat_axis=0, tiled=True)

    turned = dict(split_axis=0, concat_axis=0, tiled=True)
    same_core = [[z * 2 + c for z in range(wires.nz)] for c in range(2)]

    def add(*values):
        return low(sum(wide(value) for value in values))

    packed_width = in_weight.shape[1]
    in_turned = in_weight.T
    in_part = wires.quarter(in_turned)
    keep_row = keep_mask.astype(jnp.float32)[None]
    ends = jnp.cumsum(seq_lengths[0])
    stacked = jnp.stack([gate_weight.T, up_weight.T, down_weight])
    unit_own = pick(stacked, wires.x, 2, 1)
    unit_other = pick(stacked, 1 - wires.x, 2, 1)
    share = out_rows * size // rows
    block = jnp.concatenate([own, wires.quarter(out_weight).reshape(rows, share)], axis=1)

    flying = {}

    def beside_line(step, values):
        if step == 1:
            by_x = wires.over_x(unit_other)
            values, flying["by_x"], flying["own"], flying["in_part"], flying["out_grad"], flying["swap"] = tie(
                values, by_x, unit_own, in_part, out_grad, wires.over_core(block)
            )
        elif step == 2:
            pair = in_order([flying["own"], flying["by_x"]], wires.x, 2)
            by_x = wires.over_x(flying["out_grad"])
            values, flying["grad_x"], flying["pair"], flying["out_grad"] = tie(
                values, by_x, pair, flying["out_grad"]
            )
        elif step == wires.nz - 1:
            by_y = [wires.over_y(flying["pair"][:2], s) for s in across_y]
            halves = [wires.over_zh_half(flying["pair"][:2], s, 0) for s in range(1, wires.nzh)]
            values, flying["by_y"], flying["pair"], flying["grad_x"], flying["halves"] = tie(
                values, by_y, flying["pair"], flying["grad_x"], halves
            )
        else:
            (values,) = tie(values)
        return values

    chunks, chips = wires.line(block, beside_line)
    others = [flying["swap"]] + [wires.over_core(chunk) for chunk in chunks[1:]]
    pieces = [piece for pair in zip(chunks, others) for piece in pair]
    places = jnp.stack(
        [(chip * 2 + (wires.c ^ r)) * rows for chip in chips for r in range(2)]
    ).astype(jnp.int32)
    pieces, unit_pair, out_grad, grad_x = tie(
        pieces, flying["pair"], flying["out_grad"], flying["grad_x"]
    )

    def shares(blocks):
        return jnp.stack([piece[:, depth:].reshape(out_rows, size) for piece in blocks])

    halves = [wires.over_zh_half(unit_pair[:2], s, 1) for s in range(1, wires.nzh)]
    out_line = shares(pieces[::2])
    out_x, out_y = wires.over_x(out_line), [wires.over_y(out_line, s) for s in across_y]
    projected, normed, attended_wide, inverses, attended = attend(
        pieces, places, in_turned, keep_row, ends, heads_here
    )
    attended, out_x, out_y, unit_pair = tie(attended, out_x, out_y, unit_pair)
    attended_here = swap(attended).reshape(wires.head, rows, out_rows)
    out_across = [wires.over_x(piece) for piece in out_y]
    by_zh_gu = [
        wires.from_halves(flying["halves"][s - 1], halves[s - 1], s) for s in range(1, wires.nzh)
    ]
    by_zh_guy = on_y(by_zh_gu)
    out_line_swap = shares(pieces[1::2])
    out_x_swap, out_y_swap = wires.over_core(out_x), [wires.over_core(piece) for piece in out_y]
    attended_here, out_across, out_x_swap, out_y_swap, unit_pair, by_zh_gu, out_line_swap = tie(
        attended_here, out_across, out_x_swap, out_y_swap, unit_pair, by_zh_gu, out_line_swap
    )
    out_across_swap = [wires.over_core(piece) for piece in out_across]

    def in_layout(line, by_x, by_y, across):
        pieces = [line, by_x]
        for piece in zip(by_y, across):
            pieces += piece
        return pieces

    out_pieces = in_layout(out_line, out_x, out_y, out_across)
    out_pieces += in_layout(out_line_swap, out_x_swap, out_y_swap, out_across_swap)
    out_whole = Whole(wires, out_pieces, wires.whole_places(chips, out_rows, size), out_rows, size)
    middle, normed_two = mix(attended_here, out_whole, tokens, ffn_gain[None])

    normed_two, unit_pair, grad_x, out_grad = tie(normed_two, unit_pair, grad_x, out_grad)
    two_x, two_z = wires.over_x(normed_two), wires.over_zl(normed_two)
    by_zh_d = [wires.over_zh(unit_pair[2:], s) for s in range(1, wires.nzh)]
    by_y_d = [wires.over_y(unit_pair[2:], s) for s in across_y]
    two_swap = wires.over_core(normed_two)
    two_x, two_z, by_zh_d, two_swap, by_y_d, unit_pair, out_grad, by_zh_guy = tie(
        two_x, two_z, by_zh_d, two_swap, by_y_d, unit_pair, out_grad, by_zh_guy
    )
    two_corner = wires.over_x(two_z)
    by_zh_dy = on_y(by_zh_d)
    grad_z = wires.over_zl(out_grad)
    two_swaps = [two_swap] + [wires.over_core(piece) for piece in (two_x, two_z)]
    two_corner, by_zh_dy, two_swaps, two_x, two_z, grad_z, attended_here = tie(
        two_corner, by_zh_dy, two_swaps, two_x, two_z, grad_z, attended_here
    )

    spot = unit_pair.shape[1], unit_pair.shape[2]
    gates = [(unit_pair[:2], 0, 2, 0, 0)] + [(flying["by_y"][s - 1], 0, 2, 0, s) for s in across_y]
    for zh in range(1, wires.nzh):
        gates.append((by_zh_gu[zh - 1], 0, 2, zh, 0))
        gates += [(by_zh_guy[zh - 1][s - 1], 0, 2, zh, s) for s in across_y]
    units = Units(wires, gates, 2, *spot)

    in_line = lax.all_to_all(
        jnp.concatenate([flying["in_part"]] * wires.nz, axis=0), "head", axis_index_groups=same_core, **turned
    ).reshape(wires.nz, packed_width, size)
    grad_corner = wires.over_x(grad_z)
    two_corner_swap = wires.over_core(two_corner)
    for_other = pick(attended_here.reshape(wires.nz, 2, rows, out_rows), 1 - wires.c, 2, 1)[:, 0]
    attended_other = wires.over_core(for_other)
    grad_swaps = [wires.over_core(grad) for grad in (out_grad, grad_x)]
    first = gate_up(list(zip([normed_two, two_x, two_z], two_swaps)), units)
    first, grad_corner, two_corner, two_corner_swap, grad_z, attended_other, grad_swaps = tie(
        first, grad_corner, two_corner, two_corner_swap, grad_z, attended_other, grad_swaps
    )
    grad_swaps += [wires.over_core(grad) for grad in (grad_z, grad_corner)]
    second = gate_up([(two_corner, two_corner_swap)], units)
    second, grad_swaps, in_line = tie(second, grad_swaps, in_line)
    grad_pairs = list(zip([out_grad, grad_x, grad_z, grad_corner], grad_swaps))
    downs = [(unit_pair[2:], 0, 1, 0, 0)] + [(by_y_d[s - 1], 0, 1, 0, s) for s in across_y]
    for zh in range(1, wires.nzh):
        downs.append((by_zh_d[zh - 1], 0, 1, zh, 0))
        downs += [(by_zh_dy[zh - 1][s - 1], 0, 1, zh, s) for s in across_y]
    units = Units(
        wires, downs + [(array, at + 1, count, zh, s) for array, at, count, zh, s in gates], 3, *spot
    )

    in_x, in_y = wires.over_x(in_line), [wires.over_y(in_line, s) for s in across_y]
    in_line_swap = wires.over_core(in_line)
    outs_co, (dnormed_c, dnormed_o), (branch_c, branch_o) = down(
        [(*grad_pairs[3], second[0], 0), (*grad_pairs[0], first[0], 0)], units
    )
    outs_co, in_x, in_y, dnormed_c, dnormed_o, branch_c, in_line_swap = tie(
        outs_co, in_x, in_y, dnormed_c, dnormed_o, branch_c, in_line_swap
    )
    swap_c, swap_o = wires.over_core(dnormed_c[1]), wires.over_core(dnormed_o[1])
    swap_b = wires.over_core(branch_c[1])
    swap_c, swap_o, swap_b, outs_co, in_x = tie(swap_c, swap_o, swap_b, outs_co, in_x)
    sum_c, sum_b = add(dnormed_c[0], swap_c), add(branch_c[0], swap_b)
    to_z, to_x = wires.over_x(sum_c), wires.over_zl(sum_b)
    in_across = [wires.over_y(in_x, s) for s in across_y]
    in_swaps = [wires.over_core(piece) for piece in (in_x, *in_y)]
    grad_x_pair, grad_z_pair, *_ = tie(grad_pairs[1], grad_pairs[2], sum_c, sum_b, outs_co)
    outs_xz, (dnormed_x, dnormed_z), (branch_x, branch_z) = down(
        [(*grad_x_pair, first[0], 1), (*grad_z_pair, first[0], 2)], units
    )
    outs_xz, dnormed_x, dnormed_z, branch_x, branch_z, to_z, to_x, in_across, in_swaps = tie(
        outs_xz, dnormed_x, dnormed_z, branch_x, branch_z, to_z, to_x, in_across, in_swaps
    )
    swap_x, swap_z = wires.over_core(dnormed_x[1]), wires.over_core(dnormed_z[1])
    sum_x = add(dnormed_x[0], swap_x)
    final_x = wires.over_x(sum_x)
    sum_z = add(dnormed_z[0], swap_z, to_z)
    final_z = wires.over_zl(sum_z)

    every = (outs_co, outs_xz, first, second)

    def grad_of(every, unit):
        (units_co, grad_co), (units_xz, grad_xz), (made, normed_oxz), (made_c, normed_c) = every
        if unit == 0:
            lefts = [(made_c, (0, 0)), (made, (0, 0)), (made, (1, 0)), (made, (2, 0))]
            rights = [(grad_co, 0), (grad_co, 1), (grad_xz, 0), (grad_xz, 1)]
        else:
            lefts = [(array, (i, unit - 1)) for array in (units_co, units_xz) for i in range(2)]
            rights = [(normed_c, 0), (normed_oxz, 0), (normed_oxz, 1), (normed_oxz, 2)]
        return unit_grad(wires, lefts, rights)

    def on_y_steps(blocks):
        return [wires.over_y(blocks[s], s) for s in across_y]

    def on_zh(totals):
        return [wires.over_zh(total, -s) for s, total in enumerate(totals, 1)]

    def totals_of(parts, sent):
        return [add(part[0], *more) for part, more in zip(parts, sent)]

    def grad_last(mine, sent):
        return wide(in_order([mine, sent], wires.x, 0))

    every, sum_x, sum_z, branch_x, branch_z = tie(every, sum_x, sum_z, branch_x, branch_z)
    swap_x, swap_z = wires.over_core(branch_x[1]), wires.over_core(branch_z[1])
    in_across_swap = [wires.over_core(piece) for piece in in_across]
    gate_parts = grad_of(every, 1)
    sum_x, sum_z = add(branch_x[0], swap_x, to_x), add(branch_z[0], swap_z)
    final_x, final_z, gate_parts, sum_x, sum_z, in_across_swap = tie(
        final_x, final_z, gate_parts, sum_x, sum_z, in_across_swap
    )
    gate_sent = [on_y_steps(part) for part in gate_parts[1:]]
    d_middle, d_mixed, ffn_gain_part, d_attended = unmix(
        (dnormed_o[0], swap_o, final_x, final_z), middle, out_grad, ffn_gain[None], out_whole, wires.head
    )
    every, d_attended, d_mixed, gate_parts, sum_x, sum_z = tie(
        every, d_attended, d_mixed, gate_parts, sum_x, sum_z
    )
    d_attended = swap(d_attended).reshape(group_rows, out_rows)
    final_x, final_z = wires.over_x(sum_x), wires.over_zl(sum_z)
    gate_back = on_zh(totals_of(gate_parts[1:], gate_sent))
    gate_sent = on_y_steps(gate_parts[0])
    other_d_mixed = wires.over_core(d_mixed)
    up_parts = grad_of(every, 2)
    up_sent = [on_y_steps(part) for part in up_parts[1:]]
    out_own, out_sent = out_grad_parts(wires, attended_here, attended_other, d_mixed, other_d_mixed)
    down_parts = grad_of(every, 0)
    d_attended, final_x, final_z, gate_back, gate_sent, up_parts, up_sent, out_own, out_sent, down_parts = tie(
        d_attended, final_x, final_z, gate_back, gate_sent, up_parts, up_sent, out_own, out_sent, down_parts
    )
    up_totals = totals_of(up_parts[1:], up_sent)
    up_back = on_zh(up_totals)
    up_sent = on_y_steps(up_parts[0])
    down_sent = [on_y_steps(part) for part in down_parts[1:]]
    out_first = [wires.over_x(out_sent[s]) for s in across_y]
    d_projected = attend_back(
        projected, keep_row, ends, attended_wide, inverses, d_attended, heads_here, rows
    )
    d_projected, up_back, up_sent, down_sent, out_first = tie(
        d_projected, up_back, up_sent, down_sent, out_first
    )
    d_here = swap(d_projected)
    down_totals = totals_of(down_parts[1:], down_sent)
    out_total = [add(out_own[s], out_first[s - 1]) for s in across_y]
    down_sent = on_y_steps(down_parts[0])
    out_last = wires.over_x(out_sent[0])
    out_y = [wires.over_y(total, s) for total, s in zip(out_total, across_y)]
    swap_o = wires.over_core(branch_o[1])
    in_back, attn_gain_part = in_grad_parts(normed, d_projected, in_turned, attn_gain[None])
    firsts = [
        add(parts[0][0], *sent, *back)
        for parts, sent, back in ((gate_parts, gate_sent, gate_back), (up_parts, up_sent, up_back))
    ]
    d_here, in_back, attn_gain_part, down_sent, out_last, out_total, firsts, down_totals, swap_o = tie(
        d_here, in_back, attn_gain_part, down_sent, out_last, out_total, firsts, down_totals, swap_o
    )
    cut = packed_width // 2
    gains = jnp.concatenate([attn_gain_part, ffn_gain_part], axis=0)
    in_pieces = in_layout(in_line, in_x, in_y, in_across)
    in_pieces += in_layout(in_line_swap, in_swaps[0], in_swaps[1:], in_across_swap)
    in_whole = Whole(
        wires, in_pieces, wires.whole_places(range(wires.nz), packed_width, size), packed_width, size
    )
    down_back = on_zh(down_totals)
    in_x, in_y = wires.over_x(in_back[:cut]), [wires.over_y(in_back[cut:], s) for s in across_y]
    others = wires.over_x(jnp.stack([pick(total, 1 - wires.x, 2, 1) for total in firsts]))
    in_grad = last(d_here, in_whole, tokens, d_middle, attn_gain[None])
    in_grad, out_y, in_x, in_y, others, down_sent, down_back, gains = tie(
        in_grad, out_y, in_x, in_y, others, down_sent, down_back, gains
    )
    out_total = add(out_own[0], out_last, *out_y)
    out_turns = lax.all_to_all(out_total, "head", axis_index_groups=same_core, **turned)
    in_halves = (wires.sum_y(add(in_back[:cut], in_x)), wires.sum_x(add(in_back[cut:], *in_y)))
    totals = [*firsts, add(down_parts[0][0], *down_sent, *down_back)]
    others = [others[0], others[1], wires.over_x(pick(totals[2], 1 - wires.x, 2, 1))]
    gains = gains + wires.over_core(gains)
    out_turns, gains, others, in_halves, totals = tie(out_turns, gains, others, in_halves, totals)
    out_part = add(*[out_turns[z] for z in range(wires.nz)])
    out_x = wires.over_x(out_part)
    out_by_y = [wires.over_y(out_part, s) for s in across_y]
    output = low(middle + wide(branch_o[0]) + wide(swap_o) + wide(final_x) + wide(final_z))
    gains = gains + wires.over_zl(gains)
    gains = gains + sum(wires.over_zh(gains, s) for s in range(1, wires.nzh))
    gate_grad, up_grad, down_grad = (
        grad_last(pick(total, wires.x, 2, 1), other) for total, other in zip(totals, others)
    )
    gate_grad, up_grad = gate_grad.T, up_grad.T
    out_x, out_by_y, gains, output, gate_grad, up_grad, down_grad = tie(
        out_x, out_by_y, gains, output, gate_grad, up_grad, down_grad
    )
    out_by_yx = [wires.over_y(out_x, s) for s in across_y]
    gains_x = wires.over_x(gains)
    gains = gains + gains_x + sum(
        wires.over_y(gains, s) + wires.over_dp(gains, s) for s in across_y
    )
    out_weight_grad = wide(
        in_order(
            [
                in_order([a, b], wires.x, 1)
                for a, b in zip([out_part, *out_by_y], [out_x, *out_by_yx])
            ],
            wires.y,
            1,
        )
    )
    in_weight_grad = wide(jnp.concatenate(in_halves, axis=0)).T
    return (
        output,
        in_grad,
        gains[0],
        in_weight_grad,
        out_weight_grad,
        gains[1],
        gate_grad,
        up_grad,
        down_grad,
    )


def solution(mesh):
    return jax.shard_map(
        functools.partial(per_device, Wires(mesh)),
        mesh=mesh,
        in_specs=(
            P(("dp", "head"), None),
            P("dp"),
            P("dp", None),
            P(),
            P(None, "head"),
            P("head", None),
            P(),
            P("dp", "head"),
            P("dp", "head"),
            P("head", "dp"),
            P(("dp", "head"), None),
        ),
        out_specs=(
            P(("dp", "head"), None),
            P(("dp", "head"), None),
            P(),
            P(None, "head"),
            P("head", None),
            P(),
            P("dp", "head"),
            P("dp", "head"),
            P("head", "dp"),
        ),
        check_vma=False,
    )
```

```python
import functools
import jax
import jax.numpy as jnp
from jax import lax
from jax.experimental import pallas as pl
from jax.experimental.pallas import tpu as pltpu
from jax.sharding import PartitionSpec as P

FD = 16
VD = 128
LANES = 128
VMEM = 60 * 1024 * 1024
LITTLE = pl.CostEstimate(flops=1, bytes_accessed=1, transcendentals=0)
epsilon = 1e-05
NT = (((1,), (1,)), ((), ()))
TN = (((0,), (0,)), ((), ()))


def column_of(row):
    count = row.shape[1]
    same = lax.broadcasted_iota(jnp.int32, (count, count), 0) == lax.broadcasted_iota(
        jnp.int32, (count, count), 1
    )
    return jnp.sum(jnp.where(same, row, 0.0), axis=1, keepdims=True)


def padded(block):
    rows, columns = block.shape
    return jnp.concatenate([block, jnp.zeros((rows, -columns % LANES), block.dtype)], axis=1)


def lanes_from(block, low, count):
    width = block.shape[1]
    moved = (block if low == 0 else pltpu.roll(block, width - low, 1))[:, :LANES]
    if count == LANES:
        return moved
    lane = lax.broadcasted_iota(jnp.int32, moved.shape, 1)
    return jnp.where(lane < count, moved, 0.0)


def head_parts(block, head):
    low = head * (2 * FD + VD)
    query = lanes_from(block, low, FD) * 0.25
    return query, lanes_from(block, low + FD, FD), lanes_from(block, low + 2 * FD, VD)


def segment_start(ends_ref, positions):
    start = jnp.zeros_like(positions)
    for slot in range(ends_ref.shape[0]):
        end = ends_ref[slot]
        start = jnp.where(positions >= end, jnp.maximum(start, end), start)
    return start


def attend_kernel(heads, rows, pieces, ends_ref, at_ref, *refs):
    sources = refs[:pieces]
    weight_ref, keep_ref, projected_ref, normed_ref, y_ref, inv_ref, att_ref = refs[pieces : pieces + 7]
    normed_s, key_s, value_s, sems = refs[pieces + 7 :]
    step = pl.program_id(0)
    own = pl.ds(pl.multiple_of(step * rows, rows), rows)

    @pl.when(step == 0)
    def _():
        size = sources[0].shape[0]
        copies = [
            pltpu.make_async_copy(
                sources[i].at[:, pl.ds(0, normed_s.shape[1])], normed_s.at[pl.ds(pl.multiple_of(at_ref[i], size), size), :], sems.at[i]
            )
            for i in range(pieces)
        ]
        for copy in copies:
            copy.start()
        for copy in copies:
            copy.wait()

    keep = column_of(keep_ref[:, own])
    normed = normed_s[own, :]
    normed_ref[...] = normed
    projected = lax.dot_general(
        normed, weight_ref[...], NT, preferred_element_type=jnp.float32
    ).astype(jnp.bfloat16)
    projected_ref[...] = projected
    block = padded(projected.astype(jnp.float32))
    lane = lax.broadcasted_iota(jnp.int32, (rows, LANES), 1)
    ones = jnp.where(lane < 2, keep, 0.0).astype(jnp.bfloat16)
    queries = []
    for head in range(heads):
        query, key, value = head_parts(block, head)
        queries.append(query.astype(jnp.bfloat16))
        key_s[head, own, :] = key.astype(jnp.bfloat16)
        value_s[head, own, :VD] = (value * keep).astype(jnp.bfloat16)
        value_s[head, own, VD:] = ones
    row = step * rows + lax.broadcasted_iota(jnp.int32, (rows, 1), 0)
    start = segment_start(ends_ref, row)
    column = lax.broadcasted_iota(jnp.int32, (rows, rows), 1)

    def tile(block, totals, diagonal):
        at = pl.ds(pl.multiple_of(block * rows, rows), rows)
        allowed = column >= start - block * rows
        if diagonal:
            allowed &= column <= lax.broadcasted_iota(jnp.int32, (rows, rows), 0)
        added = []
        for head in range(heads):
            inner = lax.dot_general(
                queries[head], key_s[head, at, :], NT, preferred_element_type=jnp.float32
            )
            weights = jnp.where(allowed, (inner * 0.5 + 1.0) * inner + 1.0, 0.0).astype(jnp.bfloat16)
            added.append(
                totals[head]
                + jnp.dot(weights, value_s[head, at, :], preferred_element_type=jnp.float32)
            )
        return tuple(added)

    totals = tuple(jnp.zeros((rows, 2 * VD), jnp.float32) for _ in range(heads))
    totals = lax.fori_loop(0, step, lambda block, held: tile(block, held, False), totals)
    totals = tile(step, totals, True)
    inverses = jnp.zeros((rows, LANES), jnp.float32)
    for head in range(heads):
        inverse = 1.0 / (totals[head][:, VD : VD + 1] + 1.0 - keep)
        y = totals[head][:, :VD] * (keep * inverse)
        y_ref[:, head * VD : (head + 1) * VD] = y
        att_ref[:, head * VD : (head + 1) * VD] = y.astype(jnp.bfloat16)
        inverses = jnp.where(lane == head, inverse, inverses)
    inverses = jnp.where(lane == heads, keep, inverses)
    inv_ref[...] = inverses


def attend(pieces, places, weight, keep, ends, heads):
    size, depth = pieces[0].shape[0], weight.shape[1]
    total = size * len(pieces)
    rows = min(512, total)
    width = weight.shape[0]
    pairs = total * (total + rows) // 2 * heads
    blocked = lambda columns: pl.BlockSpec((rows, columns), lambda i, e, a: (i, 0))
    return pl.pallas_call(
        functools.partial(attend_kernel, heads, rows, len(pieces)),
        grid_spec=pltpu.PrefetchScalarGridSpec(
            num_scalar_prefetch=2,
            grid=(total // rows,),
            in_specs=[pl.BlockSpec(memory_space=pl.ANY)] * len(pieces)
            + [
                pl.BlockSpec((width, depth), lambda i, e, a: (0, 0)),
                pl.BlockSpec((1, total), lambda i, e, a: (0, 0)),
            ],
            out_specs=[
                blocked(width), blocked(depth), blocked(heads * VD), blocked(LANES), blocked(heads * VD)
            ],
            scratch_shapes=[
                pltpu.VMEM((total, depth), jnp.bfloat16),
                pltpu.VMEM((heads, total, LANES), jnp.bfloat16),
                pltpu.VMEM((heads, total, 2 * VD), jnp.bfloat16),
                pltpu.SemaphoreType.DMA((len(pieces),)),
            ],
        ),
        out_shape=[
            jax.ShapeDtypeStruct((total, width), jnp.bfloat16),
            jax.ShapeDtypeStruct((total, depth), jnp.bfloat16),
            jax.ShapeDtypeStruct((total, heads * VD), jnp.float32),
            jax.ShapeDtypeStruct((total, LANES), jnp.float32),
            jax.ShapeDtypeStruct((total, heads * VD), jnp.bfloat16),
        ],
        compiler_params=pltpu.CompilerParams(
            dimension_semantics=("arbitrary",), vmem_limit_bytes=VMEM
        ),
        cost_estimate=LITTLE,
    )(ends, places, *pieces, weight, keep)


def attend_back_kernel(
    heads, rows, ends_ref, projected_ref, y_ref, inv_ref, grad_ref, out_ref,
    key_s, query_s, value_s, error_s, dquery_s,
):
    step = pl.program_id(0)
    blocks = pl.num_programs(0)
    lane = lax.broadcasted_iota(jnp.int32, (rows, LANES), 1)

    @pl.when(step == 0)
    def _():
        dquery_s[...] = jnp.zeros_like(dquery_s)

        def fill(block, nothing):
            at = pl.ds(pl.multiple_of(block * rows, rows), rows)
            keep = inv_ref[at, heads : heads + 1]
            wide_block = padded(projected_ref[at, :].astype(jnp.float32))
            ones = jnp.where(lane < 2, keep, 0.0).astype(jnp.bfloat16)
            inverses = inv_ref[at, :]
            for head in range(heads):
                columns = slice(head * VD, (head + 1) * VD)
                query, key, value = head_parts(wide_block, head)
                key_s[head, at, :] = key.astype(jnp.bfloat16)
                query_s[head, at, :] = query.astype(jnp.bfloat16)
                value_s[head, at, :VD] = (value * keep).astype(jnp.bfloat16)
                value_s[head, at, VD:] = ones
                inverse = inverses[:, head : head + 1]
                grad = grad_ref[at, columns].astype(jnp.float32)
                error_s[head, at, :VD] = (grad * (keep * inverse)).astype(jnp.bfloat16)
                offset = -jnp.sum(grad * y_ref[at, columns], axis=1, keepdims=True) * inverse
                high = offset.astype(jnp.bfloat16).astype(jnp.float32)
                error_s[head, at, VD:] = jnp.where(
                    lane == 0, high, jnp.where(lane == 1, offset - high, 0.0)
                ).astype(jnp.bfloat16)
            return nothing

        lax.fori_loop(0, blocks, fill, 0)

    own = pl.ds(pl.multiple_of(step * rows, rows), rows)
    row = lax.broadcasted_iota(jnp.int32, (rows, rows), 0)

    def tile(block, totals, diagonal):
        at = pl.ds(pl.multiple_of(block * rows, rows), rows)
        column = block * rows + lax.broadcasted_iota(jnp.int32, (1, rows), 1)
        allowed = row >= segment_start(ends_ref, column) - step * rows
        if diagonal:
            allowed &= row <= lax.broadcasted_iota(jnp.int32, (rows, rows), 1)
        dkeys, dvalues = totals
        added, turned = [], []
        for head in range(heads):
            query = query_s[head, at, :]
            error = error_s[head, at, :]
            keys = key_s[head, own, :]
            inner = lax.dot_general(keys, query, NT, preferred_element_type=jnp.float32)
            dweight = lax.dot_general(value_s[head, own, :], error, NT, preferred_element_type=jnp.float32)
            slope = inner + 1.0
            weights = jnp.where(allowed, (slope * slope + 1.0) * 0.5, 0.0).astype(jnp.bfloat16)
            dinner = jnp.where(allowed, slope * dweight, 0.0).astype(jnp.bfloat16)
            added.append(
                dvalues[head] + jnp.dot(weights, error[:, :VD], preferred_element_type=jnp.float32)
            )
            turned.append(dkeys[head] + jnp.dot(dinner, query, preferred_element_type=jnp.float32))
            dquery_s[head, at, :] += lax.dot_general(dinner, keys, TN, preferred_element_type=jnp.float32)
        return tuple(turned), tuple(added)

    totals = (
        tuple(jnp.zeros((rows, LANES), jnp.float32) for _ in range(heads)),
        tuple(jnp.zeros((rows, VD), jnp.float32) for _ in range(heads)),
    )
    totals = tile(step, totals, True)
    dkeys, dvalues = lax.fori_loop(step + 1, blocks, lambda block, held: tile(block, held, False), totals)
    keep = inv_ref[own, heads : heads + 1]
    width = out_ref.shape[2]
    total = jnp.zeros((rows, width + -width % LANES), jnp.float32)
    blank = jnp.zeros((rows, total.shape[1] - LANES), jnp.float32)

    def put(block, low):
        spread = jnp.concatenate([block, blank], axis=1)
        return spread if low == 0 else pltpu.roll(spread, low, 1)

    for head in range(heads):
        low = head * (2 * FD + VD)
        total += put(dquery_s[head, own, :] * 0.25, low)
        total += put(dkeys[head], low + FD)
        total += put(dvalues[head] * keep, low + 2 * FD)
    out_ref[...] = total[:, :width].astype(jnp.bfloat16).reshape(out_ref.shape)


def attend_back(projected, ends, y, inverses, grad, heads, each):
    total = projected.shape[0]
    rows = min(512, total)
    width = projected.shape[1]
    whole = lambda columns: pl.BlockSpec((total, columns), lambda i, e: (0, 0))
    return pl.pallas_call(
        functools.partial(attend_back_kernel, heads, rows),
        grid_spec=pltpu.PrefetchScalarGridSpec(
            num_scalar_prefetch=1,
            grid=(total // rows,),
            in_specs=[whole(width), whole(heads * VD), whole(LANES), whole(heads * VD)],
            out_specs=pl.BlockSpec((rows // each, each, width), lambda i, e: (i, 0, 0)),
            scratch_shapes=[
                pltpu.VMEM((heads, total, LANES), jnp.bfloat16),
                pltpu.VMEM((heads, total, LANES), jnp.bfloat16),
                pltpu.VMEM((heads, total, 2 * VD), jnp.bfloat16),
                pltpu.VMEM((heads, total, 2 * VD), jnp.bfloat16),
                pltpu.VMEM((heads, total, LANES), jnp.float32),
            ],
        ),
        out_shape=jax.ShapeDtypeStruct((total // each, each, width), jnp.bfloat16),
        compiler_params=pltpu.CompilerParams(
            dimension_semantics=("arbitrary",), vmem_limit_bytes=VMEM
        ),
        cost_estimate=LITTLE,
    )(ends, projected, y, inverses, grad)


def inv_root_mean(values):
    return lax.rsqrt(jnp.mean(values * values, axis=1, keepdims=True) + epsilon)


def wide(values):
    return values.astype(jnp.float32)


def low(values):
    return values.astype(jnp.bfloat16)


def pick(values, index, count, axis):
    size = values.shape[axis] // count
    if count == 2:
        first = lax.slice_in_dim(values, 0, size, axis=axis)
        second = lax.slice_in_dim(values, size, 2 * size, axis=axis)
        return jnp.where(index == 0, first, second)
    return lax.dynamic_slice_in_dim(values, index * size, size, axis)


def in_order(pieces, index, axis):
    count = len(pieces)
    if count == 1:
        return pieces[0]
    if count == 2:
        first = jnp.where(index == 0, pieces[0], pieces[1])
        second = jnp.where(index == 0, pieces[1], pieces[0])
        return jnp.concatenate([first, second], axis=axis)
    stacked = jnp.stack(pieces)
    placed = [
        lax.dynamic_index_in_dim(stacked, (index - place) % count, 0, keepdims=False)
        for place in range(count)
    ]
    return jnp.concatenate(placed, axis=axis)


class Wires:
    def __init__(self, mesh):
        self.dp, self.head = mesh.shape["dp"], mesh.shape["head"]
        self.ny, self.nz, self.nzh = self.dp // 2, self.head // 2, self.head // 4

    def place(self):
        p, h = lax.axis_index("dp"), lax.axis_index("head")
        self.p, self.h = p, h
        self.y, self.x, self.z, self.c = p // 2, p % 2, h // 2, h % 2
        self.zh = self.z // 2

    def over_x(self, values):
        return lax.ppermute(values, "dp", [(i, i ^ 1) for i in range(self.dp)])

    def over_y(self, values, shift):
        return lax.ppermute(
            values, "dp", [(i, ((i // 2 + shift) % self.ny) * 2 + i % 2) for i in range(self.dp)]
        )

    def over_dp(self, values, shift):
        return lax.ppermute(
            values, "dp", [(i, ((i // 2 + shift) % self.ny) * 2 + (i + 1) % 2) for i in range(self.dp)]
        )

    def over_core(self, values):
        return lax.ppermute(values, "head", [(i, i ^ 1) for i in range(self.head)])

    def over_zl(self, values):
        return lax.ppermute(values, "head", [(i, i ^ 2) for i in range(self.head)])

    def over_zh(self, values, shift):
        return lax.ppermute(
            values, "head", [(i, ((i // 4 + shift) % self.nzh) * 4 + i % 4) for i in range(self.head)]
        )

    def over_zh_half(self, values, shift, parity):
        pairs = [
            (i, ((i // 4 + shift) % self.nzh) * 4 + i % 4)
            for i in range(self.head)
            if (i // 4 + i // 2 % 2) % 2 == parity
        ]
        return lax.ppermute(values, "head", pairs)

    def from_halves(self, first, second, shift):
        even = (self.zh - shift + self.z) % 2 == 0
        return jnp.where(even, first, second)

    def over_z(self, values, shift):
        return lax.ppermute(
            values, "head", [(i, ((i // 2 + shift) % self.nz) * 2 + i % 2) for i in range(self.head)]
        )

    def right(self, values, first, last):
        return lax.ppermute(
            values, "head", [(i, i + 2) for i in range(self.head) if first <= i // 2 <= last]
        )

    def left(self, values, first, last):
        return lax.ppermute(
            values, "head", [(i, i - 2) for i in range(self.head) if first <= i // 2 <= last]
        )

    def spread(self, line):
        return self.over_x(line), [self.over_y(line, s) for s in range(1, self.ny)]

    def ends(self, values):
        pairs = [(i, i + 2 if i // 2 == self.nz - 2 else i - 2) for i in range(self.head)]
        return lax.ppermute(
            values, "head", [pair for pair in pairs if pair[0] // 2 in (1, self.nz - 2)]
        )

    def arrivals(self):
        orders = []
        for z in range(self.nz):
            order = []
            for step in range(1, self.nz):
                order += [(0, step)] if z >= step else []
                order += [(1, step)] if z + step < self.nz else []
            orders.append(order)
        return orders

    def by_place(self, values):
        chosen, taken = values[0], [values[0]]
        for value in values[1:]:
            if any(value is other for other in taken):
                continue
            taken.append(value)
            here = [z for z in range(self.nz) if values[z] is value]
            chosen = jnp.where(sum((self.z == z).astype(jnp.int32) for z in here) > 0, value, chosen)
        return chosen

    def sum_y(self, values):
        total = wide(values)
        for s in range(1, self.ny):
            total = total + wide(self.over_y(values, s))
        return low(total)

    def sum_x(self, values):
        return low(wide(values) + wide(self.over_x(values)))

    def sum_all(self, values):
        values = values + self.over_core(values)
        values = values + self.over_zl(values)
        values = values + sum(self.over_zh(values, s) for s in range(1, self.nzh))
        values = values + self.over_x(values)
        return values + sum(self.over_y(values, s) for s in range(1, self.ny))

    def quarter(self, shard):
        size = shard.shape[1] // self.dp
        return lax.dynamic_slice_in_dim(shard, self.p * size, size, 1)

    def line_of(self, part):
        return [part] + [self.over_z(part, s) for s in range(1, self.nz)]

    def whole_places(self, chips, rows, size):
        at_rows = [(chip * 2 + (self.c ^ r)) * rows for r in range(2) for chip in chips]
        at_columns = [
            (((self.y - s) % self.ny) * 2 + (self.x ^ t)) * size
            for s in range(self.ny)
            for t in range(2)
        ]
        return jnp.stack(at_rows + at_columns).astype(jnp.int32)

    def line(self, block, during):
        steps = self.nz
        right = left = block
        rights, lefts = {}, {}
        orders = self.arrivals()
        chunks, chips = [block], [self.z]
        for step in range(1, steps):
            if step < steps - 1:
                right = self.right(right, step - 1, steps - 2)
                left = self.left(left, 1, steps - step)
                right, left = during(step, (right, left))
            else:
                both = jnp.where(self.z == steps - 2, right, left)
                (right, both) = during(step, (self.ends(both), both))
                left = right
            rights[step], lefts[step] = right, left
            arrived = {(0, s): rights[s] for s in rights} | {(1, s): lefts[s] for s in lefts}
            while len(chunks) < steps and all(
                orders[z][len(chunks) - 1] in arrived for z in range(steps)
            ):
                order = [orders[z][len(chunks) - 1] for z in range(steps)]
                values = [arrived[key] for key in order]
                if step == steps - 1 and values[1] is lefts[steps - 2] and values[-2] is rights[steps - 2]:
                    values[1] = values[-2] = both
                chunks.append(self.by_place(values))
                chips.append(
                    self.by_place([z - key[1] * (1 - 2 * key[0]) for z, key in enumerate(order)])
                )
        return chunks, chips


class Whole:
    def __init__(self, wires, pieces, places, rows, size):
        self.layout = [(s, t, 0, wires.nz) for s in range(wires.ny) for t in range(2)]
        self.nz = wires.nz
        self.pieces, self.rows, self.size = pieces, rows, size
        self.places = places
        self.copies = 2 * sum(count for _, _, _, count in self.layout)
        self.shape = (wires.head * rows, wires.dp * size)

    def fill(self, places_ref, refs, scratch, sems):
        copies = []
        for piece, (s, t, first, count) in enumerate(self.layout):
            column = pl.multiple_of(places_ref[2 * self.nz + 2 * s + t], self.size)
            for core in range(2):
                for slot in range(count):
                    row = pl.multiple_of(places_ref[core * self.nz + first + slot], self.rows)
                    copies.append(
                        pltpu.make_async_copy(
                            refs[core * len(self.layout) + piece].at[slot],
                            scratch.at[pl.ds(row, self.rows), pl.ds(column, self.size)],
                            sems.at[len(copies)],
                        )
                    )
        for copy in copies:
            copy.start()
        return copies


def swapped(wires, pieces):
    return [*pieces, *[wires.over_core(piece) for piece in pieces]]


def side_by_side(blocks_ref):
    return jnp.concatenate([blocks_ref[i] for i in range(blocks_ref.shape[0])], axis=1)


def by_columns(whole, places_ref, copies, weight_s, blocks, total_ref):
    each = len(copies) // len(whole.layout)
    for piece, (s, t, _, _) in enumerate(whole.layout):
        for copy in copies[piece * each : (piece + 1) * each]:
            copy.wait()
        at = pl.ds(pl.multiple_of(places_ref[2 * whole.nz + 2 * s + t], whole.size), whole.size)
        total, low = 0.0, 0
        for block in blocks:
            total += jnp.dot(
                block, weight_s[low : low + block.shape[1], at], preferred_element_type=jnp.float32
            )
            low += block.shape[1]
        total_ref[:, at] = total


def mix_kernel(whole, places_ref, *refs):
    count = len(whole.pieces)
    attended_ref, tokens_ref, gain_ref, middle_ref, normed_ref, weight_s, sems = refs[count:]
    copies = whole.fill(places_ref, refs[:count], weight_s, sems)
    by_columns(whole, places_ref, copies, weight_s, [side_by_side(attended_ref)], middle_ref)
    middle = middle_ref[...] + wide(tokens_ref[...])
    middle_ref[...] = middle
    normed_ref[...] = (middle * inv_root_mean(middle) * gain_ref[...]).astype(jnp.bfloat16)


def with_whole(kernel, whole, args, outs, flops):
    in_vmem = pl.BlockSpec(memory_space=pltpu.VMEM)
    return pl.pallas_call(
        functools.partial(kernel, whole),
        grid_spec=pltpu.PrefetchScalarGridSpec(
            num_scalar_prefetch=1,
            grid=(),
            in_specs=[pl.BlockSpec(memory_space=pl.ANY)] * len(whole.pieces) + [in_vmem] * len(args),
            out_specs=[in_vmem] * len(outs),
            scratch_shapes=[
                pltpu.VMEM(whole.shape, jnp.bfloat16),
                pltpu.SemaphoreType.DMA((whole.copies,)),
            ],
        ),
        out_shape=[jax.ShapeDtypeStruct(shape, kind) for shape, kind in outs],
        compiler_params=pltpu.CompilerParams(vmem_limit_bytes=VMEM),
        cost_estimate=LITTLE,
    )(whole.places, *whole.pieces, *args)


def mix(attended, whole, tokens, gain):
    return with_whole(
        mix_kernel,
        whole,
        (attended, tokens, gain),
        ((tokens.shape, jnp.float32), (tokens.shape, jnp.bfloat16)),
        2 * tokens.shape[0] * whole.shape[0] * whole.shape[1],
    )


def unmix_kernel(whole, places_ref, *refs):
    count = len(whole.pieces)
    parts, (middle_ref, grad_ref, gain_ref) = refs[count : count + 4], refs[count + 4 : count + 7]
    dmiddle_ref, dmixed_ref, part_ref, out_ref, weight_s, sems = refs[count + 7 :]
    copies = whole.fill(places_ref, refs[:count], weight_s, sems)
    middle = middle_ref[...]
    inv_two = inv_root_mean(middle)
    dnormed = sum(wide(part[...]) for part in parts)
    scaled = middle * inv_two
    error = dnormed * gain_ref[...]
    dmiddle = wide(grad_ref[...]) + inv_two * (
        error - scaled * jnp.mean(error * scaled, axis=1, keepdims=True)
    )
    part_ref[...] = jnp.sum(dnormed * scaled, axis=0, keepdims=True)
    dmiddle_ref[...] = dmiddle
    dmixed = dmiddle.astype(jnp.bfloat16)
    dmixed_ref[...] = dmixed
    for copy in copies:
        copy.wait()
    width = out_ref.shape[2]
    for head in range(0, out_ref.shape[0], 2):
        pair = lax.dot_general(
            dmixed, weight_s[head * width : (head + 2) * width, :], NT, preferred_element_type=jnp.float32
        ).astype(jnp.bfloat16)
        out_ref[head] = pair[:, :width]
        out_ref[head + 1] = pair[:, width:]


def unmix(parts, middle, grad, gain, whole, heads):
    rows, depth = middle.shape
    return with_whole(
        unmix_kernel,
        whole,
        (*parts, middle, grad, gain),
        (
            (middle.shape, jnp.float32),
            (middle.shape, jnp.bfloat16),
            ((1, depth), jnp.float32),
            ((heads, rows, whole.shape[0] // heads), jnp.bfloat16),
        ),
        2 * rows * whole.shape[0] * whole.shape[1],
    )


def last_kernel(whole, places_ref, *refs):
    count = len(whole.pieces)
    proj_ref, tokens_ref, dmiddle_ref, gain_ref, grad_ref, weight_s, sems = refs[count:]
    copies = whole.fill(places_ref, refs[:count], weight_s, sems)
    blocks = [proj_ref[head] for head in range(proj_ref.shape[0])]
    by_columns(whole, places_ref, copies, weight_s, blocks, grad_ref)
    dnormed = grad_ref[...]
    tokens = wide(tokens_ref[...])
    inv_one = inv_root_mean(tokens)
    scaled = tokens * inv_one
    error = dnormed * gain_ref[...]
    grad_ref[...] = dmiddle_ref[...] + inv_one * (
        error - scaled * jnp.mean(error * scaled, axis=1, keepdims=True)
    )


def last(proj, whole, tokens, dmiddle, gain):
    return with_whole(
        last_kernel,
        whole,
        (proj, tokens, dmiddle, gain),
        ((tokens.shape, jnp.float32),),
        2 * tokens.shape[0] * whole.shape[0] * whole.shape[1],
    )[0]


class Units:
    def __init__(self, wires, pieces, matrices, rows, columns):
        self.matrices = matrices
        self.layout = [piece[1:] for piece in pieces]
        self.pieces = [piece[0] for piece in pieces]
        self.rows, self.columns = rows, columns
        self.places = jnp.stack([((wires.y - s) % wires.ny) * columns for s in range(wires.ny)]).astype(
            jnp.int32
        )
        self.shape = (matrices, wires.nzh * rows, wires.ny * columns)

    def fill(self, places_ref, refs, scratch, sems):
        copies = []
        for matrix in range(self.matrices):
            for ref, (first, count, zh, y) in zip(refs, self.layout):
                if not first <= matrix < first + count:
                    continue
                column = pl.multiple_of(places_ref[y], self.columns)
                copies.append(
                    pltpu.make_async_copy(
                        ref.at[matrix - first],
                        scratch.at[
                            matrix, pl.ds(zh * self.rows, self.rows), pl.ds(column, self.columns)
                        ],
                        sems.at[len(copies)],
                    )
                )
        for copy in copies:
            copy.start()
        return copies


def with_units(kernel, units, blocks, outs, scratch, flops, transcendentals):
    anywhere = pl.BlockSpec(memory_space=pl.ANY)
    copies = sum(count for _, count, _, _ in units.layout)
    return pl.pallas_call(
        functools.partial(kernel, units),
        grid_spec=pltpu.PrefetchScalarGridSpec(
            num_scalar_prefetch=1,
            grid=(),
            in_specs=[anywhere] * (len(units.pieces) + len(blocks)),
            out_specs=[anywhere] * len(outs),
            scratch_shapes=[
                pltpu.VMEM(units.shape, jnp.bfloat16),
                pltpu.SemaphoreType.DMA((copies,)),
            ]
            + scratch,
        ),
        out_shape=[jax.ShapeDtypeStruct(shape, kind) for shape, kind in outs],
        compiler_params=pltpu.CompilerParams(vmem_limit_bytes=VMEM),
        cost_estimate=LITTLE,
    )(units.places, *units.pieces, *blocks)


def started(copies):
    for copy in copies:
        copy.start()
    return copies


def awaited(copies):
    for copy in copies:
        copy.wait()


def gate_kernel(count, units, places_ref, *refs):
    pieces, refs = refs[: len(units.pieces)], refs[len(units.pieces) :]
    blocks, (unit_ref, normed_ref) = refs[: 2 * count], refs[2 * count : 2 * count + 2]
    weight_s, sems, normed_s, unit_s, in_sems, out_sems = refs[2 * count + 2 :]
    rows = blocks[0].shape[0]

    def arrive(chunk):
        started(
            [
                pltpu.make_async_copy(
                    blocks[2 * chunk + i], normed_s.at[chunk, pl.ds(i * rows, rows)], in_sems.at[chunk]
                )
                for i in range(2)
            ]
        )

    arrive(0)
    weights = units.fill(places_ref, pieces, weight_s, sems)
    for chunk in range(1, count):
        arrive(chunk)
    each = len(weights) // units.matrices

    def sent(chunk, which):
        source, target = ((normed_s, normed_ref), (unit_s, unit_ref))[which]
        return pltpu.make_async_copy(source.at[chunk], target.at[chunk], out_sems.at[which, chunk])

    def work(chunk, nothing):
        pltpu.make_async_copy(normed_ref.at[chunk], normed_s.at[chunk], in_sems.at[chunk]).wait()
        sent(chunk, 0).start()
        pl.when(chunk == 0)(lambda: awaited(weights[:each]))
        normed = normed_s[chunk]
        gate = lax.dot_general(normed, weight_s[0], NT, preferred_element_type=jnp.float32)
        pl.when(chunk == 0)(lambda: awaited(weights[each:]))
        up = lax.dot_general(normed, weight_s[1], NT, preferred_element_type=jnp.float32)
        sigmoid = jax.nn.sigmoid(gate)
        silu = gate * sigmoid
        unit_s[chunk, 0] = (silu * up).astype(jnp.bfloat16)
        unit_s[chunk, 1] = (up * sigmoid * (1.0 + gate * (1.0 - sigmoid))).astype(jnp.bfloat16)
        unit_s[chunk, 2] = silu.astype(jnp.bfloat16)
        sent(chunk, 1).start()
        return nothing

    lax.fori_loop(0, count, work, 0)
    for chunk in range(count):
        awaited([sent(chunk, 0), sent(chunk, 1)])


def gate_up(pairs, units):
    count = len(pairs)
    rows, depth = pairs[0][0].shape
    unit, full = (count, 3, 2 * rows, units.shape[1]), (count, 2 * rows, depth)
    return with_units(
        functools.partial(gate_kernel, count),
        units,
        [block for pair in pairs for block in pair],
        ((unit, jnp.bfloat16), (full, jnp.bfloat16)),
        [
            pltpu.VMEM(full, jnp.bfloat16),
            pltpu.VMEM(unit, jnp.bfloat16),
            pltpu.SemaphoreType.DMA((count,)),
            pltpu.SemaphoreType.DMA((2, count)),
        ],
        8 * count * rows * depth * units.shape[1],
        0,
    )


def down_kernel(places, units, places_ref, *refs):
    count = len(places)
    pieces, refs = refs[: len(units.pieces)], refs[len(units.pieces) :]
    blocks, refs = refs[: 3 * count], refs[3 * count :]
    unit_ref, grad_ref, refs = refs[0], refs[1], refs[2:]
    dnormed, branches = refs[: 2 * count], refs[2 * count : 4 * count]
    weight_s, sems, given_s, grad_s, unit_s, back_s, branch_s, in_sems, out_sems = refs[4 * count :]
    rows = blocks[0].shape[0]
    both = [pl.ds(0, rows), pl.ds(rows, rows)]

    def arrive(chunk):
        one, two, given = blocks[3 * chunk : 3 * chunk + 3]
        started(
            [
                pltpu.make_async_copy(one, grad_s.at[chunk, both[0]], in_sems.at[0, chunk]),
                pltpu.make_async_copy(two, grad_s.at[chunk, both[1]], in_sems.at[0, chunk]),
                pltpu.make_async_copy(given.at[places[chunk]], given_s.at[chunk], in_sems.at[1, chunk]),
            ]
        )

    arrive(0)
    weights = units.fill(places_ref, pieces, weight_s, sems)
    for chunk in range(1, count):
        arrive(chunk)
    each = len(weights) // units.matrices
    dot = functools.partial(jnp.dot, preferred_element_type=jnp.float32)

    def sent(chunk, which):
        source, target = ((grad_s, grad_ref), (unit_s, unit_ref))[which]
        return pltpu.make_async_copy(source.at[chunk], target.at[chunk], out_sems.at[which, chunk])

    def halves_sent(chunk, source, targets, place):
        return [
            pltpu.make_async_copy(
                source.at[chunk, both[i]], targets[2 * chunk + i], out_sems.at[place + i, chunk]
            )
            for i in range(2)
        ]

    def work(chunk, nothing):
        pltpu.make_async_copy(grad_ref.at[chunk], grad_s.at[chunk], in_sems.at[0, chunk]).wait()
        sent(chunk, 0).start()
        pl.when(chunk == 0)(lambda: awaited(weights[:each]))
        dhidden = lax.dot_general(grad_s[chunk], weight_s[0], NT, preferred_element_type=jnp.float32)
        pltpu.make_async_copy(given_s.at[chunk], given_s.at[chunk], in_sems.at[1, chunk]).wait()
        dgate = (dhidden * wide(given_s[chunk, 1])).astype(jnp.bfloat16)
        dup = (dhidden * wide(given_s[chunk, 2])).astype(jnp.bfloat16)
        unit_s[chunk, 0] = dgate
        unit_s[chunk, 1] = dup
        sent(chunk, 1).start()
        branch_s[chunk] = dot(given_s[chunk, 0], weight_s[0]).astype(jnp.bfloat16)
        for k in range(count):
            pl.when(chunk == k)(lambda k=k: started(halves_sent(k, branch_s, branches, 2)) and None)
        pl.when(chunk == 0)(lambda: awaited(weights[each:]))
        back_s[chunk] = (dot(dgate, weight_s[1]) + dot(dup, weight_s[2])).astype(jnp.bfloat16)
        for k in range(count):
            pl.when(chunk == k)(lambda k=k: started(halves_sent(k, back_s, dnormed, 4)) and None)
        return nothing

    lax.fori_loop(0, count, work, 0)
    for chunk in range(count):
        awaited([sent(chunk, 0), sent(chunk, 1)])
        awaited(halves_sent(chunk, branch_s, branches, 2))
        awaited(halves_sent(chunk, back_s, dnormed, 4))


def down(given, units):
    count = len(given)
    rows, depth = given[0][0].shape
    size = units.shape[1]
    full = (count, 2 * rows, depth)
    part = ((rows, depth), jnp.bfloat16)
    outs = with_units(
        functools.partial(down_kernel, [chunk[3] for chunk in given]),
        units,
        [block for chunk in given for block in chunk[:3]],
        (((count, 2, 2 * rows, size), jnp.bfloat16), (full, jnp.bfloat16)) + (part,) * (4 * count),
        [
            pltpu.VMEM((count, 3, 2 * rows, size), jnp.bfloat16),
            pltpu.VMEM(full, jnp.bfloat16),
            pltpu.VMEM((count, 2, 2 * rows, size), jnp.bfloat16),
            pltpu.VMEM(full, jnp.bfloat16),
            pltpu.VMEM(full, jnp.bfloat16),
            pltpu.SemaphoreType.DMA((2, count)),
            pltpu.SemaphoreType.DMA((6, count)),
        ],
        16 * count * rows * depth * size,
        0,
    )
    halves = lambda parts: [parts[2 * i : 2 * i + 2] for i in range(count)]
    return outs[:2], halves(outs[2 : 2 + 2 * count]), halves(outs[2 + 2 * count :])


def unit_grad_kernel(order, ny, nzh, places_ref, *refs):
    count = len(order)
    scratch = refs[-4:]
    arrays, outs = refs[: -4 - ny * nzh], refs[-4 - ny * nzh : -4]
    left_s, right_s, total_s, sems = scratch
    for i, (left, at, right, to) in enumerate(order):
        started(
            [
                pltpu.make_async_copy(arrays[left].at[at], left_s.at[i], sems.at[0, i]),
                pltpu.make_async_copy(arrays[right].at[to], right_s.at[i], sems.at[1, i]),
            ]
        )
    total_s[...] = jnp.zeros_like(total_s)

    def work(i, nothing):
        pltpu.make_async_copy(left_s.at[i], left_s.at[i], sems.at[0, i]).wait()
        pltpu.make_async_copy(right_s.at[i], right_s.at[i], sems.at[1, i]).wait()
        total_s[...] += lax.dot_general(left_s[i], right_s[i], TN, preferred_element_type=jnp.float32)
        return nothing

    lax.fori_loop(0, count, work, 0)
    units, columns = outs[0].shape
    for y in range(ny):
        for zh in range(nzh):
            outs[y * nzh + zh][...] = total_s[
                pl.ds(zh * units, units), pl.ds(pl.multiple_of(places_ref[y], columns), columns)
            ].astype(jnp.bfloat16)


def unit_grad(wires, lefts, rights):
    ny, nzh = wires.ny, wires.nzh
    arrays = []

    def index(array):
        for i, other in enumerate(arrays):
            if other is array:
                return i
        arrays.append(array)
        return len(arrays) - 1

    order = [(index(left), at, index(right), to) for (left, at), (right, to) in zip(lefts, rights)]
    tokens, units = lefts[0][0].shape[-2:]
    depth = rights[0][0].shape[-1]
    rows, columns = units // nzh, depth // ny
    places = jnp.stack([((wires.y + s) % ny) * columns for s in range(ny)]).astype(jnp.int32)
    in_vmem = pl.BlockSpec(memory_space=pltpu.VMEM)
    outs = pl.pallas_call(
        functools.partial(unit_grad_kernel, order, ny, nzh),
        grid_spec=pltpu.PrefetchScalarGridSpec(
            num_scalar_prefetch=1,
            grid=(),
            in_specs=[pl.BlockSpec(memory_space=pl.ANY)] * len(arrays),
            out_specs=[in_vmem] * (ny * nzh),
            scratch_shapes=[
                pltpu.VMEM((len(order), tokens, units), jnp.bfloat16),
                pltpu.VMEM((len(order), tokens, depth), jnp.bfloat16),
                pltpu.VMEM((units, depth), jnp.float32),
                pltpu.SemaphoreType.DMA((2, len(order))),
            ],
        ),
        out_shape=[jax.ShapeDtypeStruct((rows, columns), jnp.bfloat16)] * (ny * nzh),
        compiler_params=pltpu.CompilerParams(vmem_limit_bytes=VMEM),
        cost_estimate=LITTLE,
    )(places, *arrays)
    return [outs[zh::nzh] for zh in range(nzh)]


def out_grad_kernel(nz, ny, places_ref, mine_ref, other_ref, grad_ref, other_grad_ref, *refs):
    outs, (left_s, right_s) = refs[: 2 * ny], refs[2 * ny :]
    step = pl.program_id(0)
    tokens, width = grad_ref.shape[0], outs[0].shape[2]

    @pl.when(step == 0)
    def _():
        right_s[:tokens] = grad_ref[...]
        right_s[tokens:] = other_grad_ref[...]

    left_s[:tokens] = mine_ref[places_ref[step]]
    left_s[tokens:] = other_ref[places_ref[step] // 2]
    left = left_s[...]
    for i, out_ref in enumerate(outs):
        column = pl.multiple_of(places_ref[nz + i], width)
        out_ref[0] = lax.dot_general(
            left, right_s[:, pl.ds(column, width)], TN, preferred_element_type=jnp.float32
        ).astype(jnp.bfloat16)


def out_grad_parts(wires, mine, other, d_mixed, other_d_mixed):
    heads, tokens, rows = mine.shape
    depth = d_mixed.shape[1]
    nz, ny, width = wires.nz, wires.ny, depth // wires.dp
    places = jnp.stack(
        [z * 2 + wires.c for z in range(nz)]
        + [(((wires.y + s) % ny) * 2 + (wires.x ^ t)) * width for t in range(2) for s in range(ny)]
    ).astype(jnp.int32)
    full = lambda *shape: pl.BlockSpec(shape, lambda i, p: (0,) * len(shape))
    outs = pl.pallas_call(
        functools.partial(out_grad_kernel, nz, ny),
        grid_spec=pltpu.PrefetchScalarGridSpec(
            num_scalar_prefetch=1,
            grid=(nz,),
            in_specs=[
                full(heads, tokens, rows),
                full(nz, tokens, rows),
                full(tokens, depth),
                full(tokens, depth),
            ],
            out_specs=[pl.BlockSpec((1, rows, width), lambda i, p: (i, 0, 0))] * (2 * ny),
            scratch_shapes=[
                pltpu.VMEM((2 * tokens, rows), jnp.bfloat16),
                pltpu.VMEM((2 * tokens, depth), jnp.bfloat16),
            ],
        ),
        out_shape=[jax.ShapeDtypeStruct((nz, rows, width), jnp.bfloat16)] * (2 * ny),
        compiler_params=pltpu.CompilerParams(
            dimension_semantics=("arbitrary",), vmem_limit_bytes=VMEM
        ),
        cost_estimate=LITTLE,
    )(places, mine, other, d_mixed, other_d_mixed)
    return outs[:ny], outs[ny:]


def in_grad_kernel(normed_ref, grad_ref, weight_ref, gain_ref, out_ref, part_ref):
    blocks, rows, width = grad_ref.shape
    grad = grad_ref[...].reshape(blocks * rows, width)
    total = lax.dot_general(grad, normed_ref[...], TN, preferred_element_type=jnp.float32)
    out_ref[...] = total.astype(jnp.bfloat16)
    part_ref[...] = jnp.sum(total * wide(weight_ref[...]), axis=0, keepdims=True) / gain_ref[...]


def in_grad_parts(normed, grad, weight, gain):
    tokens, depth = normed.shape
    width = grad.shape[2]
    size = min(512, depth)
    block = lambda rows: pl.BlockSpec((rows, size), lambda i: (0, i))
    return pl.pallas_call(
        in_grad_kernel,
        grid=(depth // size,),
        in_specs=[
            block(tokens),
            pl.BlockSpec(grad.shape, lambda i: (0, 0, 0)),
            block(width),
            block(1),
        ],
        out_specs=[block(width), block(1)],
        out_shape=[
            jax.ShapeDtypeStruct((width, depth), jnp.bfloat16),
            jax.ShapeDtypeStruct((1, depth), jnp.float32),
        ],
        compiler_params=pltpu.CompilerParams(
            dimension_semantics=("arbitrary",), vmem_limit_bytes=VMEM
        ),
        cost_estimate=LITTLE,
    )(normed, grad, weight, gain)


def tie(*values):
    return lax.optimization_barrier(values)


def per_device(
    wires,
    tokens,
    keep_mask,
    seq_lengths,
    attn_gain,
    in_weight,
    out_weight,
    ffn_gain,
    gate_weight,
    up_weight,
    down_weight,
    out_grad,
):
    wires.place()
    heads_here = in_weight.shape[1] // (2 * FD + VD)
    rows, depth = tokens.shape
    group_rows = rows * wires.head
    out_rows = heads_here * VD
    size = depth // wires.dp
    tokens_wide = wide(tokens)
    own = low(tokens_wide * inv_root_mean(tokens_wide) * attn_gain)
    across_y = range(1, wires.ny)

    def on_y(pieces):
        return [[wires.over_y(piece, s) for s in across_y] for piece in pieces]

    def swap(values):
        return lax.all_to_all(values, "head", split_axis=0, concat_axis=0, tiled=True)

    turned = dict(split_axis=0, concat_axis=0, tiled=True)
    same_core = [[z * 2 + c for z in range(wires.nz)] for c in range(2)]

    def add(*values):
        return low(sum(wide(value) for value in values))

    packed_width = in_weight.shape[1]
    in_turned = in_weight.T
    in_part = wires.quarter(in_turned)
    keep_row = keep_mask.astype(jnp.float32)[None]
    ends = jnp.cumsum(seq_lengths[0])
    stacked = jnp.stack([gate_weight.T, up_weight.T, down_weight])
    unit_own = pick(stacked, wires.x, 2, 1)
    unit_other = pick(stacked, 1 - wires.x, 2, 1)
    share = out_rows * size // rows
    block = jnp.concatenate([own, wires.quarter(out_weight).reshape(rows, share)], axis=1)

    flying = {}

    def beside_line(step, values):
        if step == 1:
            by_x = wires.over_x(unit_other)
            values, flying["by_x"], flying["own"], flying["in_part"], flying["out_grad"], flying["swap"] = tie(
                values, by_x, unit_own, in_part, out_grad, wires.over_core(block)
            )
        elif step == 2:
            pair = in_order([flying["own"], flying["by_x"]], wires.x, 2)
            by_x = wires.over_x(flying["out_grad"])
            values, flying["grad_x"], flying["pair"], flying["out_grad"] = tie(
                values, by_x, pair, flying["out_grad"]
            )
        elif step == wires.nz - 1:
            by_y = [wires.over_y(flying["pair"][:2], s) for s in across_y]
            halves = [wires.over_zh_half(flying["pair"][:2], s, 0) for s in range(1, wires.nzh)]
            values, flying["by_y"], flying["pair"], flying["grad_x"], flying["halves"] = tie(
                values, by_y, flying["pair"], flying["grad_x"], halves
            )
        else:
            (values,) = tie(values)
        return values

    chunks, chips = wires.line(block, beside_line)
    others = [flying["swap"]] + [wires.over_core(chunk) for chunk in chunks[1:]]
    pieces = [piece for pair in zip(chunks, others) for piece in pair]
    places = jnp.stack(
        [(chip * 2 + (wires.c ^ r)) * rows for chip in chips for r in range(2)]
    ).astype(jnp.int32)
    pieces, unit_pair, out_grad, grad_x = tie(
        pieces, flying["pair"], flying["out_grad"], flying["grad_x"]
    )

    def shares(blocks):
        return jnp.stack([piece[:, depth:].reshape(out_rows, size) for piece in blocks])

    halves = [wires.over_zh_half(unit_pair[:2], s, 1) for s in range(1, wires.nzh)]
    out_line = shares(pieces[::2])
    out_x, out_y = wires.over_x(out_line), [wires.over_y(out_line, s) for s in across_y]
    projected, normed, attended_wide, inverses, attended = attend(
        pieces, places, in_turned, keep_row, ends, heads_here
    )
    attended, out_x, out_y, unit_pair = tie(attended, out_x, out_y, unit_pair)
    attended_here = swap(attended).reshape(wires.head, rows, out_rows)
    out_across = [wires.over_x(piece) for piece in out_y]
    by_zh_gu = [
        wires.from_halves(flying["halves"][s - 1], halves[s - 1], s) for s in range(1, wires.nzh)
    ]
    by_zh_guy = on_y(by_zh_gu)
    out_line_swap = shares(pieces[1::2])
    out_x_swap, out_y_swap = wires.over_core(out_x), [wires.over_core(piece) for piece in out_y]
    attended_here, out_across, out_x_swap, out_y_swap, unit_pair, by_zh_gu, out_line_swap = tie(
        attended_here, out_across, out_x_swap, out_y_swap, unit_pair, by_zh_gu, out_line_swap
    )
    out_across_swap = [wires.over_core(piece) for piece in out_across]

    def in_layout(line, by_x, by_y, across):
        pieces = [line, by_x]
        for piece in zip(by_y, across):
            pieces += piece
        return pieces

    out_pieces = in_layout(out_line, out_x, out_y, out_across)
    out_pieces += in_layout(out_line_swap, out_x_swap, out_y_swap, out_across_swap)
    out_whole = Whole(wires, out_pieces, wires.whole_places(chips, out_rows, size), out_rows, size)
    middle, normed_two = mix(attended_here, out_whole, tokens, ffn_gain[None])

    normed_two, unit_pair, grad_x, out_grad = tie(normed_two, unit_pair, grad_x, out_grad)
    two_x, two_z = wires.over_x(normed_two), wires.over_zl(normed_two)
    by_zh_d = [wires.over_zh(unit_pair[2:], s) for s in range(1, wires.nzh)]
    by_y_d = [wires.over_y(unit_pair[2:], s) for s in across_y]
    two_swap = wires.over_core(normed_two)
    two_x, two_z, by_zh_d, two_swap, by_y_d, unit_pair, out_grad, by_zh_guy = tie(
        two_x, two_z, by_zh_d, two_swap, by_y_d, unit_pair, out_grad, by_zh_guy
    )
    two_corner = wires.over_x(two_z)
    by_zh_dy = on_y(by_zh_d)
    grad_z = wires.over_zl(out_grad)
    two_swaps = [two_swap] + [wires.over_core(piece) for piece in (two_x, two_z)]
    two_corner, by_zh_dy, two_swaps, two_x, two_z, grad_z, attended_here = tie(
        two_corner, by_zh_dy, two_swaps, two_x, two_z, grad_z, attended_here
    )

    spot = unit_pair.shape[1], unit_pair.shape[2]
    gates = [(unit_pair[:2], 0, 2, 0, 0)] + [(flying["by_y"][s - 1], 0, 2, 0, s) for s in across_y]
    for zh in range(1, wires.nzh):
        gates.append((by_zh_gu[zh - 1], 0, 2, zh, 0))
        gates += [(by_zh_guy[zh - 1][s - 1], 0, 2, zh, s) for s in across_y]
    units = Units(wires, gates, 2, *spot)

    in_line = lax.all_to_all(
        jnp.concatenate([flying["in_part"]] * wires.nz, axis=0), "head", axis_index_groups=same_core, **turned
    ).reshape(wires.nz, packed_width, size)
    grad_corner = wires.over_x(grad_z)
    two_corner_swap = wires.over_core(two_corner)
    for_other = pick(attended_here.reshape(wires.nz, 2, rows, out_rows), 1 - wires.c, 2, 1)[:, 0]
    attended_other = wires.over_core(for_other)
    grad_swaps = [wires.over_core(grad) for grad in (out_grad, grad_x)]
    first = gate_up(list(zip([normed_two, two_x, two_z], two_swaps)), units)
    first, grad_corner, two_corner, two_corner_swap, grad_z, attended_other, grad_swaps = tie(
        first, grad_corner, two_corner, two_corner_swap, grad_z, attended_other, grad_swaps
    )
    grad_swaps += [wires.over_core(grad) for grad in (grad_z, grad_corner)]
    second = gate_up([(two_corner, two_corner_swap)], units)
    second, grad_swaps, in_line = tie(second, grad_swaps, in_line)
    grad_pairs = list(zip([out_grad, grad_x, grad_z, grad_corner], grad_swaps))
    downs = [(unit_pair[2:], 0, 1, 0, 0)] + [(by_y_d[s - 1], 0, 1, 0, s) for s in across_y]
    for zh in range(1, wires.nzh):
        downs.append((by_zh_d[zh - 1], 0, 1, zh, 0))
        downs += [(by_zh_dy[zh - 1][s - 1], 0, 1, zh, s) for s in across_y]
    units = Units(
        wires, downs + [(array, at + 1, count, zh, s) for array, at, count, zh, s in gates], 3, *spot
    )

    in_x, in_y = wires.over_x(in_line), [wires.over_y(in_line, s) for s in across_y]
    in_line_swap = wires.over_core(in_line)
    outs_co, (dnormed_c, dnormed_o), (branch_c, branch_o) = down(
        [(*grad_pairs[3], second[0], 0), (*grad_pairs[0], first[0], 0)], units
    )
    outs_co, in_x, in_y, dnormed_c, dnormed_o, branch_c, in_line_swap = tie(
        outs_co, in_x, in_y, dnormed_c, dnormed_o, branch_c, in_line_swap
    )
    swap_c, swap_o = wires.over_core(dnormed_c[1]), wires.over_core(dnormed_o[1])
    swap_b = wires.over_core(branch_c[1])
    swap_c, swap_o, swap_b, outs_co, in_x = tie(swap_c, swap_o, swap_b, outs_co, in_x)
    sum_c, sum_b = add(dnormed_c[0], swap_c), add(branch_c[0], swap_b)
    to_z, to_x = wires.over_x(sum_c), wires.over_zl(sum_b)
    in_across = [wires.over_y(in_x, s) for s in across_y]
    in_swaps = [wires.over_core(piece) for piece in (in_x, *in_y)]
    grad_x_pair, grad_z_pair, *_ = tie(grad_pairs[1], grad_pairs[2], sum_c, sum_b, outs_co)
    outs_xz, (dnormed_x, dnormed_z), (branch_x, branch_z) = down(
        [(*grad_x_pair, first[0], 1), (*grad_z_pair, first[0], 2)], units
    )
    outs_xz, dnormed_x, dnormed_z, branch_x, branch_z, to_z, to_x, in_across, in_swaps = tie(
        outs_xz, dnormed_x, dnormed_z, branch_x, branch_z, to_z, to_x, in_across, in_swaps
    )
    swap_x, swap_z = wires.over_core(dnormed_x[1]), wires.over_core(dnormed_z[1])
    sum_x = add(dnormed_x[0], swap_x)
    final_x = wires.over_x(sum_x)
    sum_z = add(dnormed_z[0], swap_z, to_z)
    final_z = wires.over_zl(sum_z)

    every = (outs_co, outs_xz, first, second)

    def grad_of(every, unit):
        (units_co, grad_co), (units_xz, grad_xz), (made, normed_oxz), (made_c, normed_c) = every
        if unit == 0:
            lefts = [(made_c, (0, 0)), (made, (0, 0)), (made, (1, 0)), (made, (2, 0))]
            rights = [(grad_co, 0), (grad_co, 1), (grad_xz, 0), (grad_xz, 1)]
        else:
            lefts = [(array, (i, unit - 1)) for array in (units_co, units_xz) for i in range(2)]
            rights = [(normed_c, 0), (normed_oxz, 0), (normed_oxz, 1), (normed_oxz, 2)]
        return unit_grad(wires, lefts, rights)

    def on_y_steps(blocks):
        return [wires.over_y(blocks[s], s) for s in across_y]

    def on_zh(totals):
        return [wires.over_zh(total, -s) for s, total in enumerate(totals, 1)]

    def totals_of(parts, sent):
        return [add(part[0], *more) for part, more in zip(parts, sent)]

    def grad_last(mine, sent):
        return wide(in_order([mine, sent], wires.x, 0))

    every, sum_x, sum_z, branch_x, branch_z = tie(every, sum_x, sum_z, branch_x, branch_z)
    swap_x, swap_z = wires.over_core(branch_x[1]), wires.over_core(branch_z[1])
    in_across_swap = [wires.over_core(piece) for piece in in_across]
    gate_parts = grad_of(every, 1)
    sum_x, sum_z = add(branch_x[0], swap_x, to_x), add(branch_z[0], swap_z)
    final_x, final_z, gate_parts, sum_x, sum_z, in_across_swap = tie(
        final_x, final_z, gate_parts, sum_x, sum_z, in_across_swap
    )
    gate_sent = [on_y_steps(part) for part in gate_parts[1:]]
    d_middle, d_mixed, ffn_gain_part, d_attended = unmix(
        (dnormed_o[0], swap_o, final_x, final_z), middle, out_grad, ffn_gain[None], out_whole, wires.head
    )
    every, d_attended, d_mixed, gate_parts, sum_x, sum_z = tie(
        every, d_attended, d_mixed, gate_parts, sum_x, sum_z
    )
    d_attended = swap(d_attended).reshape(group_rows, out_rows)
    final_x, final_z = wires.over_x(sum_x), wires.over_zl(sum_z)
    gate_back = on_zh(totals_of(gate_parts[1:], gate_sent))
    gate_sent = on_y_steps(gate_parts[0])
    other_d_mixed = wires.over_core(d_mixed)
    up_parts = grad_of(every, 2)
    up_sent = [on_y_steps(part) for part in up_parts[1:]]
    out_own, out_sent = out_grad_parts(wires, attended_here, attended_other, d_mixed, other_d_mixed)
    down_parts = grad_of(every, 0)
    d_attended, final_x, final_z, gate_back, gate_sent, up_parts, up_sent, out_own, out_sent, down_parts = tie(
        d_attended, final_x, final_z, gate_back, gate_sent, up_parts, up_sent, out_own, out_sent, down_parts
    )
    up_totals = totals_of(up_parts[1:], up_sent)
    up_back = on_zh(up_totals)
    up_sent = on_y_steps(up_parts[0])
    down_sent = [on_y_steps(part) for part in down_parts[1:]]
    out_first = [wires.over_x(out_sent[s]) for s in across_y]
    d_projected = attend_back(
        projected, ends, attended_wide, inverses, d_attended, heads_here, rows
    )
    d_projected, up_back, up_sent, down_sent, out_first = tie(
        d_projected, up_back, up_sent, down_sent, out_first
    )
    d_here = swap(d_projected)
    down_totals = totals_of(down_parts[1:], down_sent)
    out_total = [add(out_own[s], out_first[s - 1]) for s in across_y]
    down_sent = on_y_steps(down_parts[0])
    out_last = wires.over_x(out_sent[0])
    out_y = [wires.over_y(total, s) for total, s in zip(out_total, across_y)]
    swap_o = wires.over_core(branch_o[1])
    in_back, attn_gain_part = in_grad_parts(normed, d_projected, in_turned, attn_gain[None])
    firsts = [
        add(parts[0][0], *sent, *back)
        for parts, sent, back in ((gate_parts, gate_sent, gate_back), (up_parts, up_sent, up_back))
    ]
    d_here, in_back, attn_gain_part, down_sent, out_last, out_total, firsts, down_totals, swap_o = tie(
        d_here, in_back, attn_gain_part, down_sent, out_last, out_total, firsts, down_totals, swap_o
    )
    cut = packed_width // 2
    gains = jnp.concatenate([attn_gain_part, ffn_gain_part], axis=0)
    in_pieces = in_layout(in_line, in_x, in_y, in_across)
    in_pieces += in_layout(in_line_swap, in_swaps[0], in_swaps[1:], in_across_swap)
    in_whole = Whole(
        wires, in_pieces, wires.whole_places(range(wires.nz), packed_width, size), packed_width, size
    )
    down_back = on_zh(down_totals)
    in_x, in_y = wires.over_x(in_back[:cut]), [wires.over_y(in_back[cut:], s) for s in across_y]
    others = wires.over_x(jnp.stack([pick(total, 1 - wires.x, 2, 1) for total in firsts]))
    in_grad = last(d_here, in_whole, tokens, d_middle, attn_gain[None])
    in_grad, out_y, in_x, in_y, others, down_sent, down_back, gains = tie(
        in_grad, out_y, in_x, in_y, others, down_sent, down_back, gains
    )
    out_total = add(out_own[0], out_last, *out_y)
    out_turns = lax.all_to_all(out_total, "head", axis_index_groups=same_core, **turned)
    in_halves = (wires.sum_y(add(in_back[:cut], in_x)), wires.sum_x(add(in_back[cut:], *in_y)))
    totals = [*firsts, add(down_parts[0][0], *down_sent, *down_back)]
    others = [others[0], others[1], wires.over_x(pick(totals[2], 1 - wires.x, 2, 1))]
    gains = gains + wires.over_core(gains)
    out_turns, gains, others, in_halves, totals = tie(out_turns, gains, others, in_halves, totals)
    out_part = add(*[out_turns[z] for z in range(wires.nz)])
    out_x = wires.over_x(out_part)
    out_by_y = [wires.over_y(out_part, s) for s in across_y]
    output = low(middle + wide(branch_o[0]) + wide(swap_o) + wide(final_x) + wide(final_z))
    gains = gains + wires.over_zl(gains)
    gains = gains + sum(wires.over_zh(gains, s) for s in range(1, wires.nzh))
    gate_grad, up_grad, down_grad = (
        grad_last(pick(total, wires.x, 2, 1), other) for total, other in zip(totals, others)
    )
    gate_grad, up_grad = gate_grad.T, up_grad.T
    out_x, out_by_y, gains, output, gate_grad, up_grad, down_grad = tie(
        out_x, out_by_y, gains, output, gate_grad, up_grad, down_grad
    )
    out_by_yx = [wires.over_y(out_x, s) for s in across_y]
    gains_x = wires.over_x(gains)
    gains = gains + gains_x + sum(
        wires.over_y(gains, s) + wires.over_dp(gains, s) for s in across_y
    )
    out_weight_grad = wide(
        in_order(
            [
                in_order([a, b], wires.x, 1)
                for a, b in zip([out_part, *out_by_y], [out_x, *out_by_yx])
            ],
            wires.y,
            1,
        )
    )
    in_weight_grad = wide(jnp.concatenate(in_halves, axis=0)).T
    return (
        output,
        in_grad,
        gains[0],
        in_weight_grad,
        out_weight_grad,
        gains[1],
        gate_grad,
        up_grad,
        down_grad,
    )


def solution(mesh):
    return jax.shard_map(
        functools.partial(per_device, Wires(mesh)),
        mesh=mesh,
        in_specs=(
            P(("dp", "head"), None),
            P("dp"),
            P("dp", None),
            P(),
            P(None, "head"),
            P("head", None),
            P(),
            P("dp", "head"),
            P("dp", "head"),
            P("head", "dp"),
            P(("dp", "head"), None),
        ),
        out_specs=(
            P(("dp", "head"), None),
            P(("dp", "head"), None),
            P(),
            P(None, "head"),
            P("head", None),
            P(),
            P("dp", "head"),
            P("dp", "head"),
            P("head", "dp"),
        ),
        check_vma=False,
    )
```
